32 devices in a mesh: dp: 8 (over z, x), head: 4 (over y, core).
Axes of the slice: x: 2, y: 2, z: 4, core: 2. Of those that a mesh axis runs over, the one named last changes fastest.
Arguments:
- tokens: bfloat16 [32768, 768], P(('dp', 'head')), may hold values from -6 to 6
- cotangent: bfloat16 [32768, 768], P(('dp', 'head')), may hold values from -6 to 6
- lengths: int32 [32, 8], P('dp'), may hold values from 1 to 512, 1024 in all within a row
- masters: float32 [12, 768, 768], P(None, ('dp', 'head')), may hold values from -1 to 1
- vectors: float32 [12, 768], P(None, ('dp', 'head')), may hold values from -1.5 to 1.5
- left_stats: float32 [12, 768, 768], P(None, ('dp', 'head')), may hold values from -62914.56 to 254174.822, as said below
- right_stats: float32 [12, 768, 768], P(None, ('dp', 'head')), may hold values from -62914.56 to 254174.822, as said below
- vector_second: float32 [12, 768], P(None, ('dp', 'head')), may hold values from 163.84 to 1310.72
Outputs:
- output: bfloat16 [32768, 768], P(('dp', 'head'))
- input_grad: float32 [32768, 768], P(('dp', 'head'))
- block_grads: float32 [12, 768, 768], P(None, ('dp', 'head'))
- left_new: float32 [12, 768, 768], P(None, ('dp', 'head'))
- right_new: float32 [12, 768, 768], P(None, ('dp', 'head'))
- masters_new: float32 [12, 768, 768], P(None, ('dp', 'head'))
- vector_grads: float32 [12, 768], P(None, ('dp', 'head'))
- second_new: float32 [12, 768], P(None, ('dp', 'head'))
- vectors_new: float32 [12, 768], P(None, ('dp', 'head'))
The draws below stay inside these ranges and needn't reach their ends.
Inputs may be any that keep to these rules, and one draw needn't show every extreme that they name: Row r of lengths lists, in order, the lengths of the documents packed into row r of 1024 tokens; each row sums to 1024. Each block of left_stats is symmetric. Each block of right_stats is symmetric.
All inputs are finite; a program needn't handle non-finite values.
Results may differ from the reference program's by a relative error of at most 0.012.
The reference program's roundings to bfloat16 on the way count: a program that leaves them out, or rounds other values in their place, can miss the bound.
Values may be sent and summed in bfloat16 or wider, within the bound.
A program may use at most 256 MiB of HBM per device.

```python
import math
import jax
import jax.numpy as jnp
import numpy as np
from jax import lax

D = 768
HEADS = 12
HD = 64
FF = 3072
PACK = 1024
SEGS = 8
NEWTON = 8
NB = 12
NV = 12
ROWS_ALL = 32
TOKENS = 32768


def draw_masters(key, part):
    ffn_blocks = FF // D
    normal_draw = jax.random.truncated_normal(jax.random.fold_in(key, 13), -4.0, 4.0, (NB, D, D), jnp.float32)
    block_index = jnp.arange(NB)
    fan_in = jnp.where(block_index == 3, D // 8, jnp.where(block_index >= 4 + ffn_blocks, FF, D)).astype(jnp.float32)
    return normal_draw * lax.rsqrt(fan_in)[:, None, None]


def draw_vectors(key, part):
    ffn_blocks = FF // D
    biases = 0.3 * jax.random.truncated_normal(jax.random.fold_in(key, 14), -4.0, 4.0, (NV, D), jnp.float32)
    gains = 1.0 + 0.4 * jax.random.uniform(jax.random.fold_in(key, 15), (NV, D), jnp.float32, minval=-1.0, maxval=1.0)
    row_index = jnp.arange(NV)[:, None]
    is_gain = (row_index == 4 + ffn_blocks) | (row_index == 6 + ffn_blocks)
    return jnp.where(is_gain, gains, biases)


def symmetric_stats(key):
    diag_level = 0.0025 * D * TOKENS
    spread = diag_level / (5.0 * math.sqrt(D))
    upper = jax.random.uniform(jax.random.fold_in(key, 1), (NB, D, D), jnp.float32, minval=-1.732 * spread, maxval=1.732 * spread)
    off_diag = (upper + jnp.swapaxes(upper, 1, 2)) * 0.7071
    diag_vals = diag_level * jnp.exp(jax.random.uniform(jax.random.fold_in(key, 2), (NB, D, 1), jnp.float32, minval=0.0, maxval=math.log(4.0)))
    identity = jnp.eye(D, dtype=bool)
    return jnp.where(identity[None], diag_vals, off_diag)


def draw_left_stats(key, part):
    return symmetric_stats(jax.random.fold_in(key, 21))


def draw_right_stats(key, part):
    return symmetric_stats(jax.random.fold_in(key, 22))


def block_levels(own_key, shape, shards, low, top_value):
    factor_of = 1.0
    for dim, parts in shards:
        draws = jax.random.uniform(jax.random.fold_in(jax.random.fold_in(own_key, 6), dim), (parts,), jnp.float32, low / len(shards), top_value / len(shards))
        factor_of = factor_of * jnp.repeat(jnp.exp(draws), shape[dim] // parts).reshape((-1,) + (1,) * (len(shape) - 1 - dim))
    return factor_of


def profile(amount, total, bound, skew):
    loads = [(1 << 20) // math.isqrt(rank ** skew) + 1 for rank in range(2, amount + 1)]
    spare, holding = total - bound - (amount - 1), [1] * (amount - 1)
    while spare > 0:
        candidates = [i for i in range(amount - 1) if holding[i] < bound]
        pool, left = sum([loads[i] for i in candidates]), spare
        for i in candidates:
            addition = min(bound - holding[i], max(1, left * loads[i] // pool), spare)
            holding[i] = holding[i] + addition
            spare = spare - addition
    return np.array([bound] + holding)


def uneven_parts(stream_key, amount, total, bound, slope):
    if amount == 2:
        one = jax.random.randint(stream_key, (), max(1, total - bound), min(bound, total - 1) + 1)
        return jnp.stack([one, total - one])
    sizes = jnp.asarray(profile(amount, total, bound, slope), jnp.int32)
    pairs = (amount - 1) // 2
    source_of, sink = sizes[1:1 + 2 * pairs:2], sizes[2:2 + 2 * pairs:2]
    room = jnp.minimum(source_of - 1, bound - sink)
    moved = jax.random.randint(jax.random.fold_in(stream_key, 1), (pairs,), 0, 1 << 20) % (room + 1)
    sizes = sizes.at[1:1 + 2 * pairs:2].set(source_of - moved).at[2:2 + 2 * pairs:2].set(sink + moved)
    return sizes[jax.random.permutation(jax.random.fold_in(stream_key, 2), amount)]


def noise(rng, shape, width, bound, pieces=(), kind=jnp.bfloat16):
    array = jax.random.normal(rng, shape, jnp.float32) * width
    if len(pieces) > 0:
        array = block_levels(rng, shape, pieces, -0.22, 0.18) * array
    return jnp.clip(array, min=-bound, max=bound).astype(kind)


def setup_inputs(seed: int = 0) -> dict:
    splits = jax.random.split(jax.random.key(seed), 9)
    tokens = noise(splits[0], (TOKENS, D), 1.0, 6.0, ((0, 32),))
    cotangent = noise(splits[1], (TOKENS, D), 1.0, 6.0, ((0, 32),))
    lengths = jax.vmap(lambda own: uneven_parts(own, SEGS, PACK, PACK // 2, 2))(jax.random.split(splits[2], ROWS_ALL)).reshape((ROWS_ALL, SEGS)).astype(jnp.int32)
    masters = draw_masters(jax.random.fold_in(splits[8], 71), 0)
    vectors = draw_vectors(jax.random.fold_in(splits[8], 71), 0)
    left_stats = draw_left_stats(jax.random.fold_in(splits[8], 71), 0)
    right_stats = draw_right_stats(jax.random.fold_in(splits[8], 71), 0)
    vector_second = jnp.clip(jnp.exp(math.log(1310.72) - 2.0794415 * jax.random.uniform(splits[7], (NV, D), jnp.float32) ** block_levels(splits[7], (NV, D), ((1, 32),), -0.2, 0.2)), 163.84, 1310.72)
    return dict(tokens=tokens, cotangent=cotangent, lengths=lengths, masters=masters, vectors=vectors, left_stats=left_stats, right_stats=right_stats, vector_second=vector_second)


@jax.custom_vjp
def low(v):
    return lax.optimization_barrier(v.astype(jnp.bfloat16)).astype(jnp.float32)

@jax.custom_vjp
def low_back(v):
    return v

def low_keep(v):
    return (low(v), None)

def low_pass(kept, grad):
    return (grad,)

def back_keep(v):
    return (v, None)

def back_low(kept, grad):
    return (low(grad),)
low.defvjp(low_keep, low_pass)
low_back.defvjp(back_keep, back_low)
NORM_EPS = 1e-06
ROOT_EPS = 1e-06
MASK_FILL = -1e+30
BETA = 0.95
BETA_TWO = 0.99
RATE = 1.0
RATE_VEC = 0.05
PRECISE = lax.Precision.HIGHEST

def highest(left, right):
    return jnp.dot(left, right, precision=PRECISE)

def batched(left, right):
    return jnp.einsum('kij,kjl->kil', left, right, precision=PRECISE)

def layer_norm(summed, gain_row, shift_row):
    centred = summed - lax.optimization_barrier(jnp.mean(summed, axis=-1, keepdims=True))
    return centred * lax.rsqrt(lax.optimization_barrier(jnp.mean(centred * centred, axis=-1, keepdims=True)) + NORM_EPS) * gain_row + shift_row

def segment_ids(lengths):
    doc_ends = jnp.cumsum(lengths, axis=-1)
    places = jnp.arange(PACK, dtype=jnp.int32)
    return lax.optimization_barrier(jnp.sum((places[None, :, None] >= doc_ends[:, None, :]).astype(jnp.int32), axis=-1))

def attend_row(packed):
    queries, key_rows, value_rows, segments = packed
    scores = jnp.einsum('qhd,khd->hqk', queries, key_rows, precision=PRECISE) * HD ** (-0.5)
    scores = low_back(scores)
    same_doc = segments[:, None] == segments[None, :]
    scores = jnp.where(same_doc[None], scores, MASK_FILL)
    softmax_weights = low(jax.nn.softmax(scores, axis=-1))
    return jnp.einsum('hqk,khd->qhd', softmax_weights, value_rows, precision=PRECISE)

def forward(inputs, blocks, params, segments):
    ffn_blocks = FF // D
    up_weight = jnp.transpose(blocks[4:4 + ffn_blocks], (1, 0, 2)).reshape(D, FF)
    down_weight = blocks[4 + ffn_blocks:].reshape(FF, D)
    queries = low_back(low(highest(inputs, blocks[0]) + params[0]))
    key_rows = low_back(low(highest(inputs, blocks[1])))
    value_rows = low_back(low(highest(inputs, blocks[2]) + params[1]))
    row_shape = (TOKENS // PACK, PACK, HEADS, HD)
    context = lax.map(jax.checkpoint(attend_row), (queries.reshape(row_shape), key_rows.reshape(row_shape), value_rows.reshape(row_shape), segments))
    context = low_back(low(context.reshape(TOKENS, D)))
    attn_out = low_back(highest(context, blocks[3]) + params[2])
    hidden = layer_norm(inputs + attn_out, params[4 + ffn_blocks], params[5 + ffn_blocks])
    inner_act = low_back(highest(low(hidden), up_weight) + params[3:3 + ffn_blocks].reshape(FF))
    activation = low(jax.nn.gelu(inner_act, approximate=False))
    ffn_out = low_back(highest(activation, down_weight) + params[3 + ffn_blocks])
    return layer_norm(hidden + ffn_out, params[6 + ffn_blocks], params[7 + ffn_blocks])

def newton_root(statistic):
    identity = jnp.eye(D, dtype=jnp.float32)
    frob_norm = jnp.sqrt(jnp.sum(statistic * statistic) + ROOT_EPS)
    moving = statistic / frob_norm
    inverse_root = lax.rsqrt(jnp.sqrt(frob_norm)) * identity
    for iteration in range(NEWTON):
        factor = (5.0 * identity - moving) * 0.25
        inverse_root = highest(inverse_root, factor)
        if iteration + 1 < NEWTON:
            moving = highest(highest(highest(highest(factor, factor), factor), factor), moving)
    return inverse_root

def reference(tokens, cotangent, lengths, masters, vectors, left_stats, right_stats, vector_second):
    segments = segment_ids(lengths)
    blocks = lax.optimization_barrier(masters.astype(jnp.bfloat16)).astype(jnp.float32)
    params = lax.optimization_barrier(vectors.astype(jnp.bfloat16)).astype(jnp.float32)
    inputs = tokens.astype(jnp.float32)
    output, pullback = jax.vjp(lambda first, second, third: forward(first, second, third, segments), inputs, blocks, params)
    input_grad, block_grads, vector_grads = pullback(cotangent.astype(jnp.float32))
    left_new = BETA * left_stats + (1.0 - BETA) * jnp.einsum('kij,klj->kil', block_grads, block_grads, precision=PRECISE)
    right_new = BETA * right_stats + (1.0 - BETA) * jnp.einsum('kji,kjl->kil', block_grads, block_grads, precision=PRECISE)
    left_roots = jax.vmap(newton_root)(left_new)
    right_roots = jax.vmap(newton_root)(right_new)
    update = batched(batched(left_roots, block_grads), right_roots)
    masters_new = masters - RATE * update
    second_new = BETA_TWO * vector_second + (1.0 - BETA_TWO) * vector_grads * vector_grads
    vectors_new = vectors - RATE_VEC * vector_grads / (jnp.sqrt(second_new) + 1e-08)
    return (output.astype(jnp.bfloat16), input_grad, block_grads, left_new, right_new, masters_new, vector_grads, second_new, vectors_new)
```

```python
import jax, jax.numpy as jnp, numpy as np
from functools import partial
from jax import lax
from jax.experimental import pallas as pl
from jax.experimental.pallas import tpu as pltpu
from jax.sharding import PartitionSpec as P

D=768; HEADS=12; HD=64; FF=3072; PACK=1024; NEWTON=8; NB=12
NORM_EPS=1e-6
f32=jnp.float32; bf16=jnp.bfloat16
BIG=1e30
QB=256
def dot(a,b,ca=1,cb=0):
    return lax.dot_general(a,b,(((ca,),(cb,)),((),())),preferred_element_type=f32)

def doc_column(len_ref, shape, dim):
    t=lax.broadcasted_iota(jnp.int32,shape,dim)
    end=jnp.int32(0); doc=jnp.zeros(shape,jnp.int32)
    for j in range(8):
        end=end+len_ref[0,j]
        doc=doc+(t>=end).astype(jnp.int32)
    return doc

def split3(v):
    a=v.astype(bf16).astype(f32); r=v-a
    b=r.astype(bf16).astype(f32); c=r-b
    return a,b,c

def augment(base, lane, head_lo, cols):
    keep=(lane<64) if head_lo else (lane>=64)
    off=64 if head_lo else 0
    out=jnp.where(keep, base, 0.0)
    for i,c in enumerate(cols):
        out=jnp.where(lane==off+i, c, out)
    return out.astype(bf16)

def onehot_part(base, lane, head_lo, doc, minus, scale):
    keep=(lane<64) if head_lo else (lane>=64)
    off=64 if head_lo else 0
    l=lane-off
    oh=jnp.where((l>=0)&(l<8), (jnp.where(l==doc,1.0,0.0)-minus)*scale, 0.0)
    return jnp.where(keep, base, oh)

def attn_fwd_pair(p, q_ref,k_ref,v_ref, ctx_ref, lse_ref, doc):
    cols=pl.ds(pl.multiple_of(p*128,128),128)
    lane=lax.broadcasted_iota(jnp.int32,(PACK,128),1)
    kp=k_ref[:,cols].astype(f32)
    vp=v_ref[:,cols]
    kk=[onehot_part(kp,lane,lo,doc,1.0,1.0).astype(bf16) for lo in (True,False)]
    laneb=lax.broadcasted_iota(jnp.int32,(QB,128),1)
    for b in range(PACK//QB):
        rows=pl.ds(b*QB,QB)
        qp=q_ref[rows,cols].astype(f32)*0.125
        docb=doc[b*QB:(b+1)*QB]
        outs=[]
        lse_old=lse_ref[rows,:]
        for h,lo in enumerate((True,False)):
            qa=onehot_part(qp,laneb,lo,docb,0.0,BIG).astype(bf16)
            s=dot(qa,kk[h],1,1)
            m=jnp.max(s,axis=1,keepdims=True)
            e=jnp.exp(s-m)
            l=jnp.sum(e,axis=1,keepdims=True)
            o=dot(e.astype(bf16),vp)
            outs.append(o/l)
            lse_old=jnp.where(laneb==2*p+h, m+jnp.log(l), lse_old)
        lse_ref[rows,:]=lse_old
        ctx_ref[rows,cols]=jnp.where(laneb<64,outs[0],outs[1]).astype(bf16)

def layer_norm(z):
    mu=jnp.mean(z,axis=-1,keepdims=True)
    c=z-mu
    r=lax.rsqrt(jnp.mean(c*c,axis=-1,keepdims=True)+NORM_EPS)
    return c*r, r

def ka_body(len_ref,x_ref,wa_ref,p_ref,q_ref,k_ref,v_ref,ctx_ref,lse_ref,hid_ref,r1_ref,w_ref):
    pltpu.sync_copy(wa_ref.at[pl.ds(0,4)],w_ref)
    doc=doc_column(len_ref,(PACK,1),0)
    for i,(o,b) in enumerate(((q_ref,0),(k_ref,None),(v_ref,1))):
        for t in range(4):
            rows=pl.ds(t*256,256)
            y=dot(x_ref[rows,:],w_ref[i])
            if b is not None: y=y+p_ref[b:b+1,:]
            o[rows,:]=y.astype(bf16)
    def body(p,c):
        attn_fwd_pair(p,q_ref,k_ref,v_ref,ctx_ref,lse_ref,doc)
        return c
    lax.fori_loop(0,6,body,0)
    for t in range(4):
        rows=pl.ds(t*256,256)
        z=x_ref[rows,:].astype(f32)+(dot(ctx_ref[rows,:],w_ref[3])+p_ref[2:3,:])
        n,r=layer_norm(z)
        hid_ref[rows,:]=n
        r1_ref[rows,:]=jnp.broadcast_to(r,(256,128))

def call_a(lengths,x,w,params):
    V=pltpu.VMEM
    return pl.pallas_call(ka_body,
        in_specs=[pl.BlockSpec(memory_space=pltpu.SMEM),pl.BlockSpec(memory_space=V),pl.BlockSpec(memory_space=pl.ANY),pl.BlockSpec(memory_space=V)],
        out_specs=[pl.BlockSpec(memory_space=V)]*7,
        out_shape=[jax.ShapeDtypeStruct((PACK,D),bf16)]*4+[jax.ShapeDtypeStruct((PACK,128),f32),jax.ShapeDtypeStruct((PACK,D),f32),jax.ShapeDtypeStruct((PACK,128),f32)],
        scratch_shapes=[V((4,D,D),bf16)],
        compiler_params=pltpu.CompilerParams(vmem_limit_bytes=60<<20))(lengths,x,w,params)

def gelu_both(x):
    z=jnp.abs(x)*0.7071067811865476
    t=1.0/(1.0+0.3275911*z)
    e=jnp.exp(-0.5*x*x)
    poly=t*(0.254829592+t*(-0.284496736+t*(1.421413741+t*(-1.453152027+t*1.061405429))))
    half=0.5*poly*e
    phi_c=jnp.where(x>=0,1.0-half,half)
    return x*phi_c, phi_c+x*(e*0.3989422804014327)

def kb_body(cot_ref,n1_ref,r1_ref,ctx_ref,w_ref,p_ref, out_ref,dz1_ref,dctx_ref,dwo_ref,dw1_ref,dw2_ref,vec_ref, act_ref,gp_ref,dffn_ref,hlow_ref):
    TT=256
    g1,s1,g2,s2=(p_ref[i:i+1,:] for i in (8,9,10,11))
    b2=p_ref[7:8,:]
    vec_ref[...]=jnp.zeros_like(vec_ref)
    def tile(t,carry):
        rows=pl.ds(pl.multiple_of(t*TT,TT),TT)
        n1=n1_ref[rows,:]
        hid=n1*g1+s1
        hl=hid.astype(bf16)
        hlow_ref[rows,:]=hl
        ffn=None
        for c in range(4):
            inner=dot(hl,w_ref[4+c])+p_ref[3+c:4+c,:]
            a,gp=gelu_both(inner)
            al=a.astype(bf16)
            act_ref[rows,pl.ds(c*D,D)]=al
            gp_ref[rows,pl.ds(c*D,D)]=gp.astype(gp_ref.dtype)
            y=dot(al,w_ref[8+c])
            ffn=y if ffn is None else ffn+y
        z=hid+(ffn+b2)
        n2,r2=layer_norm(z)
        out_ref[rows,:]=(n2*g2+s2).astype(bf16)
        e=cot_ref[rows,:].astype(f32)
        c2=e*g2
        dz2=r2*(c2-jnp.mean(c2,axis=-1,keepdims=True)-n2*jnp.mean(c2*n2,axis=-1,keepdims=True))
        dffn=dz2.astype(bf16)
        dffn_ref[rows,:]=dffn
        vec_ref[10:11,:]+=jnp.sum(e*n2,axis=0,keepdims=True)
        vec_ref[11:12,:]+=jnp.sum(e,axis=0,keepdims=True)
        vec_ref[7:8,:]+=jnp.sum(dffn.astype(f32),axis=0,keepdims=True)
        dh=dz2
        for c in range(4):
            dact=dot(dffn,w_ref[8+c],1,1)
            din=(dact*gp_ref[rows,pl.ds(c*D,D)].astype(f32)).astype(bf16)
            gp_ref[rows,pl.ds(c*D,D)]=din.astype(gp_ref.dtype)
            vec_ref[3+c:4+c,:]+=jnp.sum(din.astype(f32),axis=0,keepdims=True)
            dh=dh+dot(din,w_ref[4+c],1,1)
        vec_ref[8:9,:]+=jnp.sum(dh*n1,axis=0,keepdims=True)
        vec_ref[9:10,:]+=jnp.sum(dh,axis=0,keepdims=True)
        c1=dh*g1
        dz1=r1_ref[rows,0:1]*(c1-jnp.mean(c1,axis=-1,keepdims=True)-n1*jnp.mean(c1*n1,axis=-1,keepdims=True))
        dz1_ref[rows,:]=dz1
        dat=dz1.astype(bf16)
        vec_ref[2:3,:]+=jnp.sum(dat.astype(f32),axis=0,keepdims=True)
        dctx_ref[rows,:]=dot(dat,w_ref[3],1,1).astype(bf16)
        return carry
    lax.fori_loop(0,PACK//TT,tile,0)
    for c in range(4):
        dw2_ref[c]=dot(act_ref[:,c*D:(c+1)*D],dffn_ref[...],0,0).astype(bf16)
        dw1_ref[c]=dot(hlow_ref[...],gp_ref[:,c*D:(c+1)*D].astype(bf16),0,0).astype(bf16)
    dwo_ref[...]=dot(ctx_ref[...],dz1_ref[...].astype(bf16),0,0).astype(bf16)

def call_b(cot,n1,r1,ctx,w,params):
    V=pltpu.VMEM
    S=jax.ShapeDtypeStruct
    return pl.pallas_call(kb_body,
        in_specs=[pl.BlockSpec(memory_space=V)]*6,
        out_specs=[pl.BlockSpec(memory_space=V)]*7,
        out_shape=[S((PACK,D),bf16),S((PACK,D),f32),S((PACK,D),bf16),S((D,D),bf16),S((4,D,D),bf16),S((4,D,D),bf16),S((16,D),f32)],
        scratch_shapes=[V((PACK,FF),bf16),V((PACK,FF),bf16),V((PACK,D),bf16),V((PACK,D),bf16)],
        compiler_params=pltpu.CompilerParams(vmem_limit_bytes=62<<20))(cot,n1,r1,ctx,w,params)

def kc_body(len_ref,x_ref,q_ref,k_ref,v_ref,ctx_ref,do_ref,lse_ref,dz1_ref,wa_ref, ig_ref,dw_ref,vec_ref, dqkv_ref, dqa_ref,w_ref):
    pltpu.sync_copy(wa_ref.at[pl.ds(0,3)],w_ref)
    doc=doc_column(len_ref,(PACK,1),0)
    lane=lax.broadcasted_iota(jnp.int32,(PACK,128),1)
    KB_=256
    def pair(p,carry):
        cols=pl.ds(pl.multiple_of(p*128,128),128)
        qp=q_ref[:,cols].astype(f32); kp=k_ref[:,cols].astype(f32); vp=v_ref[:,cols].astype(f32)
        dop=do_ref[:,cols].astype(f32); cp=ctx_ref[:,cols].astype(f32)
        prod=dop*cp
        qa=[];qm=[];doa=[];dom=[];ka=[];km=[];va=[]
        for h,lo in enumerate((True,False)):
            keep=(lane<64) if lo else (lane>=64)
            off=64 if lo else 0
            lse=jnp.sum(jnp.where(lane==2*p+h,lse_ref[...],0.0),axis=1,keepdims=True)
            dd=jnp.sum(jnp.where(keep,prod,0.0),axis=1,keepdims=True)
            q1=onehot_part(qp*0.125,lane,lo,doc,0.0,BIG)
            for i,c in enumerate(split3(-lse)): q1=jnp.where(lane==off+8+i,c,q1)
            qa.append(q1.astype(bf16)); qm.append(jnp.where(keep,qp*0.125,0.0).astype(bf16))
            k1=onehot_part(kp,lane,lo,doc,1.0,1.0)
            k1=jnp.where((lane>=off+8)&(lane<off+11),1.0,k1)
            ka.append(k1.astype(bf16)); km.append(jnp.where(keep,kp*0.125,0.0).astype(bf16))
            d1=jnp.where(keep,dop,0.0)
            dom.append(d1.astype(bf16))
            for i,c in enumerate(split3(-dd)): d1=jnp.where(lane==off+i,c,d1)
            doa.append(d1.astype(bf16))
            v1=jnp.where(keep,vp,0.0); v1=jnp.where((lane>=off)&(lane<off+3),1.0,v1)
            va.append(v1.astype(bf16))
        for b in range(PACK//KB_):
            rows=slice(b*KB_,(b+1)*KB_)
            dv=None;dk=None;dq=None
            for h in range(2):
                s=dot(ka[h][rows],qa[h],1,1)
                pr=jnp.exp(s)
                dp=dot(va[h][rows],doa[h],1,1)
                ds=(pr*dp).astype(bf16)
                a=dot(pr.astype(bf16),dom[h]); dv=a if dv is None else dv+a
                a=dot(ds,qm[h]); dk=a if dk is None else dk+a
                a=dot(ds,km[h][rows],0,0); dq=a if dq is None else dq+a
            if b==0: dqa_ref[...]=dq
            else: dqa_ref[...]+=dq
            dqkv_ref[1,rows,cols]=dk.astype(bf16)
            dqkv_ref[2,rows,cols]=dv.astype(bf16)
        dqkv_ref[0,:,cols]=dqa_ref[...].astype(bf16)
        for i in range(3):
            d=dqkv_ref[i,:,cols]
            dw_ref[i,:,cols]=dot(x_ref[...],d,0,0).astype(bf16)
            vec_ref[i:i+1,cols]=jnp.sum(d.astype(f32),axis=0,keepdims=True)
        return carry
    lax.fori_loop(0,6,pair,0)
    for t in range(4):
        rows=pl.ds(t*256,256)
        acc=dz1_ref[rows,:]
        for i in range(3):
            acc=acc+dot(dqkv_ref[i,rows,:],w_ref[i],1,1)
        ig_ref[rows,:]=acc

def call_c(lengths,x,q,k,v,ctx,do,lse,dz1,w):
    V=pltpu.VMEM; S=jax.ShapeDtypeStruct
    return pl.pallas_call(kc_body,
        in_specs=[pl.BlockSpec(memory_space=pltpu.SMEM)]+[pl.BlockSpec(memory_space=V)]*8+[pl.BlockSpec(memory_space=pl.ANY)],
        out_specs=[pl.BlockSpec(memory_space=V)]*3,
        out_shape=[S((PACK,D),f32),S((3,D,D),bf16),S((8,D),f32)],
        scratch_shapes=[V((3,PACK,D),bf16),V((PACK,128),f32),V((3,D,D),bf16)],
        compiler_params=pltpu.CompilerParams(vmem_limit_bytes=62<<20))(lengths,x,q,k,v,ctx,do,lse,dz1,w)

RB=256
def diag_sum(blk):
    i=lax.broadcasted_iota(jnp.int32,blk.shape,0); j=lax.broadcasted_iota(jnp.int32,blk.shape,1)
    return jnp.sum(jnp.where(i==j,blk,0.0),keepdims=True)
def eye_rows(rb):
    i=lax.broadcasted_iota(jnp.int32,(RB,D),0)+rb*RB; j=lax.broadcasted_iota(jnp.int32,(RB,D),1)
    return i==j
def newton(m_ref,x_ref,nb_ref,pb_ref,sb_ref,xb_ref):
    nblk=D//RB
    R=[slice(i*RB,(i+1)*RB) for i in range(nblk)]
    tot=jnp.zeros((1,1),f32); tr=jnp.zeros((1,1),f32)
    for i in range(nblk):
        blk=m_ref[R[i],:]
        tot=tot+jnp.sum(blk*blk,keepdims=True)
        tr=tr+diag_sum(blk[:,R[i]])
    c=jnp.sqrt(tot+1e-6)
    inv=1.0/c
    al=tr*inv/D
    s=lax.rsqrt(jnp.sqrt(c))
    for i in range(nblk):
        m_ref[R[i],:]=m_ref[R[i],:]*inv
    def iteration(k,al,be,first=False,last=False):
        u=5-al
        u2=u*u;u3=u2*u;u4=u2*u2
        c0=al*u4*(1/256); c1=(u4-4*al*u3)*(1/256); c2=(12*al*u2-8*u3)*(1/512)
        c3=(36*u2-24*al*u)*(1/1536); c4=(24*al-96*u)*(1/6144); c5=1/256
        for i in range(nblk):
            nb_ref[R[i],:]=jnp.where(eye_rows(i),m_ref[R[i],:]-al,m_ref[R[i],:]).astype(bf16)
            if not first: xb_ref[R[i],:]=jnp.where(eye_rows(i),x_ref[R[i],:]-be,x_ref[R[i],:]).astype(bf16)
        be2=jnp.zeros((1,1),f32); al2=jnp.zeros((1,1),f32)
        for i in range(nblk):
            n=jnp.where(eye_rows(i),m_ref[R[i],:]-al,m_ref[R[i],:])
            if not last:
                p=dot(nb_ref[R[i],:],nb_ref[...])
                pb_ref[R[i],:]=p.astype(bf16)
                m=c1*n+c2*p
                m_ref[R[i],:]=jnp.where(eye_rows(i),m+c0,m)
            if first:
                x=jnp.where(eye_rows(i),1.25-al*0.25,0.0)-0.25*n
            else:
                x=(1.25-al*0.25)*x_ref[R[i],:]-0.25*(be*n+dot(xb_ref[R[i],:],nb_ref[...]))
            x_ref[R[i],:]=x
            be2=be2+diag_sum(x[:,R[i]])
        if not last:
            for i in range(nblk):
                q=dot(nb_ref[R[i],:],pb_ref[...])
                sb_ref[R[i],:]=(c3*nb_ref[R[i],:].astype(f32)+c4*pb_ref[R[i],:].astype(f32)+c5*q).astype(bf16)
            for i in range(nblk):
                m=m_ref[R[i],:]+dot(pb_ref[R[i],:],sb_ref[...])
                m_ref[R[i],:]=m
                al2=al2+diag_sum(m[:,R[i]])
        return al2*(1/D),be2*(1/D)
    al,be=iteration(0,al,None,first=True)
    al,be=lax.fori_loop(1,7,lambda k,ab:iteration(k,*ab),(al,be))
    iteration(7,al,be,last=True)
    for i in range(nblk):
        x_ref[R[i],:]=x_ref[R[i],:]*s
def body(a_ref,x_ref,m_ref,nb,pb,sb,xb):
    m_ref[...]=a_ref[...]
    newton(m_ref,x_ref,nb,pb,sb,xb)
def call_newton(a):
    V=pltpu.VMEM
    return pl.pallas_call(body,in_specs=[pl.BlockSpec(memory_space=V)],out_specs=pl.BlockSpec(memory_space=V),
      out_shape=jax.ShapeDtypeStruct((D,D),f32),scratch_shapes=[V((D,D),f32)]+[V((D,D),bf16)]*4,
      compiler_params=pltpu.CompilerParams(vmem_limit_bytes=60<<20))(a)

NZ=4; MR=48; HC=384
MESH=pl.DeviceIdType.MESH
def rcopy(src,dst,ss,rs,dev):
    return pltpu.make_async_remote_copy(src_ref=src,dst_ref=dst,send_sem=ss,recv_sem=rs,device_id=dev,device_id_type=MESH)

class Place:
    def __init__(self):
        self.dp=lax.axis_index("dp"); self.head=lax.axis_index("head")
        self.z=self.dp//2; self.x=self.dp%2; self.y=self.head//2; self.c=self.head%2
        self.xy=self.x*2+self.y
        self.chip=self.z*4+self.xy
        self.me=self.dp*4+self.head
        self.xn=((self.dp//2)*2+(1-self.x), self.head)
        self.yn=(self.dp,(1-self.y)*2+self.c)
        self.sib=(self.dp,self.y*2+(1-self.c))
        self.cols=pl.ds(pl.multiple_of(self.c*HC,128),HC)
        self.ocols=pl.ds(pl.multiple_of((1-self.c)*HC,128),HC)
    def zpeer(self,k):
        return (((self.z+k)%NZ)*2+self.x,self.head)
    def zfrom(self,k):
        return (self.z+NZ-k)%NZ
    def neighbours(self):
        return [self.zpeer(1),self.zpeer(2),self.zpeer(3),self.xn,self.yn,self.sib]

def greet(devs):
    bar=pltpu.get_barrier_semaphore()
    for d in devs:
        pl.semaphore_signal(bar,inc=1,device_id=d,device_id_type=MESH)
    pl.semaphore_wait(bar,len(devs))

def greet_all(pc):
    bar=pltpu.get_barrier_semaphore()
    def sig(k,carry):
        t=(pc.me+k)%32
        pl.semaphore_signal(bar,inc=1,device_id=(t//4,t%4),device_id_type=MESH)
        return carry
    lax.fori_loop(1,32,sig,0)
    pl.semaphore_wait(bar,31)

class Gather:
    def __init__(self,pc,buf,ss,rs):
        self.pc,self.buf,self.ss,self.rs=pc,buf,ss,rs
    def region(self,z,xy,mine=True):
        pc=self.pc
        return self.buf.at[z,xy,:,pc.cols if mine else pc.ocols]
    def copies(self):
        pc=self.pc; al=pl.ds(0,4); lo=pl.ds(0,2); hi=pl.ds(2,2)
        xo=(1-pc.x)*2+pc.y; yo=pc.x*2+(1-pc.y); dg=(1-pc.x)*2+(1-pc.y)
        R=self.region
        def mk(i,src,dst,dev):
            return rcopy(src,dst,self.ss.at[i],self.rs.at[i],dev)
        send={}
        for k in (1,2,3): send[k-1]=(R(pc.z,pc.xy),pc.zpeer(k))
        send[3]=(R(al,pc.xy),pc.xn); send[4]=(R(al,pc.xy),pc.yn)
        send[5]=(R(hi,yo),pc.xn); send[6]=(R(lo,xo),pc.yn)
        send[7]=(R(al,pc.xy),pc.sib); send[8]=(R(al,xo),pc.sib); send[9]=(R(al,yo),pc.sib); send[10]=(R(al,dg),pc.sib)
        recv={}
        for k in (1,2,3): recv[k-1]=R(pc.zfrom(k),pc.xy)
        recv[3]=R(al,xo); recv[4]=R(al,yo); recv[5]=R(hi,dg); recv[6]=R(lo,dg)
        recv[7]=R(al,pc.xy,False); recv[8]=R(al,xo,False); recv[9]=R(al,yo,False); recv[10]=R(al,dg,False)
        self.send=[mk(i,send[i][0],send[i][0],send[i][1]) for i in range(11)]
        self.recv=[mk(i,recv[i],recv[i],pc.sib) for i in range(11)]
        return self
    def step0(self):
        for i in (0,1,2): self.send[i].start()
    def step1(self):
        for i in (0,1,2): self.recv[i].wait_recv()
        for i in (3,4,7): self.send[i].start()
    def step2(self):
        self.recv[3].wait_recv()
        for i in (6,8): self.send[i].start()
        self.recv[4].wait_recv()
        for i in (5,9): self.send[i].start()
    def step3(self):
        for i in (5,6): self.recv[i].wait_recv()
        self.send[10].start()
    def step4(self):
        for i in (7,8,9,10): self.recv[i].wait_recv()
    def done(self):
        for i in range(11): self.send[i].wait_send()
    def step(self,i):
        (self.step0,self.step1,self.step2,self.step3,self.step4)[i]()

ORDER=(0,1,2,3,4,8,5,9,6,10,7,11)
def ag_body(mas_ref,pv_ref,left_ref,right_ref, w_ref,pg_ref,st_ref, sibm,ss,rs,cs,cr,ts,tr,lsem):
    pc=Place()
    greet_all(pc)
    half=rcopy(mas_ref.at[:,:,pc.ocols],sibm,cs,cr,pc.sib)
    half.start()
    def stat(b,act):
        t=(b%4)*4+b//4
        for side,ref in enumerate((left_ref,right_ref)):
            dev=((t//2),(t%2)*2+side)
            idx=b*2+side
            mine=(pc.chip==t)&(pc.c==side)
            act(idx,ref.at[b],dev,mine)
    half.wait_recv()
    lo=pl.ds(0,24); hi=pl.ds(24,24)
    for b in ORDER:
        own=mas_ref[b,:,pc.cols]; oth=sibm[b]
        first=jnp.where(pc.c==0,own,oth); second=jnp.where(pc.c==0,oth,own)
        w_ref[b,pc.z,pc.xy,:,pc.cols]=jnp.concatenate([first,second],axis=0).astype(bf16)
    pg_ref[pc.z,pc.xy,:,pc.cols]=pv_ref[...]
    half.wait_send()
    gs=[Gather(pc,pg_ref,ss.at[12],rs.at[12]).copies()]+[Gather(pc,w_ref.at[b],ss.at[b],rs.at[b]).copies() for b in ORDER]
    for t in range(len(gs)+4):
        for s in range(5):
            if 0<=t-s<len(gs): gs[t-s].step(s)
    def start(b,carry):
        def act(idx,src,dev,mine):
            @pl.when(mine)
            def _(): pltpu.make_async_copy(src,st_ref.at[pc.me],tr).start()
            @pl.when(jnp.logical_not(mine))
            def _(): rcopy(src,st_ref.at[pc.me],ts.at[idx],tr,dev).start()
        stat(b,act)
        return carry
    lax.fori_loop(0,NB,start,0)
    for g in gs: g.done()
    def fin(b,carry):
        def act(idx,src,dev,mine):
            @pl.when(jnp.logical_not(mine))
            def _(): rcopy(src,st_ref.at[pc.me],ts.at[idx],tr,dev).wait_send()
        stat(b,act)
        return carry
    lax.fori_loop(0,NB,fin,0)
    @pl.when(pc.xy<3)
    def _(): pltpu.make_async_copy(st_ref,st_ref,tr).wait()

def call_ag(masters,pv,left,right):
    V=pltpu.VMEM; S=jax.ShapeDtypeStruct; A=pl.ANY
    B=lambda m: pl.BlockSpec(memory_space=m)
    sem=pltpu.SemaphoreType.DMA
    return pl.pallas_call(ag_body,in_specs=[B(V),B(V),B(A),B(A)],out_specs=[B(V),B(V),B(A)],
        out_shape=[S((NB,4,4,MR,D),bf16),S((4,4,16,D),bf16),S((32,24,D),f32)],
        scratch_shapes=[V((NB,24,HC),f32),sem((13,11)),sem((13,11)),sem,sem,sem((24,)),sem,sem],
        compiler_params=pltpu.CompilerParams(vmem_limit_bytes=60<<20,collective_id=0,has_side_effects=True))(masters,pv,left,right)

def params_of(pg):
    t=pg.reshape(16,16,2,HC)[:,:12,:,:24]
    return jnp.transpose(t,(1,0,2,3)).reshape(12,D).astype(f32)


class Scatter:
    def __init__(self,pc,b,g_ref,R,out_ref,gown_ref,ss,rs,os_,orr):
        self.pc,self.b,self.g=pc,b,g_ref.at[b]
        self.out,self.gown=out_ref,gown_ref
        self.os_,self.orr=os_,orr
        self.R={k:v.at[b] for k,v in R.items()}
        R=self.R
        s1,rc=R["s1"],R["rc"]
        def mk(i,src,dst,dev): return rcopy(src,dst,ss.at[b,i],rs.at[b,i],dev)
        lo=pl.ds(0,2); hi=pl.ds(2,2); al=pl.ds(0,4)
        self.core=mk(0,self.g.at[:,:,:,pc.ocols],rc,pc.sib)
        self.xa=mk(1,s1.at[lo,pl.ds((1-pc.x)*2,2)],R["xa"],pc.xn)
        self.yb=[mk(2+i,s1.at[hi,i*2+1-pc.y],R["yb"].at[i],pc.yn) for i in range(2)]
        self.ya=mk(4,R["s2a"],R["ya"],pc.yn)
        self.xb=mk(5,R["s2b"],R["xb"],pc.xn)
        self.zz=[mk(6+k-1,R["s3"].at[(pc.z+k)%NZ],R["zr"].at[k-1],pc.zpeer(k)) for k in (1,2,3)]
        self.home=mk(9,R["fin"].at[pl.ds(pl.multiple_of((1-pc.c)*24,8),24)],R["hr"],pc.sib)
        t=(b%4)*4+b//4
        self.t=t
        self.owner=[((t//2),(t%2)*2+side) for side in range(2)]
        self.to_owner=[rcopy(R["finb"],gown_ref.at[pc.chip,:,pc.cols],os_.at[b,side],orr,self.owner[side]) for side in range(2)]
        self.to_self=pltpu.make_async_copy(R["finb"],gown_ref.at[pc.chip,:,pc.cols],orr)
    def step0(self):
        self.core.start()
    def step1(self):
        pc=self.pc; R=self.R
        self.core.wait_recv()
        for z in range(4):
            R["s1"][z]=(self.g[z,:,:,pc.cols].astype(f32)+R["rc"][z].astype(f32)).astype(bf16)
        self.xa.start()
        for d in self.yb: d.start()
    def step2(self):
        pc=self.pc; R=self.R
        self.xa.wait_recv()
        s=R["s1"][0:2,pl.ds(pc.x*2,2)].astype(f32)+R["xa"][...].astype(f32)
        keep=jnp.where(pc.y==0,s[:,0],s[:,1]); give=jnp.where(pc.y==0,s[:,1],s[:,0])
        R["k2"][0:2]=keep; R["s2a"][...]=give.astype(bf16)
        self.ya.start()
        for d in self.yb: d.wait_recv()
        s0=R["s1"][2:4,pc.y].astype(f32)+R["yb"][0].astype(f32)
        s1=R["s1"][2:4,2+pc.y].astype(f32)+R["yb"][1].astype(f32)
        keep=jnp.where(pc.x==0,s0,s1); give=jnp.where(pc.x==0,s1,s0)
        R["k2"][2:4]=keep; R["s2b"][...]=give.astype(bf16)
        self.xb.start()
    def step3(self):
        R=self.R
        self.ya.wait_recv(); self.xb.wait_recv()
        a=R["k2"][0:2]+R["ya"][...].astype(f32)
        b=R["k2"][2:4]+R["xb"][...].astype(f32)
        R["k2"][0:2]=a; R["k2"][2:4]=b
        R["s3"][0:2]=a.astype(bf16); R["s3"][2:4]=b.astype(bf16)
        for d in self.zz: d.start()
    def step4(self):
        pc=self.pc; R=self.R
        for d in self.zz: d.wait_recv()
        s=R["k2"][pc.z]
        for k in range(3): s=s+R["zr"][k].astype(f32)
        R["fin"][...]=s
        R["finb"][...]=s.astype(bf16)
        self.home.start()
        @pl.when(pc.chip==self.t)
        def _():
            self.to_self.start()
            for side in range(2):
                @pl.when(pc.c!=side)
                def _(): self.to_owner[side].start()
        @pl.when(pc.chip!=self.t)
        def _():
            for d in self.to_owner: d.start()
    def step5(self):
        pc=self.pc; R=self.R
        self.home.wait_recv()
        own=R["fin"][pl.ds(pl.multiple_of(pc.c*24,8),24)]; oth=R["hr"][...]
        self.out[self.b,:,pc.cols]=own
        self.out[self.b,:,pc.ocols]=oth
    def step(self,i): (self.step0,self.step1,self.step2,self.step3,self.step4,self.step5)[i]()
    def done(self):
        pc=self.pc
        for d in [self.core,self.xa,*self.yb,self.ya,self.xb,*self.zz,self.home]: d.wait_send()
        @pl.when(pc.chip==self.t)
        def _():
            for side in range(2):
                @pl.when(pc.c!=side)
                def _(): self.to_owner[side].wait_send()
        @pl.when(pc.chip!=self.t)
        def _():
            for d in self.to_owner: d.wait_send()

def scatter_scratch(nb=NB):
    V=pltpu.VMEM
    return dict(s1=V((nb,4,4,MR,HC),bf16),rc=V((nb,4,4,MR,HC),bf16),xa=V((nb,2,2,MR,HC),bf16),yb=V((nb,2,2,MR,HC),bf16),
        s2a=V((nb,2,MR,HC),bf16),s2b=V((nb,2,MR,HC),bf16),ya=V((nb,2,MR,HC),bf16),xb=V((nb,2,MR,HC),bf16),
        k2=V((nb,4,MR,HC),f32),s3=V((nb,4,MR,HC),bf16),zr=V((nb,3,MR,HC),bf16),fin=V((nb,MR,HC),f32),finb=V((nb,MR,HC),bf16),hr=V((nb,24,HC),f32))

class VecSum:
    def __init__(self,pc,cur,buf,ss,rs):
        self.pc,self.cur,self.buf=pc,cur,buf
        zp=lambda bit: ((pc.z^bit)*2+pc.x,pc.head)
        z1=(pc.z+1-2*(pc.z%2)); z2=(pc.z+2)%4
        partners=[pc.sib,pc.xn,pc.yn,(z1*2+pc.x,pc.head),(z2*2+pc.x,pc.head)]
        self.d=[rcopy(cur.at[i],buf.at[i],ss.at[i],rs.at[i],p) for i,p in enumerate(partners)]
    def step(self,i):
        if i>0:
            self.d[i-1].wait_recv()
            self.cur[i]=self.cur[i-1]+self.buf[i-1]
        if i<5: self.d[i].start()
    def done(self):
        for d in self.d: d.wait_send()

RSORDER=(8,4,9,5,10,6,11,7,3,2,1,0)
KEYS=list(scatter_scratch())
def rs_body(g_ref,vec_ref,out_ref,vout_ref,gown_ref,*rest):
    R=dict(zip(KEYS,rest[:len(KEYS)])); vcur,vbuf,ss,rs,os_,orr,vs,vr=rest[len(KEYS):]
    pc=Place()
    greet_all(pc)
    vcur[0]=vec_ref[...]
    vsum=VecSum(pc,vcur,vbuf,vs,vr)
    sc=[Scatter(pc,b,g_ref,R,out_ref,gown_ref,ss,rs,os_,orr) for b in RSORDER]
    for t in range(len(sc)+5):
        for s in range(6):
            if 0<=t-s<len(sc): sc[t-s].step(s)
        if t<=5: vsum.step(t)
    vout_ref[...]=vcur[5]
    for s in sc: s.done()
    vsum.done()
    @pl.when(pc.xy<3)
    def _(): pltpu.make_async_copy(gown_ref,gown_ref,orr).wait()

def call_rs(g,vec):
    V=pltpu.VMEM; S=jax.ShapeDtypeStruct
    B=pl.BlockSpec(memory_space=V); sem=pltpu.SemaphoreType.DMA
    return pl.pallas_call(rs_body,in_specs=[B,B],out_specs=[B,B,B],
        out_shape=[S((NB,24,D),f32),S((16,D),f32),S((16,MR,D),bf16)],
        scratch_shapes=list(scatter_scratch().values())+[V((6,16,D),f32),V((5,16,D),f32),sem((NB,10)),sem((NB,10)),sem((NB,2)),sem,sem((5,)),sem((5,))],
        compiler_params=pltpu.CompilerParams(vmem_limit_bytes=62<<20,collective_id=1,has_side_effects=True))(g,vec)

BETA=0.95; BETA_TWO=0.99; RATE=1.0; RATE_VEC=0.05

def pack(rows):
    return jnp.concatenate([rows[:,:HC],rows[:,HC:]],axis=0).astype(bf16)
def unpack(p):
    p=p.astype(f32)
    return jnp.concatenate([p[:24],p[24:]],axis=1)

def send_rows(pc,n,base,slots,dst,ss,rsem,start):
    def one(j,carry):
        t=base+j
        @pl.when(t==pc.me)
        def _():
            if start: pltpu.make_async_copy(slots.at[j],dst,rsem).start()
        @pl.when(t!=pc.me)
        def _():
            d=rcopy(slots.at[j],dst,ss.at[j],rsem,(t//4,t%4))
            if start: d.start()
            else: d.wait_send()
        return carry
    lax.fori_loop(0,n,one,0)

def newton_body(gown_ref,stat_ref,left_ref,right_ref,mas_ref,va_ref,vec_ref,sec_ref,
                ln_ref,rn_ref,mn_ref,vg_ref,sn_ref,vn_ref,
                m_ref,x_ref,nb,pb,sb,xb,slots,ggr,uslots,ur,tb,rt,rho, gs,gr,us,ur_sem,es,er):
    pc=Place()
    greet_all(pc)
    b=pc.xy*4+pc.z
    owner=pc.xy<3
    nblk=D//RB
    @pl.when(owner)
    def _():
        for c in range(2):
            @pl.when(pc.c==c)
            def _():
                for i in range(nblk):
                    r=slice(i*RB,(i+1)*RB)
                    if c==0: p=dot(gown_ref[r,:],gown_ref[...],1,1)
                    else: p=dot(gown_ref[:,r],gown_ref[...],0,0)
                    x_ref[r,:]=(1-BETA)*p
                    m_ref[r,:]=BETA*stat_ref[r,:]+(1-BETA)*p
        def pk(i,carry):
            slots[i]=pack(x_ref[pl.ds(pl.multiple_of(i*24,8),24),:])
            return carry
        lax.fori_loop(0,32,pk,0)
        send_rows(pc,32,0,slots,ggr.at[2*b+pc.c],gs,gr,True)
        newton(m_ref,x_ref,nb,pb,sb,xb)
        tr=jnp.zeros((1,1),f32)
        for i in range(nblk):
            r=slice(i*RB,(i+1)*RB); tr=tr+diag_sum(x_ref[r,r])
        lam=tr*(1/D)
        for i in range(nblk):
            r=slice(i*RB,(i+1)*RB)
            xb[r,:]=jnp.where(eye_rows(i),x_ref[r,:]-lam,x_ref[r,:]).astype(bf16)
        H=D//2
        send_t=rcopy(tb.at[pl.ds(H,H)],tb.at[pl.ds(H,H)],es.at[0],er.at[0],pc.sib)
        send_r=rcopy(xb,rt,es.at[1],er.at[1],pc.sib)
        send_l=rcopy(rho.at[0],rho.at[1],es.at[2],er.at[2],pc.sib)
        def update(trows,right,lam_r):
            for i in range(2):
                r=pl.ds(trows+i*192,192)
                t=tb[r,:]
                m_ref[pl.ds(i*192,192),:]=lam_r*t.astype(f32)+dot(t,right[...])
        rho[0]=jnp.broadcast_to(lam,(8,128))
        @pl.when(pc.c==0)
        def _():
            for h in (1,0):
                for i in range(2):
                    r=slice(h*H+i*192,h*H+(i+1)*192)
                    tb[r,:]=(lam*gown_ref[r,:].astype(f32)+dot(xb[r,:],gown_ref[...])).astype(bf16)
                if h==1: send_t.start()
            send_r.wait_recv(); send_l.wait_recv()
            update(0,rt,rho[1,0:1,0:1])
            send_t.wait_send()
        @pl.when(pc.c==1)
        def _():
            send_r.start(); send_l.start()
            send_t.wait_recv()
            update(H,xb,lam)
            send_r.wait_send(); send_l.wait_send()
        def pk2(i,carry):
            uslots[i]=pack(m_ref[pl.ds(pl.multiple_of(i*24,8),24),:])
            return carry
        lax.fori_loop(0,16,pk2,0)
        send_rows(pc,16,pc.c*16,uslots,ur.at[b],us,ur_sem,True)
    r=lax.broadcasted_iota(jnp.int32,(D,128),1); j=lax.broadcasted_iota(jnp.int32,(D,128),0)
    pick=jnp.where((j==pc.me*24+r)&(r<24),1.0,0.0).astype(f32)
    vg=lax.dot_general(va_ref[...],pick,(((1,),(0,)),((),())),precision=lax.Precision.HIGHEST,preferred_element_type=f32)[:12,:24]
    sn=BETA_TWO*sec_ref[...]+(1-BETA_TWO)*vg*vg
    vg_ref[...]=vg; sn_ref[...]=sn
    vn_ref[...]=vec_ref[...]-RATE_VEC*vg/(jnp.sqrt(sn)+1e-8)
    pltpu.make_async_copy(ggr,ggr,gr).wait()
    def stats(i,carry):
        ln_ref[i]=BETA*left_ref[i]+unpack(ggr[2*i])
        rn_ref[i]=BETA*right_ref[i]+unpack(ggr[2*i+1])
        return carry
    lax.fori_loop(0,NB,stats,0)
    pltpu.make_async_copy(ur,ur,ur_sem).wait()
    def upd(i,carry):
        mn_ref[i]=mas_ref[i]-RATE*unpack(ur[i])
        return carry
    lax.fori_loop(0,NB,upd,0)
    @pl.when(owner)
    def _():
        send_rows(pc,32,0,slots,ggr.at[2*b+pc.c],gs,gr,False)
        send_rows(pc,16,pc.c*16,uslots,ur.at[b],us,ur_sem,False)

def call_newton_step(gown,stat,left,right,mas,va,vec,sec):
    V=pltpu.VMEM; S=jax.ShapeDtypeStruct
    B=pl.BlockSpec(memory_space=V); sem=pltpu.SemaphoreType.DMA
    rows=S((NB,24,D),f32); small=S((NB,24),f32)
    return pl.pallas_call(newton_body,in_specs=[B]*8,out_specs=[B]*6,out_shape=[rows]*3+[small]*3,
        scratch_shapes=[V((D,D),f32)]*2+[V((D,D),bf16)]*4+[V((32,48,HC),bf16),V((24,48,HC),bf16),V((16,48,HC),bf16),V((12,48,HC),bf16),V((D,D),bf16),V((D,D),bf16),V((2,8,128),f32),
            sem((32,)),sem,sem((16,)),sem,sem((3,)),sem((3,))],
        compiler_params=pltpu.CompilerParams(vmem_limit_bytes=62<<20,collective_id=2,has_side_effects=True))(gown,stat,left,right,mas,va,vec,sec)


def gather_rows(a):
    return lax.all_gather(a,("dp","head"),axis=1,tiled=True)

def doc_lengths(lengths):
    return lax.dynamic_slice_in_dim(lengths,lax.axis_index("head"),1,axis=0)

def layer(tokens,cotangent,lengths,w,params):
    q,k,v,ctx,lse,n1,r1=call_a(lengths,tokens,w,params)
    out,dz1,dctx,dwo,dw1,dw2,vec=call_b(cotangent,n1,r1,ctx,w,params)
    ig,dwqkv,vq=call_c(lengths,tokens,q,k,v,ctx,dctx,lse,dz1,w)
    terms=jnp.concatenate([dwqkv,dwo[None],dw1,dw2],axis=0)
    vec=jnp.concatenate([vq[0:1],vq[2:3],vec[2:]],axis=0)
    return out,ig,terms,vec

def on_slice(tokens,cotangent,lengths,masters,vectors,left,right,second):
    pv=jnp.pad(vectors,((0,4),(0,HC-24))).astype(bf16)
    w,pg,stat=call_ag(masters,pv,left,right)
    w=w.reshape(NB,D,D)
    params=params_of(pg)
    out,ig,terms,vec=layer(tokens,cotangent,doc_lengths(lengths),w,params)
    grads,vec_all,gown=call_rs(terms.reshape(NB,4,4,MR,D),vec)
    ln,rn,mn,vg,sn,vn=call_newton_step(gown.reshape(D,D),stat.reshape(D,D),left,right,masters,vec_all,vectors,second)
    return out,ig,grads,ln,rn,mn,vg,sn,vn

def on_any(tokens,cotangent,lengths,masters,vectors,left,right,second):
    axes=("dp","head")
    me=lax.axis_index("dp")*lax.axis_size("head")+lax.axis_index("head")
    share=masters.shape[1]
    w=gather_rows(masters.astype(bf16))
    params=gather_rows(vectors.astype(bf16)).astype(f32)
    out,ig,terms,vec=layer(tokens,cotangent,doc_lengths(lengths),w,params)
    grads=lax.psum_scatter(terms.astype(f32),axes,scatter_dimension=1,tiled=True)
    vg=lax.psum_scatter(vec[:12],axes,scatter_dimension=1,tiled=True)
    low=grads.astype(bf16)
    g=gather_rows(low)
    ein=partial(jnp.einsum,preferred_element_type=f32)
    cols=lax.dynamic_slice_in_dim(g,me*share,share,axis=2)
    ln=BETA*left+(1-BETA)*ein("kid,kjd->kij",low,g)
    rn=BETA*right+(1-BETA)*ein("kdi,kdj->kij",cols,g)
    item=jnp.minimum(me,2*NB-1)
    own=lax.dynamic_index_in_dim(jnp.concatenate([gather_rows(ln),gather_rows(rn)],axis=0),item,0,keepdims=False)
    root=call_newton(own)
    place=jnp.where((jnp.arange(2*NB)==me)[:,None,None],root[None],0.0)
    rows=lax.psum_scatter(place,axes,scatter_dimension=1,tiled=True)
    rr=gather_rows(rows[NB:])
    hi=partial(jnp.einsum,"kij,kjl->kil",precision=lax.Precision.HIGHEST)
    mn=masters-RATE*hi(hi(rows[:NB],g.astype(f32)),rr)
    sn=BETA_TWO*second+(1-BETA_TWO)*vg*vg
    vn=vectors-RATE_VEC*vg/(jnp.sqrt(sn)+1e-8)
    return out,ig,grads,ln,rn,mn,vg,sn,vn

def solution(mesh):
    rows=P(("dp","head"),None); blocks=P(None,("dp","head"),None); vecs=P(None,("dp","head"))
    on_device=on_slice if dict(mesh.shape)=={"dp":8,"head":4} else on_any
    return jax.shard_map(on_device,mesh=mesh,
        in_specs=(rows,rows,P("dp",None),blocks,vecs,blocks,blocks,vecs),
        out_specs=(rows,rows,blocks,blocks,blocks,blocks,vecs,vecs,vecs),check_vma=False)
```

```python
import jax, jax.numpy as jnp, numpy as np
from functools import partial
from jax import lax
from jax.experimental import pallas as pl
from jax.experimental.pallas import tpu as pltpu
from jax.sharding import PartitionSpec as P

D=768; HEADS=12; HD=64; FF=3072; PACK=1024; NEWTON=8; NB=12
NORM_EPS=1e-6
f32=jnp.float32; bf16=jnp.bfloat16
BIG=1e30
QB=256
def dot(a,b,ca=1,cb=0):
    return lax.dot_general(a,b,(((ca,),(cb,)),((),())),preferred_element_type=f32)

def doc_column(len_ref, shape, dim):
    t=lax.broadcasted_iota(jnp.int32,shape,dim)
    end=jnp.int32(0); doc=jnp.zeros(shape,jnp.int32)
    for j in range(8):
        end=end+len_ref[0,j]
        doc=doc+(t>=end).astype(jnp.int32)
    return doc

def split3(v):
    a=v.astype(bf16).astype(f32); r=v-a
    b=r.astype(bf16).astype(f32); c=r-b
    return a,b,c

def augment(base, lane, head_lo, cols):
    keep=(lane<64) if head_lo else (lane>=64)
    off=64 if head_lo else 0
    out=jnp.where(keep, base, 0.0)
    for i,c in enumerate(cols):
        out=jnp.where(lane==off+i, c, out)
    return out.astype(bf16)

def onehot_part(base, lane, head_lo, doc, minus, scale):
    keep=(lane<64) if head_lo else (lane>=64)
    off=64 if head_lo else 0
    l=lane-off
    oh=jnp.where((l>=0)&(l<8), (jnp.where(l==doc,1.0,0.0)-minus)*scale, 0.0)
    return jnp.where(keep, base, oh)

def attn_fwd_pair(p, q_ref,k_ref,v_ref, ctx_ref, lse_ref, doc):
    cols=pl.ds(pl.multiple_of(p*128,128),128)
    lane=lax.broadcasted_iota(jnp.int32,(PACK,128),1)
    kp=k_ref[:,cols].astype(f32)
    vp=v_ref[:,cols]
    kk=[onehot_part(kp,lane,lo,doc,1.0,1.0).astype(bf16) for lo in (True,False)]
    laneb=lax.broadcasted_iota(jnp.int32,(QB,128),1)
    for b in range(PACK//QB):
        rows=pl.ds(b*QB,QB)
        qp=q_ref[rows,cols].astype(f32)*0.125
        docb=doc[b*QB:(b+1)*QB]
        outs=[]
        lse_old=lse_ref[rows,:]
        for h,lo in enumerate((True,False)):
            qa=onehot_part(qp,laneb,lo,docb,0.0,BIG).astype(bf16)
            s=dot(qa,kk[h],1,1)
            m=jnp.max(s,axis=1,keepdims=True)
            e=jnp.exp(s-m)
            l=jnp.sum(e,axis=1,keepdims=True)
            o=dot(e.astype(bf16),vp)
            outs.append(o/l)
            lse_old=jnp.where(laneb==2*p+h, m+jnp.log(l), lse_old)
        lse_ref[rows,:]=lse_old
        ctx_ref[rows,cols]=jnp.where(laneb<64,outs[0],outs[1]).astype(bf16)

def layer_norm(z):
    mu=jnp.mean(z,axis=-1,keepdims=True)
    c=z-mu
    r=lax.rsqrt(jnp.mean(c*c,axis=-1,keepdims=True)+NORM_EPS)
    return c*r, r

def ka_body(len_ref,x_ref,wa_ref,p_ref,q_ref,k_ref,v_ref,ctx_ref,lse_ref,hid_ref,r1_ref,w_ref):
    pltpu.sync_copy(wa_ref.at[pl.ds(0,4)],w_ref)
    doc=doc_column(len_ref,(PACK,1),0)
    for i,(o,b) in enumerate(((q_ref,0),(k_ref,None),(v_ref,1))):
        for t in range(4):
            rows=pl.ds(t*256,256)
            y=dot(x_ref[rows,:],w_ref[i])
            if b is not None: y=y+p_ref[b:b+1,:]
            o[rows,:]=y.astype(bf16)
    def body(p,c):
        attn_fwd_pair(p,q_ref,k_ref,v_ref,ctx_ref,lse_ref,doc)
        return c
    lax.fori_loop(0,6,body,0)
    for t in range(4):
        rows=pl.ds(t*256,256)
        z=x_ref[rows,:].astype(f32)+(dot(ctx_ref[rows,:],w_ref[3])+p_ref[2:3,:])
        n,r=layer_norm(z)
        hid_ref[rows,:]=n
        r1_ref[rows,:]=jnp.broadcast_to(r,(256,128))

def call_a(lengths,x,w,params):
    V=pltpu.VMEM
    return pl.pallas_call(ka_body,
        in_specs=[pl.BlockSpec(memory_space=pltpu.SMEM),pl.BlockSpec(memory_space=V),pl.BlockSpec(memory_space=pl.ANY),pl.BlockSpec(memory_space=V)],
        out_specs=[pl.BlockSpec(memory_space=V)]*7,
        out_shape=[jax.ShapeDtypeStruct((PACK,D),bf16)]*4+[jax.ShapeDtypeStruct((PACK,128),f32),jax.ShapeDtypeStruct((PACK,D),f32),jax.ShapeDtypeStruct((PACK,128),f32)],
        scratch_shapes=[V((4,D,D),bf16)],
        compiler_params=pltpu.CompilerParams(vmem_limit_bytes=60<<20))(lengths,x,w,params)

def gelu_both(x):
    z=jnp.abs(x)*0.7071067811865476
    t=1.0/(1.0+0.3275911*z)
    e=jnp.exp(-0.5*x*x)
    poly=t*(0.254829592+t*(-0.284496736+t*(1.421413741+t*(-1.453152027+t*1.061405429))))
    half=0.5*poly*e
    phi_c=jnp.where(x>=0,1.0-half,half)
    return x*phi_c, phi_c+x*(e*0.3989422804014327)

def kb_body(cot_ref,n1_ref,r1_ref,ctx_ref,w_ref,p_ref, out_ref,dz1_ref,dctx_ref,dwo_ref,dw1_ref,dw2_ref,vec_ref, act_ref,gp_ref,dffn_ref,hlow_ref):
    TT=256
    g1,s1,g2,s2=(p_ref[i:i+1,:] for i in (8,9,10,11))
    b2=p_ref[7:8,:]
    vec_ref[...]=jnp.zeros_like(vec_ref)
    def tile(t,carry):
        rows=pl.ds(pl.multiple_of(t*TT,TT),TT)
        n1=n1_ref[rows,:]
        hid=n1*g1+s1
        hl=hid.astype(bf16)
        hlow_ref[rows,:]=hl
        ffn=None
        for c in range(4):
            inner=dot(hl,w_ref[4+c])+p_ref[3+c:4+c,:]
            a,gp=gelu_both(inner)
            al=a.astype(bf16)
            act_ref[rows,pl.ds(c*D,D)]=al
            gp_ref[rows,pl.ds(c*D,D)]=gp.astype(gp_ref.dtype)
            y=dot(al,w_ref[8+c])
            ffn=y if ffn is None else ffn+y
        z=hid+(ffn+b2)
        n2,r2=layer_norm(z)
        out_ref[rows,:]=(n2*g2+s2).astype(bf16)
        e=cot_ref[rows,:].astype(f32)
        c2=e*g2
        dz2=r2*(c2-jnp.mean(c2,axis=-1,keepdims=True)-n2*jnp.mean(c2*n2,axis=-1,keepdims=True))
        dffn=dz2.astype(bf16)
        dffn_ref[rows,:]=dffn
        vec_ref[10:11,:]+=jnp.sum(e*n2,axis=0,keepdims=True)
        vec_ref[11:12,:]+=jnp.sum(e,axis=0,keepdims=True)
        vec_ref[7:8,:]+=jnp.sum(dffn.astype(f32),axis=0,keepdims=True)
        dh=dz2
        for c in range(4):
            dact=dot(dffn,w_ref[8+c],1,1)
            din=(dact*gp_ref[rows,pl.ds(c*D,D)].astype(f32)).astype(bf16)
            gp_ref[rows,pl.ds(c*D,D)]=din.astype(gp_ref.dtype)
            vec_ref[3+c:4+c,:]+=jnp.sum(din.astype(f32),axis=0,keepdims=True)
            dh=dh+dot(din,w_ref[4+c],1,1)
        vec_ref[8:9,:]+=jnp.sum(dh*n1,axis=0,keepdims=True)
        vec_ref[9:10,:]+=jnp.sum(dh,axis=0,keepdims=True)
        c1=dh*g1
        dz1=r1_ref[rows,0:1]*(c1-jnp.mean(c1,axis=-1,keepdims=True)-n1*jnp.mean(c1*n1,axis=-1,keepdims=True))
        dz1_ref[rows,:]=dz1
        dat=dz1.astype(bf16)
        vec_ref[2:3,:]+=jnp.sum(dat.astype(f32),axis=0,keepdims=True)
        dctx_ref[rows,:]=dot(dat,w_ref[3],1,1).astype(bf16)
        return carry
    lax.fori_loop(0,PACK//TT,tile,0)
    for c in range(4):
        dw2_ref[c]=dot(act_ref[:,c*D:(c+1)*D],dffn_ref[...],0,0).astype(bf16)
        dw1_ref[c]=dot(hlow_ref[...],gp_ref[:,c*D:(c+1)*D].astype(bf16),0,0).astype(bf16)
    dwo_ref[...]=dot(ctx_ref[...],dz1_ref[...].astype(bf16),0,0).astype(bf16)

def call_b(cot,n1,r1,ctx,w,params):
    V=pltpu.VMEM
    S=jax.ShapeDtypeStruct
    return pl.pallas_call(kb_body,
        in_specs=[pl.BlockSpec(memory_space=V)]*6,
        out_specs=[pl.BlockSpec(memory_space=V)]*7,
        out_shape=[S((PACK,D),bf16),S((PACK,D),f32),S((PACK,D),bf16),S((D,D),bf16),S((4,D,D),bf16),S((4,D,D),bf16),S((16,D),f32)],
        scratch_shapes=[V((PACK,FF),bf16),V((PACK,FF),bf16),V((PACK,D),bf16),V((PACK,D),bf16)],
        compiler_params=pltpu.CompilerParams(vmem_limit_bytes=62<<20))(cot,n1,r1,ctx,w,params)

def kc_body(len_ref,x_ref,q_ref,k_ref,v_ref,ctx_ref,do_ref,lse_ref,dz1_ref,wa_ref, ig_ref,dw_ref,vec_ref, dqkv_ref, dqa_ref,w_ref):
    pltpu.sync_copy(wa_ref.at[pl.ds(0,3)],w_ref)
    doc=doc_column(len_ref,(PACK,1),0)
    lane=lax.broadcasted_iota(jnp.int32,(PACK,128),1)
    KB_=256
    def pair(p,carry):
        cols=pl.ds(pl.multiple_of(p*128,128),128)
        qp=q_ref[:,cols].astype(f32); kp=k_ref[:,cols].astype(f32); vp=v_ref[:,cols].astype(f32)
        dop=do_ref[:,cols].astype(f32); cp=ctx_ref[:,cols].astype(f32)
        prod=dop*cp
        qa=[];qm=[];doa=[];dom=[];ka=[];km=[];va=[]
        for h,lo in enumerate((True,False)):
            keep=(lane<64) if lo else (lane>=64)
            off=64 if lo else 0
            lse=jnp.sum(jnp.where(lane==2*p+h,lse_ref[...],0.0),axis=1,keepdims=True)
            dd=jnp.sum(jnp.where(keep,prod,0.0),axis=1,keepdims=True)
            q1=onehot_part(qp*0.125,lane,lo,doc,0.0,BIG)
            for i,c in enumerate(split3(-lse)): q1=jnp.where(lane==off+8+i,c,q1)
            qa.append(q1.astype(bf16)); qm.append(jnp.where(keep,qp*0.125,0.0).astype(bf16))
            k1=onehot_part(kp,lane,lo,doc,1.0,1.0)
            k1=jnp.where((lane>=off+8)&(lane<off+11),1.0,k1)
            ka.append(k1.astype(bf16)); km.append(jnp.where(keep,kp*0.125,0.0).astype(bf16))
            d1=jnp.where(keep,dop,0.0)
            dom.append(d1.astype(bf16))
            for i,c in enumerate(split3(-dd)): d1=jnp.where(lane==off+i,c,d1)
            doa.append(d1.astype(bf16))
            v1=jnp.where(keep,vp,0.0); v1=jnp.where((lane>=off)&(lane<off+3),1.0,v1)
            va.append(v1.astype(bf16))
        for b in range(PACK//KB_):
            rows=slice(b*KB_,(b+1)*KB_)
            dv=None;dk=None;dq=None
            for h in range(2):
                s=dot(ka[h][rows],qa[h],1,1)
                pr=jnp.exp(s)
                dp=dot(va[h][rows],doa[h],1,1)
                ds=(pr*dp).astype(bf16)
                a=dot(pr.astype(bf16),dom[h]); dv=a if dv is None else dv+a
                a=dot(ds,qm[h]); dk=a if dk is None else dk+a
                a=dot(ds,km[h][rows],0,0); dq=a if dq is None else dq+a
            if b==0: dqa_ref[...]=dq
            else: dqa_ref[...]+=dq
            dqkv_ref[1,rows,cols]=dk.astype(bf16)
            dqkv_ref[2,rows,cols]=dv.astype(bf16)
        dqkv_ref[0,:,cols]=dqa_ref[...].astype(bf16)
        for i in range(3):
            d=dqkv_ref[i,:,cols]
            dw_ref[i,:,cols]=dot(x_ref[...],d,0,0).astype(bf16)
            vec_ref[i:i+1,cols]=jnp.sum(d.astype(f32),axis=0,keepdims=True)
        return carry
    lax.fori_loop(0,6,pair,0)
    for t in range(4):
        rows=pl.ds(t*256,256)
        acc=dz1_ref[rows,:]
        for i in range(3):
            acc=acc+dot(dqkv_ref[i,rows,:],w_ref[i],1,1)
        ig_ref[rows,:]=acc

def call_c(lengths,x,q,k,v,ctx,do,lse,dz1,w):
    V=pltpu.VMEM; S=jax.ShapeDtypeStruct
    return pl.pallas_call(kc_body,
        in_specs=[pl.BlockSpec(memory_space=pltpu.SMEM)]+[pl.BlockSpec(memory_space=V)]*8+[pl.BlockSpec(memory_space=pl.ANY)],
        out_specs=[pl.BlockSpec(memory_space=V)]*3,
        out_shape=[S((PACK,D),f32),S((3,D,D),bf16),S((8,D),f32)],
        scratch_shapes=[V((3,PACK,D),bf16),V((PACK,128),f32),V((3,D,D),bf16)],
        compiler_params=pltpu.CompilerParams(vmem_limit_bytes=62<<20))(lengths,x,q,k,v,ctx,do,lse,dz1,w)

RB=256
def diag_sum(blk):
    i=lax.broadcasted_iota(jnp.int32,blk.shape,0); j=lax.broadcasted_iota(jnp.int32,blk.shape,1)
    return jnp.sum(jnp.where(i==j,blk,0.0),keepdims=True)
def eye_rows(rb):
    i=lax.broadcasted_iota(jnp.int32,(RB,D),0)+rb*RB; j=lax.broadcasted_iota(jnp.int32,(RB,D),1)
    return i==j
def newton(m_ref,x_ref,nb_ref,pb_ref,sb_ref,xb_ref):
    nblk=D//RB
    R=[slice(i*RB,(i+1)*RB) for i in range(nblk)]
    tot=jnp.zeros((1,1),f32); tr=jnp.zeros((1,1),f32)
    for i in range(nblk):
        blk=m_ref[R[i],:]
        tot=tot+jnp.sum(blk*blk,keepdims=True)
        tr=tr+diag_sum(blk[:,R[i]])
    c=jnp.sqrt(tot+1e-6)
    inv=1.0/c
    al=tr*inv/D
    s=lax.rsqrt(jnp.sqrt(c))
    for i in range(nblk):
        m_ref[R[i],:]=m_ref[R[i],:]*inv
    def iteration(k,al,be,first=False,last=False):
        u=5-al
        u2=u*u;u3=u2*u;u4=u2*u2
        c0=al*u4*(1/256); c1=(u4-4*al*u3)*(1/256); c2=(12*al*u2-8*u3)*(1/512)
        c3=(36*u2-24*al*u)*(1/1536); c4=(24*al-96*u)*(1/6144); c5=1/256
        for i in range(nblk):
            nb_ref[R[i],:]=jnp.where(eye_rows(i),m_ref[R[i],:]-al,m_ref[R[i],:]).astype(bf16)
            if not first: xb_ref[R[i],:]=jnp.where(eye_rows(i),x_ref[R[i],:]-be,x_ref[R[i],:]).astype(bf16)
        be2=jnp.zeros((1,1),f32); al2=jnp.zeros((1,1),f32)
        for i in range(nblk):
            n=jnp.where(eye_rows(i),m_ref[R[i],:]-al,m_ref[R[i],:])
            if not last:
                p=dot(nb_ref[R[i],:],nb_ref[...])
                pb_ref[R[i],:]=p.astype(bf16)
                m=c1*n+c2*p
                m_ref[R[i],:]=jnp.where(eye_rows(i),m+c0,m)
            if first:
                x=jnp.where(eye_rows(i),1.25-al*0.25,0.0)-0.25*n
            else:
                x=(1.25-al*0.25)*x_ref[R[i],:]-0.25*(be*n+dot(xb_ref[R[i],:],nb_ref[...]))
            x_ref[R[i],:]=x
            be2=be2+diag_sum(x[:,R[i]])
        if not last:
            for i in range(nblk):
                q=dot(nb_ref[R[i],:],pb_ref[...])
                sb_ref[R[i],:]=(c3*nb_ref[R[i],:].astype(f32)+c4*pb_ref[R[i],:].astype(f32)+c5*q).astype(bf16)
            for i in range(nblk):
                m=m_ref[R[i],:]+dot(pb_ref[R[i],:],sb_ref[...])
                m_ref[R[i],:]=m
                al2=al2+diag_sum(m[:,R[i]])
        return al2*(1/D),be2*(1/D)
    al,be=iteration(0,al,None,first=True)
    al,be=lax.fori_loop(1,7,lambda k,ab:iteration(k,*ab),(al,be))
    iteration(7,al,be,last=True)
    for i in range(nblk):
        x_ref[R[i],:]=x_ref[R[i],:]*s
def body(a_ref,x_ref,m_ref,nb,pb,sb,xb):
    m_ref[...]=a_ref[...]
    newton(m_ref,x_ref,nb,pb,sb,xb)
def call_newton(a):
    V=pltpu.VMEM
    return pl.pallas_call(body,in_specs=[pl.BlockSpec(memory_space=V)],out_specs=pl.BlockSpec(memory_space=V),
      out_shape=jax.ShapeDtypeStruct((D,D),f32),scratch_shapes=[V((D,D),f32)]+[V((D,D),bf16)]*4,
      compiler_params=pltpu.CompilerParams(vmem_limit_bytes=60<<20))(a)

NZ=4; MR=48; HC=384
MESH=pl.DeviceIdType.MESH
def rcopy(src,dst,ss,rs,dev):
    return pltpu.make_async_remote_copy(src_ref=src,dst_ref=dst,send_sem=ss,recv_sem=rs,device_id=dev,device_id_type=MESH)

class Place:
    def __init__(self):
        self.dp=lax.axis_index("dp"); self.head=lax.axis_index("head")
        self.z=self.dp//2; self.x=self.dp%2; self.y=self.head//2; self.c=self.head%2
        self.xy=self.x*2+self.y
        self.chip=self.z*4+self.xy
        self.me=self.dp*4+self.head
        self.xn=((self.dp//2)*2+(1-self.x), self.head)
        self.yn=(self.dp,(1-self.y)*2+self.c)
        self.sib=(self.dp,self.y*2+(1-self.c))
        self.cols=pl.ds(pl.multiple_of(self.c*HC,128),HC)
        self.ocols=pl.ds(pl.multiple_of((1-self.c)*HC,128),HC)
    def zpeer(self,k):
        return (((self.z+k)%NZ)*2+self.x,self.head)
    def zfrom(self,k):
        return (self.z+NZ-k)%NZ
    def neighbours(self):
        return [self.zpeer(1),self.zpeer(2),self.zpeer(3),self.xn,self.yn,self.sib]

def greet(devs):
    bar=pltpu.get_barrier_semaphore()
    for d in devs:
        pl.semaphore_signal(bar,inc=1,device_id=d,device_id_type=MESH)
    pl.semaphore_wait(bar,len(devs))

def greet_all(pc):
    bar=pltpu.get_barrier_semaphore()
    def sig(k,carry):
        t=(pc.me+k)%32
        pl.semaphore_signal(bar,inc=1,device_id=(t//4,t%4),device_id_type=MESH)
        return carry
    lax.fori_loop(1,32,sig,0)
    pl.semaphore_wait(bar,31)

class Gather:
    def __init__(self,pc,buf,ss,rs):
        self.pc,self.buf,self.ss,self.rs=pc,buf,ss,rs
    def region(self,z,xy,mine=True):
        pc=self.pc
        return self.buf.at[z,xy,:,pc.cols if mine else pc.ocols]
    def copies(self):
        pc=self.pc; al=pl.ds(0,4); lo=pl.ds(0,2); hi=pl.ds(2,2)
        xo=(1-pc.x)*2+pc.y; yo=pc.x*2+(1-pc.y); dg=(1-pc.x)*2+(1-pc.y)
        R=self.region
        def mk(i,src,dst,dev):
            return rcopy(src,dst,self.ss.at[i],self.rs.at[i],dev)
        send={}
        for k in (1,2,3): send[k-1]=(R(pc.z,pc.xy),pc.zpeer(k))
        send[3]=(R(al,pc.xy),pc.xn); send[4]=(R(al,pc.xy),pc.yn)
        send[5]=(R(hi,yo),pc.xn); send[6]=(R(lo,xo),pc.yn)
        send[7]=(R(al,pc.xy),pc.sib); send[8]=(R(al,xo),pc.sib); send[9]=(R(al,yo),pc.sib); send[10]=(R(al,dg),pc.sib)
        recv={}
        for k in (1,2,3): recv[k-1]=R(pc.zfrom(k),pc.xy)
        recv[3]=R(al,xo); recv[4]=R(al,yo); recv[5]=R(hi,dg); recv[6]=R(lo,dg)
        recv[7]=R(al,pc.xy,False); recv[8]=R(al,xo,False); recv[9]=R(al,yo,False); recv[10]=R(al,dg,False)
        self.send=[partial(mk,i,send[i][0],send[i][0],send[i][1]) for i in range(11)]
        self.recv=[partial(mk,i,recv[i],recv[i],pc.sib) for i in range(11)]
        return self
    def step0(self):
        for i in (0,1,2): self.send[i]().start()
    def step1(self):
        for i in (0,1,2): self.recv[i]().wait_recv()
        for i in (3,4,7): self.send[i]().start()
    def step2(self):
        self.recv[3]().wait_recv()
        for i in (6,8): self.send[i]().start()
        self.recv[4]().wait_recv()
        for i in (5,9): self.send[i]().start()
    def step3(self):
        for i in (5,6): self.recv[i]().wait_recv()
        self.send[10]().start()
    def step4(self):
        for i in (7,8,9,10): self.recv[i]().wait_recv()
    def done(self):
        for i in range(11): self.send[i]().wait_send()
    def step(self,i):
        (self.step0,self.step1,self.step2,self.step3,self.step4)[i]()

ORDER=(0,1,2,3,4,8,5,9,6,10,7,11)
def ag_body(mas_ref,pv_ref,left_ref,right_ref, w_ref,pg_ref,st_ref, sibm,ss,rs,cs,cr,ts,tr,lsem):
    pc=Place()
    greet_all(pc)
    half=rcopy(mas_ref.at[:,:,pc.ocols],sibm,cs,cr,pc.sib)
    half.start()
    def stat(b,act):
        t=(b%4)*4+b//4
        for side,ref in enumerate((left_ref,right_ref)):
            dev=((t//2),(t%2)*2+side)
            idx=b*2+side
            mine=(pc.chip==t)&(pc.c==side)
            act(idx,ref.at[b],dev,mine)
    half.wait_recv()
    lo=pl.ds(0,24); hi=pl.ds(24,24)
    for b in ORDER:
        own=mas_ref[b,:,pc.cols]; oth=sibm[b]
        first=jnp.where(pc.c==0,own,oth); second=jnp.where(pc.c==0,oth,own)
        w_ref[b,pc.z,pc.xy,:,pc.cols]=jnp.concatenate([first,second],axis=0).astype(bf16)
    pg_ref[pc.z,pc.xy,:,pc.cols]=pv_ref[...]
    half.wait_send()
    gs=[Gather(pc,pg_ref,ss.at[12],rs.at[12]).copies()]+[Gather(pc,w_ref.at[b],ss.at[b],rs.at[b]).copies() for b in ORDER]
    for t in range(len(gs)+4):
        for s in range(5):
            if 0<=t-s<len(gs): gs[t-s].step(s)
    def start(b,carry):
        def act(idx,src,dev,mine):
            @pl.when(mine)
            def _(): pltpu.make_async_copy(src,st_ref.at[pc.me],tr).start()
            @pl.when(jnp.logical_not(mine))
            def _(): rcopy(src,st_ref.at[pc.me],ts.at[idx],tr,dev).start()
        stat(b,act)
        return carry
    lax.fori_loop(0,NB,start,0)
    for g in gs: g.done()
    def fin(b,carry):
        def act(idx,src,dev,mine):
            @pl.when(jnp.logical_not(mine))
            def _(): rcopy(src,st_ref.at[pc.me],ts.at[idx],tr,dev).wait_send()
        stat(b,act)
        return carry
    lax.fori_loop(0,NB,fin,0)
    @pl.when(pc.xy<3)
    def _(): pltpu.make_async_copy(st_ref,st_ref,tr).wait()

def call_ag(masters,pv,left,right):
    V=pltpu.VMEM; S=jax.ShapeDtypeStruct; A=pl.ANY
    B=lambda m: pl.BlockSpec(memory_space=m)
    sem=pltpu.SemaphoreType.DMA
    return pl.pallas_call(ag_body,in_specs=[B(V),B(V),B(A),B(A)],out_specs=[B(V),B(V),B(A)],
        out_shape=[S((NB,4,4,MR,D),bf16),S((4,4,16,D),bf16),S((32,24,D),f32)],
        scratch_shapes=[V((NB,24,HC),f32),sem((13,11)),sem((13,11)),sem,sem,sem((24,)),sem,sem],
        compiler_params=pltpu.CompilerParams(vmem_limit_bytes=60<<20,collective_id=0,has_side_effects=True))(masters,pv,left,right)

def params_of(pg):
    t=pg.reshape(16,16,2,HC)[:,:12,:,:24]
    return jnp.transpose(t,(1,0,2,3)).reshape(12,D).astype(f32)


class Scatter:
    def __init__(self,pc,b,g_ref,R,out_ref,gown_ref,ss,rs,os_,orr):
        self.pc,self.b,self.g=pc,b,g_ref.at[b]
        self.out,self.gown=out_ref,gown_ref
        self.os_,self.orr=os_,orr
        self.R={k:v.at[b] for k,v in R.items()}
        R=self.R
        s1,rc=R["s1"],R["rc"]
        def mk(i,src,dst,dev): return rcopy(src,dst,ss.at[b,i],rs.at[b,i],dev)
        lo=pl.ds(0,2); hi=pl.ds(2,2); al=pl.ds(0,4)
        self.core=mk(0,self.g.at[:,:,:,pc.ocols],rc,pc.sib)
        self.xa=mk(1,s1.at[lo,pl.ds((1-pc.x)*2,2)],R["xa"],pc.xn)
        self.yb=[mk(2+i,s1.at[hi,i*2+1-pc.y],R["yb"].at[i],pc.yn) for i in range(2)]
        self.ya=mk(4,R["s2a"],R["ya"],pc.yn)
        self.xb=mk(5,R["s2b"],R["xb"],pc.xn)
        self.zz=[mk(6+k-1,R["s3"].at[(pc.z+k)%NZ],R["zr"].at[k-1],pc.zpeer(k)) for k in (1,2,3)]
        self.home=mk(9,R["fin"].at[pl.ds(pl.multiple_of((1-pc.c)*24,8),24)],R["hr"],pc.sib)
        t=(b%4)*4+b//4
        self.t=t
        self.owner=[((t//2),(t%2)*2+side) for side in range(2)]
        self.to_owner=[rcopy(R["finb"],gown_ref.at[pc.chip,:,pc.cols],os_.at[b,side],orr,self.owner[side]) for side in range(2)]
        self.to_self=pltpu.make_async_copy(R["finb"],gown_ref.at[pc.chip,:,pc.cols],orr)
    def step0(self):
        self.core.start()
    def step1(self):
        pc=self.pc; R=self.R
        self.core.wait_recv()
        for z in range(4):
            R["s1"][z]=(self.g[z,:,:,pc.cols].astype(f32)+R["rc"][z].astype(f32)).astype(bf16)
        self.xa.start()
        for d in self.yb: d.start()
    def step2(self):
        pc=self.pc; R=self.R
        self.xa.wait_recv()
        s=R["s1"][0:2,pl.ds(pc.x*2,2)].astype(f32)+R["xa"][...].astype(f32)
        keep=jnp.where(pc.y==0,s[:,0],s[:,1]); give=jnp.where(pc.y==0,s[:,1],s[:,0])
        R["k2"][0:2]=keep; R["s2a"][...]=give.astype(bf16)
        self.ya.start()
        for d in self.yb: d.wait_recv()
        s0=R["s1"][2:4,pc.y].astype(f32)+R["yb"][0].astype(f32)
        s1=R["s1"][2:4,2+pc.y].astype(f32)+R["yb"][1].astype(f32)
        keep=jnp.where(pc.x==0,s0,s1); give=jnp.where(pc.x==0,s1,s0)
        R["k2"][2:4]=keep; R["s2b"][...]=give.astype(bf16)
        self.xb.start()
    def step3(self):
        R=self.R
        self.ya.wait_recv(); self.xb.wait_recv()
        a=R["k2"][0:2]+R["ya"][...].astype(f32)
        b=R["k2"][2:4]+R["xb"][...].astype(f32)
        R["k2"][0:2]=a; R["k2"][2:4]=b
        R["s3"][0:2]=a.astype(bf16); R["s3"][2:4]=b.astype(bf16)
        for d in self.zz: d.start()
    def step4(self):
        pc=self.pc; R=self.R
        for d in self.zz: d.wait_recv()
        s=R["k2"][pc.z]
        for k in range(3): s=s+R["zr"][k].astype(f32)
        R["fin"][...]=s
        R["finb"][...]=s.astype(bf16)
        self.home.start()
        @pl.when(pc.chip==self.t)
        def _():
            self.to_self.start()
            for side in range(2):
                @pl.when(pc.c!=side)
                def _(): self.to_owner[side].start()
        @pl.when(pc.chip!=self.t)
        def _():
            for d in self.to_owner: d.start()
    def step5(self):
        pc=self.pc; R=self.R
        self.home.wait_recv()
        own=R["fin"][pl.ds(pl.multiple_of(pc.c*24,8),24)]; oth=R["hr"][...]
        self.out[self.b,:,pc.cols]=own
        self.out[self.b,:,pc.ocols]=oth
    def step(self,i): (self.step0,self.step1,self.step2,self.step3,self.step4,self.step5)[i]()
    def done(self):
        pc=self.pc
        for d in [self.core,self.xa,*self.yb,self.ya,self.xb,*self.zz,self.home]: d.wait_send()
        @pl.when(pc.chip==self.t)
        def _():
            for side in range(2):
                @pl.when(pc.c!=side)
                def _(): self.to_owner[side].wait_send()
        @pl.when(pc.chip!=self.t)
        def _():
            for d in self.to_owner: d.wait_send()

def scatter_scratch(nb=NB):
    V=pltpu.VMEM
    return dict(s1=V((nb,4,4,MR,HC),bf16),rc=V((nb,4,4,MR,HC),bf16),xa=V((nb,2,2,MR,HC),bf16),yb=V((nb,2,2,MR,HC),bf16),
        s2a=V((nb,2,MR,HC),bf16),s2b=V((nb,2,MR,HC),bf16),ya=V((nb,2,MR,HC),bf16),xb=V((nb,2,MR,HC),bf16),
        k2=V((nb,4,MR,HC),f32),s3=V((nb,4,MR,HC),bf16),zr=V((nb,3,MR,HC),bf16),fin=V((nb,MR,HC),f32),finb=V((nb,MR,HC),bf16),hr=V((nb,24,HC),f32))

class VecSum:
    def __init__(self,pc,cur,buf,ss,rs):
        self.pc,self.cur,self.buf=pc,cur,buf
        zp=lambda bit: ((pc.z^bit)*2+pc.x,pc.head)
        z1=(pc.z+1-2*(pc.z%2)); z2=(pc.z+2)%4
        partners=[pc.sib,pc.xn,pc.yn,(z1*2+pc.x,pc.head),(z2*2+pc.x,pc.head)]
        self.d=[rcopy(cur.at[i],buf.at[i],ss.at[i],rs.at[i],p) for i,p in enumerate(partners)]
    def step(self,i):
        if i>0:
            self.d[i-1].wait_recv()
            self.cur[i]=self.cur[i-1]+self.buf[i-1]
        if i<5: self.d[i].start()
    def done(self):
        for d in self.d: d.wait_send()

RSORDER=(8,4,9,5,10,6,11,7,3,2,1,0)
KEYS=list(scatter_scratch())
def rs_body(g_ref,vec_ref,out_ref,vout_ref,gown_ref,*rest):
    R=dict(zip(KEYS,rest[:len(KEYS)])); vcur,vbuf,ss,rs,os_,orr,vs,vr=rest[len(KEYS):]
    pc=Place()
    greet_all(pc)
    vcur[0]=vec_ref[...]
    vsum=VecSum(pc,vcur,vbuf,vs,vr)
    sc=[Scatter(pc,b,g_ref,R,out_ref,gown_ref,ss,rs,os_,orr) for b in RSORDER]
    for t in range(len(sc)+5):
        for s in range(6):
            if 0<=t-s<len(sc): sc[t-s].step(s)
        if t<=5: vsum.step(t)
    vout_ref[...]=vcur[5]
    for s in sc: s.done()
    vsum.done()
    @pl.when(pc.xy<3)
    def _(): pltpu.make_async_copy(gown_ref,gown_ref,orr).wait()

def call_rs(g,vec):
    V=pltpu.VMEM; S=jax.ShapeDtypeStruct
    B=pl.BlockSpec(memory_space=V); sem=pltpu.SemaphoreType.DMA
    return pl.pallas_call(rs_body,in_specs=[B,B],out_specs=[B,B,B],
        out_shape=[S((NB,24,D),f32),S((16,D),f32),S((16,MR,D),bf16)],
        scratch_shapes=list(scatter_scratch().values())+[V((6,16,D),f32),V((5,16,D),f32),sem((NB,10)),sem((NB,10)),sem((NB,2)),sem,sem((5,)),sem((5,))],
        compiler_params=pltpu.CompilerParams(vmem_limit_bytes=62<<20,collective_id=1,has_side_effects=True))(g,vec)

BETA=0.95; BETA_TWO=0.99; RATE=1.0; RATE_VEC=0.05

def pack(rows):
    return jnp.concatenate([rows[:,:HC],rows[:,HC:]],axis=0).astype(bf16)
def unpack(p):
    p=p.astype(f32)
    return jnp.concatenate([p[:24],p[24:]],axis=1)

def send_rows(pc,n,base,slots,dst,ss,rsem,start):
    def one(j,carry):
        t=base+j
        @pl.when(t==pc.me)
        def _():
            if start: pltpu.make_async_copy(slots.at[j],dst,rsem).start()
        @pl.when(t!=pc.me)
        def _():
            d=rcopy(slots.at[j],dst,ss.at[j],rsem,(t//4,t%4))
            if start: d.start()
            else: d.wait_send()
        return carry
    lax.fori_loop(0,n,one,0)

def newton_body(gown_ref,stat_ref,left_ref,right_ref,mas_ref,va_ref,vec_ref,sec_ref,
                ln_ref,rn_ref,mn_ref,vg_ref,sn_ref,vn_ref,
                m_ref,x_ref,nb,pb,sb,xb,slots,ggr,uslots,ur,tb,rt,rho, gs,gr,us,ur_sem,es,er):
    pc=Place()
    greet_all(pc)
    b=pc.xy*4+pc.z
    owner=pc.xy<3
    nblk=D//RB
    @pl.when(owner)
    def _():
        for c in range(2):
            @pl.when(pc.c==c)
            def _():
                for i in range(nblk):
                    r=slice(i*RB,(i+1)*RB)
                    if c==0: p=dot(gown_ref[r,:],gown_ref[...],1,1)
                    else: p=dot(gown_ref[:,r],gown_ref[...],0,0)
                    x_ref[r,:]=(1-BETA)*p
                    m_ref[r,:]=BETA*stat_ref[r,:]+(1-BETA)*p
        def pk(i,carry):
            slots[i]=pack(x_ref[pl.ds(pl.multiple_of(i*24,8),24),:])
            return carry
        lax.fori_loop(0,32,pk,0)
        send_rows(pc,32,0,slots,ggr.at[2*b+pc.c],gs,gr,True)
        newton(m_ref,x_ref,nb,pb,sb,xb)
        tr=jnp.zeros((1,1),f32)
        for i in range(nblk):
            r=slice(i*RB,(i+1)*RB); tr=tr+diag_sum(x_ref[r,r])
        lam=tr*(1/D)
        for i in range(nblk):
            r=slice(i*RB,(i+1)*RB)
            xb[r,:]=jnp.where(eye_rows(i),x_ref[r,:]-lam,x_ref[r,:]).astype(bf16)
        H=D//2
        send_t=rcopy(tb.at[pl.ds(H,H)],tb.at[pl.ds(H,H)],es.at[0],er.at[0],pc.sib)
        send_r=rcopy(xb,rt,es.at[1],er.at[1],pc.sib)
        send_l=rcopy(rho.at[0],rho.at[1],es.at[2],er.at[2],pc.sib)
        def update(trows,right,lam_r):
            for i in range(2):
                r=pl.ds(trows+i*192,192)
                t=tb[r,:]
                m_ref[pl.ds(i*192,192),:]=lam_r*t.astype(f32)+dot(t,right[...])
        rho[0]=jnp.broadcast_to(lam,(8,128))
        @pl.when(pc.c==0)
        def _():
            for h in (1,0):
                for i in range(2):
                    r=slice(h*H+i*192,h*H+(i+1)*192)
                    tb[r,:]=(lam*gown_ref[r,:].astype(f32)+dot(xb[r,:],gown_ref[...])).astype(bf16)
                if h==1: send_t.start()
            send_r.wait_recv(); send_l.wait_recv()
            update(0,rt,rho[1,0:1,0:1])
            send_t.wait_send()
        @pl.when(pc.c==1)
        def _():
            send_r.start(); send_l.start()
            send_t.wait_recv()
            update(H,xb,lam)
            send_r.wait_send(); send_l.wait_send()
        def pk2(i,carry):
            uslots[i]=pack(m_ref[pl.ds(pl.multiple_of(i*24,8),24),:])
            return carry
        lax.fori_loop(0,16,pk2,0)
        send_rows(pc,16,pc.c*16,uslots,ur.at[b],us,ur_sem,True)
    r=lax.broadcasted_iota(jnp.int32,(D,128),1); j=lax.broadcasted_iota(jnp.int32,(D,128),0)
    pick=jnp.where((j==pc.me*24+r)&(r<24),1.0,0.0).astype(f32)
    vg=lax.dot_general(va_ref[...],pick,(((1,),(0,)),((),())),precision=lax.Precision.HIGHEST,preferred_element_type=f32)[:12,:24]
    sn=BETA_TWO*sec_ref[...]+(1-BETA_TWO)*vg*vg
    vg_ref[...]=vg; sn_ref[...]=sn
    vn_ref[...]=vec_ref[...]-RATE_VEC*vg/(jnp.sqrt(sn)+1e-8)
    pltpu.make_async_copy(ggr,ggr,gr).wait()
    def stats(i,carry):
        ln_ref[i]=BETA*left_ref[i]+unpack(ggr[2*i])
        rn_ref[i]=BETA*right_ref[i]+unpack(ggr[2*i+1])
        return carry
    lax.fori_loop(0,NB,stats,0)
    pltpu.make_async_copy(ur,ur,ur_sem).wait()
    def upd(i,carry):
        mn_ref[i]=mas_ref[i]-RATE*unpack(ur[i])
        return carry
    lax.fori_loop(0,NB,upd,0)
    @pl.when(owner)
    def _():
        send_rows(pc,32,0,slots,ggr.at[2*b+pc.c],gs,gr,False)
        send_rows(pc,16,pc.c*16,uslots,ur.at[b],us,ur_sem,False)

def call_newton_step(gown,stat,left,right,mas,va,vec,sec):
    V=pltpu.VMEM; S=jax.ShapeDtypeStruct
    B=pl.BlockSpec(memory_space=V); sem=pltpu.SemaphoreType.DMA
    rows=S((NB,24,D),f32); small=S((NB,24),f32)
    return pl.pallas_call(newton_body,in_specs=[B]*8,out_specs=[B]*6,out_shape=[rows]*3+[small]*3,
        scratch_shapes=[V((D,D),f32)]*2+[V((D,D),bf16)]*4+[V((32,48,HC),bf16),V((24,48,HC),bf16),V((16,48,HC),bf16),V((12,48,HC),bf16),V((D,D),bf16),V((D,D),bf16),V((2,8,128),f32),
            sem((32,)),sem,sem((16,)),sem,sem((3,)),sem((3,))],
        compiler_params=pltpu.CompilerParams(vmem_limit_bytes=62<<20,collective_id=2,has_side_effects=True))(gown,stat,left,right,mas,va,vec,sec)


def place_params(pg_ref,p_ref):
    r=lax.broadcasted_iota(jnp.int32,(128,D),0); j=lax.broadcasted_iota(jnp.int32,(128,D),1)
    p_ref[...]=jnp.zeros_like(p_ref)
    def chip(m,carry):
        for c in range(2):
            sel=jnp.where((j==(m*2+c)*24+r)&(r<24),1.0,0.0).astype(bf16)
            p_ref[...]+=dot(pg_ref[m//4,m%4,:,c*HC:c*HC+128],sel)
        return carry
    lax.fori_loop(0,16,chip,0)

def keys_of_pair(p,k_ref,ka_ref,doc):
    cols=pl.ds(pl.multiple_of(p*128,128),128)
    lane=lax.broadcasted_iota(jnp.int32,(PACK,128),1)
    kp=k_ref[:,cols].astype(f32)
    for h,lo in enumerate((True,False)):
        ka_ref[h]=onehot_part(kp,lane,lo,doc,1.0,1.0).astype(bf16)

def attend_block(p,b,q_ref,v_ref,ka_ref,ctx_ref,lse_ref,doc_ref):
    cols=pl.ds(pl.multiple_of(p*128,128),128)
    rows=pl.ds(pl.multiple_of(b*QB,QB),QB)
    lane=lax.broadcasted_iota(jnp.int32,(QB,128),1)
    vp=v_ref[:,cols]
    qp=q_ref[rows,cols].astype(f32)*0.125
    doc=doc_ref[rows,:]
    outs=[]
    lse=lse_ref[rows,:]
    for h,lo in enumerate((True,False)):
        qa=onehot_part(qp,lane,lo,doc,0.0,BIG).astype(bf16)
        s=dot(qa,ka_ref[h],1,1)
        m=jnp.max(s,axis=1,keepdims=True)
        e=jnp.exp(s-m)
        l=jnp.sum(e,axis=1,keepdims=True)
        o=dot(e.astype(bf16),vp)
        outs.append(o/l)
        lse=jnp.where(lane==2*p+h,m+jnp.log(l),lse)
    lse_ref[rows,:]=lse
    ctx_ref[rows,cols]=jnp.where(lane<64,outs[0],outs[1]).astype(bf16)

AORDER=(0,1,2,3,4,8,5,9,6,10,7,11)
TT=256
def front_body(len_ref,x_ref,cot_ref,mas_ref,pv_ref,left_ref,right_ref,
               out_o,q_o,k_o,v_o,ctx_o,lse_o,act_o,din_o,dffn_o,hlow_o,dz1_o,dctx_o,wq_o,vec_o,st_ref,
               w_ref,pg_ref,p_ref,sibm,q,k,v,ctx,lse,doc,ka,n1,r1,hlow,acc,act,gp,dffn,dctx,out,
               ss,rs,cs,cr,ts,tr,lsem):
    pc=Place()
    greet_all(pc)
    half=rcopy(mas_ref.at[:,:,pc.ocols],sibm,cs,cr,pc.sib)
    half.start()
    pg_ref[pc.z,pc.xy,:,pc.cols]=pv_ref[...]
    t_=lax.broadcasted_iota(jnp.int32,(PACK,128),0)
    end=jnp.int32(0); dd=jnp.zeros((PACK,128),jnp.int32)
    for j in range(8):
        end=end+len_ref[0,j]
        dd=dd+(t_>=end).astype(jnp.int32)
    doc[...]=dd
    half.wait_recv()
    for pos,b in enumerate(AORDER):
        own=mas_ref[b,:,pc.cols]; oth=sibm[b]
        first=jnp.where(pc.c==0,own,oth); second=jnp.where(pc.c==0,oth,own)
        w_ref[pos,pc.z,pc.xy,:,pc.cols]=jnp.concatenate([first,second],axis=0).astype(bf16)
    half.wait_send()
    def group(g):
        if isinstance(g,int) and g==0: return Gather(pc,pg_ref,ss.at[0],rs.at[0]).copies()
        return Gather(pc,w_ref.at[g-1],ss.at[g],rs.at[g]).copies()
    NG=13
    def tick(t):
        for s in range(5):
            if isinstance(t,int):
                if 0<=t-s<NG: group(t-s).step(s)
            else:
                @pl.when(t-s<NG)
                def _(): group(t-s).step(s)
    def stat(b,start):
        t=(b%4)*4+b//4
        for side,ref in enumerate((left_ref,right_ref)):
            mine=(pc.chip==t)&(pc.c==side)
            d=rcopy(ref.at[b],st_ref.at[pc.me],ts.at[b*2+side],tr,(t//2,(t%2)*2+side))
            if start:
                @pl.when(mine)
                def _(): pltpu.make_async_copy(ref.at[b],st_ref.at[pc.me],tr).start()
            @pl.when(jnp.logical_not(mine))
            def _():
                if start: d.start()
                else: d.wait_send()
    copies=[]
    def away(src,dst):
        i=len(copies)
        c=pltpu.make_async_copy(src,dst,lsem.at[i]); c.start(); copies.append(c)
    W=lambda pos: w_ref[pos].reshape(D,D)
    for t in range(5): tick(t)
    place_params(pg_ref,p_ref)
    for i,(o,b,dst) in enumerate(((q,0,q_o),(k,None,k_o),(v,1,v_o))):
        tick(5+i)
        for tl in range(4):
            rows=pl.ds(tl*TT,TT)
            y=dot(x_ref[rows,:],W(i))
            if b is not None: y=y+p_ref[b:b+1,:]
            o[rows,:]=y.astype(bf16)
        away(o,dst)
        away(w_ref.at[i],wq_o.at[i])
    def slot(n,carry):
        p=n//4; b=n%4
        @pl.when(b==0)
        def _(): keys_of_pair(p,k,ka,doc[...])
        attend_block(p,b,q,v,ka,ctx,lse,doc)
        @pl.when(b==3)
        def _(): tick(8+p)
        return carry
    lax.fori_loop(0,24,slot,0)
    away(ctx,ctx_o); away(lse,lse_o)
    g1,s1,g2,s2=(p_ref[i:i+1,:] for i in (8,9,10,11))
    vec_o[...]=jnp.zeros_like(vec_o)
    def out_proj(tl,carry):
        rows=pl.ds(pl.multiple_of(tl*TT,TT),TT)
        z=x_ref[rows,:].astype(f32)+(dot(ctx[rows,:],W(3))+p_ref[2:3,:])
        n,r=layer_norm(z)
        n1[rows,:]=n
        r1[rows,:]=jnp.broadcast_to(r,(TT,128))
        hlow[rows,:]=(n*g1+s1).astype(bf16)
        return carry
    lax.fori_loop(0,4,out_proj,0)
    tick(14)
    def chunk(c,carry):
        lane=pl.ds(pl.multiple_of(c*D,128),D)
        bias=p_ref[pl.ds(3+c,1),:]
        for tl in range(4):
            rows=pl.ds(tl*TT,TT)
            inner=dot(hlow[rows,:],W(4+2*c))+bias
            a,g=gelu_both(inner)
            al=a.astype(bf16)
            act[rows,lane]=al
            gp[rows,lane]=g.astype(bf16)
            y=dot(al,W(5+2*c))
            @pl.when(c==0)
            def _(): acc[rows,:]=y
            @pl.when(c>0)
            def _(): acc[rows,:]+=y
        @pl.when(c<2)
        def _(): tick(15+c)
        return carry
    lax.fori_loop(0,4,chunk,0)
    lax.fori_loop(0,NB,lambda b,c: (stat(b,True),c)[1],0)
    away(hlow,hlow_o); away(act,act_o)
    pltpu.make_async_copy(cot_ref,out,lsem.at[20]).start()
    pltpu.make_async_copy(cot_ref,out,lsem.at[20]).wait()
    def tile(tl,carry):
        rows=pl.ds(pl.multiple_of(tl*TT,TT),TT)
        n1t=n1[rows,:]
        z=(n1t*g1+s1)+(acc[rows,:]+p_ref[7:8,:])
        n2,r2=layer_norm(z)
        e=out[rows,:].astype(f32)
        out[rows,:]=(n2*g2+s2).astype(bf16)
        c2=e*g2
        dz2=r2*(c2-jnp.mean(c2,axis=-1,keepdims=True)-n2*jnp.mean(c2*n2,axis=-1,keepdims=True))
        df=dz2.astype(bf16)
        dffn[rows,:]=df
        vec_o[10:11,:]+=jnp.sum(e*n2,axis=0,keepdims=True)
        vec_o[11:12,:]+=jnp.sum(e,axis=0,keepdims=True)
        vec_o[7:8,:]+=jnp.sum(df.astype(f32),axis=0,keepdims=True)
        dh=dz2
        for c in range(4):
            lane=pl.ds(c*D,D)
            dact=dot(df,W(5+2*c),1,1)
            din=(dact*gp[rows,lane].astype(f32)).astype(bf16)
            gp[rows,lane]=din
            vec_o[3+c:4+c,:]+=jnp.sum(din.astype(f32),axis=0,keepdims=True)
            dh=dh+dot(din,W(4+2*c),1,1)
        vec_o[8:9,:]+=jnp.sum(dh*n1t,axis=0,keepdims=True)
        vec_o[9:10,:]+=jnp.sum(dh,axis=0,keepdims=True)
        c1=dh*g1
        dz1=r1[rows,0:1]*(c1-jnp.mean(c1,axis=-1,keepdims=True)-n1t*jnp.mean(c1*n1t,axis=-1,keepdims=True))
        acc[rows,:]=dz1
        dat=dz1.astype(bf16)
        vec_o[2:3,:]+=jnp.sum(dat.astype(f32),axis=0,keepdims=True)
        dctx[rows,:]=dot(dat,W(3),1,1).astype(bf16)
        return carry
    lax.fori_loop(0,4,tile,0)
    away(out,out_o); away(gp,din_o); away(dffn,dffn_o); away(acc,dz1_o); away(dctx,dctx_o)
    for c in copies: c.wait()
    group(0).done()
    lax.fori_loop(1,NG,lambda g,c: (group(g).done(),c)[1],0)
    lax.fori_loop(0,NB,lambda b,c: (stat(b,False),c)[1],0)
    @pl.when(pc.xy<3)
    def _(): pltpu.make_async_copy(st_ref,st_ref,tr).wait()

def call_front(lengths,x,cot,masters,pv,left,right):
    V=pltpu.VMEM; S=jax.ShapeDtypeStruct; A=pl.ANY
    B=lambda m: pl.BlockSpec(memory_space=m)
    sem=pltpu.SemaphoreType.DMA
    T=lambda w,d: S((PACK,w),d)
    return pl.pallas_call(front_body,
        in_specs=[B(pltpu.SMEM),B(V),B(A),B(V),B(V),B(A),B(A)],
        out_specs=[B(A)]*13+[B(V),B(A)],
        out_shape=[T(D,bf16)]*5+[T(128,f32),T(FF,bf16),T(FF,bf16),T(D,bf16),T(D,bf16),T(D,f32),T(D,bf16),S((3,4,4,MR,D),bf16),S((16,D),f32),S((32,24,D),f32)],
        scratch_shapes=[V((NB,4,4,MR,D),bf16),V((4,4,16,D),bf16),V((16,D),f32),V((NB,24,HC),f32)]+[V((PACK,D),bf16)]*4+
            [V((PACK,128),f32),V((PACK,128),jnp.int32),V((2,PACK,128),bf16),V((PACK,D),f32),V((PACK,128),f32),V((PACK,D),bf16),V((PACK,D),f32),
             V((PACK,FF),bf16),V((PACK,FF),bf16),V((PACK,D),bf16),V((PACK,D),bf16),V((PACK,D),bf16),
             sem((13,11)),sem((13,11)),sem,sem,sem((24,)),sem,sem((24,))],
        compiler_params=pltpu.CompilerParams(vmem_limit_bytes=63<<20,collective_id=0,has_side_effects=True))(lengths,x,cot,masters,pv,left,right)


NGR=12
def sum_scratch():
    V=pltpu.VMEM; nb=NGR
    return dict(rc=V((nb,4,4,MR,HC),bf16),xa=V((nb,2,2,MR,HC),bf16),yb=V((nb,2,2,MR,HC),bf16),
        s2a=V((nb,2,MR,HC),bf16),s2b=V((nb,2,MR,HC),bf16),ya=V((nb,2,MR,HC),bf16),xb=V((nb,2,MR,HC),bf16),
        s3=V((nb,4,MR,HC),bf16),zr=V((nb,3,MR,HC),bf16),fin=V((nb,MR,HC),f32),finb=V((nb,MR,HC),bf16),hr=V((nb,24,HC),f32))
SKEYS=list(sum_scratch())

class GroupSum:
    def __init__(self,pc,g_ref,R,out_ref,gown_ref,ss,rs,os_,orr):
        self.pc,self.gr,self.RR,self.out,self.gown=pc,g_ref,R,out_ref,gown_ref
        self.ss,self.rs,self.os_,self.orr=ss,rs,os_,orr
    def mk(self,g,i,src,dst,dev): return rcopy(src,dst,self.ss.at[g,i],self.rs.at[g,i],dev)
    def of(self,g): return self.gr.at[g],{k:v.at[g] for k,v in self.RR.items()}
    def core(self,g):
        G,R=self.of(g); return self.mk(g,0,G.at[:,:,:,self.pc.ocols],R["rc"],self.pc.sib)
    def xa(self,g):
        G,R=self.of(g); pc=self.pc; return self.mk(g,1,G.at[pl.ds(0,2),pl.ds((1-pc.x)*2,2),:,pc.cols],R["xa"],pc.xn)
    def yb(self,g,i):
        G,R=self.of(g); pc=self.pc; return self.mk(g,2+i,G.at[pl.ds(2,2),i*2+1-pc.y,:,pc.cols],R["yb"].at[i],pc.yn)
    def ya(self,g):
        G,R=self.of(g); return self.mk(g,4,R["s2a"],R["ya"],self.pc.yn)
    def xb(self,g):
        G,R=self.of(g); return self.mk(g,5,R["s2b"],R["xb"],self.pc.xn)
    def zz(self,g,k):
        G,R=self.of(g); pc=self.pc; return self.mk(g,5+k,R["s3"].at[(pc.z+k)%NZ],R["zr"].at[k-1],pc.zpeer(k))
    def home(self,g):
        G,R=self.of(g); pc=self.pc; return self.mk(g,9,R["fin"].at[pl.ds(pl.multiple_of((1-pc.c)*24,8),24)],R["hr"],pc.sib)
    def step0(self,g): self.core(g).start()
    def step1(self,g):
        pc=self.pc; G,R=self.of(g)
        self.core(g).wait_recv()
        for z in range(4):
            G[z,:,:,pc.cols]=(G[z,:,:,pc.cols].astype(f32)+R["rc"][z].astype(f32)).astype(bf16)
        self.xa(g).start()
        for i in range(2): self.yb(g,i).start()
    def step2(self,g):
        pc=self.pc; G,R=self.of(g)
        self.xa(g).wait_recv()
        R["s2a"][...]=(G[0:2,pc.x*2+1-pc.y,:,pc.cols].astype(f32)+R["xa"][:,1-pc.y].astype(f32)).astype(bf16)
        self.ya(g).start()
        for i in range(2): self.yb(g,i).wait_recv()
        R["s2b"][...]=(G[2:4,(1-pc.x)*2+pc.y,:,pc.cols].astype(f32)+R["yb"][1-pc.x].astype(f32)).astype(bf16)
        self.xb(g).start()
    def step3(self,g):
        pc=self.pc; G,R=self.of(g)
        self.ya(g).wait_recv(); self.xb(g).wait_recv()
        a=G[0:2,pc.xy,:,pc.cols].astype(f32)+R["xa"][:,pc.y].astype(f32)+R["ya"][...].astype(f32)
        b=G[2:4,pc.xy,:,pc.cols].astype(f32)+R["yb"][pc.x].astype(f32)+R["xb"][...].astype(f32)
        R["s3"][0:2]=a.astype(bf16); R["s3"][2:4]=b.astype(bf16)
        ab=jnp.where(pc.z%2==0,jnp.stack([a[0],b[0]]),jnp.stack([a[1],b[1]]))
        R["fin"][...]=jnp.where(pc.z<2,ab[0],ab[1])
        for k in (1,2,3): self.zz(g,k).start()
    def targets(self,g,act):
        pc=self.pc; G,R=self.of(g)
        def whole(b):
            t=(b%4)*4+b//4
            for side in range(2): act(R["finb"],self.gown.at[pc.chip,:,pc.cols],side,t,side)
        def slab(j):
            lane=pl.ds(pl.multiple_of((pc.c*3+j)*128,128),128)
            for i in range(3):
                for side in range(2): act(R["finb"].at[:,pl.ds(i*128,128)],self.gown.at[pc.chip,:,lane],i*2+side,i*4,side)
        if isinstance(g,int):
            if g<9: whole(8+g//2-4*(g%2)-9*(g//8))
            else: slab(g-9)
        else:
            @pl.when(g<9)
            def _(): whole(8+g//2-4*(g%2)-9*(g//8))
            @pl.when(g>=9)
            def _(): slab(g-9)
    def step4(self,g):
        pc=self.pc; G,R=self.of(g)
        for k in (1,2,3): self.zz(g,k).wait_recv()
        s=R["fin"][...]
        for k in range(3): s=s+R["zr"][k].astype(f32)
        R["fin"][...]=s
        R["finb"][...]=s.astype(bf16)
        self.home(g).start()
        def send(src,dst,i,t,side):
            mine=(pc.chip==t)&(pc.c==side)
            @pl.when(mine)
            def _(): pltpu.make_async_copy(src,dst,self.orr).start()
            @pl.when(jnp.logical_not(mine))
            def _(): rcopy(src,dst,self.os_.at[g,i],self.orr,(t//2,(t%2)*2+side)).start()
        self.targets(g,send)
    def step5(self,g):
        pc=self.pc; G,R=self.of(g)
        self.home(g).wait_recv()
        def whole(b):
            self.out[b,:,pc.cols]=R["fin"][pl.ds(pl.multiple_of(pc.c*24,8),24)]
            self.out[b,:,pc.ocols]=R["hr"][...]
        def slab(j):
            for i in range(3):
                self.out[i,:,pl.ds(pl.multiple_of((pc.c*3+j)*128,128),128)]=R["fin"][pl.ds(pl.multiple_of(pc.c*24,8),24),i*128:(i+1)*128]
                self.out[i,:,pl.ds(pl.multiple_of(((1-pc.c)*3+j)*128,128),128)]=R["hr"][:,i*128:(i+1)*128]
        if isinstance(g,int):
            if g<9: whole(8+g//2-4*(g%2)-9*(g//8))
            else: slab(g-9)
        else:
            @pl.when(g<9)
            def _(): whole(8+g//2-4*(g%2)-9*(g//8))
            @pl.when(g>=9)
            def _(): slab(g-9)
    def done(self,g):
        pc=self.pc
        for d in (self.core,self.xa,self.ya,self.xb,self.home): d(g).wait_send()
        for i in range(2): self.yb(g,i).wait_send()
        for k in (1,2,3): self.zz(g,k).wait_send()
        def wait(src,dst,i,t,side):
            @pl.when(jnp.logical_not((pc.chip==t)&(pc.c==side)))
            def _(): rcopy(src,dst,self.os_.at[g,i],self.orr,(t//2,(t%2)*2+side)).wait_send()
        self.targets(g,wait)

KB_=256
def prepare_pair(p,q,k,v,ctx,do,lse,doc_ref,qa,doa,ka,va):
    cols=pl.ds(pl.multiple_of(p*128,128),128)
    lane=lax.broadcasted_iota(jnp.int32,(KB_,128),1)
    def tile(t,carry):
        rows=pl.ds(pl.multiple_of(t*KB_,KB_),KB_)
        doc=doc_ref[rows,:]
        qp=q[rows,cols].astype(f32)*0.125; kp=k[rows,cols].astype(f32); vp=v[rows,cols].astype(f32)
        dop=do[rows,cols].astype(f32); prod=dop*ctx[rows,cols].astype(f32)
        ls=lse[rows,:]
        for h,lo in enumerate((True,False)):
            keep=(lane<64) if lo else (lane>=64)
            off=64 if lo else 0
            l=jnp.sum(jnp.where(lane==2*p+h,ls,0.0),axis=1,keepdims=True)
            dd=jnp.sum(jnp.where(keep,prod,0.0),axis=1,keepdims=True)
            q1=onehot_part(qp,lane,lo,doc,0.0,BIG)
            for i,c in enumerate(split3(-l)): q1=jnp.where(lane==off+8+i,c,q1)
            qa[h,rows,:]=q1.astype(bf16)
            k1=onehot_part(kp,lane,lo,doc,1.0,1.0)
            ka[h,rows,:]=jnp.where((lane>=off+8)&(lane<off+11),1.0,k1).astype(bf16)
            d1=jnp.where(keep,dop,0.0)
            for i,c in enumerate(split3(-dd)): d1=jnp.where(lane==off+i,c,d1)
            doa[h,rows,:]=d1.astype(bf16)
            v1=jnp.where(keep,vp,0.0)
            va[h,rows,:]=jnp.where((lane>=off)&(lane<off+3),1.0,v1).astype(bf16)
        return carry
    lax.fori_loop(0,PACK//KB_,tile,0)

def back_block(p,b,q,k,v,do,qa,doa,ka,va,dqa):
    cols=pl.ds(pl.multiple_of(p*128,128),128)
    rows=pl.ds(pl.multiple_of(b*KB_,KB_),KB_)
    low=lax.broadcasted_iota(jnp.int32,(KB_,128),1)<64
    lowq=lax.broadcasted_iota(jnp.int32,(PACK,128),1)<64
    qp=q[:,cols]; dop=do[:,cols]; kp=k[rows,cols]
    r=[]
    for h in range(2):
        s=dot(ka[h,rows,:],qa[h],1,1)
        pr=jnp.exp(s)
        dp=dot(va[h,rows,:],doa[h],1,1)
        ds=(pr*dp).astype(bf16)
        r.append((dot(pr.astype(bf16),dop),dot(ds,qp),dot(ds,kp,0,0)))
    dq=jnp.where(lowq,r[0][2],r[1][2])
    @pl.when(b==0)
    def _(): dqa[...]=dq
    @pl.when(b>0)
    def _(): dqa[...]+=dq
    v[rows,cols]=jnp.where(low,r[0][0],r[1][0]).astype(bf16)
    k[rows,cols]=(jnp.where(low,r[0][1],r[1][1])*0.125).astype(bf16)

def back_body(len_ref,x_ref,q_i,k_i,v_i,ctx_i,do_i,lse_i,act_i,din_i,dffn_i,hlow_i,dz1_i,wq_i,vec_ref,
              ig_o,out_ref,vout_ref,gown_ref,*rest):
    R=dict(zip(SKEYS,rest[:len(SKEYS)]))
    (g_ref,ctx,w_last,lse,doc,act,din,dffn,hlow,acc,qa,doa,ka,va,dqa,vcur,vbuf,
     ss,rs,os_,orr,vs,vr,lsem)=rest[len(SKEYS):]
    pc=Place()
    loads={}
    def load(name,src,dst):
        c=pltpu.make_async_copy(src,dst,lsem.at[len(loads)]); c.start(); loads[name]=c
    half=lambda ref,c: ref.at[:,pl.ds(c*D,D)]
    load("act0",half(act_i,0),act.at[0]); load("dffn",dffn_i,dffn)
    load("hlow",hlow_i,hlow); load("din0",half(din_i,0),din.at[0])
    load("act1",half(act_i,1),act.at[1]); load("din1",half(din_i,1),din.at[1])
    for n,s,d in (("acc",dz1_i,acc),("ctx",ctx_i,ctx),("lse",lse_i,lse)): load(n,s,d)
    q,v,do,k=act.at[0],din.at[0],dffn,act.at[1]
    late={4:("q",q_i,q),5:("v",v_i,v),6:("k",k_i,k),7:("do",do_i,do)}
    greet_all(pc)
    gs=GroupSum(pc,g_ref,R,out_ref,gown_ref,ss,rs,os_,orr)
    vsum=VecSum(pc,vcur,vbuf,vs,vr)
    t_=lax.broadcasted_iota(jnp.int32,(PACK,128),0)
    end=jnp.int32(0); dd=jnp.zeros((PACK,128),jnp.int32)
    for j in range(8):
        end=end+len_ref[0,j]
        dd=dd+(t_>=end).astype(jnp.int32)
    doc[...]=dd
    def product(g,a,b):
        for r in range(4):
            g_ref[g,r]=dot(a[:,r*192:(r+1)*192],b,0,0).astype(bf16).reshape(4,MR,D)
    loads["dffn"].wait()
    for i in range(9):
        c=i//2
        if i==8:
            loads["ctx"].wait(); loads["acc"].wait()
            product(i,ctx,acc[...].astype(bf16))
        elif i%2==0:
            loads[f"act{c}"].wait()
            product(i,act.at[c%2],dffn[...])
            if c<2: load(f"act{c+2}",half(act_i,c+2),act.at[c%2])
        else:
            if c==0: loads["hlow"].wait()
            loads[f"din{c}"].wait()
            product(i,hlow,din[c%2])
            if c<2: load(f"din{c+2}",half(din_i,c+2),din.at[c%2])
        if i in late: load(*late[i])
        gs.step0(i)
        if i>=1: gs.step1(i-1)
    gs.step2(0)
    wrow=pl.ds(0,D)
    wdst=[din.at[1,wrow],hlow.at[wrow],w_last]
    for i in range(3): load(f"w{i}",wq_i.at[i],wdst[i])
    for n in ("q","k","v","do","lse"): loads[n].wait()
    def slot(n,carry):
        pi=n//4; b=n%4; j=pi//2; cc=pi%2; p=3*cc+j
        cols=pl.ds(pl.multiple_of(p*128,128),128)
        @pl.when(b==0)
        def _(): prepare_pair(p,q,k,v,ctx,do,lse,doc,qa,doa,ka,va)
        back_block(p,b,q,k,v,do,qa,doa,ka,va,dqa)
        @pl.when(b==3)
        def _():
            q[:,cols]=(dqa[...]*0.125).astype(bf16)
            al=jnp.concatenate([q[:,cols],k[:,cols],v[:,cols]],axis=1)
            lane=pl.ds(pl.multiple_of(cc*HC,128),HC)
            for r in range(4):
                g_ref[9+j,r,:,:,lane]=dot(x_ref[:,r*192:(r+1)*192],al,0,0).astype(bf16).reshape(4,MR,HC)
            vcur[0,0:1,cols]=jnp.sum(q[:,cols].astype(f32),axis=0,keepdims=True)
            vcur[0,1:2,cols]=jnp.sum(v[:,cols].astype(f32),axis=0,keepdims=True)
        m=n//2
        @pl.when(n==0)
        def _(): gs.step1(8)
        @pl.when(n%2==0)
        def _():
            @pl.when(m<=9)
            def _(): gs.step2(1+m)
            @pl.when(m<=10)
            def _(): gs.step3(m)
            @pl.when(m>=1)
            def _(): gs.step4(m-1)
            @pl.when(m>=2)
            def _(): gs.step5(m-2)
        @pl.when((n==9)|(n==17))
        def _(): gs.step1(9+n//16)
        @pl.when((n==7)|(n==15))
        def _(): gs.step0(9+n//15)
        return carry
    vcur[0]=vec_ref[...]
    lax.fori_loop(0,24,slot,0)
    gs.step0(11)
    vsum.step(0)
    for i in range(3): loads[f"w{i}"].wait()
    def grad_tile(t):
        rows=pl.ds(t*256,256)
        a=acc[rows,:]
        for d,w in zip((q,k,v),wdst): a=a+dot(d[rows,:],w[...],1,1)
        acc[rows,:]=a
    grad_tile(0);
    gs.step5(10); gs.step1(11); vsum.step(1)
    grad_tile(1); grad_tile(2); vsum.step(2)
    gs.step2(11); grad_tile(3); vsum.step(3)
    away=pltpu.make_async_copy(acc,ig_o,lsem.at[31]); away.start()
    gs.step3(11); vsum.step(4)
    gs.step4(11); vsum.step(5)
    gs.step5(11)
    vout_ref[...]=vcur[5]
    vsum.done()
    lax.fori_loop(0,NGR,lambda g,c: (gs.done(g),c)[1],0)
    away.wait()
    @pl.when(pc.xy<3)
    def _(): pltpu.make_async_copy(gown_ref,gown_ref,orr).wait()

def call_back(lengths,x,q,k,v,ctx,dctx,lse,act,din,dffn,hlow,dz1,wq,vec):
    V=pltpu.VMEM; S=jax.ShapeDtypeStruct; A=pl.ANY
    B=lambda m: pl.BlockSpec(memory_space=m)
    sem=pltpu.SemaphoreType.DMA
    T=V((PACK,D),bf16); H=V((2,PACK,128),bf16)
    return pl.pallas_call(back_body,
        in_specs=[B(pltpu.SMEM),B(V)]+[B(A)]*12+[B(V)],
        out_specs=[B(A),B(V),B(V),B(A)],
        out_shape=[S((PACK,D),f32),S((NB,24,D),f32),S((16,D),f32),S((16,MR,D),bf16)],
        scratch_shapes=list(sum_scratch().values())+[V((NGR,4,4,MR,D),bf16),T,V((D,D),bf16)]+[V((PACK,128),f32),V((PACK,128),jnp.int32),V((2,PACK,D),bf16),V((2,PACK,D),bf16),T,T,V((PACK,D),f32)]+[H]*4+
            [V((PACK,128),f32),V((6,16,D),f32),V((5,16,D),f32),sem((NGR,10)),sem((NGR,10)),sem((NGR,6)),sem,sem((5,)),sem((5,)),sem((32,))],
        compiler_params=pltpu.CompilerParams(vmem_limit_bytes=63<<20,collective_id=1,has_side_effects=True))(lengths,x,q,k,v,ctx,dctx,lse,act,din,dffn,hlow,dz1,wq,vec)


def gather_rows(a):
    return lax.all_gather(a,("dp","head"),axis=1,tiled=True)

def doc_lengths(lengths):
    return lax.dynamic_slice_in_dim(lengths,lax.axis_index("head"),1,axis=0)

def layer(tokens,cotangent,lengths,w,params):
    q,k,v,ctx,lse,n1,r1=call_a(lengths,tokens,w,params)
    out,dz1,dctx,dwo,dw1,dw2,vec=call_b(cotangent,n1,r1,ctx,w,params)
    ig,dwqkv,vq=call_c(lengths,tokens,q,k,v,ctx,dctx,lse,dz1,w)
    terms=jnp.concatenate([dwqkv,dwo[None],dw1,dw2],axis=0)
    vec=jnp.concatenate([vq[0:1],vq[2:3],vec[2:]],axis=0)
    return out,ig,terms,vec

def on_slice(tokens,cotangent,lengths,masters,vectors,left,right,second):
    pv=jnp.pad(vectors,((0,4),(0,HC-24))).astype(bf16)
    lens=doc_lengths(lengths)
    out,q,k,v,ctx,lse,act,din,dffn,hlow,dz1,dctx,wq,vec,stat=call_front(lens,tokens,cotangent,masters,pv,left,right)
    ig,grads,vec_all,gown=call_back(lens,tokens,q,k,v,ctx,dctx,lse,act,din,dffn,hlow,dz1,wq.reshape(3,D,D),vec)
    ln,rn,mn,vg,sn,vn=call_newton_step(gown.reshape(D,D),stat.reshape(D,D),left,right,masters,vec_all,vectors,second)
    return out,ig,grads,ln,rn,mn,vg,sn,vn

def on_any(tokens,cotangent,lengths,masters,vectors,left,right,second):
    axes=("dp","head")
    me=lax.axis_index("dp")*lax.axis_size("head")+lax.axis_index("head")
    share=masters.shape[1]
    w=gather_rows(masters.astype(bf16))
    params=gather_rows(vectors.astype(bf16)).astype(f32)
    out,ig,terms,vec=layer(tokens,cotangent,doc_lengths(lengths),w,params)
    grads=lax.psum_scatter(terms.astype(f32),axes,scatter_dimension=1,tiled=True)
    vg=lax.psum_scatter(vec[:12],axes,scatter_dimension=1,tiled=True)
    low=grads.astype(bf16)
    g=gather_rows(low)
    ein=partial(jnp.einsum,preferred_element_type=f32)
    cols=lax.dynamic_slice_in_dim(g,me*share,share,axis=2)
    ln=BETA*left+(1-BETA)*ein("kid,kjd->kij",low,g)
    rn=BETA*right+(1-BETA)*ein("kdi,kdj->kij",cols,g)
    item=jnp.minimum(me,2*NB-1)
    own=lax.dynamic_index_in_dim(jnp.concatenate([gather_rows(ln),gather_rows(rn)],axis=0),item,0,keepdims=False)
    root=call_newton(own)
    place=jnp.where((jnp.arange(2*NB)==me)[:,None,None],root[None],0.0)
    rows=lax.psum_scatter(place,axes,scatter_dimension=1,tiled=True)
    rr=gather_rows(rows[NB:])
    hi=partial(jnp.einsum,"kij,kjl->kil",precision=lax.Precision.HIGHEST)
    mn=masters-RATE*hi(hi(rows[:NB],g.astype(f32)),rr)
    sn=BETA_TWO*second+(1-BETA_TWO)*vg*vg
    vn=vectors-RATE_VEC*vg/(jnp.sqrt(sn)+1e-8)
    return out,ig,grads,ln,rn,mn,vg,sn,vn

def solution(mesh):
    rows=P(("dp","head"),None); blocks=P(None,("dp","head"),None); vecs=P(None,("dp","head"))
    on_device=on_slice if dict(mesh.shape)=={"dp":8,"head":4} else on_any
    return jax.shard_map(on_device,mesh=mesh,
        in_specs=(rows,rows,P("dp",None),blocks,vecs,blocks,blocks,vecs),
        out_specs=(rows,rows,blocks,blocks,blocks,blocks,vecs,vecs,vecs),check_vma=False)
```

```python
import jax, jax.numpy as jnp, numpy as np
from functools import partial
from jax import lax
from jax.experimental import pallas as pl
from jax.experimental.pallas import tpu as pltpu
from jax.sharding import PartitionSpec as P

D=768; HEADS=12; HD=64; FF=3072; PACK=1024; NEWTON=8; NB=12
NORM_EPS=1e-6
f32=jnp.float32; bf16=jnp.bfloat16
BIG=1e30
QB=256
def dot(a,b,ca=1,cb=0):
    return lax.dot_general(a,b,(((ca,),(cb,)),((),())),preferred_element_type=f32)

def doc_column(len_ref, shape, dim):
    t=lax.broadcasted_iota(jnp.int32,shape,dim)
    end=jnp.int32(0); doc=jnp.zeros(shape,jnp.int32)
    for j in range(8):
        end=end+len_ref[0,j]
        doc=doc+(t>=end).astype(jnp.int32)
    return doc

def split3(v):
    a=v.astype(bf16).astype(f32); r=v-a
    b=r.astype(bf16).astype(f32); c=r-b
    return a,b,c

def augment(base, lane, head_lo, cols):
    keep=(lane<64) if head_lo else (lane>=64)
    off=64 if head_lo else 0
    out=jnp.where(keep, base, 0.0)
    for i,c in enumerate(cols):
        out=jnp.where(lane==off+i, c, out)
    return out.astype(bf16)

def onehot_part(base, lane, head_lo, doc, minus, scale):
    keep=(lane<64) if head_lo else (lane>=64)
    off=64 if head_lo else 0
    l=lane-off
    oh=jnp.where((l>=0)&(l<8), (jnp.where(l==doc,1.0,0.0)-minus)*scale, 0.0)
    return jnp.where(keep, base, oh)

def attn_fwd_pair(p, q_ref,k_ref,v_ref, ctx_ref, lse_ref, doc):
    cols=pl.ds(pl.multiple_of(p*128,128),128)
    lane=lax.broadcasted_iota(jnp.int32,(PACK,128),1)
    kp=k_ref[:,cols].astype(f32)
    vp=v_ref[:,cols]
    kk=[onehot_part(kp,lane,lo,doc,1.0,1.0).astype(bf16) for lo in (True,False)]
    laneb=lax.broadcasted_iota(jnp.int32,(QB,128),1)
    for b in range(PACK//QB):
        rows=pl.ds(b*QB,QB)
        qp=q_ref[rows,cols].astype(f32)*0.125
        docb=doc[b*QB:(b+1)*QB]
        outs=[]
        lse_old=lse_ref[rows,:]
        for h,lo in enumerate((True,False)):
            qa=onehot_part(qp,laneb,lo,docb,0.0,BIG).astype(bf16)
            s=dot(qa,kk[h],1,1)
            m=jnp.max(s,axis=1,keepdims=True)
            e=jnp.exp(s-m)
            l=jnp.sum(e,axis=1,keepdims=True)
            o=dot(e.astype(bf16),vp)
            outs.append(o/l)
            lse_old=jnp.where(laneb==2*p+h, m+jnp.log(l), lse_old)
        lse_ref[rows,:]=lse_old
        ctx_ref[rows,cols]=jnp.where(laneb<64,outs[0],outs[1]).astype(bf16)

def layer_norm(z):
    mu=jnp.mean(z,axis=-1,keepdims=True)
    c=z-mu
    r=lax.rsqrt(jnp.mean(c*c,axis=-1,keepdims=True)+NORM_EPS)
    return c*r, r

def ka_body(len_ref,x_ref,wa_ref,p_ref,q_ref,k_ref,v_ref,ctx_ref,lse_ref,hid_ref,r1_ref,w_ref):
    pltpu.sync_copy(wa_ref.at[pl.ds(0,4)],w_ref)
    doc=doc_column(len_ref,(PACK,1),0)
    for i,(o,b) in enumerate(((q_ref,0),(k_ref,None),(v_ref,1))):
        for t in range(4):
            rows=pl.ds(t*256,256)
            y=dot(x_ref[rows,:],w_ref[i])
            if b is not None: y=y+p_ref[b:b+1,:]
            o[rows,:]=y.astype(bf16)
    def body(p,c):
        attn_fwd_pair(p,q_ref,k_ref,v_ref,ctx_ref,lse_ref,doc)
        return c
    lax.fori_loop(0,6,body,0)
    for t in range(4):
        rows=pl.ds(t*256,256)
        z=x_ref[rows,:].astype(f32)+(dot(ctx_ref[rows,:],w_ref[3])+p_ref[2:3,:])
        n,r=layer_norm(z)
        hid_ref[rows,:]=n
        r1_ref[rows,:]=jnp.broadcast_to(r,(256,128))

def call_a(lengths,x,w,params):
    V=pltpu.VMEM
    return pl.pallas_call(ka_body,
        in_specs=[pl.BlockSpec(memory_space=pltpu.SMEM),pl.BlockSpec(memory_space=V),pl.BlockSpec(memory_space=pl.ANY),pl.BlockSpec(memory_space=V)],
        out_specs=[pl.BlockSpec(memory_space=V)]*7,
        out_shape=[jax.ShapeDtypeStruct((PACK,D),bf16)]*4+[jax.ShapeDtypeStruct((PACK,128),f32),jax.ShapeDtypeStruct((PACK,D),f32),jax.ShapeDtypeStruct((PACK,128),f32)],
        scratch_shapes=[V((4,D,D),bf16)],
        compiler_params=pltpu.CompilerParams(vmem_limit_bytes=60<<20))(lengths,x,w,params)

def gelu_both(x):
    z=jnp.abs(x)*0.7071067811865476
    t=1.0/(1.0+0.3275911*z)
    e=jnp.exp(-0.5*x*x)
    poly=t*(0.254829592+t*(-0.284496736+t*(1.421413741+t*(-1.453152027+t*1.061405429))))
    half=0.5*poly*e
    phi_c=jnp.where(x>=0,1.0-half,half)
    return x*phi_c, phi_c+x*(e*0.3989422804014327)

def kb_body(cot_ref,n1_ref,r1_ref,ctx_ref,w_ref,p_ref, out_ref,dz1_ref,dctx_ref,dwo_ref,dw1_ref,dw2_ref,vec_ref, act_ref,gp_ref,dffn_ref,hlow_ref):
    TT=256
    g1,s1,g2,s2=(p_ref[i:i+1,:] for i in (8,9,10,11))
    b2=p_ref[7:8,:]
    vec_ref[...]=jnp.zeros_like(vec_ref)
    def tile(t,carry):
        rows=pl.ds(pl.multiple_of(t*TT,TT),TT)
        n1=n1_ref[rows,:]
        hid=n1*g1+s1
        hl=hid.astype(bf16)
        hlow_ref[rows,:]=hl
        ffn=None
        for c in range(4):
            inner=dot(hl,w_ref[4+c])+p_ref[3+c:4+c,:]
            a,gp=gelu_both(inner)
            al=a.astype(bf16)
            act_ref[rows,pl.ds(c*D,D)]=al
            gp_ref[rows,pl.ds(c*D,D)]=gp.astype(gp_ref.dtype)
            y=dot(al,w_ref[8+c])
            ffn=y if ffn is None else ffn+y
        z=hid+(ffn+b2)
        n2,r2=layer_norm(z)
        out_ref[rows,:]=(n2*g2+s2).astype(bf16)
        e=cot_ref[rows,:].astype(f32)
        c2=e*g2
        dz2=r2*(c2-jnp.mean(c2,axis=-1,keepdims=True)-n2*jnp.mean(c2*n2,axis=-1,keepdims=True))
        dffn=dz2.astype(bf16)
        dffn_ref[rows,:]=dffn
        vec_ref[10:11,:]+=jnp.sum(e*n2,axis=0,keepdims=True)
        vec_ref[11:12,:]+=jnp.sum(e,axis=0,keepdims=True)
        vec_ref[7:8,:]+=jnp.sum(dffn.astype(f32),axis=0,keepdims=True)
        dh=dz2
        for c in range(4):
            dact=dot(dffn,w_ref[8+c],1,1)
            din=(dact*gp_ref[rows,pl.ds(c*D,D)].astype(f32)).astype(bf16)
            gp_ref[rows,pl.ds(c*D,D)]=din.astype(gp_ref.dtype)
            vec_ref[3+c:4+c,:]+=jnp.sum(din.astype(f32),axis=0,keepdims=True)
            dh=dh+dot(din,w_ref[4+c],1,1)
        vec_ref[8:9,:]+=jnp.sum(dh*n1,axis=0,keepdims=True)
        vec_ref[9:10,:]+=jnp.sum(dh,axis=0,keepdims=True)
        c1=dh*g1
        dz1=r1_ref[rows,0:1]*(c1-jnp.mean(c1,axis=-1,keepdims=True)-n1*jnp.mean(c1*n1,axis=-1,keepdims=True))
        dz1_ref[rows,:]=dz1
        dat=dz1.astype(bf16)
        vec_ref[2:3,:]+=jnp.sum(dat.astype(f32),axis=0,keepdims=True)
        dctx_ref[rows,:]=dot(dat,w_ref[3],1,1).astype(bf16)
        return carry
    lax.fori_loop(0,PACK//TT,tile,0)
    for c in range(4):
        dw2_ref[c]=dot(act_ref[:,c*D:(c+1)*D],dffn_ref[...],0,0).astype(bf16)
        dw1_ref[c]=dot(hlow_ref[...],gp_ref[:,c*D:(c+1)*D].astype(bf16),0,0).astype(bf16)
    dwo_ref[...]=dot(ctx_ref[...],dz1_ref[...].astype(bf16),0,0).astype(bf16)

def call_b(cot,n1,r1,ctx,w,params):
    V=pltpu.VMEM
    S=jax.ShapeDtypeStruct
    return pl.pallas_call(kb_body,
        in_specs=[pl.BlockSpec(memory_space=V)]*6,
        out_specs=[pl.BlockSpec(memory_space=V)]*7,
        out_shape=[S((PACK,D),bf16),S((PACK,D),f32),S((PACK,D),bf16),S((D,D),bf16),S((4,D,D),bf16),S((4,D,D),bf16),S((16,D),f32)],
        scratch_shapes=[V((PACK,FF),bf16),V((PACK,FF),bf16),V((PACK,D),bf16),V((PACK,D),bf16)],
        compiler_params=pltpu.CompilerParams(vmem_limit_bytes=62<<20))(cot,n1,r1,ctx,w,params)

def kc_body(len_ref,x_ref,q_ref,k_ref,v_ref,ctx_ref,do_ref,lse_ref,dz1_ref,wa_ref, ig_ref,dw_ref,vec_ref, dqkv_ref, dqa_ref,w_ref):
    pltpu.sync_copy(wa_ref.at[pl.ds(0,3)],w_ref)
    doc=doc_column(len_ref,(PACK,1),0)
    lane=lax.broadcasted_iota(jnp.int32,(PACK,128),1)
    KB_=256
    def pair(p,carry):
        cols=pl.ds(pl.multiple_of(p*128,128),128)
        qp=q_ref[:,cols].astype(f32); kp=k_ref[:,cols].astype(f32); vp=v_ref[:,cols].astype(f32)
        dop=do_ref[:,cols].astype(f32); cp=ctx_ref[:,cols].astype(f32)
        prod=dop*cp
        qa=[];qm=[];doa=[];dom=[];ka=[];km=[];va=[]
        for h,lo in enumerate((True,False)):
            keep=(lane<64) if lo else (lane>=64)
            off=64 if lo else 0
            lse=jnp.sum(jnp.where(lane==2*p+h,lse_ref[...],0.0),axis=1,keepdims=True)
            dd=jnp.sum(jnp.where(keep,prod,0.0),axis=1,keepdims=True)
            q1=onehot_part(qp*0.125,lane,lo,doc,0.0,BIG)
            for i,c in enumerate(split3(-lse)): q1=jnp.where(lane==off+8+i,c,q1)
            qa.append(q1.astype(bf16)); qm.append(jnp.where(keep,qp*0.125,0.0).astype(bf16))
            k1=onehot_part(kp,lane,lo,doc,1.0,1.0)
            k1=jnp.where((lane>=off+8)&(lane<off+11),1.0,k1)
            ka.append(k1.astype(bf16)); km.append(jnp.where(keep,kp*0.125,0.0).astype(bf16))
            d1=jnp.where(keep,dop,0.0)
            dom.append(d1.astype(bf16))
            for i,c in enumerate(split3(-dd)): d1=jnp.where(lane==off+i,c,d1)
            doa.append(d1.astype(bf16))
            v1=jnp.where(keep,vp,0.0); v1=jnp.where((lane>=off)&(lane<off+3),1.0,v1)
            va.append(v1.astype(bf16))
        for b in range(PACK//KB_):
            rows=slice(b*KB_,(b+1)*KB_)
            dv=None;dk=None;dq=None
            for h in range(2):
                s=dot(ka[h][rows],qa[h],1,1)
                pr=jnp.exp(s)
                dp=dot(va[h][rows],doa[h],1,1)
                ds=(pr*dp).astype(bf16)
                a=dot(pr.astype(bf16),dom[h]); dv=a if dv is None else dv+a
                a=dot(ds,qm[h]); dk=a if dk is None else dk+a
                a=dot(ds,km[h][rows],0,0); dq=a if dq is None else dq+a
            if b==0: dqa_ref[...]=dq
            else: dqa_ref[...]+=dq
            dqkv_ref[1,rows,cols]=dk.astype(bf16)
            dqkv_ref[2,rows,cols]=dv.astype(bf16)
        dqkv_ref[0,:,cols]=dqa_ref[...].astype(bf16)
        for i in range(3):
            d=dqkv_ref[i,:,cols]
            dw_ref[i,:,cols]=dot(x_ref[...],d,0,0).astype(bf16)
            vec_ref[i:i+1,cols]=jnp.sum(d.astype(f32),axis=0,keepdims=True)
        return carry
    lax.fori_loop(0,6,pair,0)
    for t in range(4):
        rows=pl.ds(t*256,256)
        acc=dz1_ref[rows,:]
        for i in range(3):
            acc=acc+dot(dqkv_ref[i,rows,:],w_ref[i],1,1)
        ig_ref[rows,:]=acc

def call_c(lengths,x,q,k,v,ctx,do,lse,dz1,w):
    V=pltpu.VMEM; S=jax.ShapeDtypeStruct
    return pl.pallas_call(kc_body,
        in_specs=[pl.BlockSpec(memory_space=pltpu.SMEM)]+[pl.BlockSpec(memory_space=V)]*8+[pl.BlockSpec(memory_space=pl.ANY)],
        out_specs=[pl.BlockSpec(memory_space=V)]*3,
        out_shape=[S((PACK,D),f32),S((3,D,D),bf16),S((8,D),f32)],
        scratch_shapes=[V((3,PACK,D),bf16),V((PACK,128),f32),V((3,D,D),bf16)],
        compiler_params=pltpu.CompilerParams(vmem_limit_bytes=62<<20))(lengths,x,q,k,v,ctx,do,lse,dz1,w)

RB=256
def diag_sum(blk):
    i=lax.broadcasted_iota(jnp.int32,blk.shape,0); j=lax.broadcasted_iota(jnp.int32,blk.shape,1)
    return jnp.sum(jnp.where(i==j,blk,0.0),keepdims=True)
def eye_rows(rb):
    i=lax.broadcasted_iota(jnp.int32,(RB,D),0)+rb*RB; j=lax.broadcasted_iota(jnp.int32,(RB,D),1)
    return i==j
def newton(m_ref,x_ref,nb_ref,pb_ref,sb_ref,xb_ref):
    nblk=D//RB
    R=[slice(i*RB,(i+1)*RB) for i in range(nblk)]
    tot=jnp.zeros((1,1),f32); tr=jnp.zeros((1,1),f32)
    for i in range(nblk):
        blk=m_ref[R[i],:]
        tot=tot+jnp.sum(blk*blk,keepdims=True)
        tr=tr+diag_sum(blk[:,R[i]])
    c=jnp.sqrt(tot+1e-6)
    inv=1.0/c
    al=tr*inv/D
    s=lax.rsqrt(jnp.sqrt(c))
    for i in range(nblk):
        m_ref[R[i],:]=m_ref[R[i],:]*inv
    def iteration(k,al,be,first=False,last=False):
        u=5-al
        u2=u*u;u3=u2*u;u4=u2*u2
        c0=al*u4*(1/256); c1=(u4-4*al*u3)*(1/256); c2=(12*al*u2-8*u3)*(1/512)
        c3=(36*u2-24*al*u)*(1/1536); c4=(24*al-96*u)*(1/6144); c5=1/256
        for i in range(nblk):
            nb_ref[R[i],:]=jnp.where(eye_rows(i),m_ref[R[i],:]-al,m_ref[R[i],:]).astype(bf16)
            if not first: xb_ref[R[i],:]=jnp.where(eye_rows(i),x_ref[R[i],:]-be,x_ref[R[i],:]).astype(bf16)
        be2=jnp.zeros((1,1),f32); al2=jnp.zeros((1,1),f32)
        for i in range(nblk):
            n=jnp.where(eye_rows(i),m_ref[R[i],:]-al,m_ref[R[i],:])
            if not last:
                p=dot(nb_ref[R[i],:],nb_ref[...])
                pb_ref[R[i],:]=p.astype(bf16)
                m=c1*n+c2*p
                m_ref[R[i],:]=jnp.where(eye_rows(i),m+c0,m)
            if first:
                x=jnp.where(eye_rows(i),1.25-al*0.25,0.0)-0.25*n
            else:
                x=(1.25-al*0.25)*x_ref[R[i],:]-0.25*(be*n+dot(xb_ref[R[i],:],nb_ref[...]))
            x_ref[R[i],:]=x
            be2=be2+diag_sum(x[:,R[i]])
        if not last:
            for i in range(nblk):
                q=dot(nb_ref[R[i],:],pb_ref[...])
                sb_ref[R[i],:]=(c3*nb_ref[R[i],:].astype(f32)+c4*pb_ref[R[i],:].astype(f32)+c5*q).astype(bf16)
            for i in range(nblk):
                m=m_ref[R[i],:]+dot(pb_ref[R[i],:],sb_ref[...])
                m_ref[R[i],:]=m
                al2=al2+diag_sum(m[:,R[i]])
        return al2*(1/D),be2*(1/D)
    al,be=iteration(0,al,None,first=True)
    al,be=lax.fori_loop(1,7,lambda k,ab:iteration(k,*ab),(al,be))
    iteration(7,al,be,last=True)
    for i in range(nblk):
        x_ref[R[i],:]=x_ref[R[i],:]*s
def body(a_ref,x_ref,m_ref,nb,pb,sb,xb):
    m_ref[...]=a_ref[...]
    newton(m_ref,x_ref,nb,pb,sb,xb)
def call_newton(a):
    V=pltpu.VMEM
    return pl.pallas_call(body,in_specs=[pl.BlockSpec(memory_space=V)],out_specs=pl.BlockSpec(memory_space=V),
      out_shape=jax.ShapeDtypeStruct((D,D),f32),scratch_shapes=[V((D,D),f32)]+[V((D,D),bf16)]*4,
      compiler_params=pltpu.CompilerParams(vmem_limit_bytes=60<<20))(a)

NZ=4; MR=48; HC=384
MESH=pl.DeviceIdType.MESH
def rcopy(src,dst,ss,rs,dev):
    return pltpu.make_async_remote_copy(src_ref=src,dst_ref=dst,send_sem=ss,recv_sem=rs,device_id=dev,device_id_type=MESH)

class Place:
    def __init__(self):
        self.dp=lax.axis_index("dp"); self.head=lax.axis_index("head")
        self.z=self.dp//2; self.x=self.dp%2; self.y=self.head//2; self.c=self.head%2
        self.xy=self.x*2+self.y
        self.chip=self.z*4+self.xy
        self.me=self.dp*4+self.head
        self.xn=((self.dp//2)*2+(1-self.x), self.head)
        self.yn=(self.dp,(1-self.y)*2+self.c)
        self.sib=(self.dp,self.y*2+(1-self.c))
        self.cols=pl.ds(pl.multiple_of(self.c*HC,128),HC)
        self.ocols=pl.ds(pl.multiple_of((1-self.c)*HC,128),HC)
    def zpeer(self,k):
        return (((self.z+k)%NZ)*2+self.x,self.head)
    def zfrom(self,k):
        return (self.z+NZ-k)%NZ
    def neighbours(self):
        return [self.zpeer(1),self.zpeer(2),self.zpeer(3),self.xn,self.yn,self.sib]

def greet(devs):
    bar=pltpu.get_barrier_semaphore()
    for d in devs:
        pl.semaphore_signal(bar,inc=1,device_id=d,device_id_type=MESH)
    pl.semaphore_wait(bar,len(devs))

def greet_all(pc):
    bar=pltpu.get_barrier_semaphore()
    def sig(k,carry):
        t=(pc.me+k)%32
        pl.semaphore_signal(bar,inc=1,device_id=(t//4,t%4),device_id_type=MESH)
        return carry
    lax.fori_loop(1,32,sig,0)
    pl.semaphore_wait(bar,31)

class Gather:
    def __init__(self,pc,buf,ss,rs):
        self.pc,self.buf,self.ss,self.rs=pc,buf,ss,rs
    def region(self,z,xy,mine=True):
        pc=self.pc
        return self.buf.at[z,xy,:,pc.cols if mine else pc.ocols]
    def copies(self):
        pc=self.pc; al=pl.ds(0,4); lo=pl.ds(0,2); hi=pl.ds(2,2)
        xo=(1-pc.x)*2+pc.y; yo=pc.x*2+(1-pc.y); dg=(1-pc.x)*2+(1-pc.y)
        R=self.region
        def mk(i,src,dst,dev):
            return rcopy(src,dst,self.ss.at[i],self.rs.at[i],dev)
        send={}
        for k in (1,2,3): send[k-1]=(R(pc.z,pc.xy),pc.zpeer(k))
        send[3]=(R(al,pc.xy),pc.xn); send[4]=(R(al,pc.xy),pc.yn)
        send[5]=(R(hi,yo),pc.xn); send[6]=(R(lo,xo),pc.yn)
        send[7]=(R(al,pc.xy),pc.sib); send[8]=(R(al,xo),pc.sib); send[9]=(R(al,yo),pc.sib); send[10]=(R(al,dg),pc.sib)
        recv={}
        for k in (1,2,3): recv[k-1]=R(pc.zfrom(k),pc.xy)
        recv[3]=R(al,xo); recv[4]=R(al,yo); recv[5]=R(hi,dg); recv[6]=R(lo,dg)
        recv[7]=R(al,pc.xy,False); recv[8]=R(al,xo,False); recv[9]=R(al,yo,False); recv[10]=R(al,dg,False)
        self.send=[partial(mk,i,send[i][0],send[i][0],send[i][1]) for i in range(11)]
        self.recv=[partial(mk,i,recv[i],recv[i],pc.sib) for i in range(11)]
        return self
    def step0(self):
        for i in (0,1,2): self.send[i]().start()
    def step1(self):
        for i in (0,1,2): self.recv[i]().wait_recv()
        for i in (3,4,7): self.send[i]().start()
    def step2(self):
        self.recv[3]().wait_recv()
        for i in (6,8): self.send[i]().start()
        self.recv[4]().wait_recv()
        for i in (5,9): self.send[i]().start()
    def step3(self):
        for i in (5,6): self.recv[i]().wait_recv()
        self.send[10]().start()
    def step4(self):
        for i in (7,8,9,10): self.recv[i]().wait_recv()
    def done(self):
        for i in range(11): self.send[i]().wait_send()
    def step(self,i):
        (self.step0,self.step1,self.step2,self.step3,self.step4)[i]()

ORDER=(0,1,2,3,4,8,5,9,6,10,7,11)
def ag_body(mas_ref,pv_ref,left_ref,right_ref, w_ref,pg_ref,st_ref, sibm,ss,rs,cs,cr,ts,tr,lsem):
    pc=Place()
    greet_all(pc)
    half=rcopy(mas_ref.at[:,:,pc.ocols],sibm,cs,cr,pc.sib)
    half.start()
    def stat(b,act):
        t=(b%4)*4+b//4
        for side,ref in enumerate((left_ref,right_ref)):
            dev=((t//2),(t%2)*2+side)
            idx=b*2+side
            mine=(pc.chip==t)&(pc.c==side)
            act(idx,ref.at[b],dev,mine)
    half.wait_recv()
    lo=pl.ds(0,24); hi=pl.ds(24,24)
    for b in ORDER:
        own=mas_ref[b,:,pc.cols]; oth=sibm[b]
        first=jnp.where(pc.c==0,own,oth); second=jnp.where(pc.c==0,oth,own)
        w_ref[b,pc.z,pc.xy,:,pc.cols]=jnp.concatenate([first,second],axis=0).astype(bf16)
    pg_ref[pc.z,pc.xy,:,pc.cols]=pv_ref[...]
    half.wait_send()
    gs=[Gather(pc,pg_ref,ss.at[12],rs.at[12]).copies()]+[Gather(pc,w_ref.at[b],ss.at[b],rs.at[b]).copies() for b in ORDER]
    for t in range(len(gs)+4):
        for s in range(5):
            if 0<=t-s<len(gs): gs[t-s].step(s)
    def start(b,carry):
        def act(idx,src,dev,mine):
            @pl.when(mine)
            def _(): pltpu.make_async_copy(src,st_ref.at[pc.me],tr).start()
            @pl.when(jnp.logical_not(mine))
            def _(): rcopy(src,st_ref.at[pc.me],ts.at[idx],tr,dev).start()
        stat(b,act)
        return carry
    lax.fori_loop(0,NB,start,0)
    for g in gs: g.done()
    def fin(b,carry):
        def act(idx,src,dev,mine):
            @pl.when(jnp.logical_not(mine))
            def _(): rcopy(src,st_ref.at[pc.me],ts.at[idx],tr,dev).wait_send()
        stat(b,act)
        return carry
    lax.fori_loop(0,NB,fin,0)
    @pl.when(pc.xy<3)
    def _(): pltpu.make_async_copy(st_ref,st_ref,tr).wait()

def call_ag(masters,pv,left,right):
    V=pltpu.VMEM; S=jax.ShapeDtypeStruct; A=pl.ANY
    B=lambda m: pl.BlockSpec(memory_space=m)
    sem=pltpu.SemaphoreType.DMA
    return pl.pallas_call(ag_body,in_specs=[B(V),B(V),B(A),B(A)],out_specs=[B(V),B(V),B(A)],
        out_shape=[S((NB,4,4,MR,D),bf16),S((4,4,16,D),bf16),S((32,24,D),f32)],
        scratch_shapes=[V((NB,24,HC),f32),sem((13,11)),sem((13,11)),sem,sem,sem((24,)),sem,sem],
        compiler_params=pltpu.CompilerParams(vmem_limit_bytes=60<<20,collective_id=0,has_side_effects=True))(masters,pv,left,right)

def params_of(pg):
    t=pg.reshape(16,16,2,HC)[:,:12,:,:24]
    return jnp.transpose(t,(1,0,2,3)).reshape(12,D).astype(f32)


class Scatter:
    def __init__(self,pc,b,g_ref,R,out_ref,gown_ref,ss,rs,os_,orr):
        self.pc,self.b,self.g=pc,b,g_ref.at[b]
        self.out,self.gown=out_ref,gown_ref
        self.os_,self.orr=os_,orr
        self.R={k:v.at[b] for k,v in R.items()}
        R=self.R
        s1,rc=R["s1"],R["rc"]
        def mk(i,src,dst,dev): return rcopy(src,dst,ss.at[b,i],rs.at[b,i],dev)
        lo=pl.ds(0,2); hi=pl.ds(2,2); al=pl.ds(0,4)
        self.core=mk(0,self.g.at[:,:,:,pc.ocols],rc,pc.sib)
        self.xa=mk(1,s1.at[lo,pl.ds((1-pc.x)*2,2)],R["xa"],pc.xn)
        self.yb=[mk(2+i,s1.at[hi,i*2+1-pc.y],R["yb"].at[i],pc.yn) for i in range(2)]
        self.ya=mk(4,R["s2a"],R["ya"],pc.yn)
        self.xb=mk(5,R["s2b"],R["xb"],pc.xn)
        self.zz=[mk(6+k-1,R["s3"].at[(pc.z+k)%NZ],R["zr"].at[k-1],pc.zpeer(k)) for k in (1,2,3)]
        self.home=mk(9,R["fin"].at[pl.ds(pl.multiple_of((1-pc.c)*24,8),24)],R["hr"],pc.sib)
        t=(b%4)*4+b//4
        self.t=t
        self.owner=[((t//2),(t%2)*2+side) for side in range(2)]
        self.to_owner=[rcopy(R["finb"],gown_ref.at[pc.chip,:,pc.cols],os_.at[b,side],orr,self.owner[side]) for side in range(2)]
        self.to_self=pltpu.make_async_copy(R["finb"],gown_ref.at[pc.chip,:,pc.cols],orr)
    def step0(self):
        self.core.start()
    def step1(self):
        pc=self.pc; R=self.R
        self.core.wait_recv()
        for z in range(4):
            R["s1"][z]=(self.g[z,:,:,pc.cols].astype(f32)+R["rc"][z].astype(f32)).astype(bf16)
        self.xa.start()
        for d in self.yb: d.start()
    def step2(self):
        pc=self.pc; R=self.R
        self.xa.wait_recv()
        s=R["s1"][0:2,pl.ds(pc.x*2,2)].astype(f32)+R["xa"][...].astype(f32)
        keep=jnp.where(pc.y==0,s[:,0],s[:,1]); give=jnp.where(pc.y==0,s[:,1],s[:,0])
        R["k2"][0:2]=keep; R["s2a"][...]=give.astype(bf16)
        self.ya.start()
        for d in self.yb: d.wait_recv()
        s0=R["s1"][2:4,pc.y].astype(f32)+R["yb"][0].astype(f32)
        s1=R["s1"][2:4,2+pc.y].astype(f32)+R["yb"][1].astype(f32)
        keep=jnp.where(pc.x==0,s0,s1); give=jnp.where(pc.x==0,s1,s0)
        R["k2"][2:4]=keep; R["s2b"][...]=give.astype(bf16)
        self.xb.start()
    def step3(self):
        R=self.R
        self.ya.wait_recv(); self.xb.wait_recv()
        a=R["k2"][0:2]+R["ya"][...].astype(f32)
        b=R["k2"][2:4]+R["xb"][...].astype(f32)
        R["k2"][0:2]=a; R["k2"][2:4]=b
        R["s3"][0:2]=a.astype(bf16); R["s3"][2:4]=b.astype(bf16)
        for d in self.zz: d.start()
    def step4(self):
        pc=self.pc; R=self.R
        for d in self.zz: d.wait_recv()
        s=R["k2"][pc.z]
        for k in range(3): s=s+R["zr"][k].astype(f32)
        R["fin"][...]=s
        R["finb"][...]=s.astype(bf16)
        self.home.start()
        @pl.when(pc.chip==self.t)
        def _():
            self.to_self.start()
            for side in range(2):
                @pl.when(pc.c!=side)
                def _(): self.to_owner[side].start()
        @pl.when(pc.chip!=self.t)
        def _():
            for d in self.to_owner: d.start()
    def step5(self):
        pc=self.pc; R=self.R
        self.home.wait_recv()
        own=R["fin"][pl.ds(pl.multiple_of(pc.c*24,8),24)]; oth=R["hr"][...]
        self.out[self.b,:,pc.cols]=own
        self.out[self.b,:,pc.ocols]=oth
    def step(self,i): (self.step0,self.step1,self.step2,self.step3,self.step4,self.step5)[i]()
    def done(self):
        pc=self.pc
        for d in [self.core,self.xa,*self.yb,self.ya,self.xb,*self.zz,self.home]: d.wait_send()
        @pl.when(pc.chip==self.t)
        def _():
            for side in range(2):
                @pl.when(pc.c!=side)
                def _(): self.to_owner[side].wait_send()
        @pl.when(pc.chip!=self.t)
        def _():
            for d in self.to_owner: d.wait_send()

def scatter_scratch(nb=NB):
    V=pltpu.VMEM
    return dict(s1=V((nb,4,4,MR,HC),bf16),rc=V((nb,4,4,MR,HC),bf16),xa=V((nb,2,2,MR,HC),bf16),yb=V((nb,2,2,MR,HC),bf16),
        s2a=V((nb,2,MR,HC),bf16),s2b=V((nb,2,MR,HC),bf16),ya=V((nb,2,MR,HC),bf16),xb=V((nb,2,MR,HC),bf16),
        k2=V((nb,4,MR,HC),f32),s3=V((nb,4,MR,HC),bf16),zr=V((nb,3,MR,HC),bf16),fin=V((nb,MR,HC),f32),finb=V((nb,MR,HC),bf16),hr=V((nb,24,HC),f32))

class VecSum:
    def __init__(self,pc,cur,buf,ss,rs):
        self.pc,self.cur,self.buf=pc,cur,buf
        zp=lambda bit: ((pc.z^bit)*2+pc.x,pc.head)
        z1=(pc.z+1-2*(pc.z%2)); z2=(pc.z+2)%4
        partners=[pc.sib,pc.xn,pc.yn,(z1*2+pc.x,pc.head),(z2*2+pc.x,pc.head)]
        self.d=[rcopy(cur.at[i],buf.at[i],ss.at[i],rs.at[i],p) for i,p in enumerate(partners)]
    def step(self,i):
        if i>0:
            self.d[i-1].wait_recv()
            self.cur[i]=self.cur[i-1]+self.buf[i-1]
        if i<5: self.d[i].start()
    def done(self):
        for d in self.d: d.wait_send()

RSORDER=(8,4,9,5,10,6,11,7,3,2,1,0)
KEYS=list(scatter_scratch())
def rs_body(g_ref,vec_ref,out_ref,vout_ref,gown_ref,*rest):
    R=dict(zip(KEYS,rest[:len(KEYS)])); vcur,vbuf,ss,rs,os_,orr,vs,vr=rest[len(KEYS):]
    pc=Place()
    greet_all(pc)
    vcur[0]=vec_ref[...]
    vsum=VecSum(pc,vcur,vbuf,vs,vr)
    sc=[Scatter(pc,b,g_ref,R,out_ref,gown_ref,ss,rs,os_,orr) for b in RSORDER]
    for t in range(len(sc)+5):
        for s in range(6):
            if 0<=t-s<len(sc): sc[t-s].step(s)
        if t<=5: vsum.step(t)
    vout_ref[...]=vcur[5]
    for s in sc: s.done()
    vsum.done()
    @pl.when(pc.xy<3)
    def _(): pltpu.make_async_copy(gown_ref,gown_ref,orr).wait()

def call_rs(g,vec):
    V=pltpu.VMEM; S=jax.ShapeDtypeStruct
    B=pl.BlockSpec(memory_space=V); sem=pltpu.SemaphoreType.DMA
    return pl.pallas_call(rs_body,in_specs=[B,B],out_specs=[B,B,B],
        out_shape=[S((NB,24,D),f32),S((16,D),f32),S((16,MR,D),bf16)],
        scratch_shapes=list(scatter_scratch().values())+[V((6,16,D),f32),V((5,16,D),f32),sem((NB,10)),sem((NB,10)),sem((NB,2)),sem,sem((5,)),sem((5,))],
        compiler_params=pltpu.CompilerParams(vmem_limit_bytes=62<<20,collective_id=1,has_side_effects=True))(g,vec)

BETA=0.95; BETA_TWO=0.99; RATE=1.0; RATE_VEC=0.05

def owner_of(b):
    return ((b//3+(b%3)%2+1)%4)*4+b%3
def owned_by(pc):
    return 3*((pc.z+3-pc.xy%2)%4)+pc.xy

def pack(rows):
    return jnp.concatenate([rows[:,:HC],rows[:,HC:]],axis=0).astype(bf16)
def unpack(p):
    p=p.astype(f32)
    return jnp.concatenate([p[:24],p[24:]],axis=1)

def send_rows(pc,n,base,slots,dst,ss,rsem,start):
    def one(j,carry):
        t=base+j
        @pl.when(t==pc.me)
        def _():
            if start: pltpu.make_async_copy(slots.at[j],dst,rsem).start()
        @pl.when(t!=pc.me)
        def _():
            d=rcopy(slots.at[j],dst,ss.at[j],rsem,(t//4,t%4))
            if start: d.start()
            else: d.wait_send()
        return carry
    lax.fori_loop(0,n,one,0)

def newton_body(ghalf_ref,stat_ref,left_ref,right_ref,mas_ref,va_ref,vec_ref,sec_ref,
                ln_ref,rn_ref,mn_ref,vg_ref,sn_ref,vn_ref,
                m_ref,x_ref,nb,pb,sb,xb,slots,ggr,uslots,ur,tb,rt,rho,gown_ref, gs,gr,us,ur_sem,es,er):
    pc=Place()
    gown_ref[:,pc.cols]=ghalf_ref[...]
    greet_all(pc)
    b=owned_by(pc)
    owner=pc.xy<3
    nblk=D//RB
    @pl.when(owner)
    def _():
        swap=rcopy(gown_ref.at[:,pc.cols],gown_ref.at[:,pc.cols],es.at[3],er.at[3],pc.sib)
        swap.start()
        swap.wait_recv()
        for c in range(2):
            @pl.when(pc.c==c)
            def _():
                for i in range(nblk):
                    r=slice(i*RB,(i+1)*RB)
                    if c==0: p=dot(gown_ref[r,:],gown_ref[...],1,1)
                    else: p=dot(gown_ref[:,r],gown_ref[...],0,0)
                    x_ref[r,:]=(1-BETA)*p
                    m_ref[r,:]=BETA*stat_ref[r,:]+(1-BETA)*p
        def pk(i,carry):
            slots[i]=pack(x_ref[pl.ds(pl.multiple_of(i*24,8),24),:])
            return carry
        lax.fori_loop(0,32,pk,0)
        send_rows(pc,32,0,slots,ggr.at[2*b+pc.c],gs,gr,True)
        newton(m_ref,x_ref,nb,pb,sb,xb)
        tr=jnp.zeros((1,1),f32)
        for i in range(nblk):
            r=slice(i*RB,(i+1)*RB); tr=tr+diag_sum(x_ref[r,r])
        lam=tr*(1/D)
        for i in range(nblk):
            r=slice(i*RB,(i+1)*RB)
            xb[r,:]=jnp.where(eye_rows(i),x_ref[r,:]-lam,x_ref[r,:]).astype(bf16)
        H=D//2
        send_t=rcopy(tb.at[pl.ds(H,H)],tb.at[pl.ds(H,H)],es.at[0],er.at[0],pc.sib)
        send_r=rcopy(xb,rt,es.at[1],er.at[1],pc.sib)
        send_l=rcopy(rho.at[0],rho.at[1],es.at[2],er.at[2],pc.sib)
        def update(trows,right,lam_r):
            for i in range(2):
                r=pl.ds(trows+i*192,192)
                t=tb[r,:]
                m_ref[pl.ds(i*192,192),:]=lam_r*t.astype(f32)+dot(t,right[...])
        rho[0]=jnp.broadcast_to(lam,(8,128))
        @pl.when(pc.c==0)
        def _():
            for h in (1,0):
                for i in range(2):
                    r=slice(h*H+i*192,h*H+(i+1)*192)
                    tb[r,:]=(lam*gown_ref[r,:].astype(f32)+dot(xb[r,:],gown_ref[...])).astype(bf16)
                if h==1: send_t.start()
            send_r.wait_recv(); send_l.wait_recv()
            update(0,rt,rho[1,0:1,0:1])
            send_t.wait_send()
        @pl.when(pc.c==1)
        def _():
            send_r.start(); send_l.start()
            send_t.wait_recv()
            update(H,xb,lam)
            send_r.wait_send(); send_l.wait_send()
        def pk2(i,carry):
            uslots[i]=pack(m_ref[pl.ds(pl.multiple_of(i*24,8),24),:])
            return carry
        lax.fori_loop(0,16,pk2,0)
        send_rows(pc,16,pc.c*16,uslots,ur.at[b],us,ur_sem,True)
    r=lax.broadcasted_iota(jnp.int32,(D,128),1); j=lax.broadcasted_iota(jnp.int32,(D,128),0)
    pick=jnp.where((j==pc.me*24+r)&(r<24),1.0,0.0).astype(f32)
    vg=lax.dot_general(va_ref[...],pick,(((1,),(0,)),((),())),precision=lax.Precision.HIGHEST,preferred_element_type=f32)[:12,:24]
    sn=BETA_TWO*sec_ref[...]+(1-BETA_TWO)*vg*vg
    vg_ref[...]=vg; sn_ref[...]=sn
    vn_ref[...]=vec_ref[...]-RATE_VEC*vg/(jnp.sqrt(sn)+1e-8)
    pltpu.make_async_copy(ggr,ggr,gr).wait()
    def stats(i,carry):
        ln_ref[i]=BETA*left_ref[i]+unpack(ggr[2*i])
        rn_ref[i]=BETA*right_ref[i]+unpack(ggr[2*i+1])
        return carry
    lax.fori_loop(0,NB,stats,0)
    pltpu.make_async_copy(ur,ur,ur_sem).wait()
    def upd(i,carry):
        mn_ref[i]=mas_ref[i]-RATE*unpack(ur[i])
        return carry
    lax.fori_loop(0,NB,upd,0)
    @pl.when(owner)
    def _():
        rcopy(gown_ref.at[:,pc.cols],gown_ref.at[:,pc.cols],es.at[3],er.at[3],pc.sib).wait_send()
        send_rows(pc,32,0,slots,ggr.at[2*b+pc.c],gs,gr,False)
        send_rows(pc,16,pc.c*16,uslots,ur.at[b],us,ur_sem,False)

def call_newton_step(gown,stat,left,right,mas,va,vec,sec):
    V=pltpu.VMEM; S=jax.ShapeDtypeStruct
    B=pl.BlockSpec(memory_space=V); sem=pltpu.SemaphoreType.DMA
    rows=S((NB,24,D),f32); small=S((NB,24),f32)
    return pl.pallas_call(newton_body,in_specs=[B]*8,out_specs=[B]*6,out_shape=[rows]*3+[small]*3,
        scratch_shapes=[V((D,D),f32)]*2+[V((D,D),bf16)]*4+[V((32,48,HC),bf16),V((24,48,HC),bf16),V((16,48,HC),bf16),V((12,48,HC),bf16),V((D,D),bf16),V((D,D),bf16),V((2,8,128),f32),V((D,D),bf16),
            sem((32,)),sem,sem((16,)),sem,sem((4,)),sem((4,))],
        compiler_params=pltpu.CompilerParams(vmem_limit_bytes=62<<20,collective_id=2,has_side_effects=True))(gown,stat,left,right,mas,va,vec,sec)


def place_params(pg_ref,p_ref):
    r=lax.broadcasted_iota(jnp.int32,(128,D),0); j=lax.broadcasted_iota(jnp.int32,(128,D),1)
    p_ref[...]=jnp.zeros_like(p_ref)
    def chip(m,carry):
        for c in range(2):
            sel=jnp.where((j==(m*2+c)*24+r)&(r<24),1.0,0.0).astype(bf16)
            p_ref[...]+=dot(pg_ref[m//4,m%4,:,c*HC:c*HC+128],sel)
        return carry
    lax.fori_loop(0,16,chip,0)

def keys_of_pair(p,k_ref,ka_ref,v_ref,va_ref,doc_ref):
    cols=pl.ds(pl.multiple_of(p*128,128),128)
    lane=lax.broadcasted_iota(jnp.int32,(256,128),1)
    for t in range(PACK//256):
        rows=pl.ds(t*256,256)
        kp=k_ref[rows,cols].astype(f32); vp=v_ref[rows,cols].astype(f32)
        doc=doc_ref[rows,:]
        for h,lo in enumerate((True,False)):
            off=64 if lo else 0
            k1=onehot_part(kp,lane,lo,doc,1.0,1.0)
            ka_ref[h,rows,:]=jnp.where((lane>=off+8)&(lane<off+11),1.0,k1).astype(bf16)
            va_ref[h,rows,:]=jnp.where((lane<64)==lo,vp,1.0).astype(bf16)

QF=512
def attend_block(p,b,q_ref,ka_ref,va_ref,qa_ref,ctx_ref,doc_ref):
    cols=pl.ds(pl.multiple_of(p*128,128),128)
    rows=pl.ds(pl.multiple_of(b*QF,QF),QF)
    lane=lax.broadcasted_iota(jnp.int32,(QF,128),1)
    low=lane<64
    qp=q_ref[rows,cols].astype(f32)*0.125
    doc=doc_ref[rows,:]
    qf=[onehot_part(qp,lane,lo,doc,0.0,BIG) for lo in (True,False)]
    ss=[dot(qf[h].astype(bf16),ka_ref[h],1,1) for h in range(2)]
    os=[]
    for h,lo in enumerate((True,False)):
        off=64 if lo else 0
        m=jnp.max(ss[h],axis=1,keepdims=True)
        o=dot(jnp.exp(ss[h]-m).astype(bf16),va_ref[h])
        os.append(o)
        q1=qf[h]
        for i,c in enumerate(split3(-(m+jnp.log(o)))): q1=jnp.where(lane==off+8+i,c,q1)
        qa_ref[h,rows,:]=q1.astype(bf16)
    l=pltpu.roll(jnp.where(low,os[1],os[0]),64,1)
    ctx_ref[rows,cols]=(jnp.where(low,os[0],os[1])/l).astype(bf16)

AORDER=(0,1,2,3,4,8,5,9,6,10,7,11)
TT=256
def front_body(len_ref,x_ref,cot_ref,mas_ref,pv_ref,left_ref,right_ref,
               out_o,qa_o,ka_o,v_o,ctx_o,act_o,din_o,dffn_o,hlow_o,dz1_o,dctx_o,wq_o,vec_o,st_ref,
               w_ref,pg_ref,p_ref,sibm,q,k,v,ctx,doc,qa,ka,va,n1,r1,hlow,acc,act,gp,dffn,dctx,out,
               ss,rs,cs,cr,ts,tr,lsem,asem,osem):
    pc=Place()
    greet_all(pc)
    first=rcopy(mas_ref.at[pl.ds(0,3),:,pc.ocols],sibm.at[pl.ds(0,3)],cs.at[0],cr.at[0],pc.sib)
    other=rcopy(mas_ref.at[pl.ds(3,9),:,pc.ocols],sibm.at[pl.ds(3,9)],cs.at[1],cr.at[1],pc.sib)
    first.start(); other.start()
    pg_ref[pc.z,pc.xy,:,pc.cols]=pv_ref[...]
    def assemble(places):
        for pos in places:
            own=mas_ref[AORDER[pos],:,pc.cols]; oth=sibm[AORDER[pos]]
            upper=jnp.where(pc.c==0,own,oth); lower=jnp.where(pc.c==0,oth,own)
            w_ref[pos,pc.z,pc.xy,:,pc.cols]=jnp.concatenate([upper,lower],axis=0).astype(bf16)
    def group(g):
        if isinstance(g,int) and g==0: return Gather(pc,pg_ref,ss.at[0],rs.at[0]).copies()
        return Gather(pc,w_ref.at[g-1],ss.at[g],rs.at[g]).copies()
    NG=13
    def tick(t):
        for s in range(5):
            if isinstance(t,int):
                if 0<=t-s<NG and not (s==0 and t<4): group(t-s).step(s)
            else:
                @pl.when(t-s<NG)
                def _(): group(t-s).step(s)
    def stat(i,start):
        b=(i+pc.me)%NB
        t=owner_of(b)
        for side,ref in enumerate((left_ref,right_ref)):
            mine=(pc.chip==t)&(pc.c==side)
            d=rcopy(ref.at[b],st_ref.at[pc.me],ts.at[b*2+side],tr,(t//2,(t%2)*2+side))
            if start:
                @pl.when(mine)
                def _(): pltpu.make_async_copy(ref.at[b],st_ref.at[pc.me],tr).start()
            @pl.when(jnp.logical_not(mine))
            def _():
                if start: d.start()
                else: d.wait_send()
    copies=[]
    def away(src,dst):
        i=len(copies)
        c=pltpu.make_async_copy(src,dst,lsem.at[i]); c.start(); copies.append(c)
    W=lambda pos: w_ref[pos].reshape(D,D)
    group(0).step(0)
    first.wait_recv()
    for i in range(3):
        assemble([i])
        group(i+1).step(0)
    other.wait_recv()
    assemble(range(3,12))
    for t in range(1,5): tick(t)
    place_params(pg_ref,p_ref)
    t_=lax.broadcasted_iota(jnp.int32,(PACK,128),0)
    end=jnp.int32(0); dd=jnp.zeros((PACK,128),jnp.int32)
    for j in range(8):
        end=end+len_ref[0,j]
        dd=dd+(t_>=end).astype(jnp.int32)
    doc[...]=dd
    for i,(o,b,dst) in enumerate(((q,0,None),(k,None,None),(v,1,v_o))):
        tick(5+i)
        for tl in range(4):
            rows=pl.ds(tl*TT,TT)
            y=dot(x_ref[rows,:],W(i))
            if b is not None: y=y+p_ref[b:b+1,:]
            o[rows,:]=y.astype(bf16)
        if dst is not None: away(o,dst)
        away(w_ref.at[i],wq_o.at[i])
    def pair_copies(p):
        return [pltpu.make_async_copy(s.at[p%2],d.at[p],asem.at[i,p%2]) for i,(s,d) in enumerate(((qa,qa_o),(ka,ka_o)))]
    def slot(n,carry):
        p=n//2; b=n%2
        @pl.when(b==0)
        def _():
            @pl.when(p>=2)
            def _():
                for c in pair_copies(p-2): c.wait()
            keys_of_pair(p,k,ka.at[p%2],v,va,doc)
        attend_block(p,b,q,ka.at[p%2],va,qa.at[p%2],ctx,doc)
        @pl.when(b==1)
        def _():
            for c in pair_copies(p): c.start()
            tick(8+p)
        @pl.when(n%2==1)
        def _(): stat(n//2,True)
        return carry
    lax.fori_loop(0,12,slot,0)
    away(ctx,ctx_o)
    g1,s1,g2,s2=(p_ref[i:i+1,:] for i in (8,9,10,11))
    vec_o[...]=jnp.zeros_like(vec_o)
    def out_proj(tl,carry):
        rows=pl.ds(pl.multiple_of(tl*TT,TT),TT)
        z=x_ref[rows,:].astype(f32)+(dot(ctx[rows,:],W(3))+p_ref[2:3,:])
        n,r=layer_norm(z)
        n1[rows,:]=n
        r1[rows,:]=jnp.broadcast_to(r,(TT,128))
        hlow[rows,:]=(n*g1+s1).astype(bf16)
        return carry
    lax.fori_loop(0,4,out_proj,0)
    tick(14)
    def chunk_copy(c):
        lane=pl.ds(pl.multiple_of(c*D,128),D)
        return pltpu.make_async_copy(act.at[:,lane],act_o.at[:,lane],osem.at[5,c])
    def chunk(c,carry):
        lane=pl.ds(pl.multiple_of(c*D,128),D)
        bias=p_ref[pl.ds(3+c,1),:]
        for tl in range(4):
            rows=pl.ds(tl*TT,TT)
            inner=dot(hlow[rows,:],W(4+2*c))+bias
            a,g=gelu_both(inner)
            al=a.astype(bf16)
            act[rows,lane]=al
            gp[rows,lane]=g.astype(bf16)
            y=dot(al,W(5+2*c))
            @pl.when(c==0)
            def _(): acc[rows,:]=y
            @pl.when(c>0)
            def _(): acc[rows,:]+=y
        chunk_copy(c).start()
        @pl.when(c<2)
        def _(): tick(15+c)
        return carry
    lax.fori_loop(0,4,chunk,0)
    lax.fori_loop(6,NB,lambda b,c: (stat(b,True),c)[1],0)
    away(hlow,hlow_o)
    pltpu.make_async_copy(cot_ref,out,lsem.at[20]).start()
    pltpu.make_async_copy(cot_ref,out,lsem.at[20]).wait()
    def tile_copies(tl):
        rows=pl.ds(pl.multiple_of(tl*TT,TT),TT)
        return [pltpu.make_async_copy(s.at[rows],d.at[rows],osem.at[i,tl]) for i,(s,d) in enumerate(((out,out_o),(gp,din_o),(dffn,dffn_o),(acc,dz1_o),(dctx,dctx_o)))]
    def tile(tl,carry):
        rows=pl.ds(pl.multiple_of(tl*TT,TT),TT)
        n1t=n1[rows,:]
        z=(n1t*g1+s1)+(acc[rows,:]+p_ref[7:8,:])
        n2,r2=layer_norm(z)
        e=out[rows,:].astype(f32)
        out[rows,:]=(n2*g2+s2).astype(bf16)
        c2=e*g2
        dz2=r2*(c2-jnp.mean(c2,axis=-1,keepdims=True)-n2*jnp.mean(c2*n2,axis=-1,keepdims=True))
        df=dz2.astype(bf16)
        dffn[rows,:]=df
        vec_o[10:11,:]+=jnp.sum(e*n2,axis=0,keepdims=True)
        vec_o[11:12,:]+=jnp.sum(e,axis=0,keepdims=True)
        vec_o[7:8,:]+=jnp.sum(df.astype(f32),axis=0,keepdims=True)
        dh=dz2
        for c in range(4):
            lane=pl.ds(c*D,D)
            dact=dot(df,W(5+2*c),1,1)
            din=(dact*gp[rows,lane].astype(f32)).astype(bf16)
            gp[rows,lane]=din
            vec_o[3+c:4+c,:]+=jnp.sum(din.astype(f32),axis=0,keepdims=True)
            dh=dh+dot(din,W(4+2*c),1,1)
        vec_o[8:9,:]+=jnp.sum(dh*n1t,axis=0,keepdims=True)
        vec_o[9:10,:]+=jnp.sum(dh,axis=0,keepdims=True)
        c1=dh*g1
        dz1=r1[rows,0:1]*(c1-jnp.mean(c1,axis=-1,keepdims=True)-n1t*jnp.mean(c1*n1t,axis=-1,keepdims=True))
        acc[rows,:]=dz1
        dat=dz1.astype(bf16)
        vec_o[2:3,:]+=jnp.sum(dat.astype(f32),axis=0,keepdims=True)
        dctx[rows,:]=dot(dat,W(3),1,1).astype(bf16)
        for c in tile_copies(tl): c.start()
        return carry
    lax.fori_loop(0,4,tile,0)
    for c in copies: c.wait()
    for p in (4,5):
        for c in pair_copies(p): c.wait()
    for i in range(4):
        chunk_copy(i).wait()
        for c in tile_copies(i): c.wait()
    first.wait_send(); other.wait_send()
    group(0).done()
    lax.fori_loop(1,NG,lambda g,c: (group(g).done(),c)[1],0)
    lax.fori_loop(0,NB,lambda b,c: (stat(b,False),c)[1],0)
    @pl.when(pc.xy<3)
    def _(): pltpu.make_async_copy(st_ref,st_ref,tr).wait()

def call_front(lengths,x,cot,masters,pv,left,right):
    V=pltpu.VMEM; S=jax.ShapeDtypeStruct; A=pl.ANY
    B=lambda m: pl.BlockSpec(memory_space=m)
    sem=pltpu.SemaphoreType.DMA
    T=lambda w,d: S((PACK,w),d)
    return pl.pallas_call(front_body,
        in_specs=[B(pltpu.SMEM),B(V),B(A),B(V),B(V),B(A),B(A)],
        out_specs=[B(A)]*12+[B(V),B(A)],
        out_shape=[T(D,bf16)]+[S((6,2,PACK,128),bf16)]*2+[T(D,bf16)]*2+[T(FF,bf16),T(FF,bf16),T(D,bf16),T(D,bf16),T(D,f32),T(D,bf16),S((3,4,4,MR,D),bf16),S((16,D),f32),S((32,24,D),f32)],
        scratch_shapes=[V((NB,4,4,MR,D),bf16),V((4,4,16,D),bf16),V((16,D),f32),V((NB,24,HC),f32)]+[V((PACK,D),bf16)]*4+
            [V((PACK,128),jnp.int32),V((2,2,PACK,128),bf16),V((2,2,PACK,128),bf16),V((2,PACK,128),bf16),V((PACK,D),f32),V((PACK,128),f32),V((PACK,D),bf16),V((PACK,D),f32),
             V((PACK,FF),bf16),V((PACK,FF),bf16),V((PACK,D),bf16),V((PACK,D),bf16),V((PACK,D),bf16),
             sem((13,11)),sem((13,11)),sem((2,)),sem((2,)),sem((24,)),sem,sem((24,)),sem((2,2)),sem((6,4))],
        compiler_params=pltpu.CompilerParams(vmem_limit_bytes=63<<20,collective_id=0,has_side_effects=True))(lengths,x,cot,masters,pv,left,right)


NGR=12
def sum_scratch():
    V=pltpu.VMEM; nb=NGR
    return dict(rc=V((nb,4,4,MR,HC),bf16),xa=V((nb,2,2,MR,HC),bf16),yb=V((nb,2,2,MR,HC),bf16),
        s2a=V((nb,2,MR,HC),bf16),s2b=V((nb,2,MR,HC),bf16),ya=V((nb,2,MR,HC),bf16),xb=V((nb,2,MR,HC),bf16),
        s3=V((nb,4,MR,HC),bf16),zr=V((nb,3,MR,HC),bf16),fin=V((nb,MR,HC),f32),finb=V((nb,MR,HC),bf16),hr=V((nb,24,HC),f32))
SKEYS=list(sum_scratch())

class GroupSum:
    def __init__(self,pc,g_ref,R,out_ref,gown_ref,ss,rs,os_,orr):
        self.pc,self.gr,self.RR,self.out,self.gown=pc,g_ref,R,out_ref,gown_ref
        self.ss,self.rs,self.os_,self.orr=ss,rs,os_,orr
    def mk(self,g,i,src,dst,dev): return rcopy(src,dst,self.ss.at[g,i],self.rs.at[g,i],dev)
    def of(self,g): return self.gr.at[g],{k:v.at[g] for k,v in self.RR.items()}
    def core(self,g):
        G,R=self.of(g); return self.mk(g,0,G.at[:,:,:,self.pc.ocols],R["rc"],self.pc.sib)
    def xa(self,g):
        G,R=self.of(g); pc=self.pc; return self.mk(g,1,G.at[pl.ds(0,2),pl.ds((1-pc.x)*2,2),:,pc.cols],R["xa"],pc.xn)
    def yb(self,g,i):
        G,R=self.of(g); pc=self.pc; return self.mk(g,2+i,G.at[pl.ds(2,2),i*2+1-pc.y,:,pc.cols],R["yb"].at[i],pc.yn)
    def ya(self,g):
        G,R=self.of(g); return self.mk(g,4,R["s2a"],R["ya"],self.pc.yn)
    def xb(self,g):
        G,R=self.of(g); return self.mk(g,5,R["s2b"],R["xb"],self.pc.xn)
    def zz(self,g,k):
        G,R=self.of(g); pc=self.pc; return self.mk(g,5+k,R["s3"].at[(pc.z+k)%NZ],R["zr"].at[k-1],pc.zpeer(k))
    def home(self,g):
        G,R=self.of(g); pc=self.pc; return self.mk(g,9,R["fin"].at[pl.ds(pl.multiple_of((1-pc.c)*24,8),24)],R["hr"],pc.sib)
    def step0(self,g): self.core(g).start()
    def step1(self,g):
        pc=self.pc; G,R=self.of(g)
        self.core(g).wait_recv()
        for z in range(4):
            G[z,:,:,pc.cols]=(G[z,:,:,pc.cols].astype(f32)+R["rc"][z].astype(f32)).astype(bf16)
        self.xa(g).start()
        for i in range(2): self.yb(g,i).start()
    def step2(self,g):
        pc=self.pc; G,R=self.of(g)
        self.xa(g).wait_recv()
        R["s2a"][...]=(G[0:2,pc.x*2+1-pc.y,:,pc.cols].astype(f32)+R["xa"][:,1-pc.y].astype(f32)).astype(bf16)
        self.ya(g).start()
        for i in range(2): self.yb(g,i).wait_recv()
        R["s2b"][...]=(G[2:4,(1-pc.x)*2+pc.y,:,pc.cols].astype(f32)+R["yb"][1-pc.x].astype(f32)).astype(bf16)
        self.xb(g).start()
    def step3(self,g):
        pc=self.pc; G,R=self.of(g)
        self.ya(g).wait_recv(); self.xb(g).wait_recv()
        a=G[0:2,pc.xy,:,pc.cols].astype(f32)+R["xa"][:,pc.y].astype(f32)+R["ya"][...].astype(f32)
        b=G[2:4,pc.xy,:,pc.cols].astype(f32)+R["yb"][pc.x].astype(f32)+R["xb"][...].astype(f32)
        R["s3"][0:2]=a.astype(bf16); R["s3"][2:4]=b.astype(bf16)
        ab=jnp.where(pc.z%2==0,jnp.stack([a[0],b[0]]),jnp.stack([a[1],b[1]]))
        R["fin"][...]=jnp.where(pc.z<2,ab[0],ab[1])
        for k in (1,2,3): self.zz(g,k).start()
    def targets(self,g,act):
        pc=self.pc; G,R=self.of(g)
        def whole(b):
            act(R["finb"],self.gown.at[pc.chip],0,owner_of(b))
        def slab(j):
            for i in range(3):
                act(R["finb"].at[:,pl.ds(i*128,128)],self.gown.at[pc.chip,:,pl.ds(pl.multiple_of(j*128,128),128)],i,owner_of(i))
        if isinstance(g,int):
            if g<9: whole(8+g//2-4*(g%2)-9*(g//8))
            else: slab(g-9)
        else:
            @pl.when(g<9)
            def _(): whole(8+g//2-4*(g%2)-9*(g//8))
            @pl.when(g>=9)
            def _(): slab(g-9)
    def step4(self,g):
        pc=self.pc; G,R=self.of(g)
        for k in (1,2,3): self.zz(g,k).wait_recv()
        s=R["fin"][...]
        for k in range(3): s=s+R["zr"][k].astype(f32)
        R["fin"][...]=s
        R["finb"][...]=s.astype(bf16)
        self.home(g).start()
        def send(src,dst,i,t):
            mine=pc.chip==t
            @pl.when(mine)
            def _(): pltpu.make_async_copy(src,dst,self.orr).start()
            @pl.when(jnp.logical_not(mine))
            def _(): rcopy(src,dst,self.os_.at[g,i],self.orr,(t//2,(t%2)*2+pc.c)).start()
        self.targets(g,send)
    def step5(self,g):
        pc=self.pc; G,R=self.of(g)
        self.home(g).wait_recv()
        def whole(b):
            self.out[b,:,pc.cols]=R["fin"][pl.ds(pl.multiple_of(pc.c*24,8),24)]
            self.out[b,:,pc.ocols]=R["hr"][...]
        def slab(j):
            for i in range(3):
                self.out[i,:,pl.ds(pl.multiple_of((pc.c*3+j)*128,128),128)]=R["fin"][pl.ds(pl.multiple_of(pc.c*24,8),24),i*128:(i+1)*128]
                self.out[i,:,pl.ds(pl.multiple_of(((1-pc.c)*3+j)*128,128),128)]=R["hr"][:,i*128:(i+1)*128]
        if isinstance(g,int):
            if g<9: whole(8+g//2-4*(g%2)-9*(g//8))
            else: slab(g-9)
        else:
            @pl.when(g<9)
            def _(): whole(8+g//2-4*(g%2)-9*(g//8))
            @pl.when(g>=9)
            def _(): slab(g-9)
    def done(self,g):
        pc=self.pc
        for d in (self.core,self.xa,self.ya,self.xb,self.home): d(g).wait_send()
        for i in range(2): self.yb(g,i).wait_send()
        for k in (1,2,3): self.zz(g,k).wait_send()
        def wait(src,dst,i,t):
            @pl.when(pc.chip!=t)
            def _(): rcopy(src,dst,self.os_.at[g,i],self.orr,(t//2,(t%2)*2+pc.c)).wait_send()
        self.targets(g,wait)

KB_=512
def prepare_pair(p,v,ctx,do,doa,va):
    cols=pl.ds(pl.multiple_of(p*128,128),128)
    lane=lax.broadcasted_iota(jnp.int32,(256,128),1)
    i=lax.broadcasted_iota(jnp.int32,(128,128),0); j=lax.broadcasted_iota(jnp.int32,(128,128),1)
    cross=jnp.where((i<64)!=(j<64),-1.0,0.0).astype(bf16)
    for t in range(PACK//256):
        rows=pl.ds(t*256,256)
        vp=v[rows,cols].astype(f32)
        dop=do[rows,cols].astype(f32); prod=dop*ctx[rows,cols].astype(f32)
        dd=sum(dot(c.astype(bf16),cross) for c in split3(prod))
        parts=split3(dd)
        for h,lo in enumerate((True,False)):
            keep=(lane<64)==lo
            off=64 if lo else 0
            d1=jnp.where(keep,dop,0.0)
            for n,c in enumerate(parts): d1=jnp.where(lane==off+n,c,d1)
            doa[h,rows,:]=d1.astype(bf16)
            v1=jnp.where(keep,vp,0.0)
            va[h,rows,:]=jnp.where((lane>=off)&(lane<off+3),1.0,v1).astype(bf16)

def back_block(p,b,dk_ref,dv_ref,qa,doa,ka,va,dqa):
    cols=pl.ds(pl.multiple_of(p*128,128),128)
    rows=pl.ds(pl.multiple_of(b*KB_,KB_),KB_)
    low=lax.broadcasted_iota(jnp.int32,(KB_,128),1)<64
    lowq=lax.broadcasted_iota(jnp.int32,(PACK,128),1)<64
    r=[]
    for h in range(2):
        kh=ka[h,rows,:]
        pr=jnp.exp(dot(kh,qa[h],1,1))
        dp=dot(va[h,rows,:],doa[h],1,1)
        ds=(pr*dp).astype(bf16)
        r.append((dot(pr.astype(bf16),doa[h]),dot(ds,qa[h]),dot(ds,kh,0,0)))
    dq=jnp.where(lowq,r[0][2],r[1][2])
    @pl.when(b==0)
    def _(): dqa[...]=dq
    @pl.when(b>0)
    def _(): dqa[...]+=dq
    dv_ref[rows,cols]=jnp.where(low,r[0][0],r[1][0]).astype(bf16)
    dk_ref[rows,cols]=jnp.where(low,r[0][1],r[1][1]).astype(bf16)

def back_body(x_ref,qa_i,ka_i,v_i,ctx_i,do_i,act_i,din_i,dffn_i,hlow_i,dz1_i,wq_i,vec_ref,
              ig_o,out_ref,vout_ref,gown_ref,*rest):
    R=dict(zip(SKEYS,rest[:len(SKEYS)]))
    (g_ref,ctx,w_last,act,din,dffn,hlow,acc,qa,doa,ka,va,dqa,vcur,vbuf,
     ss,rs,os_,orr,vs,vr,lsem,asem)=rest[len(SKEYS):]
    pc=Place()
    loads={}
    def load(name,src,dst):
        c=pltpu.make_async_copy(src,dst,lsem.at[len(loads)]); c.start(); loads[name]=c
    half=lambda ref,c: ref.at[:,pl.ds(c*D,D)]
    load("act0",half(act_i,0),act.at[0]); load("dffn",dffn_i,dffn)
    load("hlow",hlow_i,hlow); load("din0",half(din_i,0),din.at[0])
    load("act1",half(act_i,1),act.at[1]); load("din1",half(din_i,1),din.at[1])
    for n,s,d in (("acc",dz1_i,acc),("ctx",ctx_i,ctx)): load(n,s,d)
    q,v,do,k=act.at[0],din.at[0],dffn,act.at[1]
    late={5:("v",v_i,v),7:("do",do_i,do)}
    def pair_loads(pi):
        p=3*(pi%2)+pi//2
        return [pltpu.make_async_copy(s.at[p],d.at[pi%2],asem.at[i,pi%2]) for i,(s,d) in enumerate(((qa_i,qa),(ka_i,ka)))]
    for c in pair_loads(0): c.start()
    greet_all(pc)
    gs=GroupSum(pc,g_ref,R,out_ref,gown_ref,ss,rs,os_,orr)
    vsum=VecSum(pc,vcur,vbuf,vs,vr)
    def product(g,a,b):
        for r in range(4):
            g_ref[g,r]=dot(a[:,r*192:(r+1)*192],b,0,0).astype(bf16).reshape(4,MR,D)
    loads["dffn"].wait()
    for i in range(9):
        c=i//2
        if i==8:
            loads["ctx"].wait(); loads["acc"].wait()
            product(i,ctx,acc[...].astype(bf16))
        elif i%2==0:
            loads[f"act{c}"].wait()
            product(i,act.at[c%2],dffn[...])
            if c<2: load(f"act{c+2}",half(act_i,c+2),act.at[c%2])
        else:
            if c==0: loads["hlow"].wait()
            loads[f"din{c}"].wait()
            product(i,hlow,din[c%2])
            if c<2: load(f"din{c+2}",half(din_i,c+2),din.at[c%2])
        if i in late: load(*late[i])
        gs.step0(i)
        if i>=1: gs.step1(i-1)
    gs.step2(0)
    wrow=pl.ds(0,D)
    wdst=[din.at[1,wrow],hlow.at[wrow],w_last]
    for i in range(3): load(f"w{i}",wq_i.at[i],wdst[i])
    for n in ("v","do"): loads[n].wait()
    def slot(n,carry):
        pi=n//2; b=n%2; j=pi//2; cc=pi%2; p=3*cc+j; side=pi%2
        cols=pl.ds(pl.multiple_of(p*128,128),128)
        @pl.when(b==0)
        def _():
            for c in pair_loads(pi): c.wait()
            @pl.when(pi<5)
            def _():
                for c in pair_loads(pi+1): c.start()
            prepare_pair(p,v,ctx,do,doa,va)
        back_block(p,b,k,v,qa.at[side],doa,ka.at[side],va,dqa)
        @pl.when(b==1)
        def _():
            q[:,cols]=(dqa[...]*0.125).astype(bf16)
            al=jnp.concatenate([q[:,cols],k[:,cols],v[:,cols]],axis=1)
            lane=pl.ds(pl.multiple_of(cc*HC,128),HC)
            for r in range(4):
                g_ref[9+j,r,:,:,lane]=dot(x_ref[:,r*192:(r+1)*192],al,0,0).astype(bf16).reshape(4,MR,HC)
            vcur[0,0:1,cols]=jnp.sum(q[:,cols].astype(f32),axis=0,keepdims=True)
            vcur[0,1:2,cols]=jnp.sum(v[:,cols].astype(f32),axis=0,keepdims=True)
        @pl.when(n==0)
        def _(): gs.step1(8)
        @pl.when(n<=9)
        def _(): gs.step2(1+n)
        @pl.when(n<=10)
        def _(): gs.step3(n)
        @pl.when(n>=1)
        def _(): gs.step4(n-1)
        @pl.when(n>=2)
        def _(): gs.step5(n-2)
        @pl.when((n==4)|(n==8))
        def _(): gs.step1(8+n//4)
        @pl.when((n==3)|(n==7))
        def _(): gs.step0(9+n//7)
        return carry
    vcur[0]=vec_ref[...]
    lax.fori_loop(0,12,slot,0)
    gs.step0(11)
    vsum.step(0)
    for i in range(3): loads[f"w{i}"].wait()
    def grad_tile(t):
        rows=pl.ds(t*256,256)
        a=acc[rows,:]
        for d,w in zip((q,k,v),wdst): a=a+dot(d[rows,:],w[...],1,1)
        acc[rows,:]=a
    grad_tile(0);
    gs.step5(10); gs.step1(11); vsum.step(1)
    grad_tile(1); grad_tile(2); vsum.step(2)
    gs.step2(11); grad_tile(3); vsum.step(3)
    away=pltpu.make_async_copy(acc,ig_o,lsem.at[31]); away.start()
    gs.step3(11); vsum.step(4)
    gs.step4(11); vsum.step(5)
    gs.step5(11)
    vout_ref[...]=vcur[5]
    vsum.done()
    lax.fori_loop(0,NGR,lambda g,c: (gs.done(g),c)[1],0)
    away.wait()
    @pl.when(pc.xy<3)
    def _(): pltpu.make_async_copy(gown_ref,gown_ref,orr).wait()

def call_back(x,qa,ka,v,ctx,dctx,act,din,dffn,hlow,dz1,wq,vec):
    V=pltpu.VMEM; S=jax.ShapeDtypeStruct; A=pl.ANY
    B=lambda m: pl.BlockSpec(memory_space=m)
    sem=pltpu.SemaphoreType.DMA
    T=V((PACK,D),bf16); H=V((2,PACK,128),bf16)
    return pl.pallas_call(back_body,
        in_specs=[B(V)]+[B(A)]*11+[B(V)],
        out_specs=[B(A),B(V),B(V),B(A)],
        out_shape=[S((PACK,D),f32),S((NB,24,D),f32),S((16,D),f32),S((16,MR,HC),bf16)],
        scratch_shapes=list(sum_scratch().values())+[V((NGR,4,4,MR,D),bf16),T,V((D,D),bf16)]+[V((2,PACK,D),bf16),V((2,PACK,D),bf16),T,T,V((PACK,D),f32)]+[V((2,2,PACK,128),bf16),H,V((2,2,PACK,128),bf16),H]+
            [V((PACK,128),f32),V((6,16,D),f32),V((5,16,D),f32),sem((NGR,10)),sem((NGR,10)),sem((NGR,3)),sem,sem((5,)),sem((5,)),sem((32,)),sem((2,2))],
        compiler_params=pltpu.CompilerParams(vmem_limit_bytes=63<<20,collective_id=1,has_side_effects=True))(x,qa,ka,v,ctx,dctx,act,din,dffn,hlow,dz1,wq,vec)


def gather_rows(a):
    return lax.all_gather(a,("dp","head"),axis=1,tiled=True)

def doc_lengths(lengths):
    return lax.dynamic_slice_in_dim(lengths,lax.axis_index("head"),1,axis=0)

def layer(tokens,cotangent,lengths,w,params):
    q,k,v,ctx,lse,n1,r1=call_a(lengths,tokens,w,params)
    out,dz1,dctx,dwo,dw1,dw2,vec=call_b(cotangent,n1,r1,ctx,w,params)
    ig,dwqkv,vq=call_c(lengths,tokens,q,k,v,ctx,dctx,lse,dz1,w)
    terms=jnp.concatenate([dwqkv,dwo[None],dw1,dw2],axis=0)
    vec=jnp.concatenate([vq[0:1],vq[2:3],vec[2:]],axis=0)
    return out,ig,terms,vec

def on_slice(tokens,cotangent,lengths,masters,vectors,left,right,second):
    pv=jnp.pad(vectors,((0,4),(0,HC-24))).astype(bf16)
    lens=doc_lengths(lengths)
    out,qa,ka,v,ctx,act,din,dffn,hlow,dz1,dctx,wq,vec,stat=call_front(lens,tokens,cotangent,masters,pv,left,right)
    ig,grads,vec_all,gown=call_back(tokens,qa,ka,v,ctx,dctx,act,din,dffn,hlow,dz1,wq.reshape(3,D,D),vec)
    ln,rn,mn,vg,sn,vn=call_newton_step(gown.reshape(D,HC),stat.reshape(D,D),left,right,masters,vec_all,vectors,second)
    return out,ig,grads,ln,rn,mn,vg,sn,vn

def on_any(tokens,cotangent,lengths,masters,vectors,left,right,second):
    axes=("dp","head")
    me=lax.axis_index("dp")*lax.axis_size("head")+lax.axis_index("head")
    share=masters.shape[1]
    w=gather_rows(masters.astype(bf16))
    params=gather_rows(vectors.astype(bf16)).astype(f32)
    out,ig,terms,vec=layer(tokens,cotangent,doc_lengths(lengths),w,params)
    grads=lax.psum_scatter(terms.astype(f32),axes,scatter_dimension=1,tiled=True)
    vg=lax.psum_scatter(vec[:12],axes,scatter_dimension=1,tiled=True)
    low=grads.astype(bf16)
    g=gather_rows(low)
    ein=partial(jnp.einsum,preferred_element_type=f32)
    cols=lax.dynamic_slice_in_dim(g,me*share,share,axis=2)
    ln=BETA*left+(1-BETA)*ein("kid,kjd->kij",low,g)
    rn=BETA*right+(1-BETA)*ein("kdi,kdj->kij",cols,g)
    item=jnp.minimum(me,2*NB-1)
    own=lax.dynamic_index_in_dim(jnp.concatenate([gather_rows(ln),gather_rows(rn)],axis=0),item,0,keepdims=False)
    root=call_newton(own)
    place=jnp.where((jnp.arange(2*NB)==me)[:,None,None],root[None],0.0)
    rows=lax.psum_scatter(place,axes,scatter_dimension=1,tiled=True)
    rr=gather_rows(rows[NB:])
    hi=partial(jnp.einsum,"kij,kjl->kil",precision=lax.Precision.HIGHEST)
    mn=masters-RATE*hi(hi(rows[:NB],g.astype(f32)),rr)
    sn=BETA_TWO*second+(1-BETA_TWO)*vg*vg
    vn=vectors-RATE_VEC*vg/(jnp.sqrt(sn)+1e-8)
    return out,ig,grads,ln,rn,mn,vg,sn,vn

def solution(mesh):
    rows=P(("dp","head"),None); blocks=P(None,("dp","head"),None); vecs=P(None,("dp","head"))
    on_device=on_slice if dict(mesh.shape)=={"dp":8,"head":4} else on_any
    return jax.shard_map(on_device,mesh=mesh,
        in_specs=(rows,rows,P("dp",None),blocks,vecs,blocks,blocks,vecs),
        out_specs=(rows,rows,blocks,blocks,blocks,blocks,vecs,vecs,vecs),check_vma=False)
```

```python
import jax, jax.numpy as jnp, numpy as np
from functools import partial
from jax import lax
from jax.experimental import pallas as pl
from jax.experimental.pallas import tpu as pltpu
from jax.sharding import PartitionSpec as P

D=768; HEADS=12; HD=64; FF=3072; PACK=1024; NEWTON=8; NB=12
NORM_EPS=1e-6
f32=jnp.float32; bf16=jnp.bfloat16
BIG=1e30
QB=256
def dot(a,b,ca=1,cb=0):
    return lax.dot_general(a,b,(((ca,),(cb,)),((),())),preferred_element_type=f32)

def doc_column(len_ref, shape, dim):
    t=lax.broadcasted_iota(jnp.int32,shape,dim)
    end=jnp.int32(0); doc=jnp.zeros(shape,jnp.int32)
    for j in range(8):
        end=end+len_ref[0,j]
        doc=doc+(t>=end).astype(jnp.int32)
    return doc

def split3(v):
    a=v.astype(bf16).astype(f32); r=v-a
    b=r.astype(bf16).astype(f32); c=r-b
    return a,b,c

def augment(base, lane, head_lo, cols):
    keep=(lane<64) if head_lo else (lane>=64)
    off=64 if head_lo else 0
    out=jnp.where(keep, base, 0.0)
    for i,c in enumerate(cols):
        out=jnp.where(lane==off+i, c, out)
    return out.astype(bf16)

def onehot_part(base, lane, head_lo, doc, minus, scale):
    keep=(lane<64) if head_lo else (lane>=64)
    off=64 if head_lo else 0
    l=lane-off
    oh=jnp.where((l>=0)&(l<8), (jnp.where(l==doc,1.0,0.0)-minus)*scale, 0.0)
    return jnp.where(keep, base, oh)

def attn_fwd_pair(p, q_ref,k_ref,v_ref, ctx_ref, lse_ref, doc):
    cols=pl.ds(pl.multiple_of(p*128,128),128)
    lane=lax.broadcasted_iota(jnp.int32,(PACK,128),1)
    kp=k_ref[:,cols].astype(f32)
    vp=v_ref[:,cols]
    kk=[onehot_part(kp,lane,lo,doc,1.0,1.0).astype(bf16) for lo in (True,False)]
    laneb=lax.broadcasted_iota(jnp.int32,(QB,128),1)
    for b in range(PACK//QB):
        rows=pl.ds(b*QB,QB)
        qp=q_ref[rows,cols].astype(f32)*0.125
        docb=doc[b*QB:(b+1)*QB]
        outs=[]
        lse_old=lse_ref[rows,:]
        for h,lo in enumerate((True,False)):
            qa=onehot_part(qp,laneb,lo,docb,0.0,BIG).astype(bf16)
            s=dot(qa,kk[h],1,1)
            m=jnp.max(s,axis=1,keepdims=True)
            e=jnp.exp(s-m)
            l=jnp.sum(e,axis=1,keepdims=True)
            o=dot(e.astype(bf16),vp)
            outs.append(o/l)
            lse_old=jnp.where(laneb==2*p+h, m+jnp.log(l), lse_old)
        lse_ref[rows,:]=lse_old
        ctx_ref[rows,cols]=jnp.where(laneb<64,outs[0],outs[1]).astype(bf16)

def layer_norm(z):
    mu=jnp.mean(z,axis=-1,keepdims=True)
    c=z-mu
    r=lax.rsqrt(jnp.mean(c*c,axis=-1,keepdims=True)+NORM_EPS)
    return c*r, r

def ka_body(len_ref,x_ref,wa_ref,p_ref,q_ref,k_ref,v_ref,ctx_ref,lse_ref,hid_ref,r1_ref,w_ref):
    pltpu.sync_copy(wa_ref.at[pl.ds(0,4)],w_ref)
    doc=doc_column(len_ref,(PACK,1),0)
    for i,(o,b) in enumerate(((q_ref,0),(k_ref,None),(v_ref,1))):
        for t in range(4):
            rows=pl.ds(t*256,256)
            y=dot(x_ref[rows,:],w_ref[i])
            if b is not None: y=y+p_ref[b:b+1,:]
            o[rows,:]=y.astype(bf16)
    def body(p,c):
        attn_fwd_pair(p,q_ref,k_ref,v_ref,ctx_ref,lse_ref,doc)
        return c
    lax.fori_loop(0,6,body,0)
    for t in range(4):
        rows=pl.ds(t*256,256)
        z=x_ref[rows,:].astype(f32)+(dot(ctx_ref[rows,:],w_ref[3])+p_ref[2:3,:])
        n,r=layer_norm(z)
        hid_ref[rows,:]=n
        r1_ref[rows,:]=jnp.broadcast_to(r,(256,128))

def call_a(lengths,x,w,params):
    V=pltpu.VMEM
    return pl.pallas_call(ka_body,
        in_specs=[pl.BlockSpec(memory_space=pltpu.SMEM),pl.BlockSpec(memory_space=V),pl.BlockSpec(memory_space=pl.ANY),pl.BlockSpec(memory_space=V)],
        out_specs=[pl.BlockSpec(memory_space=V)]*7,
        out_shape=[jax.ShapeDtypeStruct((PACK,D),bf16)]*4+[jax.ShapeDtypeStruct((PACK,128),f32),jax.ShapeDtypeStruct((PACK,D),f32),jax.ShapeDtypeStruct((PACK,128),f32)],
        scratch_shapes=[V((4,D,D),bf16)],
        compiler_params=pltpu.CompilerParams(vmem_limit_bytes=60<<20))(lengths,x,w,params)

def gelu_both(x):
    z=jnp.abs(x)*0.7071067811865476
    t=1.0/(1.0+0.3275911*z)
    e=jnp.exp(-0.5*x*x)
    poly=t*(0.254829592+t*(-0.284496736+t*(1.421413741+t*(-1.453152027+t*1.061405429))))
    half=0.5*poly*e
    phi_c=jnp.where(x>=0,1.0-half,half)
    return x*phi_c, phi_c+x*(e*0.3989422804014327)

def kb_body(cot_ref,n1_ref,r1_ref,ctx_ref,w_ref,p_ref, out_ref,dz1_ref,dctx_ref,dwo_ref,dw1_ref,dw2_ref,vec_ref, act_ref,gp_ref,dffn_ref,hlow_ref):
    TT=256
    g1,s1,g2,s2=(p_ref[i:i+1,:] for i in (8,9,10,11))
    b2=p_ref[7:8,:]
    vec_ref[...]=jnp.zeros_like(vec_ref)
    def tile(t,carry):
        rows=pl.ds(pl.multiple_of(t*TT,TT),TT)
        n1=n1_ref[rows,:]
        hid=n1*g1+s1
        hl=hid.astype(bf16)
        hlow_ref[rows,:]=hl
        ffn=None
        for c in range(4):
            inner=dot(hl,w_ref[4+c])+p_ref[3+c:4+c,:]
            a,gp=gelu_both(inner)
            al=a.astype(bf16)
            act_ref[rows,pl.ds(c*D,D)]=al
            gp_ref[rows,pl.ds(c*D,D)]=gp.astype(gp_ref.dtype)
            y=dot(al,w_ref[8+c])
            ffn=y if ffn is None else ffn+y
        z=hid+(ffn+b2)
        n2,r2=layer_norm(z)
        out_ref[rows,:]=(n2*g2+s2).astype(bf16)
        e=cot_ref[rows,:].astype(f32)
        c2=e*g2
        dz2=r2*(c2-jnp.mean(c2,axis=-1,keepdims=True)-n2*jnp.mean(c2*n2,axis=-1,keepdims=True))
        dffn=dz2.astype(bf16)
        dffn_ref[rows,:]=dffn
        vec_ref[10:11,:]+=jnp.sum(e*n2,axis=0,keepdims=True)
        vec_ref[11:12,:]+=jnp.sum(e,axis=0,keepdims=True)
        vec_ref[7:8,:]+=jnp.sum(dffn.astype(f32),axis=0,keepdims=True)
        dh=dz2
        for c in range(4):
            dact=dot(dffn,w_ref[8+c],1,1)
            din=(dact*gp_ref[rows,pl.ds(c*D,D)].astype(f32)).astype(bf16)
            gp_ref[rows,pl.ds(c*D,D)]=din.astype(gp_ref.dtype)
            vec_ref[3+c:4+c,:]+=jnp.sum(din.astype(f32),axis=0,keepdims=True)
            dh=dh+dot(din,w_ref[4+c],1,1)
        vec_ref[8:9,:]+=jnp.sum(dh*n1,axis=0,keepdims=True)
        vec_ref[9:10,:]+=jnp.sum(dh,axis=0,keepdims=True)
        c1=dh*g1
        dz1=r1_ref[rows,0:1]*(c1-jnp.mean(c1,axis=-1,keepdims=True)-n1*jnp.mean(c1*n1,axis=-1,keepdims=True))
        dz1_ref[rows,:]=dz1
        dat=dz1.astype(bf16)
        vec_ref[2:3,:]+=jnp.sum(dat.astype(f32),axis=0,keepdims=True)
        dctx_ref[rows,:]=dot(dat,w_ref[3],1,1).astype(bf16)
        return carry
    lax.fori_loop(0,PACK//TT,tile,0)
    for c in range(4):
        dw2_ref[c]=dot(act_ref[:,c*D:(c+1)*D],dffn_ref[...],0,0).astype(bf16)
        dw1_ref[c]=dot(hlow_ref[...],gp_ref[:,c*D:(c+1)*D].astype(bf16),0,0).astype(bf16)
    dwo_ref[...]=dot(ctx_ref[...],dz1_ref[...].astype(bf16),0,0).astype(bf16)

def call_b(cot,n1,r1,ctx,w,params):
    V=pltpu.VMEM
    S=jax.ShapeDtypeStruct
    return pl.pallas_call(kb_body,
        in_specs=[pl.BlockSpec(memory_space=V)]*6,
        out_specs=[pl.BlockSpec(memory_space=V)]*7,
        out_shape=[S((PACK,D),bf16),S((PACK,D),f32),S((PACK,D),bf16),S((D,D),bf16),S((4,D,D),bf16),S((4,D,D),bf16),S((16,D),f32)],
        scratch_shapes=[V((PACK,FF),bf16),V((PACK,FF),bf16),V((PACK,D),bf16),V((PACK,D),bf16)],
        compiler_params=pltpu.CompilerParams(vmem_limit_bytes=62<<20))(cot,n1,r1,ctx,w,params)

def kc_body(len_ref,x_ref,q_ref,k_ref,v_ref,ctx_ref,do_ref,lse_ref,dz1_ref,wa_ref, ig_ref,dw_ref,vec_ref, dqkv_ref, dqa_ref,w_ref):
    pltpu.sync_copy(wa_ref.at[pl.ds(0,3)],w_ref)
    doc=doc_column(len_ref,(PACK,1),0)
    lane=lax.broadcasted_iota(jnp.int32,(PACK,128),1)
    KB_=256
    def pair(p,carry):
        cols=pl.ds(pl.multiple_of(p*128,128),128)
        qp=q_ref[:,cols].astype(f32); kp=k_ref[:,cols].astype(f32); vp=v_ref[:,cols].astype(f32)
        dop=do_ref[:,cols].astype(f32); cp=ctx_ref[:,cols].astype(f32)
        prod=dop*cp
        qa=[];qm=[];doa=[];dom=[];ka=[];km=[];va=[]
        for h,lo in enumerate((True,False)):
            keep=(lane<64) if lo else (lane>=64)
            off=64 if lo else 0
            lse=jnp.sum(jnp.where(lane==2*p+h,lse_ref[...],0.0),axis=1,keepdims=True)
            dd=jnp.sum(jnp.where(keep,prod,0.0),axis=1,keepdims=True)
            q1=onehot_part(qp*0.125,lane,lo,doc,0.0,BIG)
            for i,c in enumerate(split3(-lse)): q1=jnp.where(lane==off+8+i,c,q1)
            qa.append(q1.astype(bf16)); qm.append(jnp.where(keep,qp*0.125,0.0).astype(bf16))
            k1=onehot_part(kp,lane,lo,doc,1.0,1.0)
            k1=jnp.where((lane>=off+8)&(lane<off+11),1.0,k1)
            ka.append(k1.astype(bf16)); km.append(jnp.where(keep,kp*0.125,0.0).astype(bf16))
            d1=jnp.where(keep,dop,0.0)
            dom.append(d1.astype(bf16))
            for i,c in enumerate(split3(-dd)): d1=jnp.where(lane==off+i,c,d1)
            doa.append(d1.astype(bf16))
            v1=jnp.where(keep,vp,0.0); v1=jnp.where((lane>=off)&(lane<off+3),1.0,v1)
            va.append(v1.astype(bf16))
        for b in range(PACK//KB_):
            rows=slice(b*KB_,(b+1)*KB_)
            dv=None;dk=None;dq=None
            for h in range(2):
                s=dot(ka[h][rows],qa[h],1,1)
                pr=jnp.exp(s)
                dp=dot(va[h][rows],doa[h],1,1)
                ds=(pr*dp).astype(bf16)
                a=dot(pr.astype(bf16),dom[h]); dv=a if dv is None else dv+a
                a=dot(ds,qm[h]); dk=a if dk is None else dk+a
                a=dot(ds,km[h][rows],0,0); dq=a if dq is None else dq+a
            if b==0: dqa_ref[...]=dq
            else: dqa_ref[...]+=dq
            dqkv_ref[1,rows,cols]=dk.astype(bf16)
            dqkv_ref[2,rows,cols]=dv.astype(bf16)
        dqkv_ref[0,:,cols]=dqa_ref[...].astype(bf16)
        for i in range(3):
            d=dqkv_ref[i,:,cols]
            dw_ref[i,:,cols]=dot(x_ref[...],d,0,0).astype(bf16)
            vec_ref[i:i+1,cols]=jnp.sum(d.astype(f32),axis=0,keepdims=True)
        return carry
    lax.fori_loop(0,6,pair,0)
    for t in range(4):
        rows=pl.ds(t*256,256)
        acc=dz1_ref[rows,:]
        for i in range(3):
            acc=acc+dot(dqkv_ref[i,rows,:],w_ref[i],1,1)
        ig_ref[rows,:]=acc

def call_c(lengths,x,q,k,v,ctx,do,lse,dz1,w):
    V=pltpu.VMEM; S=jax.ShapeDtypeStruct
    return pl.pallas_call(kc_body,
        in_specs=[pl.BlockSpec(memory_space=pltpu.SMEM)]+[pl.BlockSpec(memory_space=V)]*8+[pl.BlockSpec(memory_space=pl.ANY)],
        out_specs=[pl.BlockSpec(memory_space=V)]*3,
        out_shape=[S((PACK,D),f32),S((3,D,D),bf16),S((8,D),f32)],
        scratch_shapes=[V((3,PACK,D),bf16),V((PACK,128),f32),V((3,D,D),bf16)],
        compiler_params=pltpu.CompilerParams(vmem_limit_bytes=62<<20))(lengths,x,q,k,v,ctx,do,lse,dz1,w)

RB=256
def diag_sum(blk):
    i=lax.broadcasted_iota(jnp.int32,blk.shape,0); j=lax.broadcasted_iota(jnp.int32,blk.shape,1)
    return jnp.sum(jnp.where(i==j,blk,0.0),keepdims=True)
def eye_rows(rb):
    i=lax.broadcasted_iota(jnp.int32,(RB,D),0)+rb*RB; j=lax.broadcasted_iota(jnp.int32,(RB,D),1)
    return i==j
def newton(m_ref,x_ref,nb_ref,pb_ref,sb_ref,xb_ref,between=lambda k: None):
    nblk=D//RB
    R=[slice(i*RB,(i+1)*RB) for i in range(nblk)]
    tot=jnp.zeros((1,1),f32); tr=jnp.zeros((1,1),f32)
    for i in range(nblk):
        blk=m_ref[R[i],:]
        tot=tot+jnp.sum(blk*blk,keepdims=True)
        tr=tr+diag_sum(blk[:,R[i]])
    c=jnp.sqrt(tot+1e-6)
    inv=1.0/c
    al=tr*inv/D
    s=lax.rsqrt(jnp.sqrt(c))
    for i in range(nblk):
        m_ref[R[i],:]=m_ref[R[i],:]*inv
    def iteration(k,al,be,first=False,last=False):
        u=5-al
        u2=u*u;u3=u2*u;u4=u2*u2
        c0=al*u4*(1/256); c1=(u4-4*al*u3)*(1/256); c2=(12*al*u2-8*u3)*(1/512)
        c3=(36*u2-24*al*u)*(1/1536); c4=(24*al-96*u)*(1/6144); c5=1/256
        for i in range(nblk):
            nb_ref[R[i],:]=jnp.where(eye_rows(i),m_ref[R[i],:]-al,m_ref[R[i],:]).astype(bf16)
            if not first: xb_ref[R[i],:]=jnp.where(eye_rows(i),x_ref[R[i],:]-be,x_ref[R[i],:]).astype(bf16)
        be2=jnp.zeros((1,1),f32); al2=jnp.zeros((1,1),f32)
        for i in range(nblk):
            n=jnp.where(eye_rows(i),m_ref[R[i],:]-al,m_ref[R[i],:])
            if not last:
                p=dot(nb_ref[R[i],:],nb_ref[...])
                pb_ref[R[i],:]=p.astype(bf16)
                m=c1*n+c2*p
                m_ref[R[i],:]=jnp.where(eye_rows(i),m+c0,m)
            if first:
                x=jnp.where(eye_rows(i),1.25-al*0.25,0.0)-0.25*n
            else:
                x=(1.25-al*0.25)*x_ref[R[i],:]-0.25*(be*n+dot(xb_ref[R[i],:],nb_ref[...]))
            x_ref[R[i],:]=x
            be2=be2+diag_sum(x[:,R[i]])
        if not last:
            for i in range(nblk):
                q=dot(nb_ref[R[i],:],pb_ref[...])
                sb_ref[R[i],:]=(c3*nb_ref[R[i],:].astype(f32)+c4*pb_ref[R[i],:].astype(f32)+c5*q).astype(bf16)
            for i in range(nblk):
                m=m_ref[R[i],:]+dot(pb_ref[R[i],:],sb_ref[...])
                m_ref[R[i],:]=m
                al2=al2+diag_sum(m[:,R[i]])
        return al2*(1/D),be2*(1/D)
    al,be=iteration(0,al,None,first=True)
    def step(k,ab):
        ab=iteration(k,*ab)
        between(k)
        return ab
    al,be=lax.fori_loop(1,7,step,(al,be))
    iteration(7,al,be,last=True)
    for i in range(nblk):
        x_ref[R[i],:]=x_ref[R[i],:]*s
def body(a_ref,x_ref,m_ref,nb,pb,sb,xb):
    m_ref[...]=a_ref[...]
    newton(m_ref,x_ref,nb,pb,sb,xb)
def call_newton(a):
    V=pltpu.VMEM
    return pl.pallas_call(body,in_specs=[pl.BlockSpec(memory_space=V)],out_specs=pl.BlockSpec(memory_space=V),
      out_shape=jax.ShapeDtypeStruct((D,D),f32),scratch_shapes=[V((D,D),f32)]+[V((D,D),bf16)]*4,
      compiler_params=pltpu.CompilerParams(vmem_limit_bytes=60<<20))(a)

NZ=4; MR=48; HC=384
MESH=pl.DeviceIdType.MESH
def rcopy(src,dst,ss,rs,dev):
    return pltpu.make_async_remote_copy(src_ref=src,dst_ref=dst,send_sem=ss,recv_sem=rs,device_id=dev,device_id_type=MESH)

class Place:
    def __init__(self):
        self.dp=lax.axis_index("dp"); self.head=lax.axis_index("head")
        self.z=self.dp//2; self.x=self.dp%2; self.y=self.head//2; self.c=self.head%2
        self.xy=self.x*2+self.y
        self.chip=self.z*4+self.xy
        self.me=self.dp*4+self.head
        self.xn=((self.dp//2)*2+(1-self.x), self.head)
        self.yn=(self.dp,(1-self.y)*2+self.c)
        self.sib=(self.dp,self.y*2+(1-self.c))
        self.cols=pl.ds(pl.multiple_of(self.c*HC,128),HC)
        self.ocols=pl.ds(pl.multiple_of((1-self.c)*HC,128),HC)
    def zpeer(self,k):
        return (((self.z+k)%NZ)*2+self.x,self.head)
    def zfrom(self,k):
        return (self.z+NZ-k)%NZ
    def neighbours(self):
        return [self.zpeer(1),self.zpeer(2),self.zpeer(3),self.xn,self.yn,self.sib]

def greet(devs):
    bar=pltpu.get_barrier_semaphore()
    for d in devs:
        pl.semaphore_signal(bar,inc=1,device_id=d,device_id_type=MESH)
    pl.semaphore_wait(bar,len(devs))

def greet_all(pc):
    bar=pltpu.get_barrier_semaphore()
    def sig(k,carry):
        t=(pc.me+k)%32
        pl.semaphore_signal(bar,inc=1,device_id=(t//4,t%4),device_id_type=MESH)
        return carry
    lax.fori_loop(1,32,sig,0)
    pl.semaphore_wait(bar,31)

class Gather:
    def __init__(self,pc,buf,ss,rs):
        self.pc,self.buf,self.ss,self.rs=pc,buf,ss,rs
    def region(self,z,xy,mine=True):
        pc=self.pc
        return self.buf.at[z,xy,:,pc.cols if mine else pc.ocols]
    def copies(self):
        pc=self.pc; al=pl.ds(0,4); lo=pl.ds(0,2); hi=pl.ds(2,2)
        xo=(1-pc.x)*2+pc.y; yo=pc.x*2+(1-pc.y); dg=(1-pc.x)*2+(1-pc.y)
        R=self.region
        def mk(i,src,dst,dev):
            return rcopy(src,dst,self.ss.at[i],self.rs.at[i],dev)
        send={}
        for k in (1,2,3): send[k-1]=(R(pc.z,pc.xy),pc.zpeer(k))
        send[3]=(R(al,pc.xy),pc.xn); send[4]=(R(al,pc.xy),pc.yn)
        send[5]=(R(hi,yo),pc.xn); send[6]=(R(lo,xo),pc.yn)
        send[7]=(R(al,pc.xy),pc.sib); send[8]=(R(al,xo),pc.sib); send[9]=(R(al,yo),pc.sib); send[10]=(R(al,dg),pc.sib)
        recv={}
        for k in (1,2,3): recv[k-1]=R(pc.zfrom(k),pc.xy)
        recv[3]=R(al,xo); recv[4]=R(al,yo); recv[5]=R(hi,dg); recv[6]=R(lo,dg)
        recv[7]=R(al,pc.xy,False); recv[8]=R(al,xo,False); recv[9]=R(al,yo,False); recv[10]=R(al,dg,False)
        self.send=[partial(mk,i,send[i][0],send[i][0],send[i][1]) for i in range(11)]
        self.recv=[partial(mk,i,recv[i],recv[i],pc.sib) for i in range(11)]
        return self
    def step0(self):
        for i in (0,1,2): self.send[i]().start()
    def step1(self):
        for i in (0,1,2): self.recv[i]().wait_recv()
        for i in (3,4,7): self.send[i]().start()
    def step2(self):
        self.recv[3]().wait_recv()
        for i in (6,8): self.send[i]().start()
        self.recv[4]().wait_recv()
        for i in (5,9): self.send[i]().start()
    def step3(self):
        for i in (5,6): self.recv[i]().wait_recv()
        self.send[10]().start()
    def step4(self):
        for i in (7,8,9,10): self.recv[i]().wait_recv()
    def done(self):
        for i in range(11): self.send[i]().wait_send()
    def step(self,i):
        (self.step0,self.step1,self.step2,self.step3,self.step4)[i]()

ORDER=(0,1,2,3,4,8,5,9,6,10,7,11)
def ag_body(mas_ref,pv_ref,left_ref,right_ref, w_ref,pg_ref,st_ref, sibm,ss,rs,cs,cr,ts,tr,lsem):
    pc=Place()
    greet_all(pc)
    half=rcopy(mas_ref.at[:,:,pc.ocols],sibm,cs,cr,pc.sib)
    half.start()
    def stat(b,act):
        t=(b%4)*4+b//4
        for side,ref in enumerate((left_ref,right_ref)):
            dev=((t//2),(t%2)*2+side)
            idx=b*2+side
            mine=(pc.chip==t)&(pc.c==side)
            act(idx,ref.at[b],dev,mine)
    half.wait_recv()
    lo=pl.ds(0,24); hi=pl.ds(24,24)
    for b in ORDER:
        own=mas_ref[b,:,pc.cols]; oth=sibm[b]
        first=jnp.where(pc.c==0,own,oth); second=jnp.where(pc.c==0,oth,own)
        w_ref[b,pc.z,pc.xy,:,pc.cols]=jnp.concatenate([first,second],axis=0).astype(bf16)
    pg_ref[pc.z,pc.xy,:,pc.cols]=pv_ref[...]
    half.wait_send()
    gs=[Gather(pc,pg_ref,ss.at[12],rs.at[12]).copies()]+[Gather(pc,w_ref.at[b],ss.at[b],rs.at[b]).copies() for b in ORDER]
    for t in range(len(gs)+4):
        for s in range(5):
            if 0<=t-s<len(gs): gs[t-s].step(s)
    def start(b,carry):
        def act(idx,src,dev,mine):
            @pl.when(mine)
            def _(): pltpu.make_async_copy(src,st_ref.at[pc.me],tr).start()
            @pl.when(jnp.logical_not(mine))
            def _(): rcopy(src,st_ref.at[pc.me],ts.at[idx],tr,dev).start()
        stat(b,act)
        return carry
    lax.fori_loop(0,NB,start,0)
    for g in gs: g.done()
    def fin(b,carry):
        def act(idx,src,dev,mine):
            @pl.when(jnp.logical_not(mine))
            def _(): rcopy(src,st_ref.at[pc.me],ts.at[idx],tr,dev).wait_send()
        stat(b,act)
        return carry
    lax.fori_loop(0,NB,fin,0)
    @pl.when(pc.xy<3)
    def _(): pltpu.make_async_copy(st_ref,st_ref,tr).wait()

def call_ag(masters,pv,left,right):
    V=pltpu.VMEM; S=jax.ShapeDtypeStruct; A=pl.ANY
    B=lambda m: pl.BlockSpec(memory_space=m)
    sem=pltpu.SemaphoreType.DMA
    return pl.pallas_call(ag_body,in_specs=[B(V),B(V),B(A),B(A)],out_specs=[B(V),B(V),B(A)],
        out_shape=[S((NB,4,4,MR,D),bf16),S((4,4,16,D),bf16),S((32,24,D),f32)],
        scratch_shapes=[V((NB,24,HC),f32),sem((13,11)),sem((13,11)),sem,sem,sem((24,)),sem,sem],
        compiler_params=pltpu.CompilerParams(vmem_limit_bytes=60<<20,collective_id=0,has_side_effects=True))(masters,pv,left,right)

def params_of(pg):
    t=pg.reshape(16,16,2,HC)[:,:12,:,:24]
    return jnp.transpose(t,(1,0,2,3)).reshape(12,D).astype(f32)


class Scatter:
    def __init__(self,pc,b,g_ref,R,out_ref,gown_ref,ss,rs,os_,orr):
        self.pc,self.b,self.g=pc,b,g_ref.at[b]
        self.out,self.gown=out_ref,gown_ref
        self.os_,self.orr=os_,orr
        self.R={k:v.at[b] for k,v in R.items()}
        R=self.R
        s1,rc=R["s1"],R["rc"]
        def mk(i,src,dst,dev): return rcopy(src,dst,ss.at[b,i],rs.at[b,i],dev)
        lo=pl.ds(0,2); hi=pl.ds(2,2); al=pl.ds(0,4)
        self.core=mk(0,self.g.at[:,:,:,pc.ocols],rc,pc.sib)
        self.xa=mk(1,s1.at[lo,pl.ds((1-pc.x)*2,2)],R["xa"],pc.xn)
        self.yb=[mk(2+i,s1.at[hi,i*2+1-pc.y],R["yb"].at[i],pc.yn) for i in range(2)]
        self.ya=mk(4,R["s2a"],R["ya"],pc.yn)
        self.xb=mk(5,R["s2b"],R["xb"],pc.xn)
        self.zz=[mk(6+k-1,R["s3"].at[(pc.z+k)%NZ],R["zr"].at[k-1],pc.zpeer(k)) for k in (1,2,3)]
        self.home=mk(9,R["fin"].at[pl.ds(pl.multiple_of((1-pc.c)*24,8),24)],R["hr"],pc.sib)
        t=(b%4)*4+b//4
        self.t=t
        self.owner=[((t//2),(t%2)*2+side) for side in range(2)]
        self.to_owner=[rcopy(R["finb"],gown_ref.at[pc.chip,:,pc.cols],os_.at[b,side],orr,self.owner[side]) for side in range(2)]
        self.to_self=pltpu.make_async_copy(R["finb"],gown_ref.at[pc.chip,:,pc.cols],orr)
    def step0(self):
        self.core.start()
    def step1(self):
        pc=self.pc; R=self.R
        self.core.wait_recv()
        for z in range(4):
            R["s1"][z]=(self.g[z,:,:,pc.cols].astype(f32)+R["rc"][z].astype(f32)).astype(bf16)
        self.xa.start()
        for d in self.yb: d.start()
    def step2(self):
        pc=self.pc; R=self.R
        self.xa.wait_recv()
        s=R["s1"][0:2,pl.ds(pc.x*2,2)].astype(f32)+R["xa"][...].astype(f32)
        keep=jnp.where(pc.y==0,s[:,0],s[:,1]); give=jnp.where(pc.y==0,s[:,1],s[:,0])
        R["k2"][0:2]=keep; R["s2a"][...]=give.astype(bf16)
        self.ya.start()
        for d in self.yb: d.wait_recv()
        s0=R["s1"][2:4,pc.y].astype(f32)+R["yb"][0].astype(f32)
        s1=R["s1"][2:4,2+pc.y].astype(f32)+R["yb"][1].astype(f32)
        keep=jnp.where(pc.x==0,s0,s1); give=jnp.where(pc.x==0,s1,s0)
        R["k2"][2:4]=keep; R["s2b"][...]=give.astype(bf16)
        self.xb.start()
    def step3(self):
        R=self.R
        self.ya.wait_recv(); self.xb.wait_recv()
        a=R["k2"][0:2]+R["ya"][...].astype(f32)
        b=R["k2"][2:4]+R["xb"][...].astype(f32)
        R["k2"][0:2]=a; R["k2"][2:4]=b
        R["s3"][0:2]=a.astype(bf16); R["s3"][2:4]=b.astype(bf16)
        for d in self.zz: d.start()
    def step4(self):
        pc=self.pc; R=self.R
        for d in self.zz: d.wait_recv()
        s=R["k2"][pc.z]
        for k in range(3): s=s+R["zr"][k].astype(f32)
        R["fin"][...]=s
        R["finb"][...]=s.astype(bf16)
        self.home.start()
        @pl.when(pc.chip==self.t)
        def _():
            self.to_self.start()
            for side in range(2):
                @pl.when(pc.c!=side)
                def _(): self.to_owner[side].start()
        @pl.when(pc.chip!=self.t)
        def _():
            for d in self.to_owner: d.start()
    def step5(self):
        pc=self.pc; R=self.R
        self.home.wait_recv()
        own=R["fin"][pl.ds(pl.multiple_of(pc.c*24,8),24)]; oth=R["hr"][...]
        self.out[self.b,:,pc.cols]=own
        self.out[self.b,:,pc.ocols]=oth
    def step(self,i): (self.step0,self.step1,self.step2,self.step3,self.step4,self.step5)[i]()
    def done(self):
        pc=self.pc
        for d in [self.core,self.xa,*self.yb,self.ya,self.xb,*self.zz,self.home]: d.wait_send()
        @pl.when(pc.chip==self.t)
        def _():
            for side in range(2):
                @pl.when(pc.c!=side)
                def _(): self.to_owner[side].wait_send()
        @pl.when(pc.chip!=self.t)
        def _():
            for d in self.to_owner: d.wait_send()

def scatter_scratch(nb=NB):
    V=pltpu.VMEM
    return dict(s1=V((nb,4,4,MR,HC),bf16),rc=V((nb,4,4,MR,HC),bf16),xa=V((nb,2,2,MR,HC),bf16),yb=V((nb,2,2,MR,HC),bf16),
        s2a=V((nb,2,MR,HC),bf16),s2b=V((nb,2,MR,HC),bf16),ya=V((nb,2,MR,HC),bf16),xb=V((nb,2,MR,HC),bf16),
        k2=V((nb,4,MR,HC),f32),s3=V((nb,4,MR,HC),bf16),zr=V((nb,3,MR,HC),bf16),fin=V((nb,MR,HC),f32),finb=V((nb,MR,HC),bf16),hr=V((nb,24,HC),f32))

class VecSum:
    def __init__(self,pc,cur,buf,ss,rs):
        self.pc,self.cur,self.buf=pc,cur,buf
        zp=lambda bit: ((pc.z^bit)*2+pc.x,pc.head)
        z1=(pc.z+1-2*(pc.z%2)); z2=(pc.z+2)%4
        partners=[pc.sib,pc.xn,pc.yn,(z1*2+pc.x,pc.head),(z2*2+pc.x,pc.head)]
        self.d=[rcopy(cur.at[i],buf.at[i],ss.at[i],rs.at[i],p) for i,p in enumerate(partners)]
    def step(self,i):
        if i>0:
            self.d[i-1].wait_recv()
            self.cur[i]=self.cur[i-1]+self.buf[i-1]
        if i<5: self.d[i].start()
    def done(self):
        for d in self.d: d.wait_send()

RSORDER=(8,4,9,5,10,6,11,7,3,2,1,0)
KEYS=list(scatter_scratch())
def rs_body(g_ref,vec_ref,out_ref,vout_ref,gown_ref,*rest):
    R=dict(zip(KEYS,rest[:len(KEYS)])); vcur,vbuf,ss,rs,os_,orr,vs,vr=rest[len(KEYS):]
    pc=Place()
    greet_all(pc)
    vcur[0]=vec_ref[...]
    vsum=VecSum(pc,vcur,vbuf,vs,vr)
    sc=[Scatter(pc,b,g_ref,R,out_ref,gown_ref,ss,rs,os_,orr) for b in RSORDER]
    for t in range(len(sc)+5):
        for s in range(6):
            if 0<=t-s<len(sc): sc[t-s].step(s)
        if t<=5: vsum.step(t)
    vout_ref[...]=vcur[5]
    for s in sc: s.done()
    vsum.done()
    @pl.when(pc.xy<3)
    def _(): pltpu.make_async_copy(gown_ref,gown_ref,orr).wait()

def call_rs(g,vec):
    V=pltpu.VMEM; S=jax.ShapeDtypeStruct
    B=pl.BlockSpec(memory_space=V); sem=pltpu.SemaphoreType.DMA
    return pl.pallas_call(rs_body,in_specs=[B,B],out_specs=[B,B,B],
        out_shape=[S((NB,24,D),f32),S((16,D),f32),S((16,MR,D),bf16)],
        scratch_shapes=list(scatter_scratch().values())+[V((6,16,D),f32),V((5,16,D),f32),sem((NB,10)),sem((NB,10)),sem((NB,2)),sem,sem((5,)),sem((5,))],
        compiler_params=pltpu.CompilerParams(vmem_limit_bytes=62<<20,collective_id=1,has_side_effects=True))(g,vec)

BETA=0.95; BETA_TWO=0.99; RATE=1.0; RATE_VEC=0.05

def owner_of(b):
    return ((b//3+(b%3)%2+1)%4)*4+b%3
def owned_by(pc):
    return 3*((pc.z+3-pc.xy%2)%4)+pc.xy

def pack(rows):
    return jnp.concatenate([rows[:,:HC],rows[:,HC:]],axis=0).astype(bf16)
def unpack(p):
    p=p.astype(f32)
    return jnp.concatenate([p[:24],p[24:]],axis=1)

def send_row(pc,t,src,dst,ssem,rsem):
    @pl.when(t==pc.me)
    def _(): pltpu.make_async_copy(src,dst,rsem).start()
    @pl.when(t!=pc.me)
    def _(): rcopy(src,dst,ssem,rsem,(t//4,t%4)).start()

def send_rows(pc,n,base,slots,dst,ss,rsem,start):
    def one(j,carry):
        t=base+j
        @pl.when(t==pc.me)
        def _():
            if start: pltpu.make_async_copy(slots.at[j],dst,rsem).start()
        @pl.when(t!=pc.me)
        def _():
            d=rcopy(slots.at[j],dst,ss.at[j],rsem,(t//4,t%4))
            if start: d.start()
            else: d.wait_send()
        return carry
    lax.fori_loop(0,n,one,0)

def newton_body(ghalf_ref,statl_ref,statr_ref,left_ref,right_ref,mas_ref,va_ref,vec_ref,sec_ref,
                ln_ref,rn_ref,mn_ref,vg_ref,sn_ref,vn_ref,
                m_ref,x_ref,nb,pb,sb,xb,slots,ggr,uslots,ur,tb,rt,rho,gown_ref,vcur,vbuf,gg, gs,gr,us,ur_sem,es,er,vs,vr):
    pc=Place()
    gown_ref[:,pc.cols]=ghalf_ref[...]
    vcur[0]=va_ref[...]
    greet_all(pc)
    vsum=VecSum(pc,vcur,vbuf,vs,vr)
    vsum.step(0)
    b=owned_by(pc)
    owner=pc.xy<3
    nblk=D//RB
    swap=lambda: rcopy(gown_ref.at[:,pc.cols],gown_ref.at[:,pc.cols],es.at[3],er.at[3],pc.sib)
    @pl.when(owner)
    def _(): swap().start()
    vsum.step(1)
    @pl.when(owner)
    def _():
        @pl.when(pc.c==0)
        def _():
            for i in range(nblk):
                r=slice(i*RB,(i+1)*RB)
                gg[r,:]=(1-BETA)*dot(ghalf_ref[r,:],ghalf_ref[...],1,1)
            swap().wait_recv()
            for i in range(nblk):
                r=slice(i*RB,(i+1)*RB)
                p=gg[r,:]+(1-BETA)*dot(gown_ref[r,HC:],gown_ref[:,HC:],1,1)
                gg[r,:]=p
                m_ref[r,:]=BETA*statl_ref[r,:]+p
        @pl.when(pc.c==1)
        def _():
            swap().wait_recv()
            for i in range(nblk):
                r=slice(i*RB,(i+1)*RB)
                p=(1-BETA)*dot(gown_ref[:,r],gown_ref[...],0,0)
                gg[r,:]=p
                m_ref[r,:]=BETA*statr_ref[r,:]+p
        def between(k):
            def piece(t,carry):
                slots[t]=pack(gg[pl.ds(pl.multiple_of(t*24,8),24),:])
                send_row(pc,t,slots.at[t],ggr.at[2*b+pc.c],gs.at[t],gr)
                return carry
            @pl.when(k<3)
            def _(): lax.fori_loop((k-1)*16,k*16,piece,0)
            @pl.when(k==2)
            def _(): vsum.step(2)
            @pl.when(k==4)
            def _(): vsum.step(3)
            @pl.when(k==6)
            def _(): vsum.step(4)
        newton(m_ref,x_ref,nb,pb,sb,xb,between)
        tr=jnp.zeros((1,1),f32)
        for i in range(nblk):
            r=slice(i*RB,(i+1)*RB); tr=tr+diag_sum(x_ref[r,r])
        lam=tr*(1/D)
        for i in range(nblk):
            r=slice(i*RB,(i+1)*RB)
            xb[r,:]=jnp.where(eye_rows(i),x_ref[r,:]-lam,x_ref[r,:]).astype(bf16)
        H=D//2
        send_t=rcopy(tb.at[pl.ds(H,H)],tb.at[pl.ds(H,H)],es.at[0],er.at[0],pc.sib)
        send_r=rcopy(xb,rt,es.at[1],er.at[1],pc.sib)
        send_l=rcopy(rho.at[0],rho.at[1],es.at[2],er.at[2],pc.sib)
        def update(trows,right,lam_r):
            for i in range(2):
                r=pl.ds(trows+i*192,192)
                t=tb[r,:]
                m_ref[pl.ds(i*192,192),:]=lam_r*t.astype(f32)+dot(t,right[...])
        rho[0]=jnp.broadcast_to(lam,(8,128))
        @pl.when(pc.c==0)
        def _():
            for h in (1,0):
                for i in range(2):
                    r=slice(h*H+i*192,h*H+(i+1)*192)
                    tb[r,:]=(lam*gown_ref[r,:].astype(f32)+dot(xb[r,:],gown_ref[...])).astype(bf16)
                if h==1: send_t.start()
            send_r.wait_recv(); send_l.wait_recv()
            update(0,rt,rho[1,0:1,0:1])
            send_t.wait_send()
        @pl.when(pc.c==1)
        def _():
            send_r.start(); send_l.start()
            send_t.wait_recv()
            update(H,xb,lam)
            send_r.wait_send(); send_l.wait_send()
        def pk2(i,carry):
            uslots[i]=pack(m_ref[pl.ds(pl.multiple_of(i*24,8),24),:])
            send_row(pc,pc.c*16+i,uslots.at[i],ur.at[b],us.at[i],ur_sem)
            return carry
        lax.fori_loop(0,16,pk2,0)
    @pl.when(jnp.logical_not(owner))
    def _():
        for i in (2,3,4): vsum.step(i)
    vsum.step(5)
    r=lax.broadcasted_iota(jnp.int32,(D,128),1); j=lax.broadcasted_iota(jnp.int32,(D,128),0)
    pick=jnp.where((j==pc.me*24+r)&(r<24),1.0,0.0).astype(f32)
    vg=lax.dot_general(vcur[5],pick,(((1,),(0,)),((),())),precision=lax.Precision.HIGHEST,preferred_element_type=f32)[:12,:24]
    sn=BETA_TWO*sec_ref[...]+(1-BETA_TWO)*vg*vg
    vg_ref[...]=vg; sn_ref[...]=sn
    vn_ref[...]=vec_ref[...]-RATE_VEC*vg/(jnp.sqrt(sn)+1e-8)
    pltpu.make_async_copy(ggr,ggr,gr).wait()
    def stats(i,carry):
        ln_ref[i]=BETA*left_ref[i]+unpack(ggr[2*i])
        rn_ref[i]=BETA*right_ref[i]+unpack(ggr[2*i+1])
        return carry
    lax.fori_loop(0,NB,stats,0)
    pltpu.make_async_copy(ur,ur,ur_sem).wait()
    def upd(i,carry):
        mn_ref[i]=mas_ref[i]-RATE*unpack(ur[i])
        return carry
    lax.fori_loop(0,NB,upd,0)
    @pl.when(owner)
    def _():
        swap().wait_send()
        send_rows(pc,32,0,slots,ggr.at[2*b+pc.c],gs,gr,False)
        send_rows(pc,16,pc.c*16,uslots,ur.at[b],us,ur_sem,False)
    vsum.done()

def call_newton_step(gown,statl,statr,left,right,mas,va,vec,sec):
    V=pltpu.VMEM; S=jax.ShapeDtypeStruct
    B=pl.BlockSpec(memory_space=V); sem=pltpu.SemaphoreType.DMA
    rows=S((NB,24,D),f32); small=S((NB,24),f32)
    return pl.pallas_call(newton_body,in_specs=[B]*9,out_specs=[B]*6,out_shape=[rows]*3+[small]*3,
        scratch_shapes=[V((D,D),f32)]*2+[V((D,D),bf16)]*4+[V((32,48,HC),bf16),V((24,48,HC),bf16),V((16,48,HC),bf16),V((12,48,HC),bf16),V((D,D),bf16),V((D,D),bf16),V((2,8,128),f32),V((D,D),bf16),V((6,16,D),f32),V((5,16,D),f32),V((D,D),f32),
            sem((32,)),sem,sem((16,)),sem,sem((4,)),sem((4,)),sem((5,)),sem((5,))],
        compiler_params=pltpu.CompilerParams(vmem_limit_bytes=62<<20,collective_id=2,has_side_effects=True))(gown,statl,statr,left,right,mas,va,vec,sec)


def place_params(pg_ref,p_ref):
    r=lax.broadcasted_iota(jnp.int32,(128,D),0); j=lax.broadcasted_iota(jnp.int32,(128,D),1)
    p_ref[...]=jnp.zeros_like(p_ref)
    def chip(m,carry):
        for c in range(2):
            sel=jnp.where((j==(m*2+c)*24+r)&(r<24),1.0,0.0).astype(bf16)
            p_ref[...]+=dot(pg_ref[m//4,m%4,:,c*HC:c*HC+128],sel)
        return carry
    lax.fori_loop(0,16,chip,0)

def keys_of_pair(p,k_ref,ka_ref,v_ref,va_ref,doc_ref):
    cols=pl.ds(pl.multiple_of(p*128,128),128)
    lane=lax.broadcasted_iota(jnp.int32,(256,128),1)
    for t in range(PACK//256):
        rows=pl.ds(t*256,256)
        kp=k_ref[rows,cols].astype(f32); vp=v_ref[rows,cols].astype(f32)
        doc=doc_ref[rows,:]
        for h,lo in enumerate((True,False)):
            off=64 if lo else 0
            k1=onehot_part(kp,lane,lo,doc,1.0,1.0)
            ka_ref[h,rows,:]=jnp.where((lane>=off+8)&(lane<off+11),1.0,k1).astype(bf16)
            va_ref[h,rows,:]=jnp.where((lane<64)==lo,vp,1.0).astype(bf16)

QF=512
def attend_block(p,b,q_ref,ka_ref,va_ref,qa_ref,ctx_ref,doc_ref):
    cols=pl.ds(pl.multiple_of(p*128,128),128)
    rows=pl.ds(pl.multiple_of(b*QF,QF),QF)
    lane=lax.broadcasted_iota(jnp.int32,(QF,128),1)
    low=lane<64
    qp=q_ref[rows,cols].astype(f32)*0.125
    doc=doc_ref[rows,:]
    qf=[onehot_part(qp,lane,lo,doc,0.0,BIG) for lo in (True,False)]
    ss=[dot(qf[h].astype(bf16),ka_ref[h],1,1) for h in range(2)]
    os=[]
    for h,lo in enumerate((True,False)):
        off=64 if lo else 0
        m=jnp.max(ss[h],axis=1,keepdims=True)
        o=dot(jnp.exp(ss[h]-m).astype(bf16),va_ref[h])
        os.append(o)
        q1=qf[h]
        for i,c in enumerate(split3(-(m+jnp.log(o)))): q1=jnp.where(lane==off+8+i,c,q1)
        qa_ref[h,rows,:]=q1.astype(bf16)
    l=pltpu.roll(jnp.where(low,os[1],os[0]),64,1)
    ctx_ref[rows,cols]=(jnp.where(low,os[0],os[1])/l).astype(bf16)

class StatMove:
    def __init__(self,pc,src,dst,side,ss,rsem):
        self.pc,self.src,self.dst,self.side,self.ss,self.rsem=pc,src,dst,side,ss,rsem
    def move(self,i,start):
        pc=self.pc
        b=(i+pc.me)%NB
        t=owner_of(b)
        src,dst=self.src.at[b],self.dst.at[pc.me]
        mine=(pc.chip==t)&(pc.c==self.side)
        if start:
            @pl.when(mine)
            def _(): pltpu.make_async_copy(src,dst,self.rsem).start()
        @pl.when(jnp.logical_not(mine))
        def _():
            d=rcopy(src,dst,self.ss.at[b],self.rsem,(t//2,(t%2)*2+self.side))
            if start: d.start()
            else: d.wait_send()
    def done(self):
        pc=self.pc
        lax.fori_loop(0,NB,lambda i,c: (self.move(i,False),c)[1],0)
        @pl.when((pc.xy<3)&(pc.c==self.side))
        def _(): pltpu.make_async_copy(self.dst,self.dst,self.rsem).wait()

AORDER=(0,1,2,3,4,8,5,9,6,10,7,11)
TT=256
def front_body(len_ref,x_ref,cot_ref,mas_ref,pv_ref,left_ref,
               out_o,qa_o,ka_o,v_o,ctx_o,act_o,din_o,dffn_o,hlow_o,dz1_o,dctx_o,wq_o,vec_o,st_ref,
               w_ref,pg_ref,p_ref,sibm,q,k,v,ctx,doc,qa,ka,va,n1,r1,hlow,acc,act,gp,dffn,dctx,out,
               ss,rs,cs,cr,ts,tr,lsem,asem,osem):
    pc=Place()
    greet_all(pc)
    first=rcopy(mas_ref.at[pl.ds(0,3),:,pc.ocols],sibm.at[pl.ds(0,3)],cs.at[0],cr.at[0],pc.sib)
    other=rcopy(mas_ref.at[pl.ds(3,9),:,pc.ocols],sibm.at[pl.ds(3,9)],cs.at[1],cr.at[1],pc.sib)
    first.start(); other.start()
    pg_ref[pc.z,pc.xy,:,pc.cols]=pv_ref[...]
    def assemble(places):
        for pos in places:
            own=mas_ref[AORDER[pos],:,pc.cols]; oth=sibm[AORDER[pos]]
            upper=jnp.where(pc.c==0,own,oth); lower=jnp.where(pc.c==0,oth,own)
            w_ref[pos,pc.z,pc.xy,:,pc.cols]=jnp.concatenate([upper,lower],axis=0).astype(bf16)
    def group(g):
        if isinstance(g,int) and g==0: return Gather(pc,pg_ref,ss.at[0],rs.at[0]).copies()
        return Gather(pc,w_ref.at[g-1],ss.at[g],rs.at[g]).copies()
    NG=13
    def tick(t):
        for s,d in ((0,-3),(1,0),(2,1),(3,2),(4,3)):
            if isinstance(t,int):
                if 0<=t-d<NG and not (s==0 and t<1): group(t-d).step(s)
            else:
                @pl.when(t-d<NG)
                def _(): group(t-d).step(s)
    stats=StatMove(pc,left_ref,st_ref,0,ts,tr)
    copies=[]
    def away(src,dst):
        i=len(copies)
        c=pltpu.make_async_copy(src,dst,lsem.at[i]); c.start(); copies.append(c)
    W=lambda pos: w_ref[pos].reshape(D,D)
    group(0).step(0)
    first.wait_recv()
    for i in range(3):
        assemble([i])
        group(i+1).step(0)
    other.wait_recv()
    assemble(range(3,12))
    for t in range(4): tick(t)
    place_params(pg_ref,p_ref)
    t_=lax.broadcasted_iota(jnp.int32,(PACK,128),0)
    end=jnp.int32(0); dd=jnp.zeros((PACK,128),jnp.int32)
    for j in range(8):
        end=end+len_ref[0,j]
        dd=dd+(t_>=end).astype(jnp.int32)
    doc[...]=dd
    for i,(o,b,dst) in enumerate(((q,0,None),(k,None,None),(v,1,v_o))):
        tick(4+i)
        for tl in range(4):
            rows=pl.ds(tl*TT,TT)
            y=dot(x_ref[rows,:],W(i))
            if b is not None: y=y+p_ref[b:b+1,:]
            o[rows,:]=y.astype(bf16)
        if dst is not None: away(o,dst)
        away(w_ref.at[i],wq_o.at[i])
    def pair_copies(p):
        return [pltpu.make_async_copy(s.at[p%2],d.at[p],asem.at[i,p%2]) for i,(s,d) in enumerate(((qa,qa_o),(ka,ka_o)))]
    def slot(n,carry):
        p=n//2; b=n%2
        @pl.when(b==0)
        def _():
            @pl.when(p>=2)
            def _():
                for c in pair_copies(p-2): c.wait()
            keys_of_pair(p,k,ka.at[p%2],v,va,doc)
        attend_block(p,b,q,ka.at[p%2],va,qa.at[p%2],ctx,doc)
        @pl.when(b==1)
        def _():
            for c in pair_copies(p): c.start()
            tick(7+p)
        return carry
    lax.fori_loop(0,12,slot,0)
    away(ctx,ctx_o)
    g1,s1,g2,s2=(p_ref[i:i+1,:] for i in (8,9,10,11))
    vec_o[...]=jnp.zeros_like(vec_o)
    def out_proj(tl,carry):
        rows=pl.ds(pl.multiple_of(tl*TT,TT),TT)
        z=x_ref[rows,:].astype(f32)+(dot(ctx[rows,:],W(3))+p_ref[2:3,:])
        n,r=layer_norm(z)
        n1[rows,:]=n
        r1[rows,:]=jnp.broadcast_to(r,(TT,128))
        hlow[rows,:]=(n*g1+s1).astype(bf16)
        return carry
    lax.fori_loop(0,4,out_proj,0)
    def chunk_copy(c):
        lane=pl.ds(pl.multiple_of(c*D,128),D)
        return pltpu.make_async_copy(act.at[:,lane],act_o.at[:,lane],osem.at[5,c])
    def chunk(c,carry):
        lane=pl.ds(pl.multiple_of(c*D,128),D)
        bias=p_ref[pl.ds(3+c,1),:]
        for tl in range(4):
            rows=pl.ds(tl*TT,TT)
            inner=dot(hlow[rows,:],W(4+2*c))+bias
            a,g=gelu_both(inner)
            al=a.astype(bf16)
            act[rows,lane]=al
            gp[rows,lane]=g.astype(bf16)
            y=dot(al,W(5+2*c))
            @pl.when(c==0)
            def _(): acc[rows,:]=y
            @pl.when(c>0)
            def _(): acc[rows,:]+=y
        chunk_copy(c).start()
        @pl.when(c<3)
        def _(): tick(13+c)
        @pl.when(c==2)
        def _(): lax.fori_loop(0,NB,lambda i,a: (stats.move(i,True),a)[1],0)
        return carry
    lax.fori_loop(0,4,chunk,0)
    away(hlow,hlow_o)
    pltpu.make_async_copy(cot_ref,out,lsem.at[20]).start()
    pltpu.make_async_copy(cot_ref,out,lsem.at[20]).wait()
    def tile_copies(tl):
        rows=pl.ds(pl.multiple_of(tl*TT,TT),TT)
        return [pltpu.make_async_copy(s.at[rows],d.at[rows],osem.at[i,tl]) for i,(s,d) in enumerate(((out,out_o),(gp,din_o),(dffn,dffn_o),(acc,dz1_o),(dctx,dctx_o)))]
    def tile(tl,carry):
        rows=pl.ds(pl.multiple_of(tl*TT,TT),TT)
        n1t=n1[rows,:]
        z=(n1t*g1+s1)+(acc[rows,:]+p_ref[7:8,:])
        n2,r2=layer_norm(z)
        e=out[rows,:].astype(f32)
        out[rows,:]=(n2*g2+s2).astype(bf16)
        c2=e*g2
        dz2=r2*(c2-jnp.mean(c2,axis=-1,keepdims=True)-n2*jnp.mean(c2*n2,axis=-1,keepdims=True))
        df=dz2.astype(bf16)
        dffn[rows,:]=df
        vec_o[10:11,:]+=jnp.sum(e*n2,axis=0,keepdims=True)
        vec_o[11:12,:]+=jnp.sum(e,axis=0,keepdims=True)
        vec_o[7:8,:]+=jnp.sum(df.astype(f32),axis=0,keepdims=True)
        dh=dz2
        for c in range(4):
            lane=pl.ds(c*D,D)
            dact=dot(df,W(5+2*c),1,1)
            din=(dact*gp[rows,lane].astype(f32)).astype(bf16)
            gp[rows,lane]=din
            vec_o[3+c:4+c,:]+=jnp.sum(din.astype(f32),axis=0,keepdims=True)
            dh=dh+dot(din,W(4+2*c),1,1)
        vec_o[8:9,:]+=jnp.sum(dh*n1t,axis=0,keepdims=True)
        vec_o[9:10,:]+=jnp.sum(dh,axis=0,keepdims=True)
        c1=dh*g1
        dz1=r1[rows,0:1]*(c1-jnp.mean(c1,axis=-1,keepdims=True)-n1t*jnp.mean(c1*n1t,axis=-1,keepdims=True))
        acc[rows,:]=dz1
        dat=dz1.astype(bf16)
        vec_o[2:3,:]+=jnp.sum(dat.astype(f32),axis=0,keepdims=True)
        dctx[rows,:]=dot(dat,W(3),1,1).astype(bf16)
        for c in tile_copies(tl): c.start()
        return carry
    lax.fori_loop(0,4,tile,0)
    for c in copies: c.wait()
    for p in (4,5):
        for c in pair_copies(p): c.wait()
    for i in range(4):
        chunk_copy(i).wait()
        for c in tile_copies(i): c.wait()
    first.wait_send(); other.wait_send()
    group(0).done()
    lax.fori_loop(1,NG,lambda g,c: (group(g).done(),c)[1],0)
    stats.done()

def call_front(lengths,x,cot,masters,pv,left):
    V=pltpu.VMEM; S=jax.ShapeDtypeStruct; A=pl.ANY
    B=lambda m: pl.BlockSpec(memory_space=m)
    sem=pltpu.SemaphoreType.DMA
    T=lambda w,d: S((PACK,w),d)
    return pl.pallas_call(front_body,
        in_specs=[B(pltpu.SMEM),B(V),B(A),B(V),B(V),B(A)],
        out_specs=[B(A)]*12+[B(V),B(A)],
        out_shape=[T(D,bf16)]+[S((6,2,PACK,128),bf16)]*2+[T(D,bf16)]*2+[T(FF,bf16),T(FF,bf16),T(D,bf16),T(D,bf16),T(D,f32),T(D,bf16),S((3,4,4,MR,D),bf16),S((16,D),f32),S((32,24,D),f32)],
        scratch_shapes=[V((NB,4,4,MR,D),bf16),V((4,4,16,D),bf16),V((16,D),f32),V((NB,24,HC),f32)]+[V((PACK,D),bf16)]*4+
            [V((PACK,128),jnp.int32),V((2,2,PACK,128),bf16),V((2,2,PACK,128),bf16),V((2,PACK,128),bf16),V((PACK,D),f32),V((PACK,128),f32),V((PACK,D),bf16),V((PACK,D),f32),
             V((PACK,FF),bf16),V((PACK,FF),bf16),V((PACK,D),bf16),V((PACK,D),bf16),V((PACK,D),bf16),
             sem((13,11)),sem((13,11)),sem((2,)),sem((2,)),sem((NB,)),sem,sem((24,)),sem((2,2)),sem((6,4))],
        compiler_params=pltpu.CompilerParams(vmem_limit_bytes=63<<20,collective_id=0,has_side_effects=True))(lengths,x,cot,masters,pv,left)


NGR=12
def sum_scratch():
    V=pltpu.VMEM; nb=NGR
    return dict(rc=V((nb,4,4,MR,HC),bf16),xa=V((nb,2,2,MR,HC),bf16),yb=V((nb,2,2,MR,HC),bf16),
        s2a=V((nb,2,MR,HC),bf16),s2b=V((nb,2,MR,HC),bf16),ya=V((nb,2,MR,HC),bf16),xb=V((nb,2,MR,HC),bf16),
        s3=V((nb,4,MR,HC),bf16),zr=V((nb,3,MR,HC),bf16),fin=V((nb,MR,HC),f32),finb=V((nb,MR,HC),bf16),hr=V((nb,24,HC),f32))
SKEYS=list(sum_scratch())

class GroupSum:
    def __init__(self,pc,g_ref,R,out_ref,gown_ref,ss,rs,os_,orr):
        self.pc,self.gr,self.RR,self.out,self.gown=pc,g_ref,R,out_ref,gown_ref
        self.ss,self.rs,self.os_,self.orr=ss,rs,os_,orr
    def mk(self,g,i,src,dst,dev): return rcopy(src,dst,self.ss.at[g,i],self.rs.at[g,i],dev)
    def of(self,g): return self.gr.at[g],{k:v.at[g] for k,v in self.RR.items()}
    def core(self,g):
        G,R=self.of(g); return self.mk(g,0,G.at[:,:,:,self.pc.ocols],R["rc"],self.pc.sib)
    def xa(self,g):
        G,R=self.of(g); pc=self.pc; return self.mk(g,1,G.at[pl.ds(0,2),pl.ds((1-pc.x)*2,2),:,pc.cols],R["xa"],pc.xn)
    def yb(self,g,i):
        G,R=self.of(g); pc=self.pc; return self.mk(g,2+i,G.at[pl.ds(2,2),i*2+1-pc.y,:,pc.cols],R["yb"].at[i],pc.yn)
    def ya(self,g):
        G,R=self.of(g); return self.mk(g,4,R["s2a"],R["ya"],self.pc.yn)
    def xb(self,g):
        G,R=self.of(g); return self.mk(g,5,R["s2b"],R["xb"],self.pc.xn)
    def zz(self,g,k):
        G,R=self.of(g); pc=self.pc; return self.mk(g,5+k,R["s3"].at[(pc.z+k)%NZ],R["zr"].at[k-1],pc.zpeer(k))
    def home(self,g):
        G,R=self.of(g); pc=self.pc; return self.mk(g,9,R["fin"].at[pl.ds(pl.multiple_of((1-pc.c)*24,8),24)],R["hr"],pc.sib)
    def step0(self,g): self.core(g).start()
    def step1(self,g):
        pc=self.pc; G,R=self.of(g)
        self.core(g).wait_recv()
        for z in range(4):
            G[z,:,:,pc.cols]=(G[z,:,:,pc.cols].astype(f32)+R["rc"][z].astype(f32)).astype(bf16)
        self.xa(g).start()
        for i in range(2): self.yb(g,i).start()
    def step2(self,g):
        pc=self.pc; G,R=self.of(g)
        self.xa(g).wait_recv()
        R["s2a"][...]=(G[0:2,pc.x*2+1-pc.y,:,pc.cols].astype(f32)+R["xa"][:,1-pc.y].astype(f32)).astype(bf16)
        self.ya(g).start()
        for i in range(2): self.yb(g,i).wait_recv()
        R["s2b"][...]=(G[2:4,(1-pc.x)*2+pc.y,:,pc.cols].astype(f32)+R["yb"][1-pc.x].astype(f32)).astype(bf16)
        self.xb(g).start()
    def step3(self,g):
        pc=self.pc; G,R=self.of(g)
        self.ya(g).wait_recv(); self.xb(g).wait_recv()
        a=G[0:2,pc.xy,:,pc.cols].astype(f32)+R["xa"][:,pc.y].astype(f32)+R["ya"][...].astype(f32)
        b=G[2:4,pc.xy,:,pc.cols].astype(f32)+R["yb"][pc.x].astype(f32)+R["xb"][...].astype(f32)
        R["s3"][0:2]=a.astype(bf16); R["s3"][2:4]=b.astype(bf16)
        ab=jnp.where(pc.z%2==0,jnp.stack([a[0],b[0]]),jnp.stack([a[1],b[1]]))
        R["fin"][...]=jnp.where(pc.z<2,ab[0],ab[1])
        for k in (1,2,3): self.zz(g,k).start()
    def targets(self,g,act):
        pc=self.pc; G,R=self.of(g)
        def whole(b):
            act(R["finb"],self.gown.at[pc.chip],0,owner_of(b))
        def slab(j):
            for i in range(3):
                act(R["finb"].at[:,pl.ds(i*128,128)],self.gown.at[pc.chip,:,pl.ds(pl.multiple_of(j*128,128),128)],i,owner_of(i))
        if isinstance(g,int):
            if g<9: whole(8+g//2-4*(g%2)-9*(g//8))
            else: slab(g-9)
        else:
            @pl.when(g<9)
            def _(): whole(8+g//2-4*(g%2)-9*(g//8))
            @pl.when(g>=9)
            def _(): slab(g-9)
    def step4(self,g):
        pc=self.pc; G,R=self.of(g)
        for k in (1,2,3): self.zz(g,k).wait_recv()
        s=R["fin"][...]
        for k in range(3): s=s+R["zr"][k].astype(f32)
        R["fin"][...]=s
        R["finb"][...]=s.astype(bf16)
        self.home(g).start()
        def send(src,dst,i,t):
            mine=pc.chip==t
            @pl.when(mine)
            def _(): pltpu.make_async_copy(src,dst,self.orr).start()
            @pl.when(jnp.logical_not(mine))
            def _(): rcopy(src,dst,self.os_.at[g,i],self.orr,(t//2,(t%2)*2+pc.c)).start()
        self.targets(g,send)
    def step5(self,g):
        pc=self.pc; G,R=self.of(g)
        self.home(g).wait_recv()
        def whole(b):
            self.out[b,:,pc.cols]=R["fin"][pl.ds(pl.multiple_of(pc.c*24,8),24)]
            self.out[b,:,pc.ocols]=R["hr"][...]
        def slab(j):
            for i in range(3):
                self.out[i,:,pl.ds(pl.multiple_of((pc.c*3+j)*128,128),128)]=R["fin"][pl.ds(pl.multiple_of(pc.c*24,8),24),i*128:(i+1)*128]
                self.out[i,:,pl.ds(pl.multiple_of(((1-pc.c)*3+j)*128,128),128)]=R["hr"][:,i*128:(i+1)*128]
        if isinstance(g,int):
            if g<9: whole(8+g//2-4*(g%2)-9*(g//8))
            else: slab(g-9)
        else:
            @pl.when(g<9)
            def _(): whole(8+g//2-4*(g%2)-9*(g//8))
            @pl.when(g>=9)
            def _(): slab(g-9)
    def done(self,g):
        pc=self.pc
        for d in (self.core,self.xa,self.ya,self.xb,self.home): d(g).wait_send()
        for i in range(2): self.yb(g,i).wait_send()
        for k in (1,2,3): self.zz(g,k).wait_send()
        def wait(src,dst,i,t):
            @pl.when(pc.chip!=t)
            def _(): rcopy(src,dst,self.os_.at[g,i],self.orr,(t//2,(t%2)*2+pc.c)).wait_send()
        self.targets(g,wait)

KB_=512
PACE={1:(("step1",0),),4:(("step1",1),),5:(("step2",0),),7:(("step1",2),),8:(("step2",1),("step3",0))}
def prepare_pair(p,v,ctx,do,doa,va):
    cols=pl.ds(pl.multiple_of(p*128,128),128)
    lane=lax.broadcasted_iota(jnp.int32,(256,128),1)
    i=lax.broadcasted_iota(jnp.int32,(128,128),0); j=lax.broadcasted_iota(jnp.int32,(128,128),1)
    cross=jnp.where((i<64)!=(j<64),-1.0,0.0).astype(bf16)
    for t in range(PACK//256):
        rows=pl.ds(t*256,256)
        vp=v[rows,cols].astype(f32)
        dop=do[rows,cols].astype(f32); prod=dop*ctx[rows,cols].astype(f32)
        dd=sum(dot(c.astype(bf16),cross) for c in split3(prod))
        parts=split3(dd)
        for h,lo in enumerate((True,False)):
            keep=(lane<64)==lo
            off=64 if lo else 0
            d1=jnp.where(keep,dop,0.0)
            for n,c in enumerate(parts): d1=jnp.where(lane==off+n,c,d1)
            doa[h,rows,:]=d1.astype(bf16)
            v1=jnp.where(keep,vp,0.0)
            va[h,rows,:]=jnp.where((lane>=off)&(lane<off+3),1.0,v1).astype(bf16)

def back_block(p,b,dk_ref,dv_ref,qa,doa,ka,va,dqa):
    cols=pl.ds(pl.multiple_of(p*128,128),128)
    rows=pl.ds(pl.multiple_of(b*KB_,KB_),KB_)
    low=lax.broadcasted_iota(jnp.int32,(KB_,128),1)<64
    lowq=lax.broadcasted_iota(jnp.int32,(PACK,128),1)<64
    r=[]
    for h in range(2):
        kh=ka[h,rows,:]
        pr=jnp.exp(dot(kh,qa[h],1,1))
        dp=dot(va[h,rows,:],doa[h],1,1)
        ds=(pr*dp).astype(bf16)
        r.append((dot(pr.astype(bf16),doa[h]),dot(ds,qa[h]),dot(ds,kh,0,0)))
    dq=jnp.where(lowq,r[0][2],r[1][2])
    @pl.when(b==0)
    def _(): dqa[...]=dq
    @pl.when(b>0)
    def _(): dqa[...]+=dq
    dv_ref[rows,cols]=jnp.where(low,r[0][0],r[1][0]).astype(bf16)
    dk_ref[rows,cols]=jnp.where(low,r[0][1],r[1][1]).astype(bf16)

def back_body(x_ref,qa_i,ka_i,v_i,ctx_i,do_i,act_i,din_i,dffn_i,hlow_i,dz1_i,wq_i,vec_ref,right_ref,
              ig_o,out_ref,vcur,gown_ref,st_ref,*rest):
    R=dict(zip(SKEYS,rest[:len(SKEYS)]))
    (g_ref,ctx,w_last,act,din,dffn,hlow,acc,qa,doa,ka,va,dqa,
     ss,rs,os_,orr,ts,tr,lsem,asem)=rest[len(SKEYS):]
    pc=Place()
    loads={}
    def load(name,src,dst):
        c=pltpu.make_async_copy(src,dst,lsem.at[len(loads)]); c.start(); loads[name]=c
    half=lambda ref,c: ref.at[:,pl.ds(c*D,D)]
    load("act0",half(act_i,0),act.at[0]); load("dffn",dffn_i,dffn)
    load("hlow",hlow_i,hlow); load("din0",half(din_i,0),din.at[0])
    load("act1",half(act_i,1),act.at[1]); load("din1",half(din_i,1),din.at[1])
    for n,s,d in (("acc",dz1_i,acc),("ctx",ctx_i,ctx)): load(n,s,d)
    q,v,do,k=act.at[0],din.at[0],dffn,act.at[1]
    late={5:("v",v_i,v),7:("do",do_i,do)}
    def pair_loads(pi):
        p=3*(pi%2)+pi//2
        return [pltpu.make_async_copy(s.at[p],d.at[pi%2],asem.at[i,pi%2]) for i,(s,d) in enumerate(((qa_i,qa),(ka_i,ka)))]
    for c in pair_loads(0): c.start()
    greet_all(pc)
    gs=GroupSum(pc,g_ref,R,out_ref,gown_ref,ss,rs,os_,orr)
    stats=StatMove(pc,right_ref,st_ref,1,ts,tr)
    def product(g,a,b):
        for r in range(4):
            g_ref[g,r]=dot(a[:,r*192:(r+1)*192],b,0,0).astype(bf16).reshape(4,MR,D)
    lax.fori_loop(0,NB,lambda i,a: (stats.move(i,True),a)[1],0)
    loads["dffn"].wait()
    for i in range(9):
        c=i//2
        if i==8:
            loads["ctx"].wait(); loads["acc"].wait()
            product(i,ctx,acc[...].astype(bf16))
        elif i%2==0:
            loads[f"act{c}"].wait()
            product(i,act.at[c%2],dffn[...])
            if c<2: load(f"act{c+2}",half(act_i,c+2),act.at[c%2])
        else:
            if c==0: loads["hlow"].wait()
            loads[f"din{c}"].wait()
            product(i,hlow,din[c%2])
            if c<2: load(f"din{c+2}",half(din_i,c+2),din.at[c%2])
        if i in late: load(*late[i])
        gs.step0(i)
        for s,g in PACE.get(i,()): getattr(gs,s)(g)
    wrow=pl.ds(0,D)
    wdst=[din.at[1,wrow],hlow.at[wrow],w_last]
    for i in range(3): load(f"w{i}",wq_i.at[i],wdst[i])
    for n in ("v","do"): loads[n].wait()
    def slot(n,carry):
        pi=n//2; b=n%2; j=pi//2; cc=pi%2; p=3*cc+j; side=pi%2
        cols=pl.ds(pl.multiple_of(p*128,128),128)
        @pl.when(b==0)
        def _():
            for c in pair_loads(pi): c.wait()
            @pl.when(pi<5)
            def _():
                for c in pair_loads(pi+1): c.start()
            prepare_pair(p,v,ctx,do,doa,va)
        back_block(p,b,k,v,qa.at[side],doa,ka.at[side],va,dqa)
        @pl.when(b==1)
        def _():
            q[:,cols]=(dqa[...]*0.125).astype(bf16)
            al=jnp.concatenate([q[:,cols],k[:,cols],v[:,cols]],axis=1)
            lane=pl.ds(pl.multiple_of(cc*HC,128),HC)
            for r in range(4):
                g_ref[9+j,r,:,:,lane]=dot(x_ref[:,r*192:(r+1)*192],al,0,0).astype(bf16).reshape(4,MR,HC)
            vcur[0:1,cols]=jnp.sum(q[:,cols].astype(f32),axis=0,keepdims=True)
            vcur[1:2,cols]=jnp.sum(v[:,cols].astype(f32),axis=0,keepdims=True)
        @pl.when((n<=6)|(n==8))
        def _(): gs.step1(3+n-n//8)
        @pl.when((n<=7)|(n==9))
        def _(): gs.step2(2+n-n//9)
        @pl.when((n<=8)|(n==10))
        def _(): gs.step3(1+n-n//10)
        @pl.when(n>=1)
        def _(): gs.step4(n-1)
        @pl.when(n>=2)
        def _(): gs.step5(n-2)
        @pl.when((n==3)|(n==7))
        def _(): gs.step0(9+n//7)
        return carry
    vcur[...]=vec_ref[...]
    lax.fori_loop(0,12,slot,0)
    gs.step0(11)
    for i in range(3): loads[f"w{i}"].wait()
    def grad_tile(t):
        rows=pl.ds(t*256,256)
        a=acc[rows,:]
        for d,w in zip((q,k,v),wdst): a=a+dot(d[rows,:],w[...],1,1)
        acc[rows,:]=a
    grad_tile(0)
    gs.step5(10); gs.step1(11)
    grad_tile(1); grad_tile(2)
    gs.step2(11); grad_tile(3)
    away=pltpu.make_async_copy(acc,ig_o,lsem.at[31]); away.start()
    gs.step3(11)
    gs.step4(11)
    gs.step5(11)
    lax.fori_loop(0,NGR,lambda g,c: (gs.done(g),c)[1],0)
    away.wait()
    stats.done()
    @pl.when(pc.xy<3)
    def _(): pltpu.make_async_copy(gown_ref,gown_ref,orr).wait()

def call_back(x,qa,ka,v,ctx,dctx,act,din,dffn,hlow,dz1,wq,vec,right):
    V=pltpu.VMEM; S=jax.ShapeDtypeStruct; A=pl.ANY
    B=lambda m: pl.BlockSpec(memory_space=m)
    sem=pltpu.SemaphoreType.DMA
    T=V((PACK,D),bf16); H=V((2,PACK,128),bf16)
    return pl.pallas_call(back_body,
        in_specs=[B(V)]+[B(A)]*11+[B(V),B(A)],
        out_specs=[B(A),B(V),B(V),B(A),B(A)],
        out_shape=[S((PACK,D),f32),S((NB,24,D),f32),S((16,D),f32),S((16,MR,HC),bf16),S((32,24,D),f32)],
        scratch_shapes=list(sum_scratch().values())+[V((NGR,4,4,MR,D),bf16),T,V((D,D),bf16)]+[V((2,PACK,D),bf16),V((2,PACK,D),bf16),T,T,V((PACK,D),f32)]+[V((2,2,PACK,128),bf16),H,V((2,2,PACK,128),bf16),H]+
            [V((PACK,128),f32),sem((NGR,10)),sem((NGR,10)),sem((NGR,3)),sem,sem((NB,)),sem,sem((32,)),sem((2,2))],
        compiler_params=pltpu.CompilerParams(vmem_limit_bytes=63<<20,collective_id=1,has_side_effects=True))(x,qa,ka,v,ctx,dctx,act,din,dffn,hlow,dz1,wq,vec,right)


def gather_rows(a):
    return lax.all_gather(a,("dp","head"),axis=1,tiled=True)

def doc_lengths(lengths):
    return lax.dynamic_slice_in_dim(lengths,lax.axis_index("head"),1,axis=0)

def layer(tokens,cotangent,lengths,w,params):
    q,k,v,ctx,lse,n1,r1=call_a(lengths,tokens,w,params)
    out,dz1,dctx,dwo,dw1,dw2,vec=call_b(cotangent,n1,r1,ctx,w,params)
    ig,dwqkv,vq=call_c(lengths,tokens,q,k,v,ctx,dctx,lse,dz1,w)
    terms=jnp.concatenate([dwqkv,dwo[None],dw1,dw2],axis=0)
    vec=jnp.concatenate([vq[0:1],vq[2:3],vec[2:]],axis=0)
    return out,ig,terms,vec

def on_slice(tokens,cotangent,lengths,masters,vectors,left,right,second):
    pv=jnp.pad(vectors,((0,4),(0,HC-24))).astype(bf16)
    lens=doc_lengths(lengths)
    out,qa,ka,v,ctx,act,din,dffn,hlow,dz1,dctx,wq,vec,statl=call_front(lens,tokens,cotangent,masters,pv,left)
    ig,grads,vec,gown,statr=call_back(tokens,qa,ka,v,ctx,dctx,act,din,dffn,hlow,dz1,wq.reshape(3,D,D),vec,right)
    ln,rn,mn,vg,sn,vn=call_newton_step(gown.reshape(D,HC),statl.reshape(D,D),statr.reshape(D,D),left,right,masters,vec,vectors,second)
    return out,ig,grads,ln,rn,mn,vg,sn,vn

def on_any(tokens,cotangent,lengths,masters,vectors,left,right,second):
    axes=("dp","head")
    me=lax.axis_index("dp")*lax.axis_size("head")+lax.axis_index("head")
    share=masters.shape[1]
    w=gather_rows(masters.astype(bf16))
    params=gather_rows(vectors.astype(bf16)).astype(f32)
    out,ig,terms,vec=layer(tokens,cotangent,doc_lengths(lengths),w,params)
    grads=lax.psum_scatter(terms.astype(f32),axes,scatter_dimension=1,tiled=True)
    vg=lax.psum_scatter(vec[:12],axes,scatter_dimension=1,tiled=True)
    low=grads.astype(bf16)
    g=gather_rows(low)
    ein=partial(jnp.einsum,preferred_element_type=f32)
    cols=lax.dynamic_slice_in_dim(g,me*share,share,axis=2)
    ln=BETA*left+(1-BETA)*ein("kid,kjd->kij",low,g)
    rn=BETA*right+(1-BETA)*ein("kdi,kdj->kij",cols,g)
    item=jnp.minimum(me,2*NB-1)
    own=lax.dynamic_index_in_dim(jnp.concatenate([gather_rows(ln),gather_rows(rn)],axis=0),item,0,keepdims=False)
    root=call_newton(own)
    place=jnp.where((jnp.arange(2*NB)==me)[:,None,None],root[None],0.0)
    rows=lax.psum_scatter(place,axes,scatter_dimension=1,tiled=True)
    rr=gather_rows(rows[NB:])
    hi=partial(jnp.einsum,"kij,kjl->kil",precision=lax.Precision.HIGHEST)
    mn=masters-RATE*hi(hi(rows[:NB],g.astype(f32)),rr)
    sn=BETA_TWO*second+(1-BETA_TWO)*vg*vg
    vn=vectors-RATE_VEC*vg/(jnp.sqrt(sn)+1e-8)
    return out,ig,grads,ln,rn,mn,vg,sn,vn

def solution(mesh):
    rows=P(("dp","head"),None); blocks=P(None,("dp","head"),None); vecs=P(None,("dp","head"))
    on_device=on_slice if dict(mesh.shape)=={"dp":8,"head":4} else on_any
    return jax.shard_map(on_device,mesh=mesh,
        in_specs=(rows,rows,P("dp",None),blocks,vecs,blocks,blocks,vecs),
        out_specs=(rows,rows,blocks,blocks,blocks,blocks,vecs,vecs,vecs),check_vma=False)
```

```python
import jax, jax.numpy as jnp, numpy as np
from functools import partial
from jax import lax
from jax.experimental import pallas as pl
from jax.experimental.pallas import tpu as pltpu
from jax.sharding import PartitionSpec as P

D=768; HEADS=12; HD=64; FF=3072; PACK=1024; NEWTON=8; NB=12
NORM_EPS=1e-6
f32=jnp.float32; bf16=jnp.bfloat16
BIG=1e30
QB=256
def dot(a,b,ca=1,cb=0):
    return lax.dot_general(a,b,(((ca,),(cb,)),((),())),preferred_element_type=f32)

def doc_column(len_ref, shape, dim):
    t=lax.broadcasted_iota(jnp.int32,shape,dim)
    end=jnp.int32(0); doc=jnp.zeros(shape,jnp.int32)
    for j in range(8):
        end=end+len_ref[0,j]
        doc=doc+(t>=end).astype(jnp.int32)
    return doc

def split3(v):
    a=v.astype(bf16).astype(f32); r=v-a
    b=r.astype(bf16).astype(f32); c=r-b
    return a,b,c

def augment(base, lane, head_lo, cols):
    keep=(lane<64) if head_lo else (lane>=64)
    off=64 if head_lo else 0
    out=jnp.where(keep, base, 0.0)
    for i,c in enumerate(cols):
        out=jnp.where(lane==off+i, c, out)
    return out.astype(bf16)

def onehot_part(base, lane, head_lo, doc, minus, scale):
    keep=(lane<64) if head_lo else (lane>=64)
    off=64 if head_lo else 0
    l=lane-off
    oh=jnp.where((l>=0)&(l<8), (jnp.where(l==doc,1.0,0.0)-minus)*scale, 0.0)
    return jnp.where(keep, base, oh)

def attn_fwd_pair(p, q_ref,k_ref,v_ref, ctx_ref, lse_ref, doc):
    cols=pl.ds(pl.multiple_of(p*128,128),128)
    lane=lax.broadcasted_iota(jnp.int32,(PACK,128),1)
    kp=k_ref[:,cols].astype(f32)
    vp=v_ref[:,cols]
    kk=[onehot_part(kp,lane,lo,doc,1.0,1.0).astype(bf16) for lo in (True,False)]
    laneb=lax.broadcasted_iota(jnp.int32,(QB,128),1)
    for b in range(PACK//QB):
        rows=pl.ds(b*QB,QB)
        qp=q_ref[rows,cols].astype(f32)*0.125
        docb=doc[b*QB:(b+1)*QB]
        outs=[]
        lse_old=lse_ref[rows,:]
        for h,lo in enumerate((True,False)):
            qa=onehot_part(qp,laneb,lo,docb,0.0,BIG).astype(bf16)
            s=dot(qa,kk[h],1,1)
            m=jnp.max(s,axis=1,keepdims=True)
            e=jnp.exp(s-m)
            l=jnp.sum(e,axis=1,keepdims=True)
            o=dot(e.astype(bf16),vp)
            outs.append(o/l)
            lse_old=jnp.where(laneb==2*p+h, m+jnp.log(l), lse_old)
        lse_ref[rows,:]=lse_old
        ctx_ref[rows,cols]=jnp.where(laneb<64,outs[0],outs[1]).astype(bf16)

def layer_norm(z):
    mu=jnp.mean(z,axis=-1,keepdims=True)
    c=z-mu
    r=lax.rsqrt(jnp.mean(c*c,axis=-1,keepdims=True)+NORM_EPS)
    return c*r, r

def ka_body(len_ref,x_ref,wa_ref,p_ref,q_ref,k_ref,v_ref,ctx_ref,lse_ref,hid_ref,r1_ref,w_ref):
    pltpu.sync_copy(wa_ref.at[pl.ds(0,4)],w_ref)
    doc=doc_column(len_ref,(PACK,1),0)
    for i,(o,b) in enumerate(((q_ref,0),(k_ref,None),(v_ref,1))):
        for t in range(4):
            rows=pl.ds(t*256,256)
            y=dot(x_ref[rows,:],w_ref[i])
            if b is not None: y=y+p_ref[b:b+1,:]
            o[rows,:]=y.astype(bf16)
    def body(p,c):
        attn_fwd_pair(p,q_ref,k_ref,v_ref,ctx_ref,lse_ref,doc)
        return c
    lax.fori_loop(0,6,body,0)
    for t in range(4):
        rows=pl.ds(t*256,256)
        z=x_ref[rows,:].astype(f32)+(dot(ctx_ref[rows,:],w_ref[3])+p_ref[2:3,:])
        n,r=layer_norm(z)
        hid_ref[rows,:]=n
        r1_ref[rows,:]=jnp.broadcast_to(r,(256,128))

def call_a(lengths,x,w,params):
    V=pltpu.VMEM
    return pl.pallas_call(ka_body,
        in_specs=[pl.BlockSpec(memory_space=pltpu.SMEM),pl.BlockSpec(memory_space=V),pl.BlockSpec(memory_space=pl.ANY),pl.BlockSpec(memory_space=V)],
        out_specs=[pl.BlockSpec(memory_space=V)]*7,
        out_shape=[jax.ShapeDtypeStruct((PACK,D),bf16)]*4+[jax.ShapeDtypeStruct((PACK,128),f32),jax.ShapeDtypeStruct((PACK,D),f32),jax.ShapeDtypeStruct((PACK,128),f32)],
        scratch_shapes=[V((4,D,D),bf16)],
        compiler_params=pltpu.CompilerParams(vmem_limit_bytes=60<<20))(lengths,x,w,params)

def gelu_both(x):
    z=jnp.abs(x)*0.7071067811865476
    t=1.0/(1.0+0.3275911*z)
    e=jnp.exp(-0.5*x*x)
    poly=t*(0.254829592+t*(-0.284496736+t*(1.421413741+t*(-1.453152027+t*1.061405429))))
    half=0.5*poly*e
    phi_c=jnp.where(x>=0,1.0-half,half)
    return x*phi_c, phi_c+x*(e*0.3989422804014327)

def kb_body(cot_ref,n1_ref,r1_ref,ctx_ref,w_ref,p_ref, out_ref,dz1_ref,dctx_ref,dwo_ref,dw1_ref,dw2_ref,vec_ref, act_ref,gp_ref,dffn_ref,hlow_ref):
    TT=256
    g1,s1,g2,s2=(p_ref[i:i+1,:] for i in (8,9,10,11))
    b2=p_ref[7:8,:]
    vec_ref[...]=jnp.zeros_like(vec_ref)
    def tile(t,carry):
        rows=pl.ds(pl.multiple_of(t*TT,TT),TT)
        n1=n1_ref[rows,:]
        hid=n1*g1+s1
        hl=hid.astype(bf16)
        hlow_ref[rows,:]=hl
        ffn=None
        for c in range(4):
            inner=dot(hl,w_ref[4+c])+p_ref[3+c:4+c,:]
            a,gp=gelu_both(inner)
            al=a.astype(bf16)
            act_ref[rows,pl.ds(c*D,D)]=al
            gp_ref[rows,pl.ds(c*D,D)]=gp.astype(gp_ref.dtype)
            y=dot(al,w_ref[8+c])
            ffn=y if ffn is None else ffn+y
        z=hid+(ffn+b2)
        n2,r2=layer_norm(z)
        out_ref[rows,:]=(n2*g2+s2).astype(bf16)
        e=cot_ref[rows,:].astype(f32)
        c2=e*g2
        dz2=r2*(c2-jnp.mean(c2,axis=-1,keepdims=True)-n2*jnp.mean(c2*n2,axis=-1,keepdims=True))
        dffn=dz2.astype(bf16)
        dffn_ref[rows,:]=dffn
        vec_ref[10:11,:]+=jnp.sum(e*n2,axis=0,keepdims=True)
        vec_ref[11:12,:]+=jnp.sum(e,axis=0,keepdims=True)
        vec_ref[7:8,:]+=jnp.sum(dffn.astype(f32),axis=0,keepdims=True)
        dh=dz2
        for c in range(4):
            dact=dot(dffn,w_ref[8+c],1,1)
            din=(dact*gp_ref[rows,pl.ds(c*D,D)].astype(f32)).astype(bf16)
            gp_ref[rows,pl.ds(c*D,D)]=din.astype(gp_ref.dtype)
            vec_ref[3+c:4+c,:]+=jnp.sum(din.astype(f32),axis=0,keepdims=True)
            dh=dh+dot(din,w_ref[4+c],1,1)
        vec_ref[8:9,:]+=jnp.sum(dh*n1,axis=0,keepdims=True)
        vec_ref[9:10,:]+=jnp.sum(dh,axis=0,keepdims=True)
        c1=dh*g1
        dz1=r1_ref[rows,0:1]*(c1-jnp.mean(c1,axis=-1,keepdims=True)-n1*jnp.mean(c1*n1,axis=-1,keepdims=True))
        dz1_ref[rows,:]=dz1
        dat=dz1.astype(bf16)
        vec_ref[2:3,:]+=jnp.sum(dat.astype(f32),axis=0,keepdims=True)
        dctx_ref[rows,:]=dot(dat,w_ref[3],1,1).astype(bf16)
        return carry
    lax.fori_loop(0,PACK//TT,tile,0)
    for c in range(4):
        dw2_ref[c]=dot(act_ref[:,c*D:(c+1)*D],dffn_ref[...],0,0).astype(bf16)
        dw1_ref[c]=dot(hlow_ref[...],gp_ref[:,c*D:(c+1)*D].astype(bf16),0,0).astype(bf16)
    dwo_ref[...]=dot(ctx_ref[...],dz1_ref[...].astype(bf16),0,0).astype(bf16)

def call_b(cot,n1,r1,ctx,w,params):
    V=pltpu.VMEM
    S=jax.ShapeDtypeStruct
    return pl.pallas_call(kb_body,
        in_specs=[pl.BlockSpec(memory_space=V)]*6,
        out_specs=[pl.BlockSpec(memory_space=V)]*7,
        out_shape=[S((PACK,D),bf16),S((PACK,D),f32),S((PACK,D),bf16),S((D,D),bf16),S((4,D,D),bf16),S((4,D,D),bf16),S((16,D),f32)],
        scratch_shapes=[V((PACK,FF),bf16),V((PACK,FF),bf16),V((PACK,D),bf16),V((PACK,D),bf16)],
        compiler_params=pltpu.CompilerParams(vmem_limit_bytes=62<<20))(cot,n1,r1,ctx,w,params)

def kc_body(len_ref,x_ref,q_ref,k_ref,v_ref,ctx_ref,do_ref,lse_ref,dz1_ref,wa_ref, ig_ref,dw_ref,vec_ref, dqkv_ref, dqa_ref,w_ref):
    pltpu.sync_copy(wa_ref.at[pl.ds(0,3)],w_ref)
    doc=doc_column(len_ref,(PACK,1),0)
    lane=lax.broadcasted_iota(jnp.int32,(PACK,128),1)
    KB_=256
    def pair(p,carry):
        cols=pl.ds(pl.multiple_of(p*128,128),128)
        qp=q_ref[:,cols].astype(f32); kp=k_ref[:,cols].astype(f32); vp=v_ref[:,cols].astype(f32)
        dop=do_ref[:,cols].astype(f32); cp=ctx_ref[:,cols].astype(f32)
        prod=dop*cp
        qa=[];qm=[];doa=[];dom=[];ka=[];km=[];va=[]
        for h,lo in enumerate((True,False)):
            keep=(lane<64) if lo else (lane>=64)
            off=64 if lo else 0
            lse=jnp.sum(jnp.where(lane==2*p+h,lse_ref[...],0.0),axis=1,keepdims=True)
            dd=jnp.sum(jnp.where(keep,prod,0.0),axis=1,keepdims=True)
            q1=onehot_part(qp*0.125,lane,lo,doc,0.0,BIG)
            for i,c in enumerate(split3(-lse)): q1=jnp.where(lane==off+8+i,c,q1)
            qa.append(q1.astype(bf16)); qm.append(jnp.where(keep,qp*0.125,0.0).astype(bf16))
            k1=onehot_part(kp,lane,lo,doc,1.0,1.0)
            k1=jnp.where((lane>=off+8)&(lane<off+11),1.0,k1)
            ka.append(k1.astype(bf16)); km.append(jnp.where(keep,kp*0.125,0.0).astype(bf16))
            d1=jnp.where(keep,dop,0.0)
            dom.append(d1.astype(bf16))
            for i,c in enumerate(split3(-dd)): d1=jnp.where(lane==off+i,c,d1)
            doa.append(d1.astype(bf16))
            v1=jnp.where(keep,vp,0.0); v1=jnp.where((lane>=off)&(lane<off+3),1.0,v1)
            va.append(v1.astype(bf16))
        for b in range(PACK//KB_):
            rows=slice(b*KB_,(b+1)*KB_)
            dv=None;dk=None;dq=None
            for h in range(2):
                s=dot(ka[h][rows],qa[h],1,1)
                pr=jnp.exp(s)
                dp=dot(va[h][rows],doa[h],1,1)
                ds=(pr*dp).astype(bf16)
                a=dot(pr.astype(bf16),dom[h]); dv=a if dv is None else dv+a
                a=dot(ds,qm[h]); dk=a if dk is None else dk+a
                a=dot(ds,km[h][rows],0,0); dq=a if dq is None else dq+a
            if b==0: dqa_ref[...]=dq
            else: dqa_ref[...]+=dq
            dqkv_ref[1,rows,cols]=dk.astype(bf16)
            dqkv_ref[2,rows,cols]=dv.astype(bf16)
        dqkv_ref[0,:,cols]=dqa_ref[...].astype(bf16)
        for i in range(3):
            d=dqkv_ref[i,:,cols]
            dw_ref[i,:,cols]=dot(x_ref[...],d,0,0).astype(bf16)
            vec_ref[i:i+1,cols]=jnp.sum(d.astype(f32),axis=0,keepdims=True)
        return carry
    lax.fori_loop(0,6,pair,0)
    for t in range(4):
        rows=pl.ds(t*256,256)
        acc=dz1_ref[rows,:]
        for i in range(3):
            acc=acc+dot(dqkv_ref[i,rows,:],w_ref[i],1,1)
        ig_ref[rows,:]=acc

def call_c(lengths,x,q,k,v,ctx,do,lse,dz1,w):
    V=pltpu.VMEM; S=jax.ShapeDtypeStruct
    return pl.pallas_call(kc_body,
        in_specs=[pl.BlockSpec(memory_space=pltpu.SMEM)]+[pl.BlockSpec(memory_space=V)]*8+[pl.BlockSpec(memory_space=pl.ANY)],
        out_specs=[pl.BlockSpec(memory_space=V)]*3,
        out_shape=[S((PACK,D),f32),S((3,D,D),bf16),S((8,D),f32)],
        scratch_shapes=[V((3,PACK,D),bf16),V((PACK,128),f32),V((3,D,D),bf16)],
        compiler_params=pltpu.CompilerParams(vmem_limit_bytes=62<<20))(lengths,x,q,k,v,ctx,do,lse,dz1,w)

RB=256
def diag_sum(blk):
    i=lax.broadcasted_iota(jnp.int32,blk.shape,0); j=lax.broadcasted_iota(jnp.int32,blk.shape,1)
    return jnp.sum(jnp.where(i==j,blk,0.0),keepdims=True)
def eye_rows(rb):
    i=lax.broadcasted_iota(jnp.int32,(RB,D),0)+rb*RB; j=lax.broadcasted_iota(jnp.int32,(RB,D),1)
    return i==j
def newton(m_ref,x_ref,nb_ref,pb_ref,sb_ref,xb_ref,between=lambda k: None):
    nblk=D//RB
    R=[slice(i*RB,(i+1)*RB) for i in range(nblk)]
    tot=jnp.zeros((1,1),f32); tr=jnp.zeros((1,1),f32)
    for i in range(nblk):
        blk=m_ref[R[i],:]
        tot=tot+jnp.sum(blk*blk,keepdims=True)
        tr=tr+diag_sum(blk[:,R[i]])
    c=jnp.sqrt(tot+1e-6)
    inv=1.0/c
    al=tr*inv/D
    s=lax.rsqrt(jnp.sqrt(c))
    for i in range(nblk):
        m_ref[R[i],:]=m_ref[R[i],:]*inv
    def iteration(k,al,be,first=False,last=False):
        u=5-al
        u2=u*u;u3=u2*u;u4=u2*u2
        c0=al*u4*(1/256); c1=(u4-4*al*u3)*(1/256); c2=(12*al*u2-8*u3)*(1/512)
        c3=(36*u2-24*al*u)*(1/1536); c4=(24*al-96*u)*(1/6144); c5=1/256
        for i in range(nblk):
            nb_ref[R[i],:]=jnp.where(eye_rows(i),m_ref[R[i],:]-al,m_ref[R[i],:]).astype(bf16)
            if not first: xb_ref[R[i],:]=jnp.where(eye_rows(i),x_ref[R[i],:]-be,x_ref[R[i],:]).astype(bf16)
        be2=jnp.zeros((1,1),f32); al2=jnp.zeros((1,1),f32)
        for i in range(nblk):
            n=jnp.where(eye_rows(i),m_ref[R[i],:]-al,m_ref[R[i],:])
            if not last:
                p=dot(nb_ref[R[i],:],nb_ref[...])
                pb_ref[R[i],:]=p.astype(bf16)
                m=c1*n+c2*p
                m_ref[R[i],:]=jnp.where(eye_rows(i),m+c0,m)
            if first:
                x=jnp.where(eye_rows(i),1.25-al*0.25,0.0)-0.25*n
            else:
                x=(1.25-al*0.25)*x_ref[R[i],:]-0.25*(be*n+dot(xb_ref[R[i],:],nb_ref[...]))
            x_ref[R[i],:]=x
            be2=be2+diag_sum(x[:,R[i]])
        if not last:
            for i in range(nblk):
                q=dot(nb_ref[R[i],:],pb_ref[...])
                sb_ref[R[i],:]=(c3*nb_ref[R[i],:].astype(f32)+c4*pb_ref[R[i],:].astype(f32)+c5*q).astype(bf16)
            for i in range(nblk):
                m=m_ref[R[i],:]+dot(pb_ref[R[i],:],sb_ref[...])
                m_ref[R[i],:]=m
                al2=al2+diag_sum(m[:,R[i]])
        return al2*(1/D),be2*(1/D)
    al,be=iteration(0,al,None,first=True)
    def step(k,ab):
        ab=iteration(k,*ab)
        between(k)
        return ab
    al,be=lax.fori_loop(1,7,step,(al,be))
    iteration(7,al,be,last=True)
    for i in range(nblk):
        x_ref[R[i],:]=x_ref[R[i],:]*s
def body(a_ref,x_ref,m_ref,nb,pb,sb,xb):
    m_ref[...]=a_ref[...]
    newton(m_ref,x_ref,nb,pb,sb,xb)
def call_newton(a):
    V=pltpu.VMEM
    return pl.pallas_call(body,in_specs=[pl.BlockSpec(memory_space=V)],out_specs=pl.BlockSpec(memory_space=V),
      out_shape=jax.ShapeDtypeStruct((D,D),f32),scratch_shapes=[V((D,D),f32)]+[V((D,D),bf16)]*4,
      compiler_params=pltpu.CompilerParams(vmem_limit_bytes=60<<20))(a)

NZ=4; MR=48; HC=384
MESH=pl.DeviceIdType.MESH
def rcopy(src,dst,ss,rs,dev):
    return pltpu.make_async_remote_copy(src_ref=src,dst_ref=dst,send_sem=ss,recv_sem=rs,device_id=dev,device_id_type=MESH)

class Place:
    def __init__(self):
        self.dp=lax.axis_index("dp"); self.head=lax.axis_index("head")
        self.z=self.dp//2; self.x=self.dp%2; self.y=self.head//2; self.c=self.head%2
        self.xy=self.x*2+self.y
        self.chip=self.z*4+self.xy
        self.me=self.dp*4+self.head
        self.xn=((self.dp//2)*2+(1-self.x), self.head)
        self.yn=(self.dp,(1-self.y)*2+self.c)
        self.sib=(self.dp,self.y*2+(1-self.c))
        self.cols=pl.ds(pl.multiple_of(self.c*HC,128),HC)
        self.ocols=pl.ds(pl.multiple_of((1-self.c)*HC,128),HC)
    def zpeer(self,k):
        return (((self.z+k)%NZ)*2+self.x,self.head)
    def zfrom(self,k):
        return (self.z+NZ-k)%NZ
    def neighbours(self):
        return [self.zpeer(1),self.zpeer(2),self.zpeer(3),self.xn,self.yn,self.sib]

def greet(devs):
    bar=pltpu.get_barrier_semaphore()
    for d in devs:
        pl.semaphore_signal(bar,inc=1,device_id=d,device_id_type=MESH)
    pl.semaphore_wait(bar,len(devs))

def greet_all(pc):
    bar=pltpu.get_barrier_semaphore()
    def sig(k,carry):
        t=(pc.me+k)%32
        pl.semaphore_signal(bar,inc=1,device_id=(t//4,t%4),device_id_type=MESH)
        return carry
    lax.fori_loop(1,32,sig,0)
    pl.semaphore_wait(bar,31)

class Gather:
    def __init__(self,pc,at,ss,rs,whole=False):
        self.pc,self.at,self.ss,self.rs,self.whole=pc,at,ss,rs,whole
    def region(self,z,xy,mine=True):
        pc=self.pc
        return self.at(z,xy,pc.cols if mine else pc.ocols)
    def copies(self):
        pc=self.pc; al=pl.ds(0,4); lo=pl.ds(0,2); hi=pl.ds(2,2)
        xo=(1-pc.x)*2+pc.y; yo=pc.x*2+(1-pc.y); dg=(1-pc.x)*2+(1-pc.y)
        R=self.region
        def mk(i,src,dst,dev):
            return rcopy(src(),dst(),self.ss.at[i],self.rs.at[i],dev)
        send={}; recv={}
        for k in (1,2,3):
            send[k-1]=(partial(R,pc.z,pc.xy),pc.zpeer(k)); recv[k-1]=partial(R,pc.zfrom(k),pc.xy)
        send[3]=(partial(R,al,pc.xy),pc.xn); send[4]=(partial(R,al,pc.xy),pc.yn)
        send[5]=(partial(R,hi,yo),pc.xn); send[6]=(partial(R,lo,xo),pc.yn)
        recv[3]=partial(R,al,xo); recv[4]=partial(R,al,yo); recv[5]=partial(R,hi,dg); recv[6]=partial(R,lo,dg)
        if self.whole:
            send[7]=(partial(R,al,al),pc.sib); recv[7]=partial(R,al,al,False)
        else:
            for i,xy in ((7,pc.xy),(8,xo),(9,yo),(10,dg)):
                send[i]=(partial(R,al,xy),pc.sib); recv[i]=partial(R,al,xy,False)
        self.send={i:partial(mk,i,s,s,d) for i,(s,d) in send.items()}
        self.recv={i:partial(mk,i,s,s,pc.sib) for i,s in recv.items()}
        return self
    def start(self,*which):
        for i in which:
            if i in self.send and not (self.whole and i>6): self.send[i]().start()
    def step0(self): self.start(0,1,2)
    def step1(self):
        for i in (0,1,2): self.recv[i]().wait_recv()
        self.start(3,4,7)
    def step2(self):
        self.recv[3]().wait_recv()
        self.start(6,8)
        self.recv[4]().wait_recv()
        self.start(5,9)
    def step3(self):
        for i in (5,6): self.recv[i]().wait_recv()
        if self.whole: self.send[7]().start()
        else: self.start(10)
    def step4(self):
        for i in self.recv:
            if i>6: self.recv[i]().wait_recv()
    def done(self):
        for i in self.send: self.send[i]().wait_send()
    def step(self,i):
        (self.step0,self.step1,self.step2,self.step3,self.step4)[i]()

ORDER=(0,1,2,3,4,8,5,9,6,10,7,11)
def ag_body(mas_ref,pv_ref,left_ref,right_ref, w_ref,pg_ref,st_ref, sibm,ss,rs,cs,cr,ts,tr,lsem):
    pc=Place()
    greet_all(pc)
    half=rcopy(mas_ref.at[:,:,pc.ocols],sibm,cs,cr,pc.sib)
    half.start()
    def stat(b,act):
        t=(b%4)*4+b//4
        for side,ref in enumerate((left_ref,right_ref)):
            dev=((t//2),(t%2)*2+side)
            idx=b*2+side
            mine=(pc.chip==t)&(pc.c==side)
            act(idx,ref.at[b],dev,mine)
    half.wait_recv()
    lo=pl.ds(0,24); hi=pl.ds(24,24)
    for b in ORDER:
        own=mas_ref[b,:,pc.cols]; oth=sibm[b]
        first=jnp.where(pc.c==0,own,oth); second=jnp.where(pc.c==0,oth,own)
        w_ref[b,pc.z,pc.xy,:,pc.cols]=jnp.concatenate([first,second],axis=0).astype(bf16)
    pg_ref[pc.z,pc.xy,:,pc.cols]=pv_ref[...]
    half.wait_send()
    gs=[]
    for t in range(len(gs)+4):
        for s in range(5):
            if 0<=t-s<len(gs): gs[t-s].step(s)
    def start(b,carry):
        def act(idx,src,dev,mine):
            @pl.when(mine)
            def _(): pltpu.make_async_copy(src,st_ref.at[pc.me],tr).start()
            @pl.when(jnp.logical_not(mine))
            def _(): rcopy(src,st_ref.at[pc.me],ts.at[idx],tr,dev).start()
        stat(b,act)
        return carry
    lax.fori_loop(0,NB,start,0)
    for g in gs: g.done()
    def fin(b,carry):
        def act(idx,src,dev,mine):
            @pl.when(jnp.logical_not(mine))
            def _(): rcopy(src,st_ref.at[pc.me],ts.at[idx],tr,dev).wait_send()
        stat(b,act)
        return carry
    lax.fori_loop(0,NB,fin,0)
    @pl.when(pc.xy<3)
    def _(): pltpu.make_async_copy(st_ref,st_ref,tr).wait()

def call_ag(masters,pv,left,right):
    V=pltpu.VMEM; S=jax.ShapeDtypeStruct; A=pl.ANY
    B=lambda m: pl.BlockSpec(memory_space=m)
    sem=pltpu.SemaphoreType.DMA
    return pl.pallas_call(ag_body,in_specs=[B(V),B(V),B(A),B(A)],out_specs=[B(V),B(V),B(A)],
        out_shape=[S((NB,4,4,MR,D),bf16),S((4,4,16,D),bf16),S((32,24,D),f32)],
        scratch_shapes=[V((NB,24,HC),f32),sem((13,11)),sem((13,11)),sem,sem,sem((24,)),sem,sem],
        compiler_params=pltpu.CompilerParams(vmem_limit_bytes=60<<20,collective_id=0,has_side_effects=True))(masters,pv,left,right)

def params_of(pg):
    t=pg.reshape(16,16,2,HC)[:,:12,:,:24]
    return jnp.transpose(t,(1,0,2,3)).reshape(12,D).astype(f32)


class Scatter:
    def __init__(self,pc,b,g_ref,R,out_ref,gown_ref,ss,rs,os_,orr):
        self.pc,self.b,self.g=pc,b,g_ref.at[b]
        self.out,self.gown=out_ref,gown_ref
        self.os_,self.orr=os_,orr
        self.R={k:v.at[b] for k,v in R.items()}
        R=self.R
        s1,rc=R["s1"],R["rc"]
        def mk(i,src,dst,dev): return rcopy(src,dst,ss.at[b,i],rs.at[b,i],dev)
        lo=pl.ds(0,2); hi=pl.ds(2,2); al=pl.ds(0,4)
        self.core=mk(0,self.g.at[:,:,:,pc.ocols],rc,pc.sib)
        self.xa=mk(1,s1.at[lo,pl.ds((1-pc.x)*2,2)],R["xa"],pc.xn)
        self.yb=[mk(2+i,s1.at[hi,i*2+1-pc.y],R["yb"].at[i],pc.yn) for i in range(2)]
        self.ya=mk(4,R["s2a"],R["ya"],pc.yn)
        self.xb=mk(5,R["s2b"],R["xb"],pc.xn)
        self.zz=[mk(6+k-1,R["s3"].at[(pc.z+k)%NZ],R["zr"].at[k-1],pc.zpeer(k)) for k in (1,2,3)]
        self.home=mk(9,R["fin"].at[pl.ds(pl.multiple_of((1-pc.c)*24,8),24)],R["hr"],pc.sib)
        t=(b%4)*4+b//4
        self.t=t
        self.owner=[((t//2),(t%2)*2+side) for side in range(2)]
        self.to_owner=[rcopy(R["finb"],gown_ref.at[pc.chip,:,pc.cols],os_.at[b,side],orr,self.owner[side]) for side in range(2)]
        self.to_self=pltpu.make_async_copy(R["finb"],gown_ref.at[pc.chip,:,pc.cols],orr)
    def step0(self):
        self.core.start()
    def step1(self):
        pc=self.pc; R=self.R
        self.core.wait_recv()
        for z in range(4):
            R["s1"][z]=(self.g[z,:,:,pc.cols].astype(f32)+R["rc"][z].astype(f32)).astype(bf16)
        self.xa.start()
        for d in self.yb: d.start()
    def step2(self):
        pc=self.pc; R=self.R
        self.xa.wait_recv()
        s=R["s1"][0:2,pl.ds(pc.x*2,2)].astype(f32)+R["xa"][...].astype(f32)
        keep=jnp.where(pc.y==0,s[:,0],s[:,1]); give=jnp.where(pc.y==0,s[:,1],s[:,0])
        R["k2"][0:2]=keep; R["s2a"][...]=give.astype(bf16)
        self.ya.start()
        for d in self.yb: d.wait_recv()
        s0=R["s1"][2:4,pc.y].astype(f32)+R["yb"][0].astype(f32)
        s1=R["s1"][2:4,2+pc.y].astype(f32)+R["yb"][1].astype(f32)
        keep=jnp.where(pc.x==0,s0,s1); give=jnp.where(pc.x==0,s1,s0)
        R["k2"][2:4]=keep; R["s2b"][...]=give.astype(bf16)
        self.xb.start()
    def step3(self):
        R=self.R
        self.ya.wait_recv(); self.xb.wait_recv()
        a=R["k2"][0:2]+R["ya"][...].astype(f32)
        b=R["k2"][2:4]+R["xb"][...].astype(f32)
        R["k2"][0:2]=a; R["k2"][2:4]=b
        R["s3"][0:2]=a.astype(bf16); R["s3"][2:4]=b.astype(bf16)
        for d in self.zz: d.start()
    def step4(self):
        pc=self.pc; R=self.R
        for d in self.zz: d.wait_recv()
        s=R["k2"][pc.z]
        for k in range(3): s=s+R["zr"][k].astype(f32)
        R["fin"][...]=s
        R["finb"][...]=s.astype(bf16)
        self.home.start()
        @pl.when(pc.chip==self.t)
        def _():
            self.to_self.start()
            for side in range(2):
                @pl.when(pc.c!=side)
                def _(): self.to_owner[side].start()
        @pl.when(pc.chip!=self.t)
        def _():
            for d in self.to_owner: d.start()
    def step5(self):
        pc=self.pc; R=self.R
        self.home.wait_recv()
        own=R["fin"][pl.ds(pl.multiple_of(pc.c*24,8),24)]; oth=R["hr"][...]
        self.out[self.b,:,pc.cols]=own
        self.out[self.b,:,pc.ocols]=oth
    def step(self,i): (self.step0,self.step1,self.step2,self.step3,self.step4,self.step5)[i]()
    def done(self):
        pc=self.pc
        for d in [self.core,self.xa,*self.yb,self.ya,self.xb,*self.zz,self.home]: d.wait_send()
        @pl.when(pc.chip==self.t)
        def _():
            for side in range(2):
                @pl.when(pc.c!=side)
                def _(): self.to_owner[side].wait_send()
        @pl.when(pc.chip!=self.t)
        def _():
            for d in self.to_owner: d.wait_send()

def scatter_scratch(nb=NB):
    V=pltpu.VMEM
    return dict(s1=V((nb,4,4,MR,HC),bf16),rc=V((nb,4,4,MR,HC),bf16),xa=V((nb,2,2,MR,HC),bf16),yb=V((nb,2,2,MR,HC),bf16),
        s2a=V((nb,2,MR,HC),bf16),s2b=V((nb,2,MR,HC),bf16),ya=V((nb,2,MR,HC),bf16),xb=V((nb,2,MR,HC),bf16),
        k2=V((nb,4,MR,HC),f32),s3=V((nb,4,MR,HC),bf16),zr=V((nb,3,MR,HC),bf16),fin=V((nb,MR,HC),f32),finb=V((nb,MR,HC),bf16),hr=V((nb,24,HC),f32))

class VecSum:
    def __init__(self,pc,cur,buf,ss,rs):
        self.pc,self.cur,self.buf=pc,cur,buf
        zp=lambda bit: ((pc.z^bit)*2+pc.x,pc.head)
        z1=(pc.z+1-2*(pc.z%2)); z2=(pc.z+2)%4
        partners=[pc.sib,pc.xn,pc.yn,(z1*2+pc.x,pc.head),(z2*2+pc.x,pc.head)]
        self.d=[rcopy(cur.at[i],buf.at[i],ss.at[i],rs.at[i],p) for i,p in enumerate(partners)]
    def step(self,i):
        if i>0:
            self.d[i-1].wait_recv()
            self.cur[i]=self.cur[i-1]+self.buf[i-1]
        if i<5: self.d[i].start()
    def done(self):
        for d in self.d: d.wait_send()

RSORDER=(8,4,9,5,10,6,11,7,3,2,1,0)
KEYS=list(scatter_scratch())
def rs_body(g_ref,vec_ref,out_ref,vout_ref,gown_ref,*rest):
    R=dict(zip(KEYS,rest[:len(KEYS)])); vcur,vbuf,ss,rs,os_,orr,vs,vr=rest[len(KEYS):]
    pc=Place()
    greet_all(pc)
    vcur[0]=vec_ref[...]
    vsum=VecSum(pc,vcur,vbuf,vs,vr)
    sc=[Scatter(pc,b,g_ref,R,out_ref,gown_ref,ss,rs,os_,orr) for b in RSORDER]
    for t in range(len(sc)+5):
        for s in range(6):
            if 0<=t-s<len(sc): sc[t-s].step(s)
        if t<=5: vsum.step(t)
    vout_ref[...]=vcur[5]
    for s in sc: s.done()
    vsum.done()
    @pl.when(pc.xy<3)
    def _(): pltpu.make_async_copy(gown_ref,gown_ref,orr).wait()

def call_rs(g,vec):
    V=pltpu.VMEM; S=jax.ShapeDtypeStruct
    B=pl.BlockSpec(memory_space=V); sem=pltpu.SemaphoreType.DMA
    return pl.pallas_call(rs_body,in_specs=[B,B],out_specs=[B,B,B],
        out_shape=[S((NB,24,D),f32),S((16,D),f32),S((16,MR,D),bf16)],
        scratch_shapes=list(scatter_scratch().values())+[V((6,16,D),f32),V((5,16,D),f32),sem((NB,10)),sem((NB,10)),sem((NB,2)),sem,sem((5,)),sem((5,))],
        compiler_params=pltpu.CompilerParams(vmem_limit_bytes=62<<20,collective_id=1,has_side_effects=True))(g,vec)

BETA=0.95; BETA_TWO=0.99; RATE=1.0; RATE_VEC=0.05

def owner_of(b):
    return ((b//3+(b%3)%2+1)%4)*4+b%3
def owned_by(pc):
    return 3*((pc.z+3-pc.xy%2)%4)+pc.xy

def pack(rows):
    return jnp.concatenate([rows[:,:HC],rows[:,HC:]],axis=0).astype(bf16)
def unpack(p):
    p=p.astype(f32)
    return jnp.concatenate([p[:24],p[24:]],axis=1)

def send_row(pc,t,src,dst,ssem,rsem):
    @pl.when(t==pc.me)
    def _(): pltpu.make_async_copy(src,dst,rsem).start()
    @pl.when(t!=pc.me)
    def _(): rcopy(src,dst,ssem,rsem,(t//4,t%4)).start()

def send_rows(pc,n,base,slots,dst,ss,rsem,start):
    def one(j,carry):
        t=base+j
        @pl.when(t==pc.me)
        def _():
            if start: pltpu.make_async_copy(slots.at[j],dst,rsem).start()
        @pl.when(t!=pc.me)
        def _():
            d=rcopy(slots.at[j],dst,ss.at[j],rsem,(t//4,t%4))
            if start: d.start()
            else: d.wait_send()
        return carry
    lax.fori_loop(0,n,one,0)

def newton_body(ghalf_ref,statl_ref,statr_ref,left_ref,right_ref,mas_ref,va_ref,vec_ref,sec_ref,
                ln_ref,rn_ref,mn_ref,vg_ref,sn_ref,vn_ref,
                m_ref,x_ref,nb,pb,sb,xb,slots,ggr,uslots,ur,tb,rt,rho,gown_ref,vcur,vbuf,gg, gs,gr,us,ur_sem,es,er,vs,vr):
    pc=Place()
    gown_ref[:,pc.cols]=ghalf_ref[...]
    vcur[0]=va_ref[...]
    greet_all(pc)
    vsum=VecSum(pc,vcur,vbuf,vs,vr)
    vsum.step(0)
    b=owned_by(pc)
    owner=pc.xy<3
    nblk=D//RB
    swap=lambda: rcopy(gown_ref.at[:,pc.cols],gown_ref.at[:,pc.cols],es.at[3],er.at[3],pc.sib)
    @pl.when(owner)
    def _(): swap().start()
    vsum.step(1)
    @pl.when(owner)
    def _():
        @pl.when(pc.c==0)
        def _():
            for i in range(nblk):
                r=slice(i*RB,(i+1)*RB)
                gg[r,:]=(1-BETA)*dot(ghalf_ref[r,:],ghalf_ref[...],1,1)
            swap().wait_recv()
            for i in range(nblk):
                r=slice(i*RB,(i+1)*RB)
                p=gg[r,:]+(1-BETA)*dot(gown_ref[r,HC:],gown_ref[:,HC:],1,1)
                gg[r,:]=p
                m_ref[r,:]=BETA*statl_ref[r,:]+p
        @pl.when(pc.c==1)
        def _():
            swap().wait_recv()
            for i in range(nblk):
                r=slice(i*RB,(i+1)*RB)
                p=(1-BETA)*dot(gown_ref[:,r],gown_ref[...],0,0)
                gg[r,:]=p
                m_ref[r,:]=BETA*statr_ref[r,:]+p
        def between(k):
            def piece(t,carry):
                slots[t]=pack(gg[pl.ds(pl.multiple_of(t*24,8),24),:])
                send_row(pc,t,slots.at[t],ggr.at[2*b+pc.c],gs.at[t],gr)
                return carry
            @pl.when(k<3)
            def _(): lax.fori_loop((k-1)*16,k*16,piece,0)
            @pl.when(k==2)
            def _(): vsum.step(2)
            @pl.when(k==4)
            def _(): vsum.step(3)
            @pl.when(k==6)
            def _(): vsum.step(4)
        newton(m_ref,x_ref,nb,pb,sb,xb,between)
        tr=jnp.zeros((1,1),f32)
        for i in range(nblk):
            r=slice(i*RB,(i+1)*RB); tr=tr+diag_sum(x_ref[r,r])
        lam=tr*(1/D)
        for i in range(nblk):
            r=slice(i*RB,(i+1)*RB)
            xb[r,:]=jnp.where(eye_rows(i),x_ref[r,:]-lam,x_ref[r,:]).astype(bf16)
        H=D//2
        send_t=rcopy(tb.at[pl.ds(H,H)],tb.at[pl.ds(H,H)],es.at[0],er.at[0],pc.sib)
        send_r=rcopy(xb,rt,es.at[1],er.at[1],pc.sib)
        send_l=rcopy(rho.at[0],rho.at[1],es.at[2],er.at[2],pc.sib)
        def update(trows,right,lam_r):
            for i in range(2):
                r=pl.ds(trows+i*192,192)
                t=tb[r,:]
                m_ref[pl.ds(i*192,192),:]=lam_r*t.astype(f32)+dot(t,right[...])
        rho[0]=jnp.broadcast_to(lam,(8,128))
        @pl.when(pc.c==0)
        def _():
            for h in (1,0):
                for i in range(2):
                    r=slice(h*H+i*192,h*H+(i+1)*192)
                    tb[r,:]=(lam*gown_ref[r,:].astype(f32)+dot(xb[r,:],gown_ref[...])).astype(bf16)
                if h==1: send_t.start()
            send_r.wait_recv(); send_l.wait_recv()
            update(0,rt,rho[1,0:1,0:1])
            send_t.wait_send()
        @pl.when(pc.c==1)
        def _():
            send_r.start(); send_l.start()
            send_t.wait_recv()
            update(H,xb,lam)
            send_r.wait_send(); send_l.wait_send()
        def pk2(i,carry):
            uslots[i]=pack(m_ref[pl.ds(pl.multiple_of(i*24,8),24),:])
            send_row(pc,pc.c*16+i,uslots.at[i],ur.at[b],us.at[i],ur_sem)
            return carry
        lax.fori_loop(0,16,pk2,0)
    @pl.when(jnp.logical_not(owner))
    def _():
        for i in (2,3,4): vsum.step(i)
    vsum.step(5)
    r=lax.broadcasted_iota(jnp.int32,(D,128),1); j=lax.broadcasted_iota(jnp.int32,(D,128),0)
    pick=jnp.where((j==pc.me*24+r)&(r<24),1.0,0.0).astype(f32)
    vg=lax.dot_general(vcur[5],pick,(((1,),(0,)),((),())),precision=lax.Precision.HIGHEST,preferred_element_type=f32)[:12,:24]
    sn=BETA_TWO*sec_ref[...]+(1-BETA_TWO)*vg*vg
    vg_ref[...]=vg; sn_ref[...]=sn
    vn_ref[...]=vec_ref[...]-RATE_VEC*vg/(jnp.sqrt(sn)+1e-8)
    pltpu.make_async_copy(ggr,ggr,gr).wait()
    def stats(i,carry):
        ln_ref[i]=BETA*left_ref[i]+unpack(ggr[2*i])
        rn_ref[i]=BETA*right_ref[i]+unpack(ggr[2*i+1])
        return carry
    lax.fori_loop(0,NB,stats,0)
    pltpu.make_async_copy(ur,ur,ur_sem).wait()
    def upd(i,carry):
        mn_ref[i]=mas_ref[i]-RATE*unpack(ur[i])
        return carry
    lax.fori_loop(0,NB,upd,0)
    @pl.when(owner)
    def _():
        swap().wait_send()
        send_rows(pc,32,0,slots,ggr.at[2*b+pc.c],gs,gr,False)
        send_rows(pc,16,pc.c*16,uslots,ur.at[b],us,ur_sem,False)
    vsum.done()

def call_newton_step(gown,statl,statr,left,right,mas,va,vec,sec):
    V=pltpu.VMEM; S=jax.ShapeDtypeStruct
    B=pl.BlockSpec(memory_space=V); sem=pltpu.SemaphoreType.DMA
    rows=S((NB,24,D),f32); small=S((NB,24),f32)
    return pl.pallas_call(newton_body,in_specs=[B]*9,out_specs=[B]*6,out_shape=[rows]*3+[small]*3,
        scratch_shapes=[V((D,D),f32)]*2+[V((D,D),bf16)]*4+[V((32,48,HC),bf16),V((24,48,HC),bf16),V((16,48,HC),bf16),V((12,48,HC),bf16),V((D,D),bf16),V((D,D),bf16),V((2,8,128),f32),V((D,D),bf16),V((6,16,D),f32),V((5,16,D),f32),V((D,D),f32),
            sem((32,)),sem,sem((16,)),sem,sem((4,)),sem((4,)),sem((5,)),sem((5,))],
        compiler_params=pltpu.CompilerParams(vmem_limit_bytes=62<<20,collective_id=2,has_side_effects=True))(gown,statl,statr,left,right,mas,va,vec,sec)


def place_params(pg_ref,p_ref):
    r=lax.broadcasted_iota(jnp.int32,(128,D),0); j=lax.broadcasted_iota(jnp.int32,(128,D),1)
    p_ref[...]=jnp.zeros_like(p_ref)
    def chip(m,carry):
        for c in range(2):
            sel=jnp.where((j==(m*2+c)*24+r)&(r<24),1.0,0.0).astype(bf16)
            p_ref[...]+=dot(pg_ref[m//4,m%4,:,c*HC:c*HC+128],sel)
        return carry
    lax.fori_loop(0,16,chip,0)

def keys_of_pair(p,k_ref,ka_ref,v_ref,va_ref,doc_ref):
    cols=pl.ds(pl.multiple_of(p*128,128),128)
    lane=lax.broadcasted_iota(jnp.int32,(256,128),1)
    for t in range(PACK//256):
        rows=pl.ds(t*256,256)
        kp=k_ref[rows,cols].astype(f32); vp=v_ref[rows,cols].astype(f32)
        doc=doc_ref[rows,:]
        for h,lo in enumerate((True,False)):
            off=64 if lo else 0
            k1=onehot_part(kp,lane,lo,doc,1.0,1.0)
            ka_ref[h,rows,:]=jnp.where((lane>=off+8)&(lane<off+11),1.0,k1).astype(bf16)
            va_ref[h,rows,:]=jnp.where((lane<64)==lo,vp,1.0).astype(bf16)

QF=512
def attend_block(p,b,q_ref,ka_ref,va_ref,qa_ref,ctx_ref,doc_ref):
    cols=pl.ds(pl.multiple_of(p*128,128),128)
    rows=pl.ds(pl.multiple_of(b*QF,QF),QF)
    lane=lax.broadcasted_iota(jnp.int32,(QF,128),1)
    low=lane<64
    qp=q_ref[rows,cols].astype(f32)*0.125
    doc=doc_ref[rows,:]
    qf=[onehot_part(qp,lane,lo,doc,0.0,BIG) for lo in (True,False)]
    ss=[dot(qf[h].astype(bf16),ka_ref[h],1,1) for h in range(2)]
    os=[]
    for h,lo in enumerate((True,False)):
        off=64 if lo else 0
        m=jnp.max(ss[h],axis=1,keepdims=True)
        o=dot(jnp.exp(ss[h]-m).astype(bf16),va_ref[h])
        os.append(o)
        q1=qf[h]
        for i,c in enumerate(split3(-(m+jnp.log(o)))): q1=jnp.where(lane==off+8+i,c,q1)
        qa_ref[h,rows,:]=q1.astype(bf16)
    l=pltpu.roll(jnp.where(low,os[1],os[0]),64,1)
    ctx_ref[rows,cols]=(jnp.where(low,os[0],os[1])/l).astype(bf16)

class StatMove:
    def __init__(self,pc,src,dst,side,ss,rsem):
        self.pc,self.src,self.dst,self.side,self.ss,self.rsem=pc,src,dst,side,ss,rsem
    def move(self,i,start):
        pc=self.pc
        b=(i+pc.me)%NB
        t=owner_of(b)
        src,dst=self.src.at[b],self.dst.at[pc.me]
        mine=(pc.chip==t)&(pc.c==self.side)
        if start:
            @pl.when(mine)
            def _(): pltpu.make_async_copy(src,dst,self.rsem).start()
        @pl.when(jnp.logical_not(mine))
        def _():
            d=rcopy(src,dst,self.ss.at[b],self.rsem,(t//2,(t%2)*2+self.side))
            if start: d.start()
            else: d.wait_send()
    def done(self):
        pc=self.pc
        lax.fori_loop(0,NB,lambda i,c: (self.move(i,False),c)[1],0)
        @pl.when((pc.xy<3)&(pc.c==self.side))
        def _(): pltpu.make_async_copy(self.dst,self.dst,self.rsem).wait()

AORDER=(0,1,2,3,4,8,5,9,6,10,7,11)
TT=512
def front_body(len_ref,x_ref,cot_ref,mas_ref,pv_ref,left_ref,
               out_o,qa_o,ka_o,v_o,ctx_o,act_o,din_o,dffn_o,ht_o,dz1_o,dctx_o,wq_o,xt_o,vec_o,st_ref,
               w_ref,pg_ref,p_ref,sibm,q,k,v,ctx,doc,qa,ka,va,n1,r1,hlow,acc,act,gp,dffn,dctx,out,xt,
               ss,rs,cs,cr,ts,tr,lsem,asem,osem):
    pc=Place()
    greet_all(pc)
    first=rcopy(mas_ref.at[pl.ds(0,3),:,pc.ocols],sibm.at[pl.ds(0,3)],cs.at[0],cr.at[0],pc.sib)
    other=rcopy(mas_ref.at[pl.ds(3,9),:,pc.ocols],sibm.at[pl.ds(3,9)],cs.at[1],cr.at[1],pc.sib)
    first.start(); other.start()
    pg_ref[pc.z,pc.xy,:,pc.cols]=pv_ref[...]
    def stacked(own,oth):
        upper=jnp.where(pc.c==0,own,oth); lower=jnp.where(pc.c==0,oth,own)
        return jnp.concatenate([upper,lower],axis=0).astype(bf16)
    def assemble(places):
        for pos in places:
            if pos<3:
                for i in range(3):
                    own=mas_ref[i,:,pl.ds(pl.multiple_of((pc.c*3+pos)*128,128),128)]
                    w_ref[pos,pc.z,pc.xy,:,pl.ds(pl.multiple_of(pc.c*HC+i*128,128),128)]=stacked(own,sibm[i,:,pos*128:(pos+1)*128])
            else:
                w_ref[pos,pc.z,pc.xy,:,pc.cols]=stacked(mas_ref[AORDER[pos],:,pc.cols],sibm[AORDER[pos]])
    NG=10
    def single(g,pos,whole):
        return Gather(pc,lambda z,xy,cols: w_ref.at[pos,z,xy,:,cols],ss.at[g],rs.at[g],whole).copies()
    def double(g):
        return Gather(pc,lambda z,xy,cols: w_ref.at[pl.ds(4+2*(g-5),2),z,xy,:,cols],ss.at[g],rs.at[g],True).copies()
    def on_group(g,act):
        if isinstance(g,int):
            if g==0: act(Gather(pc,lambda z,xy,cols: pg_ref.at[z,xy,:,cols],ss.at[0],rs.at[0]).copies())
            elif g<4: act(single(g,g-1,False))
            elif 5<=g<8: act(double(g))
            else: act(single(g,3 if g==4 else g+2,True))
        else:
            @pl.when((g>=1)&(g<4))
            def _(): act(single(g,g-1,False))
            @pl.when((g>=5)&(g<8))
            def _(): act(double(g))
            @pl.when((g==4)|((g>=8)&(g<NG)))
            def _(): act(single(g,g-1+3*(g//8),True))
    def tick(t):
        for s,d in ((0,-3),(1,0),(2,1),(3,2),(4,3)):
            if isinstance(t,int):
                if 0<=t-d<NG and not (s==0 and t<1): on_group(t-d,lambda g: g.step(s))
            else: on_group(t-d,lambda g: g.step(s))
    stats=StatMove(pc,left_ref,st_ref,0,ts,tr)
    copies=[]
    def away(src,dst):
        i=len(copies)
        c=pltpu.make_async_copy(src,dst,lsem.at[i]); c.start(); copies.append(c)
    W=lambda pos: w_ref[pos].reshape(D,D)
    on_group(0,lambda g: g.step(0))
    first.wait_recv()
    for i in range(3):
        assemble([i])
        on_group(i+1,lambda g: g.step(0))
    other.wait_recv()
    assemble(range(3,12))
    for i in range(6): xt[i*128:(i+1)*128,:]=x_ref[:,i*128:(i+1)*128].T
    xcopy=pltpu.make_async_copy(xt,xt_o,lsem.at[21]); xcopy.start()
    for t in range(4): tick(t)
    place_params(pg_ref,p_ref)
    t_=lax.broadcasted_iota(jnp.int32,(PACK,128),0)
    end=jnp.int32(0); dd=jnp.zeros((PACK,128),jnp.int32)
    for j in range(8):
        end=end+len_ref[0,j]
        dd=dd+(t_>=end).astype(jnp.int32)
    doc[...]=dd
    tick(4)
    def project(j):
        for tl in range(2):
            rows=pl.ds(tl*512,512)
            y=dot(x_ref[rows,:],W(j))
            for c in range(2):
                cols=pl.ds(pl.multiple_of((3*c+j)*128,128),128)
                for i,(o,b) in enumerate(((q,0),(k,None),(v,1))):
                    t=y[:,c*HC+i*128:c*HC+(i+1)*128]
                    if b is not None: t=t+p_ref[b:b+1,cols]
                    o[rows,cols]=t.astype(bf16)
    def pair_copies(pi):
        return [pltpu.make_async_copy(s.at[pi%2],d.at[pi],asem.at[i,pi%2]) for i,(s,d) in enumerate(((qa,qa_o),(ka,ka_o)))]
    def slot(n,carry):
        pi=n//2; b=n%2; p=3*(pi%2)+pi//2; side=pi%2
        @pl.when(n%4==0)
        def _(): project(n//4)
        @pl.when(b==0)
        def _():
            @pl.when(pi>=2)
            def _():
                for c in pair_copies(pi-2): c.wait()
            keys_of_pair(p,k,ka.at[side],v,va,doc)
        attend_block(p,b,q,ka.at[side],va,qa.at[side],ctx,doc)
        @pl.when(b==1)
        def _():
            for c in pair_copies(pi): c.start()
            @pl.when((pi==0)|(pi%2==1))
            def _(): tick(5+(pi+1)//2)
        return carry
    lax.fori_loop(0,12,slot,0)
    away(ctx,ctx_o); away(v,v_o)
    for i in range(3): away(w_ref.at[i],wq_o.at[i])
    g1,s1,g2,s2=(p_ref[i:i+1,:] for i in (8,9,10,11))
    vec_o[...]=jnp.zeros_like(vec_o)
    def out_proj(tl,carry):
        rows=pl.ds(pl.multiple_of(tl*TT,TT),TT)
        z=x_ref[rows,:].astype(f32)+(dot(ctx[rows,:],W(3))+p_ref[2:3,:])
        n,r=layer_norm(z)
        n1[rows,:]=n
        r1[rows,:]=jnp.broadcast_to(r,(TT,128))
        hlow[rows,:]=(n*g1+s1).astype(bf16)
        return carry
    lax.fori_loop(0,PACK//TT,out_proj,0)
    xcopy.wait()
    for i in range(6): xt[i*128:(i+1)*128,:]=hlow[:,i*128:(i+1)*128].T
    away(xt,ht_o)
    def chunk_copy(c):
        lane=pl.ds(pl.multiple_of(c*D,128),D)
        return pltpu.make_async_copy(act.at[:,lane],act_o.at[:,lane],osem.at[5,c])
    def chunk(c,carry):
        lane=pl.ds(pl.multiple_of(c*D,128),D)
        bias=p_ref[pl.ds(3+c,1),:]
        for tl in range(4):
            rows=pl.ds(tl*256,256)
            inner=dot(hlow[rows,:],W(4+2*c))+bias
            a,g=gelu_both(inner)
            al=a.astype(bf16)
            act[rows,lane]=al
            gp[rows,lane]=g.astype(bf16)
            y=dot(al,W(5+2*c))
            @pl.when(c==0)
            def _(): acc[rows,:]=y
            @pl.when(c>0)
            def _(): acc[rows,:]+=y
        chunk_copy(c).start()
        @pl.when(c<3)
        def _(): tick(9+c)
        @pl.when(c==2)
        def _(): tick(12)
        @pl.when(c==2)
        def _(): lax.fori_loop(0,NB,lambda i,a: (stats.move(i,True),a)[1],0)
        return carry
    lax.fori_loop(0,4,chunk,0)
    pltpu.make_async_copy(cot_ref,out,lsem.at[20]).start()
    pltpu.make_async_copy(cot_ref,out,lsem.at[20]).wait()
    def tile_copies(tl):
        rows=pl.ds(pl.multiple_of(tl*TT,TT),TT)
        return [pltpu.make_async_copy(s.at[rows],d.at[rows],osem.at[i,tl]) for i,(s,d) in enumerate(((out,out_o),(gp,din_o),(dffn,dffn_o),(acc,dz1_o),(dctx,dctx_o)))]
    def tile(tl,carry):
        rows=pl.ds(pl.multiple_of(tl*TT,TT),TT)
        n1t=n1[rows,:]
        z=(n1t*g1+s1)+(acc[rows,:]+p_ref[7:8,:])
        n2,r2=layer_norm(z)
        e=out[rows,:].astype(f32)
        out[rows,:]=(n2*g2+s2).astype(bf16)
        c2=e*g2
        dz2=r2*(c2-jnp.mean(c2,axis=-1,keepdims=True)-n2*jnp.mean(c2*n2,axis=-1,keepdims=True))
        df=dz2.astype(bf16)
        dffn[rows,:]=df
        vec_o[10:11,:]+=jnp.sum(e*n2,axis=0,keepdims=True)
        vec_o[11:12,:]+=jnp.sum(e,axis=0,keepdims=True)
        vec_o[7:8,:]+=jnp.sum(df.astype(f32),axis=0,keepdims=True)
        dh=dz2
        for c in range(4):
            lane=pl.ds(c*D,D)
            dact=dot(df,W(5+2*c),1,1)
            din=(dact*gp[rows,lane].astype(f32)).astype(bf16)
            gp[rows,lane]=din
            vec_o[3+c:4+c,:]+=jnp.sum(din.astype(f32),axis=0,keepdims=True)
            dh=dh+dot(din,W(4+2*c),1,1)
        vec_o[8:9,:]+=jnp.sum(dh*n1t,axis=0,keepdims=True)
        vec_o[9:10,:]+=jnp.sum(dh,axis=0,keepdims=True)
        c1=dh*g1
        dz1=r1[rows,0:1]*(c1-jnp.mean(c1,axis=-1,keepdims=True)-n1t*jnp.mean(c1*n1t,axis=-1,keepdims=True))
        acc[rows,:]=dz1
        dat=dz1.astype(bf16)
        vec_o[2:3,:]+=jnp.sum(dat.astype(f32),axis=0,keepdims=True)
        dctx[rows,:]=dot(dat,W(3),1,1).astype(bf16)
        for c in tile_copies(tl): c.start()
        return carry
    lax.fori_loop(0,PACK//TT,tile,0)
    for c in copies: c.wait()
    for p in (4,5):
        for c in pair_copies(p): c.wait()
    for i in range(4):
        chunk_copy(i).wait()
    for i in range(PACK//TT):
        for c in tile_copies(i): c.wait()
    first.wait_send(); other.wait_send()
    for i in range(NG): on_group(i,lambda g: g.done())
    stats.done()

def call_front(lengths,x,cot,masters,pv,left):
    V=pltpu.VMEM; S=jax.ShapeDtypeStruct; A=pl.ANY
    B=lambda m: pl.BlockSpec(memory_space=m)
    sem=pltpu.SemaphoreType.DMA
    T=lambda w,d: S((PACK,w),d)
    return pl.pallas_call(front_body,
        in_specs=[B(pltpu.SMEM),B(V),B(A),B(V),B(V),B(A)],
        out_specs=[B(A)]*13+[B(V),B(A)],
        out_shape=[T(D,bf16)]+[S((6,2,PACK,128),bf16)]*2+[T(D,bf16)]*2+[T(FF,bf16),T(FF,bf16),T(D,bf16),S((D,PACK),bf16),T(D,f32),T(D,bf16),S((3,4,4,MR,D),bf16),S((D,PACK),bf16),S((16,D),f32),S((32,24,D),f32)],
        scratch_shapes=[V((NB,4,4,MR,D),bf16),V((4,4,16,D),bf16),V((16,D),f32),V((NB,24,HC),f32)]+[V((PACK,D),bf16)]*4+
            [V((PACK,128),jnp.int32),V((2,2,PACK,128),bf16),V((2,2,PACK,128),bf16),V((2,PACK,128),bf16),V((PACK,D),f32),V((PACK,128),f32),V((PACK,D),bf16),V((PACK,D),f32),
             V((PACK,FF),bf16),V((PACK,FF),bf16),V((PACK,D),bf16),V((PACK,D),bf16),V((PACK,D),bf16),V((D,PACK),bf16),
             sem((13,11)),sem((13,11)),sem((2,)),sem((2,)),sem((NB,)),sem,sem((24,)),sem((2,2)),sem((6,4))],
        compiler_params=pltpu.CompilerParams(vmem_limit_bytes=63<<20,collective_id=0,has_side_effects=True))(lengths,x,cot,masters,pv,left)


NGR=12
def sum_scratch():
    V=pltpu.VMEM; nb=NGR
    return dict(rc=V((nb,4,4,MR,HC),bf16),xa=V((nb,2,2,MR,HC),bf16),yb=V((nb,2,2,MR,HC),bf16),
        s2a=V((nb,2,MR,HC),bf16),s2b=V((nb,2,MR,HC),bf16),ya=V((nb,2,MR,HC),bf16),xb=V((nb,2,MR,HC),bf16),
        s3=V((nb,4,MR,HC),bf16),zr=V((nb,3,MR,HC),bf16),fin=V((nb,MR,HC),f32),finb=V((nb,MR,HC),bf16),hr=V((nb,24,HC),f32))
SKEYS=list(sum_scratch())

class GroupSum:
    def __init__(self,pc,g_ref,R,out_ref,gown_ref,ss,rs,os_,orr):
        self.pc,self.gr,self.RR,self.out,self.gown=pc,g_ref,R,out_ref,gown_ref
        self.ss,self.rs,self.os_,self.orr=ss,rs,os_,orr
    def mk(self,g,i,src,dst,dev): return rcopy(src,dst,self.ss.at[g,i],self.rs.at[g,i],dev)
    def of(self,g): return self.gr.at[g],{k:v.at[g] for k,v in self.RR.items()}
    def core(self,g):
        G,R=self.of(g); return self.mk(g,0,G.at[:,:,:,self.pc.ocols],R["rc"],self.pc.sib)
    def xa(self,g):
        G,R=self.of(g); pc=self.pc; return self.mk(g,1,G.at[pl.ds(0,2),pl.ds((1-pc.x)*2,2),:,pc.cols],R["xa"],pc.xn)
    def yb(self,g,i):
        G,R=self.of(g); pc=self.pc; return self.mk(g,2+i,G.at[pl.ds(2,2),i*2+1-pc.y,:,pc.cols],R["yb"].at[i],pc.yn)
    def ya(self,g):
        G,R=self.of(g); return self.mk(g,4,R["s2a"],R["ya"],self.pc.yn)
    def xb(self,g):
        G,R=self.of(g); return self.mk(g,5,R["s2b"],R["xb"],self.pc.xn)
    def zz(self,g,k):
        G,R=self.of(g); pc=self.pc; return self.mk(g,5+k,R["s3"].at[(pc.z+k)%NZ],R["zr"].at[k-1],pc.zpeer(k))
    def home(self,g):
        G,R=self.of(g); pc=self.pc; return self.mk(g,9,R["fin"].at[pl.ds(pl.multiple_of((1-pc.c)*24,8),24)],R["hr"],pc.sib)
    def step0(self,g): self.core(g).start()
    def step1(self,g):
        pc=self.pc; G,R=self.of(g)
        self.core(g).wait_recv()
        for z in range(4):
            G[z,:,:,pc.cols]=(G[z,:,:,pc.cols].astype(f32)+R["rc"][z].astype(f32)).astype(bf16)
        self.xa(g).start()
        for i in range(2): self.yb(g,i).start()
    def step2(self,g):
        pc=self.pc; G,R=self.of(g)
        self.xa(g).wait_recv()
        R["s2a"][...]=(G[0:2,pc.x*2+1-pc.y,:,pc.cols].astype(f32)+R["xa"][:,1-pc.y].astype(f32)).astype(bf16)
        self.ya(g).start()
        for i in range(2): self.yb(g,i).wait_recv()
        R["s2b"][...]=(G[2:4,(1-pc.x)*2+pc.y,:,pc.cols].astype(f32)+R["yb"][1-pc.x].astype(f32)).astype(bf16)
        self.xb(g).start()
    def step3(self,g):
        pc=self.pc; G,R=self.of(g)
        self.ya(g).wait_recv(); self.xb(g).wait_recv()
        a=G[0:2,pc.xy,:,pc.cols].astype(f32)+R["xa"][:,pc.y].astype(f32)+R["ya"][...].astype(f32)
        b=G[2:4,pc.xy,:,pc.cols].astype(f32)+R["yb"][pc.x].astype(f32)+R["xb"][...].astype(f32)
        R["s3"][0:2]=a.astype(bf16); R["s3"][2:4]=b.astype(bf16)
        ab=jnp.where(pc.z%2==0,jnp.stack([a[0],b[0]]),jnp.stack([a[1],b[1]]))
        R["fin"][...]=jnp.where(pc.z<2,ab[0],ab[1])
        for k in (1,2,3): self.zz(g,k).start()
    def targets(self,g,act):
        pc=self.pc; G,R=self.of(g)
        def whole(b):
            act(R["finb"],self.gown.at[pc.chip],0,owner_of(b))
        def slab(j):
            for i in range(3):
                act(R["finb"].at[:,pl.ds(i*128,128)],self.gown.at[pc.chip,:,pl.ds(pl.multiple_of(j*128,128),128)],i,owner_of(i))
        if isinstance(g,int):
            if g<9: whole(8+g//2-4*(g%2)-9*(g//8))
            else: slab(g-9)
        else:
            @pl.when(g<9)
            def _(): whole(8+g//2-4*(g%2)-9*(g//8))
            @pl.when(g>=9)
            def _(): slab(g-9)
    def step4(self,g):
        pc=self.pc; G,R=self.of(g)
        for k in (1,2,3): self.zz(g,k).wait_recv()
        s=R["fin"][...]
        for k in range(3): s=s+R["zr"][k].astype(f32)
        R["fin"][...]=s
        R["finb"][...]=s.astype(bf16)
        self.home(g).start()
        def send(src,dst,i,t):
            mine=pc.chip==t
            @pl.when(mine)
            def _(): pltpu.make_async_copy(src,dst,self.orr).start()
            @pl.when(jnp.logical_not(mine))
            def _(): rcopy(src,dst,self.os_.at[g,i],self.orr,(t//2,(t%2)*2+pc.c)).start()
        self.targets(g,send)
    def step5(self,g):
        pc=self.pc; G,R=self.of(g)
        self.home(g).wait_recv()
        def whole(b):
            self.out[b,:,pc.cols]=R["fin"][pl.ds(pl.multiple_of(pc.c*24,8),24)]
            self.out[b,:,pc.ocols]=R["hr"][...]
        def slab(j):
            for i in range(3):
                self.out[i,:,pl.ds(pl.multiple_of((pc.c*3+j)*128,128),128)]=R["fin"][pl.ds(pl.multiple_of(pc.c*24,8),24),i*128:(i+1)*128]
                self.out[i,:,pl.ds(pl.multiple_of(((1-pc.c)*3+j)*128,128),128)]=R["hr"][:,i*128:(i+1)*128]
        if isinstance(g,int):
            if g<9: whole(8+g//2-4*(g%2)-9*(g//8))
            else: slab(g-9)
        else:
            @pl.when(g<9)
            def _(): whole(8+g//2-4*(g%2)-9*(g//8))
            @pl.when(g>=9)
            def _(): slab(g-9)
    def done(self,g):
        pc=self.pc
        for d in (self.core,self.xa,self.ya,self.xb,self.home): d(g).wait_send()
        for i in range(2): self.yb(g,i).wait_send()
        for k in (1,2,3): self.zz(g,k).wait_send()
        def wait(src,dst,i,t):
            @pl.when(pc.chip!=t)
            def _(): rcopy(src,dst,self.os_.at[g,i],self.orr,(t//2,(t%2)*2+pc.c)).wait_send()
        self.targets(g,wait)

KB_=512
PACE={1:(("step1",0),),4:(("step1",1),),5:(("step2",0),),7:(("step1",2),),8:(("step2",1),("step3",0))}
def prepare_pair(p,v,ctx,do,doa,va):
    cols=pl.ds(pl.multiple_of(p*128,128),128)
    lane=lax.broadcasted_iota(jnp.int32,(256,128),1)
    i=lax.broadcasted_iota(jnp.int32,(128,128),0); j=lax.broadcasted_iota(jnp.int32,(128,128),1)
    cross=jnp.where((i<64)!=(j<64),-1.0,0.0).astype(bf16)
    for t in range(PACK//256):
        rows=pl.ds(t*256,256)
        vp=v[rows,cols].astype(f32)
        dop=do[rows,cols].astype(f32); prod=dop*ctx[rows,cols].astype(f32)
        dd=sum(dot(c.astype(bf16),cross) for c in split3(prod))
        parts=split3(dd)
        for h,lo in enumerate((True,False)):
            keep=(lane<64)==lo
            off=64 if lo else 0
            d1=jnp.where(keep,dop,0.0)
            for n,c in enumerate(parts): d1=jnp.where(lane==off+n,c,d1)
            doa[h,rows,:]=d1.astype(bf16)
            v1=jnp.where(keep,vp,0.0)
            va[h,rows,:]=jnp.where((lane>=off)&(lane<off+3),1.0,v1).astype(bf16)

def back_block(p,b,dk_ref,dv_ref,qa,doa,ka,va,dqa):
    cols=pl.ds(pl.multiple_of(p*128,128),128)
    rows=pl.ds(pl.multiple_of(b*KB_,KB_),KB_)
    low=lax.broadcasted_iota(jnp.int32,(KB_,128),1)<64
    lowq=lax.broadcasted_iota(jnp.int32,(PACK,128),1)<64
    r=[]
    for h in range(2):
        kh=ka[h,rows,:]
        pr=jnp.exp(dot(kh,qa[h],1,1))
        dp=dot(va[h,rows,:],doa[h],1,1)
        ds=(pr*dp).astype(bf16)
        r.append((dot(pr.astype(bf16),doa[h]),dot(ds,qa[h]),dot(ds,kh,0,0)))
    dq=jnp.where(lowq,r[0][2],r[1][2])
    @pl.when(b==0)
    def _(): dqa[...]=dq
    @pl.when(b>0)
    def _(): dqa[...]+=dq
    dv_ref[rows,cols]=jnp.where(low,r[0][0],r[1][0]).astype(bf16)
    dk_ref[rows,cols]=jnp.where(low,r[0][1],r[1][1]).astype(bf16)

def back_body(xt_ref,qa_i,ka_i,v_i,ctx_i,do_i,act_i,din_i,dffn_i,ht_i,dz1_i,wq_i,vec_ref,right_ref,
              ig_o,out_ref,vcur,gown_ref,st_ref,*rest):
    R=dict(zip(SKEYS,rest[:len(SKEYS)]))
    (g_ref,ctx,w_last,act,din,dffn,ht,acc,qa,doa,ka,va,dqa,
     ss,rs,os_,orr,ts,tr,lsem,asem)=rest[len(SKEYS):]
    pc=Place()
    loads={}
    def load(name,src,dst):
        c=pltpu.make_async_copy(src,dst,lsem.at[len(loads)]); c.start(); loads[name]=c
    half=lambda ref,c: ref.at[:,pl.ds(c*D,D)]
    load("act0",half(act_i,0),act.at[0]); load("dffn",dffn_i,dffn)
    load("hlow",ht_i,ht); load("din0",half(din_i,0),din.at[0])
    load("act1",half(act_i,1),act.at[1]); load("din1",half(din_i,1),din.at[1])
    for n,s,d in (("acc",dz1_i,acc),("ctx",ctx_i,ctx)): load(n,s,d)
    q,v,do,k=act.at[0],din.at[0],dffn,act.at[1]
    late={5:("v",v_i,v),7:("do",do_i,do)}
    def pair_loads(pi):
        return [pltpu.make_async_copy(s.at[pi],d.at[pi%2],asem.at[i,pi%2]) for i,(s,d) in enumerate(((qa_i,qa),(ka_i,ka)))]
    for c in pair_loads(0): c.start()
    greet_all(pc)
    gs=GroupSum(pc,g_ref,R,out_ref,gown_ref,ss,rs,os_,orr)
    stats=StatMove(pc,right_ref,st_ref,1,ts,tr)
    def product(g,a,b):
        for r in range(4):
            g_ref[g,r]=dot(a[:,r*192:(r+1)*192],b,0,0).astype(bf16).reshape(4,MR,D)
    lax.fori_loop(0,NB,lambda i,a: (stats.move(i,True),a)[1],0)
    loads["dffn"].wait()
    for i in range(9):
        c=i//2
        if i==8:
            loads["ctx"].wait(); loads["acc"].wait()
            product(i,ctx,acc[...].astype(bf16))
        elif i%2==0:
            loads[f"act{c}"].wait()
            product(i,act.at[c%2],dffn[...])
            if c<2: load(f"act{c+2}",half(act_i,c+2),act.at[c%2])
        else:
            if c==0: loads["hlow"].wait()
            loads[f"din{c}"].wait()
            for r in range(4): g_ref[i,r]=dot(ht[r*192:(r+1)*192,:],din[c%2]).astype(bf16).reshape(4,MR,D)
            if c<2: load(f"din{c+2}",half(din_i,c+2),din.at[c%2])
        if i in late: load(*late[i])
        gs.step0(i)
        for s,g in PACE.get(i,()): getattr(gs,s)(g)
    wrow=pl.ds(0,D)
    wdst=[din.at[1,wrow],ht.at[:,pl.ds(0,D)],w_last]
    for i in range(3): load(f"w{i}",wq_i.at[i],wdst[i])
    for n in ("v","do"): loads[n].wait()
    def slot(n,carry):
        pi=n//2; b=n%2; j=pi//2; cc=pi%2; p=3*cc+j; side=pi%2
        cols=pl.ds(pl.multiple_of(p*128,128),128)
        @pl.when(b==0)
        def _():
            for c in pair_loads(pi): c.wait()
            @pl.when(pi<5)
            def _():
                for c in pair_loads(pi+1): c.start()
            prepare_pair(p,v,ctx,do,doa,va)
        back_block(p,b,k,v,qa.at[side],doa,ka.at[side],va,dqa)
        @pl.when(b==1)
        def _():
            q[:,cols]=(dqa[...]*0.125).astype(bf16)
            al=jnp.concatenate([q[:,cols],k[:,cols],v[:,cols]],axis=1)
            lane=pl.ds(pl.multiple_of(cc*HC,128),HC)
            for r in range(4):
                g_ref[9+j,r,:,:,lane]=dot(xt_ref[r*192:(r+1)*192,:],al).astype(bf16).reshape(4,MR,HC)
            vcur[0:1,cols]=jnp.sum(q[:,cols].astype(f32),axis=0,keepdims=True)
            vcur[1:2,cols]=jnp.sum(v[:,cols].astype(f32),axis=0,keepdims=True)
        @pl.when((n<=6)|(n==8))
        def _(): gs.step1(3+n-n//8)
        @pl.when((n<=7)|(n==9))
        def _(): gs.step2(2+n-n//9)
        @pl.when((n<=8)|(n==10))
        def _(): gs.step3(1+n-n//10)
        @pl.when(n>=1)
        def _(): gs.step4(n-1)
        @pl.when(n>=2)
        def _(): gs.step5(n-2)
        @pl.when((n==3)|(n==7))
        def _(): gs.step0(9+n//7)
        return carry
    vcur[...]=vec_ref[...]
    lax.fori_loop(0,12,slot,0)
    gs.step0(11)
    for i in range(3): loads[f"w{i}"].wait()
    def grad_tile(t):
        rows=pl.ds(t*256,256)
        a=acc[rows,:]
        for j,w in enumerate(wdst):
            d=jnp.concatenate([t[rows,(3*c+j)*128:(3*c+j+1)*128] for c in range(2) for t in (q,k,v)],axis=1)
            a=a+dot(d,w[...],1,1)
        acc[rows,:]=a
    grad_tile(0)
    gs.step5(10); gs.step1(11)
    grad_tile(1); grad_tile(2)
    gs.step2(11); grad_tile(3)
    away=pltpu.make_async_copy(acc,ig_o,lsem.at[31]); away.start()
    gs.step3(11)
    gs.step4(11)
    gs.step5(11)
    lax.fori_loop(0,NGR,lambda g,c: (gs.done(g),c)[1],0)
    away.wait()
    stats.done()
    @pl.when(pc.xy<3)
    def _(): pltpu.make_async_copy(gown_ref,gown_ref,orr).wait()

def call_back(xt,qa,ka,v,ctx,dctx,act,din,dffn,ht,dz1,wq,vec,right):
    V=pltpu.VMEM; S=jax.ShapeDtypeStruct; A=pl.ANY
    B=lambda m: pl.BlockSpec(memory_space=m)
    sem=pltpu.SemaphoreType.DMA
    T=V((PACK,D),bf16); H=V((2,PACK,128),bf16)
    return pl.pallas_call(back_body,
        in_specs=[B(V)]+[B(A)]*11+[B(V),B(A)],
        out_specs=[B(A),B(V),B(V),B(A),B(A)],
        out_shape=[S((PACK,D),f32),S((NB,24,D),f32),S((16,D),f32),S((16,MR,HC),bf16),S((32,24,D),f32)],
        scratch_shapes=list(sum_scratch().values())+[V((NGR,4,4,MR,D),bf16),T,V((D,D),bf16)]+[V((2,PACK,D),bf16),V((2,PACK,D),bf16),T,V((D,PACK),bf16),V((PACK,D),f32)]+[V((2,2,PACK,128),bf16),H,V((2,2,PACK,128),bf16),H]+
            [V((PACK,128),f32),sem((NGR,10)),sem((NGR,10)),sem((NGR,3)),sem,sem((NB,)),sem,sem((32,)),sem((2,2))],
        compiler_params=pltpu.CompilerParams(vmem_limit_bytes=63<<20,collective_id=1,has_side_effects=True))(xt,qa,ka,v,ctx,dctx,act,din,dffn,ht,dz1,wq,vec,right)


def gather_rows(a):
    return lax.all_gather(a,("dp","head"),axis=1,tiled=True)

def doc_lengths(lengths):
    return lax.dynamic_slice_in_dim(lengths,lax.axis_index("head"),1,axis=0)

def layer(tokens,cotangent,lengths,w,params):
    q,k,v,ctx,lse,n1,r1=call_a(lengths,tokens,w,params)
    out,dz1,dctx,dwo,dw1,dw2,vec=call_b(cotangent,n1,r1,ctx,w,params)
    ig,dwqkv,vq=call_c(lengths,tokens,q,k,v,ctx,dctx,lse,dz1,w)
    terms=jnp.concatenate([dwqkv,dwo[None],dw1,dw2],axis=0)
    vec=jnp.concatenate([vq[0:1],vq[2:3],vec[2:]],axis=0)
    return out,ig,terms,vec

def on_slice(tokens,cotangent,lengths,masters,vectors,left,right,second):
    pv=jnp.pad(vectors,((0,4),(0,HC-24))).astype(bf16)
    lens=doc_lengths(lengths)
    out,qa,ka,v,ctx,act,din,dffn,ht,dz1,dctx,wq,xt,vec,statl=call_front(lens,tokens,cotangent,masters,pv,left)
    ig,grads,vec,gown,statr=call_back(xt,qa,ka,v,ctx,dctx,act,din,dffn,ht,dz1,wq.reshape(3,D,D),vec,right)
    ln,rn,mn,vg,sn,vn=call_newton_step(gown.reshape(D,HC),statl.reshape(D,D),statr.reshape(D,D),left,right,masters,vec,vectors,second)
    return out,ig,grads,ln,rn,mn,vg,sn,vn

def on_any(tokens,cotangent,lengths,masters,vectors,left,right,second):
    axes=("dp","head")
    me=lax.axis_index("dp")*lax.axis_size("head")+lax.axis_index("head")
    share=masters.shape[1]
    w=gather_rows(masters.astype(bf16))
    params=gather_rows(vectors.astype(bf16)).astype(f32)
    out,ig,terms,vec=layer(tokens,cotangent,doc_lengths(lengths),w,params)
    grads=lax.psum_scatter(terms.astype(f32),axes,scatter_dimension=1,tiled=True)
    vg=lax.psum_scatter(vec[:12],axes,scatter_dimension=1,tiled=True)
    low=grads.astype(bf16)
    g=gather_rows(low)
    ein=partial(jnp.einsum,preferred_element_type=f32)
    cols=lax.dynamic_slice_in_dim(g,me*share,share,axis=2)
    ln=BETA*left+(1-BETA)*ein("kid,kjd->kij",low,g)
    rn=BETA*right+(1-BETA)*ein("kdi,kdj->kij",cols,g)
    item=jnp.minimum(me,2*NB-1)
    own=lax.dynamic_index_in_dim(jnp.concatenate([gather_rows(ln),gather_rows(rn)],axis=0),item,0,keepdims=False)
    root=call_newton(own)
    place=jnp.where((jnp.arange(2*NB)==me)[:,None,None],root[None],0.0)
    rows=lax.psum_scatter(place,axes,scatter_dimension=1,tiled=True)
    rr=gather_rows(rows[NB:])
    hi=partial(jnp.einsum,"kij,kjl->kil",precision=lax.Precision.HIGHEST)
    mn=masters-RATE*hi(hi(rows[:NB],g.astype(f32)),rr)
    sn=BETA_TWO*second+(1-BETA_TWO)*vg*vg
    vn=vectors-RATE_VEC*vg/(jnp.sqrt(sn)+1e-8)
    return out,ig,grads,ln,rn,mn,vg,sn,vn

def solution(mesh):
    rows=P(("dp","head"),None); blocks=P(None,("dp","head"),None); vecs=P(None,("dp","head"))
    on_device=on_slice if dict(mesh.shape)=={"dp":8,"head":4} else on_any
    return jax.shard_map(on_device,mesh=mesh,
        in_specs=(rows,rows,P("dp",None),blocks,vecs,blocks,blocks,vecs),
        out_specs=(rows,rows,blocks,blocks,blocks,blocks,vecs,vecs,vecs),check_vma=False)
```

```python
import jax, jax.numpy as jnp, numpy as np
from functools import partial
from jax import lax
from jax.experimental import pallas as pl
from jax.experimental.pallas import tpu as pltpu
from jax.sharding import PartitionSpec as P

D=768; HEADS=12; HD=64; FF=3072; PACK=1024; NEWTON=8; NB=12
NORM_EPS=1e-6
f32=jnp.float32; bf16=jnp.bfloat16
BIG=1e30
QB=256
def dot(a,b,ca=1,cb=0):
    return lax.dot_general(a,b,(((ca,),(cb,)),((),())),preferred_element_type=f32)

def doc_column(len_ref, shape, dim):
    t=lax.broadcasted_iota(jnp.int32,shape,dim)
    end=jnp.int32(0); doc=jnp.zeros(shape,jnp.int32)
    for j in range(8):
        end=end+len_ref[0,j]
        doc=doc+(t>=end).astype(jnp.int32)
    return doc

def split3(v):
    a=v.astype(bf16).astype(f32); r=v-a
    b=r.astype(bf16).astype(f32); c=r-b
    return a,b,c

def augment(base, lane, head_lo, cols):
    keep=(lane<64) if head_lo else (lane>=64)
    off=64 if head_lo else 0
    out=jnp.where(keep, base, 0.0)
    for i,c in enumerate(cols):
        out=jnp.where(lane==off+i, c, out)
    return out.astype(bf16)

def onehot_part(base, lane, head_lo, doc, minus, scale):
    keep=(lane<64) if head_lo else (lane>=64)
    off=64 if head_lo else 0
    l=lane-off
    oh=jnp.where((l>=0)&(l<8), (jnp.where(l==doc,1.0,0.0)-minus)*scale, 0.0)
    return jnp.where(keep, base, oh)

def attn_fwd_pair(p, q_ref,k_ref,v_ref, ctx_ref, lse_ref, doc):
    cols=pl.ds(pl.multiple_of(p*128,128),128)
    lane=lax.broadcasted_iota(jnp.int32,(PACK,128),1)
    kp=k_ref[:,cols].astype(f32)
    vp=v_ref[:,cols]
    kk=[onehot_part(kp,lane,lo,doc,1.0,1.0).astype(bf16) for lo in (True,False)]
    laneb=lax.broadcasted_iota(jnp.int32,(QB,128),1)
    for b in range(PACK//QB):
        rows=pl.ds(b*QB,QB)
        qp=q_ref[rows,cols].astype(f32)*0.125
        docb=doc[b*QB:(b+1)*QB]
        outs=[]
        lse_old=lse_ref[rows,:]
        for h,lo in enumerate((True,False)):
            qa=onehot_part(qp,laneb,lo,docb,0.0,BIG).astype(bf16)
            s=dot(qa,kk[h],1,1)
            m=jnp.max(s,axis=1,keepdims=True)
            e=jnp.exp(s-m)
            l=jnp.sum(e,axis=1,keepdims=True)
            o=dot(e.astype(bf16),vp)
            outs.append(o/l)
            lse_old=jnp.where(laneb==2*p+h, m+jnp.log(l), lse_old)
        lse_ref[rows,:]=lse_old
        ctx_ref[rows,cols]=jnp.where(laneb<64,outs[0],outs[1]).astype(bf16)

def layer_norm(z):
    mu=jnp.mean(z,axis=-1,keepdims=True)
    c=z-mu
    r=lax.rsqrt(jnp.mean(c*c,axis=-1,keepdims=True)+NORM_EPS)
    return c*r, r

def ka_body(len_ref,x_ref,wa_ref,p_ref,q_ref,k_ref,v_ref,ctx_ref,lse_ref,hid_ref,r1_ref,w_ref):
    pltpu.sync_copy(wa_ref.at[pl.ds(0,4)],w_ref)
    doc=doc_column(len_ref,(PACK,1),0)
    for i,(o,b) in enumerate(((q_ref,0),(k_ref,None),(v_ref,1))):
        for t in range(4):
            rows=pl.ds(t*256,256)
            y=dot(x_ref[rows,:],w_ref[i])
            if b is not None: y=y+p_ref[b:b+1,:]
            o[rows,:]=y.astype(bf16)
    def body(p,c):
        attn_fwd_pair(p,q_ref,k_ref,v_ref,ctx_ref,lse_ref,doc)
        return c
    lax.fori_loop(0,6,body,0)
    for t in range(4):
        rows=pl.ds(t*256,256)
        z=x_ref[rows,:].astype(f32)+(dot(ctx_ref[rows,:],w_ref[3])+p_ref[2:3,:])
        n,r=layer_norm(z)
        hid_ref[rows,:]=n
        r1_ref[rows,:]=jnp.broadcast_to(r,(256,128))

def call_a(lengths,x,w,params):
    V=pltpu.VMEM
    return pl.pallas_call(ka_body,
        in_specs=[pl.BlockSpec(memory_space=pltpu.SMEM),pl.BlockSpec(memory_space=V),pl.BlockSpec(memory_space=pl.ANY),pl.BlockSpec(memory_space=V)],
        out_specs=[pl.BlockSpec(memory_space=V)]*7,
        out_shape=[jax.ShapeDtypeStruct((PACK,D),bf16)]*4+[jax.ShapeDtypeStruct((PACK,128),f32),jax.ShapeDtypeStruct((PACK,D),f32),jax.ShapeDtypeStruct((PACK,128),f32)],
        scratch_shapes=[V((4,D,D),bf16)],
        compiler_params=pltpu.CompilerParams(vmem_limit_bytes=60<<20))(lengths,x,w,params)

def gelu_both(x):
    z=jnp.abs(x)*0.7071067811865476
    t=1.0/(1.0+0.3275911*z)
    e=jnp.exp(-0.5*x*x)
    poly=t*(0.254829592+t*(-0.284496736+t*(1.421413741+t*(-1.453152027+t*1.061405429))))
    half=0.5*poly*e
    phi_c=jnp.where(x>=0,1.0-half,half)
    return x*phi_c, phi_c+x*(e*0.3989422804014327)

def kb_body(cot_ref,n1_ref,r1_ref,ctx_ref,w_ref,p_ref, out_ref,dz1_ref,dctx_ref,dwo_ref,dw1_ref,dw2_ref,vec_ref, act_ref,gp_ref,dffn_ref,hlow_ref):
    TT=256
    g1,s1,g2,s2=(p_ref[i:i+1,:] for i in (8,9,10,11))
    b2=p_ref[7:8,:]
    vec_ref[...]=jnp.zeros_like(vec_ref)
    def tile(t,carry):
        rows=pl.ds(pl.multiple_of(t*TT,TT),TT)
        n1=n1_ref[rows,:]
        hid=n1*g1+s1
        hl=hid.astype(bf16)
        hlow_ref[rows,:]=hl
        ffn=None
        for c in range(4):
            inner=dot(hl,w_ref[4+c])+p_ref[3+c:4+c,:]
            a,gp=gelu_both(inner)
            al=a.astype(bf16)
            act_ref[rows,pl.ds(c*D,D)]=al
            gp_ref[rows,pl.ds(c*D,D)]=gp.astype(gp_ref.dtype)
            y=dot(al,w_ref[8+c])
            ffn=y if ffn is None else ffn+y
        z=hid+(ffn+b2)
        n2,r2=layer_norm(z)
        out_ref[rows,:]=(n2*g2+s2).astype(bf16)
        e=cot_ref[rows,:].astype(f32)
        c2=e*g2
        dz2=r2*(c2-jnp.mean(c2,axis=-1,keepdims=True)-n2*jnp.mean(c2*n2,axis=-1,keepdims=True))
        dffn=dz2.astype(bf16)
        dffn_ref[rows,:]=dffn
        vec_ref[10:11,:]+=jnp.sum(e*n2,axis=0,keepdims=True)
        vec_ref[11:12,:]+=jnp.sum(e,axis=0,keepdims=True)
        vec_ref[7:8,:]+=jnp.sum(dffn.astype(f32),axis=0,keepdims=True)
        dh=dz2
        for c in range(4):
            dact=dot(dffn,w_ref[8+c],1,1)
            din=(dact*gp_ref[rows,pl.ds(c*D,D)].astype(f32)).astype(bf16)
            gp_ref[rows,pl.ds(c*D,D)]=din.astype(gp_ref.dtype)
            vec_ref[3+c:4+c,:]+=jnp.sum(din.astype(f32),axis=0,keepdims=True)
            dh=dh+dot(din,w_ref[4+c],1,1)
        vec_ref[8:9,:]+=jnp.sum(dh*n1,axis=0,keepdims=True)
        vec_ref[9:10,:]+=jnp.sum(dh,axis=0,keepdims=True)
        c1=dh*g1
        dz1=r1_ref[rows,0:1]*(c1-jnp.mean(c1,axis=-1,keepdims=True)-n1*jnp.mean(c1*n1,axis=-1,keepdims=True))
        dz1_ref[rows,:]=dz1
        dat=dz1.astype(bf16)
        vec_ref[2:3,:]+=jnp.sum(dat.astype(f32),axis=0,keepdims=True)
        dctx_ref[rows,:]=dot(dat,w_ref[3],1,1).astype(bf16)
        return carry
    lax.fori_loop(0,PACK//TT,tile,0)
    for c in range(4):
        dw2_ref[c]=dot(act_ref[:,c*D:(c+1)*D],dffn_ref[...],0,0).astype(bf16)
        dw1_ref[c]=dot(hlow_ref[...],gp_ref[:,c*D:(c+1)*D].astype(bf16),0,0).astype(bf16)
    dwo_ref[...]=dot(ctx_ref[...],dz1_ref[...].astype(bf16),0,0).astype(bf16)

def call_b(cot,n1,r1,ctx,w,params):
    V=pltpu.VMEM
    S=jax.ShapeDtypeStruct
    return pl.pallas_call(kb_body,
        in_specs=[pl.BlockSpec(memory_space=V)]*6,
        out_specs=[pl.BlockSpec(memory_space=V)]*7,
        out_shape=[S((PACK,D),bf16),S((PACK,D),f32),S((PACK,D),bf16),S((D,D),bf16),S((4,D,D),bf16),S((4,D,D),bf16),S((16,D),f32)],
        scratch_shapes=[V((PACK,FF),bf16),V((PACK,FF),bf16),V((PACK,D),bf16),V((PACK,D),bf16)],
        compiler_params=pltpu.CompilerParams(vmem_limit_bytes=62<<20))(cot,n1,r1,ctx,w,params)

def kc_body(len_ref,x_ref,q_ref,k_ref,v_ref,ctx_ref,do_ref,lse_ref,dz1_ref,wa_ref, ig_ref,dw_ref,vec_ref, dqkv_ref, dqa_ref,w_ref):
    pltpu.sync_copy(wa_ref.at[pl.ds(0,3)],w_ref)
    doc=doc_column(len_ref,(PACK,1),0)
    lane=lax.broadcasted_iota(jnp.int32,(PACK,128),1)
    KB_=256
    def pair(p,carry):
        cols=pl.ds(pl.multiple_of(p*128,128),128)
        qp=q_ref[:,cols].astype(f32); kp=k_ref[:,cols].astype(f32); vp=v_ref[:,cols].astype(f32)
        dop=do_ref[:,cols].astype(f32); cp=ctx_ref[:,cols].astype(f32)
        prod=dop*cp
        qa=[];qm=[];doa=[];dom=[];ka=[];km=[];va=[]
        for h,lo in enumerate((True,False)):
            keep=(lane<64) if lo else (lane>=64)
            off=64 if lo else 0
            lse=jnp.sum(jnp.where(lane==2*p+h,lse_ref[...],0.0),axis=1,keepdims=True)
            dd=jnp.sum(jnp.where(keep,prod,0.0),axis=1,keepdims=True)
            q1=onehot_part(qp*0.125,lane,lo,doc,0.0,BIG)
            for i,c in enumerate(split3(-lse)): q1=jnp.where(lane==off+8+i,c,q1)
            qa.append(q1.astype(bf16)); qm.append(jnp.where(keep,qp*0.125,0.0).astype(bf16))
            k1=onehot_part(kp,lane,lo,doc,1.0,1.0)
            k1=jnp.where((lane>=off+8)&(lane<off+11),1.0,k1)
            ka.append(k1.astype(bf16)); km.append(jnp.where(keep,kp*0.125,0.0).astype(bf16))
            d1=jnp.where(keep,dop,0.0)
            dom.append(d1.astype(bf16))
            for i,c in enumerate(split3(-dd)): d1=jnp.where(lane==off+i,c,d1)
            doa.append(d1.astype(bf16))
            v1=jnp.where(keep,vp,0.0); v1=jnp.where((lane>=off)&(lane<off+3),1.0,v1)
            va.append(v1.astype(bf16))
        for b in range(PACK//KB_):
            rows=slice(b*KB_,(b+1)*KB_)
            dv=None;dk=None;dq=None
            for h in range(2):
                s=dot(ka[h][rows],qa[h],1,1)
                pr=jnp.exp(s)
                dp=dot(va[h][rows],doa[h],1,1)
                ds=(pr*dp).astype(bf16)
                a=dot(pr.astype(bf16),dom[h]); dv=a if dv is None else dv+a
                a=dot(ds,qm[h]); dk=a if dk is None else dk+a
                a=dot(ds,km[h][rows],0,0); dq=a if dq is None else dq+a
            if b==0: dqa_ref[...]=dq
            else: dqa_ref[...]+=dq
            dqkv_ref[1,rows,cols]=dk.astype(bf16)
            dqkv_ref[2,rows,cols]=dv.astype(bf16)
        dqkv_ref[0,:,cols]=dqa_ref[...].astype(bf16)
        for i in range(3):
            d=dqkv_ref[i,:,cols]
            dw_ref[i,:,cols]=dot(x_ref[...],d,0,0).astype(bf16)
            vec_ref[i:i+1,cols]=jnp.sum(d.astype(f32),axis=0,keepdims=True)
        return carry
    lax.fori_loop(0,6,pair,0)
    for t in range(4):
        rows=pl.ds(t*256,256)
        acc=dz1_ref[rows,:]
        for i in range(3):
            acc=acc+dot(dqkv_ref[i,rows,:],w_ref[i],1,1)
        ig_ref[rows,:]=acc

def call_c(lengths,x,q,k,v,ctx,do,lse,dz1,w):
    V=pltpu.VMEM; S=jax.ShapeDtypeStruct
    return pl.pallas_call(kc_body,
        in_specs=[pl.BlockSpec(memory_space=pltpu.SMEM)]+[pl.BlockSpec(memory_space=V)]*8+[pl.BlockSpec(memory_space=pl.ANY)],
        out_specs=[pl.BlockSpec(memory_space=V)]*3,
        out_shape=[S((PACK,D),f32),S((3,D,D),bf16),S((8,D),f32)],
        scratch_shapes=[V((3,PACK,D),bf16),V((PACK,128),f32),V((3,D,D),bf16)],
        compiler_params=pltpu.CompilerParams(vmem_limit_bytes=62<<20))(lengths,x,q,k,v,ctx,do,lse,dz1,w)

RB=256
def diag_sum(blk):
    i=lax.broadcasted_iota(jnp.int32,blk.shape,0); j=lax.broadcasted_iota(jnp.int32,blk.shape,1)
    return jnp.sum(jnp.where(i==j,blk,0.0),keepdims=True)
def eye_rows(rb):
    i=lax.broadcasted_iota(jnp.int32,(RB,D),0)+rb*RB; j=lax.broadcasted_iota(jnp.int32,(RB,D),1)
    return i==j
def newton(m_ref,x_ref,nb_ref,pb_ref,sb_ref,xb_ref,between=lambda k: None):
    nblk=D//RB
    R=[slice(i*RB,(i+1)*RB) for i in range(nblk)]
    tot=jnp.zeros((1,1),f32); tr=jnp.zeros((1,1),f32)
    for i in range(nblk):
        blk=m_ref[R[i],:]
        tot=tot+jnp.sum(blk*blk,keepdims=True)
        tr=tr+diag_sum(blk[:,R[i]])
    c=jnp.sqrt(tot+1e-6)
    inv=1.0/c
    al=tr*inv/D
    s=lax.rsqrt(jnp.sqrt(c))
    for i in range(nblk):
        m_ref[R[i],:]=m_ref[R[i],:]*inv
    def iteration(k,al,be,first=False,last=False):
        u=5-al
        u2=u*u;u3=u2*u;u4=u2*u2
        c0=al*u4*(1/256); c1=(u4-4*al*u3)*(1/256); c2=(12*al*u2-8*u3)*(1/512)
        c3=(36*u2-24*al*u)*(1/1536); c4=(24*al-96*u)*(1/6144); c5=1/256
        for i in range(nblk):
            nb_ref[R[i],:]=jnp.where(eye_rows(i),m_ref[R[i],:]-al,m_ref[R[i],:]).astype(bf16)
            if not first: xb_ref[R[i],:]=jnp.where(eye_rows(i),x_ref[R[i],:]-be,x_ref[R[i],:]).astype(bf16)
        be2=jnp.zeros((1,1),f32); al2=jnp.zeros((1,1),f32)
        for i in range(nblk):
            n=jnp.where(eye_rows(i),m_ref[R[i],:]-al,m_ref[R[i],:])
            if not last:
                p=dot(nb_ref[R[i],:],nb_ref[...])
                pb_ref[R[i],:]=p.astype(bf16)
                m=c1*n+c2*p
                m_ref[R[i],:]=jnp.where(eye_rows(i),m+c0,m)
            if first:
                x=jnp.where(eye_rows(i),1.25-al*0.25,0.0)-0.25*n
            else:
                x=(1.25-al*0.25)*x_ref[R[i],:]-0.25*(be*n+dot(xb_ref[R[i],:],nb_ref[...]))
            x_ref[R[i],:]=x
            be2=be2+diag_sum(x[:,R[i]])
        if not last:
            for i in range(nblk):
                q=dot(nb_ref[R[i],:],pb_ref[...])
                sb_ref[R[i],:]=(c3*nb_ref[R[i],:].astype(f32)+c4*pb_ref[R[i],:].astype(f32)+c5*q).astype(bf16)
            for i in range(nblk):
                m=m_ref[R[i],:]+dot(pb_ref[R[i],:],sb_ref[...])
                m_ref[R[i],:]=m
                al2=al2+diag_sum(m[:,R[i]])
        return al2*(1/D),be2*(1/D)
    al,be=iteration(0,al,None,first=True)
    def step(k,ab):
        ab=iteration(k,*ab)
        between(k)
        return ab
    al,be=lax.fori_loop(1,7,step,(al,be))
    iteration(7,al,be,last=True)
    for i in range(nblk):
        x_ref[R[i],:]=x_ref[R[i],:]*s
def body(a_ref,x_ref,m_ref,nb,pb,sb,xb):
    m_ref[...]=a_ref[...]
    newton(m_ref,x_ref,nb,pb,sb,xb)
def call_newton(a):
    V=pltpu.VMEM
    return pl.pallas_call(body,in_specs=[pl.BlockSpec(memory_space=V)],out_specs=pl.BlockSpec(memory_space=V),
      out_shape=jax.ShapeDtypeStruct((D,D),f32),scratch_shapes=[V((D,D),f32)]+[V((D,D),bf16)]*4,
      compiler_params=pltpu.CompilerParams(vmem_limit_bytes=60<<20))(a)

NZ=4; MR=48; HC=384
MESH=pl.DeviceIdType.MESH
def rcopy(src,dst,ss,rs,dev):
    return pltpu.make_async_remote_copy(src_ref=src,dst_ref=dst,send_sem=ss,recv_sem=rs,device_id=dev,device_id_type=MESH)

class Place:
    def __init__(self):
        self.dp=lax.axis_index("dp"); self.head=lax.axis_index("head")
        self.z=self.dp//2; self.x=self.dp%2; self.y=self.head//2; self.c=self.head%2
        self.xy=self.x*2+self.y
        self.chip=self.z*4+self.xy
        self.me=self.dp*4+self.head
        self.xn=((self.dp//2)*2+(1-self.x), self.head)
        self.yn=(self.dp,(1-self.y)*2+self.c)
        self.sib=(self.dp,self.y*2+(1-self.c))
        self.cols=pl.ds(pl.multiple_of(self.c*HC,128),HC)
        self.ocols=pl.ds(pl.multiple_of((1-self.c)*HC,128),HC)
    def zpeer(self,k):
        return (((self.z+k)%NZ)*2+self.x,self.head)
    def zfrom(self,k):
        return (self.z+NZ-k)%NZ
    def neighbours(self):
        return [self.zpeer(1),self.zpeer(2),self.zpeer(3),self.xn,self.yn,self.sib]

def greet(devs):
    bar=pltpu.get_barrier_semaphore()
    for d in devs:
        pl.semaphore_signal(bar,inc=1,device_id=d,device_id_type=MESH)
    pl.semaphore_wait(bar,len(devs))

def greet_all(pc):
    bar=pltpu.get_barrier_semaphore()
    def sig(k,carry):
        t=(pc.me+k)%32
        pl.semaphore_signal(bar,inc=1,device_id=(t//4,t%4),device_id_type=MESH)
        return carry
    lax.fori_loop(1,32,sig,0)
    pl.semaphore_wait(bar,31)

class Gather:
    def __init__(self,pc,at,ss,rs,whole=False):
        self.pc,self.at,self.ss,self.rs,self.whole=pc,at,ss,rs,whole
    def region(self,z,xy,mine=True):
        pc=self.pc
        return self.at(z,xy,pc.cols if mine else pc.ocols)
    def copies(self):
        pc=self.pc; al=pl.ds(0,4); lo=pl.ds(0,2); hi=pl.ds(2,2)
        xo=(1-pc.x)*2+pc.y; yo=pc.x*2+(1-pc.y); dg=(1-pc.x)*2+(1-pc.y)
        R=self.region
        def mk(i,src,dst,dev):
            return rcopy(src(),dst(),self.ss.at[i],self.rs.at[i],dev)
        send={}; recv={}
        for k in (1,2,3):
            send[k-1]=(partial(R,pc.z,pc.xy),pc.zpeer(k)); recv[k-1]=partial(R,pc.zfrom(k),pc.xy)
        send[3]=(partial(R,al,pc.xy),pc.xn); send[4]=(partial(R,al,pc.xy),pc.yn)
        send[5]=(partial(R,hi,yo),pc.xn); send[6]=(partial(R,lo,xo),pc.yn)
        recv[3]=partial(R,al,xo); recv[4]=partial(R,al,yo); recv[5]=partial(R,hi,dg); recv[6]=partial(R,lo,dg)
        if self.whole:
            send[7]=(partial(R,al,al),pc.sib); recv[7]=partial(R,al,al,False)
        else:
            for i,xy in ((7,pc.xy),(8,xo),(9,yo),(10,dg)):
                send[i]=(partial(R,al,xy),pc.sib); recv[i]=partial(R,al,xy,False)
        self.send={i:partial(mk,i,s,s,d) for i,(s,d) in send.items()}
        self.recv={i:partial(mk,i,s,s,pc.sib) for i,s in recv.items()}
        return self
    def start(self,*which):
        for i in which:
            if i in self.send and not (self.whole and i>6): self.send[i]().start()
    def step0(self): self.start(0,1,2)
    def step1(self):
        for i in (0,1,2): self.recv[i]().wait_recv()
        self.start(3,4,7)
    def step2(self):
        self.recv[3]().wait_recv()
        self.start(6,8)
        self.recv[4]().wait_recv()
        self.start(5,9)
    def step3(self):
        for i in (5,6): self.recv[i]().wait_recv()
        if self.whole: self.send[7]().start()
        else: self.start(10)
    def step4(self):
        for i in self.recv:
            if i>6: self.recv[i]().wait_recv()
    def done(self):
        for i in self.send: self.send[i]().wait_send()
    def step(self,i):
        (self.step0,self.step1,self.step2,self.step3,self.step4)[i]()

ORDER=(0,1,2,3,4,8,5,9,6,10,7,11)
def ag_body(mas_ref,pv_ref,left_ref,right_ref, w_ref,pg_ref,st_ref, sibm,ss,rs,cs,cr,ts,tr,lsem):
    pc=Place()
    greet_all(pc)
    half=rcopy(mas_ref.at[:,:,pc.ocols],sibm,cs,cr,pc.sib)
    half.start()
    def stat(b,act):
        t=(b%4)*4+b//4
        for side,ref in enumerate((left_ref,right_ref)):
            dev=((t//2),(t%2)*2+side)
            idx=b*2+side
            mine=(pc.chip==t)&(pc.c==side)
            act(idx,ref.at[b],dev,mine)
    half.wait_recv()
    lo=pl.ds(0,24); hi=pl.ds(24,24)
    for b in ORDER:
        own=mas_ref[b,:,pc.cols]; oth=sibm[b]
        first=jnp.where(pc.c==0,own,oth); second=jnp.where(pc.c==0,oth,own)
        w_ref[b,pc.z,pc.xy,:,pc.cols]=jnp.concatenate([first,second],axis=0).astype(bf16)
    pg_ref[pc.z,pc.xy,:,pc.cols]=pv_ref[...]
    half.wait_send()
    gs=[]
    for t in range(len(gs)+4):
        for s in range(5):
            if 0<=t-s<len(gs): gs[t-s].step(s)
    def start(b,carry):
        def act(idx,src,dev,mine):
            @pl.when(mine)
            def _(): pltpu.make_async_copy(src,st_ref.at[pc.me],tr).start()
            @pl.when(jnp.logical_not(mine))
            def _(): rcopy(src,st_ref.at[pc.me],ts.at[idx],tr,dev).start()
        stat(b,act)
        return carry
    lax.fori_loop(0,NB,start,0)
    for g in gs: g.done()
    def fin(b,carry):
        def act(idx,src,dev,mine):
            @pl.when(jnp.logical_not(mine))
            def _(): rcopy(src,st_ref.at[pc.me],ts.at[idx],tr,dev).wait_send()
        stat(b,act)
        return carry
    lax.fori_loop(0,NB,fin,0)
    @pl.when(pc.xy<3)
    def _(): pltpu.make_async_copy(st_ref,st_ref,tr).wait()

def call_ag(masters,pv,left,right):
    V=pltpu.VMEM; S=jax.ShapeDtypeStruct; A=pl.ANY
    B=lambda m: pl.BlockSpec(memory_space=m)
    sem=pltpu.SemaphoreType.DMA
    return pl.pallas_call(ag_body,in_specs=[B(V),B(V),B(A),B(A)],out_specs=[B(V),B(V),B(A)],
        out_shape=[S((NB,4,4,MR,D),bf16),S((4,4,16,D),bf16),S((32,24,D),f32)],
        scratch_shapes=[V((NB,24,HC),f32),sem((13,11)),sem((13,11)),sem,sem,sem((24,)),sem,sem],
        compiler_params=pltpu.CompilerParams(vmem_limit_bytes=60<<20,collective_id=0,has_side_effects=True))(masters,pv,left,right)

def params_of(pg):
    t=pg.reshape(16,16,2,HC)[:,:12,:,:24]
    return jnp.transpose(t,(1,0,2,3)).reshape(12,D).astype(f32)


class Scatter:
    def __init__(self,pc,b,g_ref,R,out_ref,gown_ref,ss,rs,os_,orr):
        self.pc,self.b,self.g=pc,b,g_ref.at[b]
        self.out,self.gown=out_ref,gown_ref
        self.os_,self.orr=os_,orr
        self.R={k:v.at[b] for k,v in R.items()}
        R=self.R
        s1,rc=R["s1"],R["rc"]
        def mk(i,src,dst,dev): return rcopy(src,dst,ss.at[b,i],rs.at[b,i],dev)
        lo=pl.ds(0,2); hi=pl.ds(2,2); al=pl.ds(0,4)
        self.core=mk(0,self.g.at[:,:,:,pc.ocols],rc,pc.sib)
        self.xa=mk(1,s1.at[lo,pl.ds((1-pc.x)*2,2)],R["xa"],pc.xn)
        self.yb=[mk(2+i,s1.at[hi,i*2+1-pc.y],R["yb"].at[i],pc.yn) for i in range(2)]
        self.ya=mk(4,R["s2a"],R["ya"],pc.yn)
        self.xb=mk(5,R["s2b"],R["xb"],pc.xn)
        self.zz=[mk(6+k-1,R["s3"].at[(pc.z+k)%NZ],R["zr"].at[k-1],pc.zpeer(k)) for k in (1,2,3)]
        self.home=mk(9,R["fin"].at[pl.ds(pl.multiple_of((1-pc.c)*24,8),24)],R["hr"],pc.sib)
        t=(b%4)*4+b//4
        self.t=t
        self.owner=[((t//2),(t%2)*2+side) for side in range(2)]
        self.to_owner=[rcopy(R["finb"],gown_ref.at[pc.chip,:,pc.cols],os_.at[b,side],orr,self.owner[side]) for side in range(2)]
        self.to_self=pltpu.make_async_copy(R["finb"],gown_ref.at[pc.chip,:,pc.cols],orr)
    def step0(self):
        self.core.start()
    def step1(self):
        pc=self.pc; R=self.R
        self.core.wait_recv()
        for z in range(4):
            R["s1"][z]=(self.g[z,:,:,pc.cols].astype(f32)+R["rc"][z].astype(f32)).astype(bf16)
        self.xa.start()
        for d in self.yb: d.start()
    def step2(self):
        pc=self.pc; R=self.R
        self.xa.wait_recv()
        s=R["s1"][0:2,pl.ds(pc.x*2,2)].astype(f32)+R["xa"][...].astype(f32)
        keep=jnp.where(pc.y==0,s[:,0],s[:,1]); give=jnp.where(pc.y==0,s[:,1],s[:,0])
        R["k2"][0:2]=keep; R["s2a"][...]=give.astype(bf16)
        self.ya.start()
        for d in self.yb: d.wait_recv()
        s0=R["s1"][2:4,pc.y].astype(f32)+R["yb"][0].astype(f32)
        s1=R["s1"][2:4,2+pc.y].astype(f32)+R["yb"][1].astype(f32)
        keep=jnp.where(pc.x==0,s0,s1); give=jnp.where(pc.x==0,s1,s0)
        R["k2"][2:4]=keep; R["s2b"][...]=give.astype(bf16)
        self.xb.start()
    def step3(self):
        R=self.R
        self.ya.wait_recv(); self.xb.wait_recv()
        a=R["k2"][0:2]+R["ya"][...].astype(f32)
        b=R["k2"][2:4]+R["xb"][...].astype(f32)
        R["k2"][0:2]=a; R["k2"][2:4]=b
        R["s3"][0:2]=a.astype(bf16); R["s3"][2:4]=b.astype(bf16)
        for d in self.zz: d.start()
    def step4(self):
        pc=self.pc; R=self.R
        for d in self.zz: d.wait_recv()
        s=R["k2"][pc.z]
        for k in range(3): s=s+R["zr"][k].astype(f32)
        R["fin"][...]=s
        R["finb"][...]=s.astype(bf16)
        self.home.start()
        @pl.when(pc.chip==self.t)
        def _():
            self.to_self.start()
            for side in range(2):
                @pl.when(pc.c!=side)
                def _(): self.to_owner[side].start()
        @pl.when(pc.chip!=self.t)
        def _():
            for d in self.to_owner: d.start()
    def step5(self):
        pc=self.pc; R=self.R
        self.home.wait_recv()
        own=R["fin"][pl.ds(pl.multiple_of(pc.c*24,8),24)]; oth=R["hr"][...]
        self.out[self.b,:,pc.cols]=own
        self.out[self.b,:,pc.ocols]=oth
    def step(self,i): (self.step0,self.step1,self.step2,self.step3,self.step4,self.step5)[i]()
    def done(self):
        pc=self.pc
        for d in [self.core,self.xa,*self.yb,self.ya,self.xb,*self.zz,self.home]: d.wait_send()
        @pl.when(pc.chip==self.t)
        def _():
            for side in range(2):
                @pl.when(pc.c!=side)
                def _(): self.to_owner[side].wait_send()
        @pl.when(pc.chip!=self.t)
        def _():
            for d in self.to_owner: d.wait_send()

def scatter_scratch(nb=NB):
    V=pltpu.VMEM
    return dict(s1=V((nb,4,4,MR,HC),bf16),rc=V((nb,4,4,MR,HC),bf16),xa=V((nb,2,2,MR,HC),bf16),yb=V((nb,2,2,MR,HC),bf16),
        s2a=V((nb,2,MR,HC),bf16),s2b=V((nb,2,MR,HC),bf16),ya=V((nb,2,MR,HC),bf16),xb=V((nb,2,MR,HC),bf16),
        k2=V((nb,4,MR,HC),f32),s3=V((nb,4,MR,HC),bf16),zr=V((nb,3,MR,HC),bf16),fin=V((nb,MR,HC),f32),finb=V((nb,MR,HC),bf16),hr=V((nb,24,HC),f32))

class VecSum:
    def __init__(self,pc,cur,buf,ss,rs):
        self.pc,self.cur,self.buf=pc,cur,buf
        zp=lambda bit: ((pc.z^bit)*2+pc.x,pc.head)
        z1=(pc.z+1-2*(pc.z%2)); z2=(pc.z+2)%4
        partners=[pc.sib,pc.xn,pc.yn,(z1*2+pc.x,pc.head),(z2*2+pc.x,pc.head)]
        self.d=[rcopy(cur.at[i],buf.at[i],ss.at[i],rs.at[i],p) for i,p in enumerate(partners)]
    def step(self,i):
        if i>0:
            self.d[i-1].wait_recv()
            self.cur[i]=self.cur[i-1]+self.buf[i-1]
        if i<5: self.d[i].start()
    def done(self):
        for d in self.d: d.wait_send()

RSORDER=(8,4,9,5,10,6,11,7,3,2,1,0)
KEYS=list(scatter_scratch())
def rs_body(g_ref,vec_ref,out_ref,vout_ref,gown_ref,*rest):
    R=dict(zip(KEYS,rest[:len(KEYS)])); vcur,vbuf,ss,rs,os_,orr,vs,vr=rest[len(KEYS):]
    pc=Place()
    greet_all(pc)
    vcur[0]=vec_ref[...]
    vsum=VecSum(pc,vcur,vbuf,vs,vr)
    sc=[Scatter(pc,b,g_ref,R,out_ref,gown_ref,ss,rs,os_,orr) for b in RSORDER]
    for t in range(len(sc)+5):
        for s in range(6):
            if 0<=t-s<len(sc): sc[t-s].step(s)
        if t<=5: vsum.step(t)
    vout_ref[...]=vcur[5]
    for s in sc: s.done()
    vsum.done()
    @pl.when(pc.xy<3)
    def _(): pltpu.make_async_copy(gown_ref,gown_ref,orr).wait()

def call_rs(g,vec):
    V=pltpu.VMEM; S=jax.ShapeDtypeStruct
    B=pl.BlockSpec(memory_space=V); sem=pltpu.SemaphoreType.DMA
    return pl.pallas_call(rs_body,in_specs=[B,B],out_specs=[B,B,B],
        out_shape=[S((NB,24,D),f32),S((16,D),f32),S((16,MR,D),bf16)],
        scratch_shapes=list(scatter_scratch().values())+[V((6,16,D),f32),V((5,16,D),f32),sem((NB,10)),sem((NB,10)),sem((NB,2)),sem,sem((5,)),sem((5,))],
        compiler_params=pltpu.CompilerParams(vmem_limit_bytes=62<<20,collective_id=1,has_side_effects=True))(g,vec)

BETA=0.95; BETA_TWO=0.99; RATE=1.0; RATE_VEC=0.05

def owner_of(b):
    return ((b//3+(b%3)%2+1)%4)*4+b%3
def owned_by(pc):
    return 3*((pc.z+3-pc.xy%2)%4)+pc.xy

def pack(rows):
    return jnp.concatenate([rows[:,:HC],rows[:,HC:]],axis=0).astype(bf16)
def unpack(p):
    p=p.astype(f32)
    return jnp.concatenate([p[:24],p[24:]],axis=1)

def send_row(pc,t,src,dst,ssem,rsem):
    @pl.when(t==pc.me)
    def _(): pltpu.make_async_copy(src,dst,rsem).start()
    @pl.when(t!=pc.me)
    def _(): rcopy(src,dst,ssem,rsem,(t//4,t%4)).start()

def send_rows(pc,n,base,slots,dst,ss,rsem,start):
    def one(j,carry):
        t=base+j
        @pl.when(t==pc.me)
        def _():
            if start: pltpu.make_async_copy(slots.at[j],dst,rsem).start()
        @pl.when(t!=pc.me)
        def _():
            d=rcopy(slots.at[j],dst,ss.at[j],rsem,(t//4,t%4))
            if start: d.start()
            else: d.wait_send()
        return carry
    lax.fori_loop(0,n,one,0)

def newton_body(ghalf_ref,statl_ref,statr_ref,left_ref,right_ref,mas_ref,va_ref,vec_ref,sec_ref,
                ln_ref,rn_ref,mn_ref,vg_ref,sn_ref,vn_ref,
                m_ref,x_ref,nb,pb,sb,xb,slots,ggr,uslots,ur,tb,rt,rho,gown_ref,vcur,vbuf,gg, gs,gr,us,ur_sem,es,er,vs,vr):
    pc=Place()
    gown_ref[:,pc.cols]=ghalf_ref[...]
    vcur[0]=va_ref[...]
    greet_all(pc)
    vsum=VecSum(pc,vcur,vbuf,vs,vr)
    vsum.step(0)
    b=owned_by(pc)
    owner=pc.xy<3
    nblk=D//RB
    swap=lambda: rcopy(gown_ref.at[:,pc.cols],gown_ref.at[:,pc.cols],es.at[3],er.at[3],pc.sib)
    @pl.when(owner)
    def _(): swap().start()
    vsum.step(1)
    @pl.when(owner)
    def _():
        @pl.when(pc.c==0)
        def _():
            for i in range(nblk):
                r=slice(i*RB,(i+1)*RB)
                gg[r,:]=(1-BETA)*dot(ghalf_ref[r,:],ghalf_ref[...],1,1)
            swap().wait_recv()
            for i in range(nblk):
                r=slice(i*RB,(i+1)*RB)
                p=gg[r,:]+(1-BETA)*dot(gown_ref[r,HC:],gown_ref[:,HC:],1,1)
                gg[r,:]=p
                m_ref[r,:]=BETA*statl_ref[r,:]+p
        @pl.when(pc.c==1)
        def _():
            swap().wait_recv()
            for i in range(nblk):
                r=slice(i*RB,(i+1)*RB)
                p=(1-BETA)*dot(gown_ref[:,r],gown_ref[...],0,0)
                gg[r,:]=p
                m_ref[r,:]=BETA*statr_ref[r,:]+p
        def between(k):
            def piece(t,carry):
                slots[t]=pack(gg[pl.ds(pl.multiple_of(t*24,8),24),:])
                send_row(pc,t,slots.at[t],ggr.at[2*b+pc.c],gs.at[t],gr)
                return carry
            @pl.when(k<3)
            def _(): lax.fori_loop((k-1)*16,k*16,piece,0)
            @pl.when(k==2)
            def _(): vsum.step(2)
            @pl.when(k==4)
            def _(): vsum.step(3)
            @pl.when(k==6)
            def _(): vsum.step(4)
        newton(m_ref,x_ref,nb,pb,sb,xb,between)
        tr=jnp.zeros((1,1),f32)
        for i in range(nblk):
            r=slice(i*RB,(i+1)*RB); tr=tr+diag_sum(x_ref[r,r])
        lam=tr*(1/D)
        for i in range(nblk):
            r=slice(i*RB,(i+1)*RB)
            xb[r,:]=jnp.where(eye_rows(i),x_ref[r,:]-lam,x_ref[r,:]).astype(bf16)
        H=D//2
        send_t=rcopy(tb.at[pl.ds(H,H)],tb.at[pl.ds(H,H)],es.at[0],er.at[0],pc.sib)
        send_r=rcopy(xb,rt,es.at[1],er.at[1],pc.sib)
        send_l=rcopy(rho.at[0],rho.at[1],es.at[2],er.at[2],pc.sib)
        def update(trows,right,lam_r):
            for i in range(2):
                r=pl.ds(trows+i*192,192)
                t=tb[r,:]
                m_ref[pl.ds(i*192,192),:]=lam_r*t.astype(f32)+dot(t,right[...])
        rho[0]=jnp.broadcast_to(lam,(8,128))
        @pl.when(pc.c==0)
        def _():
            for h in (1,0):
                for i in range(2):
                    r=slice(h*H+i*192,h*H+(i+1)*192)
                    tb[r,:]=(lam*gown_ref[r,:].astype(f32)+dot(xb[r,:],gown_ref[...])).astype(bf16)
                if h==1: send_t.start()
            send_r.wait_recv(); send_l.wait_recv()
            update(0,rt,rho[1,0:1,0:1])
            send_t.wait_send()
        @pl.when(pc.c==1)
        def _():
            send_r.start(); send_l.start()
            send_t.wait_recv()
            update(H,xb,lam)
            send_r.wait_send(); send_l.wait_send()
        def pk2(i,carry):
            uslots[i]=pack(m_ref[pl.ds(pl.multiple_of(i*24,8),24),:])
            send_row(pc,pc.c*16+i,uslots.at[i],ur.at[b],us.at[i],ur_sem)
            return carry
        lax.fori_loop(0,16,pk2,0)
    @pl.when(jnp.logical_not(owner))
    def _():
        for i in (2,3,4): vsum.step(i)
    vsum.step(5)
    r=lax.broadcasted_iota(jnp.int32,(D,128),1); j=lax.broadcasted_iota(jnp.int32,(D,128),0)
    pick=jnp.where((j==pc.me*24+r)&(r<24),1.0,0.0).astype(f32)
    vg=lax.dot_general(vcur[5],pick,(((1,),(0,)),((),())),precision=lax.Precision.HIGHEST,preferred_element_type=f32)[:12,:24]
    sn=BETA_TWO*sec_ref[...]+(1-BETA_TWO)*vg*vg
    vg_ref[...]=vg; sn_ref[...]=sn
    vn_ref[...]=vec_ref[...]-RATE_VEC*vg/(jnp.sqrt(sn)+1e-8)
    pltpu.make_async_copy(ggr,ggr,gr).wait()
    def stats(i,carry):
        ln_ref[i]=BETA*left_ref[i]+unpack(ggr[2*i])
        rn_ref[i]=BETA*right_ref[i]+unpack(ggr[2*i+1])
        return carry
    lax.fori_loop(0,NB,stats,0)
    pltpu.make_async_copy(ur,ur,ur_sem).wait()
    def upd(i,carry):
        mn_ref[i]=mas_ref[i]-RATE*unpack(ur[i])
        return carry
    lax.fori_loop(0,NB,upd,0)
    @pl.when(owner)
    def _():
        swap().wait_send()
        send_rows(pc,32,0,slots,ggr.at[2*b+pc.c],gs,gr,False)
        send_rows(pc,16,pc.c*16,uslots,ur.at[b],us,ur_sem,False)
    vsum.done()

def call_newton_step(gown,statl,statr,left,right,mas,va,vec,sec):
    V=pltpu.VMEM; S=jax.ShapeDtypeStruct
    B=pl.BlockSpec(memory_space=V); sem=pltpu.SemaphoreType.DMA
    rows=S((NB,24,D),f32); small=S((NB,24),f32)
    return pl.pallas_call(newton_body,in_specs=[B]*9,out_specs=[B]*6,out_shape=[rows]*3+[small]*3,
        scratch_shapes=[V((D,D),f32)]*2+[V((D,D),bf16)]*4+[V((32,48,HC),bf16),V((24,48,HC),bf16),V((16,48,HC),bf16),V((12,48,HC),bf16),V((D,D),bf16),V((D,D),bf16),V((2,8,128),f32),V((D,D),bf16),V((6,16,D),f32),V((5,16,D),f32),V((D,D),f32),
            sem((32,)),sem,sem((16,)),sem,sem((4,)),sem((4,)),sem((5,)),sem((5,))],
        compiler_params=pltpu.CompilerParams(vmem_limit_bytes=62<<20,collective_id=2,has_side_effects=True))(gown,statl,statr,left,right,mas,va,vec,sec)


def place_params(pg_ref,p_ref):
    r=lax.broadcasted_iota(jnp.int32,(128,D),0); j=lax.broadcasted_iota(jnp.int32,(128,D),1)
    p_ref[...]=jnp.zeros_like(p_ref)
    def chip(m,carry):
        for c in range(2):
            sel=jnp.where((j==(m*2+c)*24+r)&(r<24),1.0,0.0).astype(bf16)
            p_ref[...]+=dot(pg_ref[m//4,m%4,:,c*HC:c*HC+128],sel)
        return carry
    lax.fori_loop(0,16,chip,0)

def keys_of_pair(p,k_ref,ka_ref,v_ref,va_ref,doc_ref):
    cols=pl.ds(pl.multiple_of(p*128,128),128)
    lane=lax.broadcasted_iota(jnp.int32,(256,128),1)
    for t in range(PACK//256):
        rows=pl.ds(t*256,256)
        kp=k_ref[rows,cols].astype(f32); vp=v_ref[rows,cols].astype(f32)
        doc=doc_ref[rows,:]
        for h,lo in enumerate((True,False)):
            off=64 if lo else 0
            k1=onehot_part(kp,lane,lo,doc,1.0,1.0)
            ka_ref[h,rows,:]=jnp.where((lane>=off+8)&(lane<off+11),1.0,k1).astype(bf16)
            va_ref[h,rows,:]=jnp.where((lane<64)==lo,vp,1.0).astype(bf16)

QF=512
def attend_block(p,b,q_ref,ka_ref,va_ref,qa_ref,ctx_ref,doc_ref):
    cols=pl.ds(pl.multiple_of(p*128,128),128)
    rows=pl.ds(pl.multiple_of(b*QF,QF),QF)
    lane=lax.broadcasted_iota(jnp.int32,(QF,128),1)
    low=lane<64
    qp=q_ref[rows,cols].astype(f32)*0.125
    doc=doc_ref[rows,:]
    qf=[onehot_part(qp,lane,lo,doc,0.0,BIG) for lo in (True,False)]
    ss=[dot(qf[h].astype(bf16),ka_ref[h],1,1) for h in range(2)]
    os=[]
    for h,lo in enumerate((True,False)):
        off=64 if lo else 0
        m=jnp.max(ss[h],axis=1,keepdims=True)
        o=dot(jnp.exp(ss[h]-m).astype(bf16),va_ref[h])
        os.append(o)
        q1=qf[h]
        for i,c in enumerate(split3(-(m+jnp.log(o)))): q1=jnp.where(lane==off+8+i,c,q1)
        qa_ref[h,rows,:]=q1.astype(bf16)
    l=pltpu.roll(jnp.where(low,os[1],os[0]),64,1)
    ctx_ref[rows,cols]=(jnp.where(low,os[0],os[1])/l).astype(bf16)

class StatMove:
    def __init__(self,pc,src,dst,side,ss,rsem):
        self.pc,self.src,self.dst,self.side,self.ss,self.rsem=pc,src,dst,side,ss,rsem
    def move(self,i,start):
        pc=self.pc
        b=(i+pc.me)%NB
        t=owner_of(b)
        src,dst=self.src.at[b],self.dst.at[pc.me]
        mine=(pc.chip==t)&(pc.c==self.side)
        if start:
            @pl.when(mine)
            def _(): pltpu.make_async_copy(src,dst,self.rsem).start()
        @pl.when(jnp.logical_not(mine))
        def _():
            d=rcopy(src,dst,self.ss.at[b],self.rsem,(t//2,(t%2)*2+self.side))
            if start: d.start()
            else: d.wait_send()
    def done(self):
        pc=self.pc
        lax.fori_loop(0,NB,lambda i,c: (self.move(i,False),c)[1],0)
        @pl.when((pc.xy<3)&(pc.c==self.side))
        def _(): pltpu.make_async_copy(self.dst,self.dst,self.rsem).wait()

AORDER=(0,1,2,3,4,8,5,9,6,10,7,11)
TT=512
def front_body(len_ref,x_ref,cot_ref,mas_ref,pv_ref,left_ref,
               out_o,qa_o,ka_o,v_o,ctx_o,act_o,din_o,dffn_o,ht_o,dz1_o,dctx_o,wq_o,xt_o,vec_o,st_ref,
               w_ref,pg_ref,p_ref,sibm,q,k,v,ctx,doc,qa,ka,va,n1,r1,hlow,acc,act,gp,dffn,dctx,out,xt,
               ss,rs,cs,cr,ts,tr,lsem,asem,osem):
    pc=Place()
    greet_all(pc)
    first=rcopy(mas_ref.at[pl.ds(0,3),:,pc.ocols],sibm.at[pl.ds(0,3)],cs.at[0],cr.at[0],pc.sib)
    other=rcopy(mas_ref.at[pl.ds(3,9),:,pc.ocols],sibm.at[pl.ds(3,9)],cs.at[1],cr.at[1],pc.sib)
    first.start(); other.start()
    pg_ref[pc.z,pc.xy,:,pc.cols]=pv_ref[...]
    def stacked(own,oth):
        upper=jnp.where(pc.c==0,own,oth); lower=jnp.where(pc.c==0,oth,own)
        return jnp.concatenate([upper,lower],axis=0).astype(bf16)
    def assemble(places):
        for pos in places:
            if pos<3:
                for i in range(3):
                    own=mas_ref[i,:,pl.ds(pl.multiple_of((pc.c*3+pos)*128,128),128)]
                    w_ref[pos,pc.z,pc.xy,:,pl.ds(pl.multiple_of(pc.c*HC+i*128,128),128)]=stacked(own,sibm[i,:,pos*128:(pos+1)*128])
            else:
                w_ref[pos,pc.z,pc.xy,:,pc.cols]=stacked(mas_ref[AORDER[pos],:,pc.cols],sibm[AORDER[pos]])
    NG=10
    def single(g,pos,whole):
        return Gather(pc,lambda z,xy,cols: w_ref.at[pos,z,xy,:,cols],ss.at[g],rs.at[g],whole).copies()
    def double(g):
        return Gather(pc,lambda z,xy,cols: w_ref.at[pl.ds(4+2*(g-5),2),z,xy,:,cols],ss.at[g],rs.at[g],True).copies()
    def on_group(g,act):
        if isinstance(g,int):
            if g==0: act(Gather(pc,lambda z,xy,cols: pg_ref.at[z,xy,:,cols],ss.at[0],rs.at[0]).copies())
            elif g<4: act(single(g,g-1,False))
            elif 5<=g<8: act(double(g))
            else: act(single(g,3 if g==4 else g+2,True))
        else:
            @pl.when((g>=1)&(g<4))
            def _(): act(single(g,g-1,False))
            @pl.when((g>=5)&(g<8))
            def _(): act(double(g))
            @pl.when((g==4)|((g>=8)&(g<NG)))
            def _(): act(single(g,g-1+3*(g//8),True))
    def tick(t):
        for s,d in ((0,-3),(1,0),(2,1),(3,2),(4,3)):
            if isinstance(t,int):
                if 0<=t-d<NG and not (s==0 and t<1): on_group(t-d,lambda g: g.step(s))
            else: on_group(t-d,lambda g: g.step(s))
    stats=StatMove(pc,left_ref,st_ref,0,ts,tr)
    copies=[]
    def away(src,dst):
        i=len(copies)
        c=pltpu.make_async_copy(src,dst,lsem.at[i]); c.start(); copies.append(c)
    W=lambda pos: w_ref[pos].reshape(D,D)
    on_group(0,lambda g: g.step(0))
    first.wait_recv()
    for i in range(3):
        assemble([i])
        on_group(i+1,lambda g: g.step(0))
    other.wait_recv()
    assemble(range(3,12))
    for i in range(6): xt[i*128:(i+1)*128,:]=x_ref[:,i*128:(i+1)*128].T
    xcopy=pltpu.make_async_copy(xt,xt_o,lsem.at[21]); xcopy.start()
    for t in range(4): tick(t)
    place_params(pg_ref,p_ref)
    t_=lax.broadcasted_iota(jnp.int32,(PACK,128),0)
    end=jnp.int32(0); dd=jnp.zeros((PACK,128),jnp.int32)
    for j in range(8):
        end=end+len_ref[0,j]
        dd=dd+(t_>=end).astype(jnp.int32)
    doc[...]=dd
    tick(4)
    def project(j):
        for tl in range(2):
            rows=pl.ds(tl*512,512)
            y=dot(x_ref[rows,:],W(j))
            for c in range(2):
                cols=pl.ds(pl.multiple_of((3*c+j)*128,128),128)
                for i,(o,b) in enumerate(((q,0),(k,None),(v,1))):
                    t=y[:,c*HC+i*128:c*HC+(i+1)*128]
                    if b is not None: t=t+p_ref[b:b+1,cols]
                    o[rows,cols]=t.astype(bf16)
    def pair_copies(pi):
        return [pltpu.make_async_copy(s.at[pi%2],d.at[pi],asem.at[i,pi%2]) for i,(s,d) in enumerate(((qa,qa_o),(ka,ka_o)))]
    def slot(n,carry):
        pi=n//2; b=n%2; p=3*(pi%2)+pi//2; side=pi%2
        @pl.when(n%4==0)
        def _(): project(n//4)
        @pl.when(b==0)
        def _():
            @pl.when(pi>=2)
            def _():
                for c in pair_copies(pi-2): c.wait()
            keys_of_pair(p,k,ka.at[side],v,va,doc)
        attend_block(p,b,q,ka.at[side],va,qa.at[side],ctx,doc)
        @pl.when(b==1)
        def _():
            for c in pair_copies(pi): c.start()
            @pl.when((pi==0)|(pi%2==1))
            def _(): tick(5+(pi+1)//2)
        return carry
    lax.fori_loop(0,12,slot,0)
    away(ctx,ctx_o); away(v,v_o)
    for i in range(3): away(w_ref.at[i],wq_o.at[i])
    g1,s1,g2,s2=(p_ref[i:i+1,:] for i in (8,9,10,11))
    vec_o[...]=jnp.zeros_like(vec_o)
    def out_proj(tl,carry):
        rows=pl.ds(pl.multiple_of(tl*TT,TT),TT)
        z=x_ref[rows,:].astype(f32)+(dot(ctx[rows,:],W(3))+p_ref[2:3,:])
        n,r=layer_norm(z)
        n1[rows,:]=n
        r1[rows,:]=jnp.broadcast_to(r,(TT,128))
        hlow[rows,:]=(n*g1+s1).astype(bf16)
        return carry
    lax.fori_loop(0,PACK//TT,out_proj,0)
    xcopy.wait()
    for i in range(6): xt[i*128:(i+1)*128,:]=hlow[:,i*128:(i+1)*128].T
    away(xt,ht_o)
    def chunk_copy(c):
        lane=pl.ds(pl.multiple_of(c*D,128),D)
        return pltpu.make_async_copy(act.at[:,lane],act_o.at[:,lane],osem.at[5,c])
    def chunk(c,carry):
        lane=pl.ds(pl.multiple_of(c*D,128),D)
        bias=p_ref[pl.ds(3+c,1),:]
        for tl in range(4):
            rows=pl.ds(tl*256,256)
            inner=dot(hlow[rows,:],W(4+2*c))+bias
            a,g=gelu_both(inner)
            al=a.astype(bf16)
            act[rows,lane]=al
            gp[rows,lane]=g.astype(bf16)
            y=dot(al,W(5+2*c))
            @pl.when(c==0)
            def _(): acc[rows,:]=y
            @pl.when(c>0)
            def _(): acc[rows,:]+=y
        chunk_copy(c).start()
        @pl.when(c<3)
        def _(): tick(9+c)
        @pl.when(c==2)
        def _(): tick(12)
        @pl.when(c==2)
        def _(): lax.fori_loop(0,NB,lambda i,a: (stats.move(i,True),a)[1],0)
        return carry
    lax.fori_loop(0,4,chunk,0)
    pltpu.make_async_copy(cot_ref,out,lsem.at[20]).start()
    pltpu.make_async_copy(cot_ref,out,lsem.at[20]).wait()
    def tile_copies(tl):
        rows=pl.ds(pl.multiple_of(tl*TT,TT),TT)
        return [pltpu.make_async_copy(s.at[rows],d.at[rows],osem.at[i,tl]) for i,(s,d) in enumerate(((out,out_o),(gp,din_o),(dffn,dffn_o),(acc,dz1_o),(dctx,dctx_o)))]
    def tile(tl,carry):
        rows=pl.ds(pl.multiple_of(tl*TT,TT),TT)
        n1t=n1[rows,:]
        z=(n1t*g1+s1)+(acc[rows,:]+p_ref[7:8,:])
        n2,r2=layer_norm(z)
        e=out[rows,:].astype(f32)
        out[rows,:]=(n2*g2+s2).astype(bf16)
        c2=e*g2
        dz2=r2*(c2-jnp.mean(c2,axis=-1,keepdims=True)-n2*jnp.mean(c2*n2,axis=-1,keepdims=True))
        df=dz2.astype(bf16)
        dffn[rows,:]=df
        vec_o[10:11,:]+=jnp.sum(e*n2,axis=0,keepdims=True)
        vec_o[11:12,:]+=jnp.sum(e,axis=0,keepdims=True)
        vec_o[7:8,:]+=jnp.sum(df.astype(f32),axis=0,keepdims=True)
        dh=dz2
        for c in range(4):
            lane=pl.ds(c*D,D)
            dact=dot(df,W(5+2*c),1,1)
            din=(dact*gp[rows,lane].astype(f32)).astype(bf16)
            gp[rows,lane]=din
            vec_o[3+c:4+c,:]+=jnp.sum(din.astype(f32),axis=0,keepdims=True)
            dh=dh+dot(din,W(4+2*c),1,1)
        vec_o[8:9,:]+=jnp.sum(dh*n1t,axis=0,keepdims=True)
        vec_o[9:10,:]+=jnp.sum(dh,axis=0,keepdims=True)
        c1=dh*g1
        dz1=r1[rows,0:1]*(c1-jnp.mean(c1,axis=-1,keepdims=True)-n1t*jnp.mean(c1*n1t,axis=-1,keepdims=True))
        acc[rows,:]=dz1
        dat=dz1.astype(bf16)
        vec_o[2:3,:]+=jnp.sum(dat.astype(f32),axis=0,keepdims=True)
        dctx[rows,:]=dot(dat,W(3),1,1).astype(bf16)
        for c in tile_copies(tl): c.start()
        return carry
    lax.fori_loop(0,PACK//TT,tile,0)
    for c in copies: c.wait()
    for p in (4,5):
        for c in pair_copies(p): c.wait()
    for i in range(4):
        chunk_copy(i).wait()
    for i in range(PACK//TT):
        for c in tile_copies(i): c.wait()
    first.wait_send(); other.wait_send()
    for i in range(NG): on_group(i,lambda g: g.done())
    stats.done()

def call_front(lengths,x,cot,masters,pv,left):
    V=pltpu.VMEM; S=jax.ShapeDtypeStruct; A=pl.ANY
    B=lambda m: pl.BlockSpec(memory_space=m)
    sem=pltpu.SemaphoreType.DMA
    T=lambda w,d: S((PACK,w),d)
    return pl.pallas_call(front_body,
        in_specs=[B(pltpu.SMEM),B(V),B(A),B(V),B(V),B(A)],
        out_specs=[B(A)]*13+[B(V),B(A)],
        out_shape=[T(D,bf16)]+[S((6,2,PACK,128),bf16)]*2+[T(D,bf16)]*2+[T(FF,bf16),T(FF,bf16),T(D,bf16),S((D,PACK),bf16),T(D,f32),T(D,bf16),S((3,4,4,MR,D),bf16),S((D,PACK),bf16),S((16,D),f32),S((32,24,D),f32)],
        scratch_shapes=[V((NB,4,4,MR,D),bf16),V((4,4,16,D),bf16),V((16,D),f32),V((NB,24,HC),f32)]+[V((PACK,D),bf16)]*4+
            [V((PACK,128),jnp.int32),V((2,2,PACK,128),bf16),V((2,2,PACK,128),bf16),V((2,PACK,128),bf16),V((PACK,D),f32),V((PACK,128),f32),V((PACK,D),bf16),V((PACK,D),f32),
             V((PACK,FF),bf16),V((PACK,FF),bf16),V((PACK,D),bf16),V((PACK,D),bf16),V((PACK,D),bf16),V((D,PACK),bf16),
             sem((13,11)),sem((13,11)),sem((2,)),sem((2,)),sem((NB,)),sem,sem((24,)),sem((2,2)),sem((6,4))],
        compiler_params=pltpu.CompilerParams(vmem_limit_bytes=63<<20,collective_id=0,has_side_effects=True))(lengths,x,cot,masters,pv,left)


NGR=12
def sum_scratch():
    V=pltpu.VMEM; nb=NGR
    return dict(rc=V((nb,4,4,MR,HC),bf16),xa=V((nb,2,2,MR,HC),bf16),yb=V((nb,2,2,MR,HC),bf16),
        s2a=V((nb,2,MR,HC),bf16),s2b=V((nb,2,MR,HC),bf16),ya=V((nb,2,MR,HC),bf16),xb=V((nb,2,MR,HC),bf16),
        s3=V((nb,4,MR,HC),bf16),zr=V((nb,3,MR,HC),bf16),fin=V((nb,MR,HC),f32),finb=V((nb,MR,HC),bf16),hr=V((nb,24,HC),f32))
SKEYS=list(sum_scratch())

class GroupSum:
    def __init__(self,pc,g_ref,R,out_ref,gown_ref,ss,rs,os_,orr):
        self.pc,self.gr,self.RR,self.out,self.gown=pc,g_ref,R,out_ref,gown_ref
        self.ss,self.rs,self.os_,self.orr=ss,rs,os_,orr
    def mk(self,g,i,src,dst,dev): return rcopy(src,dst,self.ss.at[g,i],self.rs.at[g,i],dev)
    def of(self,g): return self.gr.at[g],{k:v.at[g] for k,v in self.RR.items()}
    def core(self,g):
        G,R=self.of(g); return self.mk(g,0,G.at[:,:,:,self.pc.ocols],R["rc"],self.pc.sib)
    def xa(self,g):
        G,R=self.of(g); pc=self.pc; return self.mk(g,1,G.at[pl.ds(0,2),pl.ds((1-pc.x)*2,2),:,pc.cols],R["xa"],pc.xn)
    def yb(self,g,i):
        G,R=self.of(g); pc=self.pc; return self.mk(g,2+i,G.at[pl.ds(2,2),i*2+1-pc.y,:,pc.cols],R["yb"].at[i],pc.yn)
    def ya(self,g):
        G,R=self.of(g); return self.mk(g,4,R["s2a"],R["ya"],self.pc.yn)
    def xb(self,g):
        G,R=self.of(g); return self.mk(g,5,R["s2b"],R["xb"],self.pc.xn)
    def zz(self,g,k):
        G,R=self.of(g); pc=self.pc; return self.mk(g,5+k,R["s3"].at[(pc.z+k)%NZ],R["zr"].at[k-1],pc.zpeer(k))
    def home(self,g):
        G,R=self.of(g); pc=self.pc; return self.mk(g,9,R["fin"].at[pl.ds(pl.multiple_of((1-pc.c)*24,8),24)],R["hr"],pc.sib)
    def step0(self,g): self.core(g).start()
    def step1(self,g):
        pc=self.pc; G,R=self.of(g)
        self.core(g).wait_recv()
        for z in range(4):
            G[z,:,:,pc.cols]=(G[z,:,:,pc.cols].astype(f32)+R["rc"][z].astype(f32)).astype(bf16)
        self.xa(g).start()
        for i in range(2): self.yb(g,i).start()
    def step2(self,g):
        pc=self.pc; G,R=self.of(g)
        self.xa(g).wait_recv()
        R["s2a"][...]=(G[0:2,pc.x*2+1-pc.y,:,pc.cols].astype(f32)+R["xa"][:,1-pc.y].astype(f32)).astype(bf16)
        self.ya(g).start()
        for i in range(2): self.yb(g,i).wait_recv()
        R["s2b"][...]=(G[2:4,(1-pc.x)*2+pc.y,:,pc.cols].astype(f32)+R["yb"][1-pc.x].astype(f32)).astype(bf16)
        self.xb(g).start()
    def step3(self,g):
        pc=self.pc; G,R=self.of(g)
        self.ya(g).wait_recv(); self.xb(g).wait_recv()
        a=G[0:2,pc.xy,:,pc.cols].astype(f32)+R["xa"][:,pc.y].astype(f32)+R["ya"][...].astype(f32)
        b=G[2:4,pc.xy,:,pc.cols].astype(f32)+R["yb"][pc.x].astype(f32)+R["xb"][...].astype(f32)
        R["s3"][0:2]=a.astype(bf16); R["s3"][2:4]=b.astype(bf16)
        ab=jnp.where(pc.z%2==0,jnp.stack([a[0],b[0]]),jnp.stack([a[1],b[1]]))
        R["fin"][...]=jnp.where(pc.z<2,ab[0],ab[1])
        for k in (1,2,3): self.zz(g,k).start()
    def targets(self,g,act):
        pc=self.pc; G,R=self.of(g)
        def whole(b):
            act(R["finb"],self.gown.at[pc.chip],0,owner_of(b))
        def slab(j):
            for i in range(3):
                act(R["finb"].at[:,pl.ds(i*128,128)],self.gown.at[pc.chip,:,pl.ds(pl.multiple_of(j*128,128),128)],i,owner_of(i))
        if isinstance(g,int):
            if g<9: whole(8+g//2-4*(g%2)-9*(g//8))
            else: slab(g-9)
        else:
            @pl.when(g<9)
            def _(): whole(8+g//2-4*(g%2)-9*(g//8))
            @pl.when(g>=9)
            def _(): slab(g-9)
    def step4(self,g):
        pc=self.pc; G,R=self.of(g)
        for k in (1,2,3): self.zz(g,k).wait_recv()
        s=R["fin"][...]
        for k in range(3): s=s+R["zr"][k].astype(f32)
        R["fin"][...]=s
        R["finb"][...]=s.astype(bf16)
        self.home(g).start()
        def send(src,dst,i,t):
            mine=pc.chip==t
            @pl.when(mine)
            def _(): pltpu.make_async_copy(src,dst,self.orr).start()
            @pl.when(jnp.logical_not(mine))
            def _(): rcopy(src,dst,self.os_.at[g,i],self.orr,(t//2,(t%2)*2+pc.c)).start()
        self.targets(g,send)
    def step5(self,g):
        pc=self.pc; G,R=self.of(g)
        self.home(g).wait_recv()
        def whole(b):
            self.out[b,:,pc.cols]=R["fin"][pl.ds(pl.multiple_of(pc.c*24,8),24)]
            self.out[b,:,pc.ocols]=R["hr"][...]
        def slab(j):
            for i in range(3):
                self.out[i,:,pl.ds(pl.multiple_of((pc.c*3+j)*128,128),128)]=R["fin"][pl.ds(pl.multiple_of(pc.c*24,8),24),i*128:(i+1)*128]
                self.out[i,:,pl.ds(pl.multiple_of(((1-pc.c)*3+j)*128,128),128)]=R["hr"][:,i*128:(i+1)*128]
        if isinstance(g,int):
            if g<9: whole(8+g//2-4*(g%2)-9*(g//8))
            else: slab(g-9)
        else:
            @pl.when(g<9)
            def _(): whole(8+g//2-4*(g%2)-9*(g//8))
            @pl.when(g>=9)
            def _(): slab(g-9)
    def done(self,g):
        pc=self.pc
        for d in (self.core,self.xa,self.ya,self.xb,self.home): d(g).wait_send()
        for i in range(2): self.yb(g,i).wait_send()
        for k in (1,2,3): self.zz(g,k).wait_send()
        def wait(src,dst,i,t):
            @pl.when(pc.chip!=t)
            def _(): rcopy(src,dst,self.os_.at[g,i],self.orr,(t//2,(t%2)*2+pc.c)).wait_send()
        self.targets(g,wait)

KB_=512
PACE={1:(("step1",0),),5:(("step1",1),),7:(("step2",0),)}
def prepare_pair(p,v,ctx,do,doa,va):
    cols=pl.ds(pl.multiple_of(p*128,128),128)
    lane=lax.broadcasted_iota(jnp.int32,(256,128),1)
    i=lax.broadcasted_iota(jnp.int32,(128,128),0); j=lax.broadcasted_iota(jnp.int32,(128,128),1)
    cross=jnp.where((i<64)!=(j<64),-1.0,0.0).astype(bf16)
    for t in range(PACK//256):
        rows=pl.ds(t*256,256)
        vp=v[rows,cols].astype(f32)
        dop=do[rows,cols].astype(f32); prod=dop*ctx[rows,cols].astype(f32)
        dd=sum(dot(c.astype(bf16),cross) for c in split3(prod))
        parts=split3(dd)
        for h,lo in enumerate((True,False)):
            keep=(lane<64)==lo
            off=64 if lo else 0
            d1=jnp.where(keep,dop,0.0)
            for n,c in enumerate(parts): d1=jnp.where(lane==off+n,c,d1)
            doa[h,rows,:]=d1.astype(bf16)
            v1=jnp.where(keep,vp,0.0)
            va[h,rows,:]=jnp.where((lane>=off)&(lane<off+3),1.0,v1).astype(bf16)

def back_block(p,b,dk_ref,dv_ref,qa,doa,ka,va,dqa):
    cols=pl.ds(pl.multiple_of(p*128,128),128)
    rows=pl.ds(pl.multiple_of(b*KB_,KB_),KB_)
    low=lax.broadcasted_iota(jnp.int32,(KB_,128),1)<64
    lowq=lax.broadcasted_iota(jnp.int32,(PACK,128),1)<64
    r=[]
    for h in range(2):
        kh=ka[h,rows,:]
        pr=jnp.exp(dot(kh,qa[h],1,1))
        dp=dot(va[h,rows,:],doa[h],1,1)
        ds=(pr*dp).astype(bf16)
        r.append((dot(pr.astype(bf16),doa[h]),dot(ds,qa[h]),dot(ds,kh,0,0)))
    dq=jnp.where(lowq,r[0][2],r[1][2])
    @pl.when(b==0)
    def _(): dqa[...]=dq
    @pl.when(b>0)
    def _(): dqa[...]+=dq
    dv_ref[rows,cols]=jnp.where(low,r[0][0],r[1][0]).astype(bf16)
    dk_ref[rows,cols]=jnp.where(low,r[0][1],r[1][1]).astype(bf16)

def back_body(xt_ref,qa_i,ka_i,v_i,ctx_i,do_i,act_i,din_i,dffn_i,ht_i,dz1_i,wq_i,vec_ref,right_ref,
              ig_o,out_ref,vcur,gown_ref,st_ref,*rest):
    R=dict(zip(SKEYS,rest[:len(SKEYS)]))
    (g_ref,ctx,w_last,act,din,dffn,ht,acc,qa,doa,ka,va,dqa,
     ss,rs,os_,orr,ts,tr,lsem,asem)=rest[len(SKEYS):]
    pc=Place()
    loads={}
    def load(name,src,dst):
        c=pltpu.make_async_copy(src,dst,lsem.at[len(loads)]); c.start(); loads[name]=c
    half=lambda ref,c: ref.at[:,pl.ds(c*D,D)]
    load("act0",half(act_i,0),act.at[0]); load("dffn",dffn_i,dffn)
    load("hlow",ht_i,ht); load("din0",half(din_i,0),din.at[0])
    load("act1",half(act_i,1),act.at[1]); load("din1",half(din_i,1),din.at[1])
    for n,s,d in (("acc",dz1_i,acc),("ctx",ctx_i,ctx)): load(n,s,d)
    q,v,do,k=act.at[0],din.at[0],dffn,act.at[1]
    late={5:("v",v_i,v),7:("do",do_i,do)}
    def pair_loads(pi):
        return [pltpu.make_async_copy(s.at[pi],d.at[pi%2],asem.at[i,pi%2]) for i,(s,d) in enumerate(((qa_i,qa),(ka_i,ka)))]
    for c in pair_loads(0): c.start()
    greet_all(pc)
    gs=GroupSum(pc,g_ref,R,out_ref,gown_ref,ss,rs,os_,orr)
    stats=StatMove(pc,right_ref,st_ref,1,ts,tr)
    def product(g,a,b):
        for r in range(4):
            g_ref[g,r]=dot(a[:,r*192:(r+1)*192],b,0,0).astype(bf16).reshape(4,MR,D)
    lax.fori_loop(0,NB,lambda i,a: (stats.move(i,True),a)[1],0)
    loads["dffn"].wait()
    for i in range(9):
        c=i//2
        if i==8:
            loads["ctx"].wait(); loads["acc"].wait()
            product(i,ctx,acc[...].astype(bf16))
        elif i%2==0:
            loads[f"act{c}"].wait()
            product(i,act.at[c%2],dffn[...])
            if c<2: load(f"act{c+2}",half(act_i,c+2),act.at[c%2])
        else:
            if c==0: loads["hlow"].wait()
            loads[f"din{c}"].wait()
            for r in range(4): g_ref[i,r]=dot(ht[r*192:(r+1)*192,:],din[c%2]).astype(bf16).reshape(4,MR,D)
            if c<2: load(f"din{c+2}",half(din_i,c+2),din.at[c%2])
        if i in late: load(*late[i])
        gs.step0(i)
        for s,g in PACE.get(i,()): getattr(gs,s)(g)
    wrow=pl.ds(0,D)
    wdst=[din.at[1,wrow],ht.at[:,pl.ds(0,D)],w_last]
    for i in range(3): load(f"w{i}",wq_i.at[i],wdst[i])
    for n in ("v","do"): loads[n].wait()
    def slot(n,carry):
        pi=n//2; b=n%2; j=pi//2; cc=pi%2; p=3*cc+j; side=pi%2
        cols=pl.ds(pl.multiple_of(p*128,128),128)
        @pl.when(b==0)
        def _():
            for c in pair_loads(pi): c.wait()
            @pl.when(pi<5)
            def _():
                for c in pair_loads(pi+1): c.start()
            prepare_pair(p,v,ctx,do,doa,va)
        back_block(p,b,k,v,qa.at[side],doa,ka.at[side],va,dqa)
        @pl.when(b==1)
        def _():
            q[:,cols]=(dqa[...]*0.125).astype(bf16)
            al=jnp.concatenate([q[:,cols],k[:,cols],v[:,cols]],axis=1)
            lane=pl.ds(pl.multiple_of(cc*HC,128),HC)
            for r in range(4):
                g_ref[9+j,r,:,:,lane]=dot(xt_ref[r*192:(r+1)*192,:],al).astype(bf16).reshape(4,MR,HC)
            vcur[0:1,cols]=jnp.sum(q[:,cols].astype(f32),axis=0,keepdims=True)
            vcur[1:2,cols]=jnp.sum(v[:,cols].astype(f32),axis=0,keepdims=True)
        @pl.when(n<=8)
        def _(): gs.step1(2+n)
        @pl.when(n<=9)
        def _(): gs.step2(1+n)
        @pl.when(n<=10)
        def _(): gs.step3(n)
        @pl.when(n>=1)
        def _(): gs.step4(n-1)
        @pl.when(n>=2)
        def _(): gs.step5(n-2)
        @pl.when((n==3)|(n==7))
        def _(): gs.step0(9+n//7)
        return carry
    vcur[...]=vec_ref[...]
    lax.fori_loop(0,12,slot,0)
    gs.step0(11)
    for i in range(3): loads[f"w{i}"].wait()
    def grad_tile(t):
        rows=pl.ds(t*256,256)
        a=acc[rows,:]
        for j,w in enumerate(wdst):
            d=jnp.concatenate([t[rows,(3*c+j)*128:(3*c+j+1)*128] for c in range(2) for t in (q,k,v)],axis=1)
            a=a+dot(d,w[...],1,1)
        acc[rows,:]=a
    grad_tile(0)
    gs.step5(10); gs.step1(11)
    grad_tile(1); grad_tile(2)
    gs.step2(11); grad_tile(3)
    away=pltpu.make_async_copy(acc,ig_o,lsem.at[31]); away.start()
    gs.step3(11)
    gs.step4(11)
    gs.step5(11)
    lax.fori_loop(0,NGR,lambda g,c: (gs.done(g),c)[1],0)
    away.wait()
    stats.done()
    @pl.when(pc.xy<3)
    def _(): pltpu.make_async_copy(gown_ref,gown_ref,orr).wait()

def call_back(xt,qa,ka,v,ctx,dctx,act,din,dffn,ht,dz1,wq,vec,right):
    V=pltpu.VMEM; S=jax.ShapeDtypeStruct; A=pl.ANY
    B=lambda m: pl.BlockSpec(memory_space=m)
    sem=pltpu.SemaphoreType.DMA
    T=V((PACK,D),bf16); H=V((2,PACK,128),bf16)
    return pl.pallas_call(back_body,
        in_specs=[B(V)]+[B(A)]*11+[B(V),B(A)],
        out_specs=[B(A),B(V),B(V),B(A),B(A)],
        out_shape=[S((PACK,D),f32),S((NB,24,D),f32),S((16,D),f32),S((16,MR,HC),bf16),S((32,24,D),f32)],
        scratch_shapes=list(sum_scratch().values())+[V((NGR,4,4,MR,D),bf16),T,V((D,D),bf16)]+[V((2,PACK,D),bf16),V((2,PACK,D),bf16),T,V((D,PACK),bf16),V((PACK,D),f32)]+[V((2,2,PACK,128),bf16),H,V((2,2,PACK,128),bf16),H]+
            [V((PACK,128),f32),sem((NGR,10)),sem((NGR,10)),sem((NGR,3)),sem,sem((NB,)),sem,sem((32,)),sem((2,2))],
        compiler_params=pltpu.CompilerParams(vmem_limit_bytes=63<<20,collective_id=1,has_side_effects=True))(xt,qa,ka,v,ctx,dctx,act,din,dffn,ht,dz1,wq,vec,right)


def gather_rows(a):
    return lax.all_gather(a,("dp","head"),axis=1,tiled=True)

def doc_lengths(lengths):
    return lax.dynamic_slice_in_dim(lengths,lax.axis_index("head"),1,axis=0)

def layer(tokens,cotangent,lengths,w,params):
    q,k,v,ctx,lse,n1,r1=call_a(lengths,tokens,w,params)
    out,dz1,dctx,dwo,dw1,dw2,vec=call_b(cotangent,n1,r1,ctx,w,params)
    ig,dwqkv,vq=call_c(lengths,tokens,q,k,v,ctx,dctx,lse,dz1,w)
    terms=jnp.concatenate([dwqkv,dwo[None],dw1,dw2],axis=0)
    vec=jnp.concatenate([vq[0:1],vq[2:3],vec[2:]],axis=0)
    return out,ig,terms,vec

def on_slice(tokens,cotangent,lengths,masters,vectors,left,right,second):
    pv=jnp.pad(vectors,((0,4),(0,HC-24))).astype(bf16)
    lens=doc_lengths(lengths)
    out,qa,ka,v,ctx,act,din,dffn,ht,dz1,dctx,wq,xt,vec,statl=call_front(lens,tokens,cotangent,masters,pv,left)
    ig,grads,vec,gown,statr=call_back(xt,qa,ka,v,ctx,dctx,act,din,dffn,ht,dz1,wq.reshape(3,D,D),vec,right)
    ln,rn,mn,vg,sn,vn=call_newton_step(gown.reshape(D,HC),statl.reshape(D,D),statr.reshape(D,D),left,right,masters,vec,vectors,second)
    return out,ig,grads,ln,rn,mn,vg,sn,vn

def on_any(tokens,cotangent,lengths,masters,vectors,left,right,second):
    axes=("dp","head")
    me=lax.axis_index("dp")*lax.axis_size("head")+lax.axis_index("head")
    share=masters.shape[1]
    w=gather_rows(masters.astype(bf16))
    params=gather_rows(vectors.astype(bf16)).astype(f32)
    out,ig,terms,vec=layer(tokens,cotangent,doc_lengths(lengths),w,params)
    grads=lax.psum_scatter(terms.astype(f32),axes,scatter_dimension=1,tiled=True)
    vg=lax.psum_scatter(vec[:12],axes,scatter_dimension=1,tiled=True)
    low=grads.astype(bf16)
    g=gather_rows(low)
    ein=partial(jnp.einsum,preferred_element_type=f32)
    cols=lax.dynamic_slice_in_dim(g,me*share,share,axis=2)
    ln=BETA*left+(1-BETA)*ein("kid,kjd->kij",low,g)
    rn=BETA*right+(1-BETA)*ein("kdi,kdj->kij",cols,g)
    item=jnp.minimum(me,2*NB-1)
    own=lax.dynamic_index_in_dim(jnp.concatenate([gather_rows(ln),gather_rows(rn)],axis=0),item,0,keepdims=False)
    root=call_newton(own)
    place=jnp.where((jnp.arange(2*NB)==me)[:,None,None],root[None],0.0)
    rows=lax.psum_scatter(place,axes,scatter_dimension=1,tiled=True)
    rr=gather_rows(rows[NB:])
    hi=partial(jnp.einsum,"kij,kjl->kil",precision=lax.Precision.HIGHEST)
    mn=masters-RATE*hi(hi(rows[:NB],g.astype(f32)),rr)
    sn=BETA_TWO*second+(1-BETA_TWO)*vg*vg
    vn=vectors-RATE_VEC*vg/(jnp.sqrt(sn)+1e-8)
    return out,ig,grads,ln,rn,mn,vg,sn,vn

def solution(mesh):
    rows=P(("dp","head"),None); blocks=P(None,("dp","head"),None); vecs=P(None,("dp","head"))
    on_device=on_slice if dict(mesh.shape)=={"dp":8,"head":4} else on_any
    return jax.shard_map(on_device,mesh=mesh,
        in_specs=(rows,rows,P("dp",None),blocks,vecs,blocks,blocks,vecs),
        out_specs=(rows,rows,blocks,blocks,blocks,blocks,vecs,vecs,vecs),check_vma=False)
```
